32 devices in a mesh: left: 8 (over z, y), right: 4 (over x, core).
Axes of the slice: x: 2, y: 2, z: 4, core: 2. Of those that a mesh axis runs over, the one named last changes fastest.
Arguments:
- left_table: float32 [4096, 400], P(('left', 'right')), may hold values from -2 to 2
- left_state: float32 [4096], P(('left', 'right')), may hold values from 0.05 to 0.5
- right_table: float32 [4096, 400], P(('left', 'right')), may hold values from -2 to 2
- right_state: float32 [4096], P(('left', 'right')), may hold values from 0.05 to 0.5
- relation_table: float32 [256, 400], replicated, may hold values from -6 to 6
- relation_state: float32 [256], replicated, may hold values from 0.05 to 0.5
- source_ids: int32 [8, 4, 1024], P('left', 'right'), may hold values from 0 to 511
- target_ids: int32 [8, 4, 1024], P('left', 'right'), may hold values from 0 to 1023
- relation_ids: int32 [8, 4, 1024], P('left', 'right'), may hold values from 0 to 255
- negative_ids: int32 [8, 4, 2, 1024], P('left', 'right'), may hold values from 0 to 1023
Outputs:
- left_new: float32 [4096, 400], P(('left', 'right'))
- left_state_new: float32 [4096], P(('left', 'right'))
- right_new: float32 [4096, 400], P(('left', 'right'))
- right_state_new: float32 [4096], P(('left', 'right'))
- relation_new: float32 [256, 400], replicated
- relation_state_new: float32 [256], replicated
The draws below stay inside these ranges and needn't reach their ends.
All inputs are finite; a program needn't handle non-finite values.
Results may differ from the reference program's by a relative error of at most 0.0021.
Values may be sent and summed in bfloat16 or wider, within the bound.
No kernel may reach another device: no remote copies, remote signals or barrier semaphores. Data moves between devices by JAX's collectives and lax.ppermute only.
A program may use at most 64 MiB of HBM per device.

```python
import math
import jax
import jax.numpy as jnp
import numpy as np
from jax import lax

EMBED_WIDTH = 400
NREL = 256
ROWS = 128
EDGES = 1024
NEG = 1024
GROUPS = 2
LEFT_ROWS = 512
RIGHT_ROWS = 1024
ENTITIES = 4096
N_LEFT = 8
N_RIGHT = 4


def with_ends(values, own_key, low, top_value):
    extent = values.shape
    spot = [jax.random.randint(jax.random.fold_in(own_key, axis), (), 0, extent[axis]) for axis in range(len(extent))]
    values = values.at[tuple(spot)].set(low)
    longest = extent.index(max(extent))
    spot[longest] = (spot[longest] + 1) % extent[longest]
    return values.at[tuple(spot)].set(top_value)


def shard_levels(own_key, dims, split, least, high):
    factor_of = 1.0
    for dim, parts in split:
        steps = jax.random.uniform(jax.random.fold_in(jax.random.fold_in(own_key, 6), dim), (parts,), jnp.float32, least / len(split), high / len(split))
        factor_of = factor_of * jnp.repeat(jnp.exp(steps), dims[dim] // parts).reshape((-1,) + (1,) * (len(dims) - 1 - dim))
    return factor_of


def rank_table(amount, slope):
    loads = [(1 << 20) // math.isqrt(grade ** slope) + 1 for grade in range(1, amount + 1)]
    spread = 1 + sum(loads) // (1 << 30)
    return np.cumsum(np.array([max(1, weight // spread) for weight in loads]))


def skewed_ids(own_key, shape, amount, lean):
    table = rank_table(amount, lean)
    ticket = jax.random.randint(jax.random.fold_in(own_key, 1), shape, 0, int(table[amount - 1]))
    rank = jnp.searchsorted(jnp.asarray(table, jnp.int32), ticket, side="right")
    return jax.random.permutation(jax.random.fold_in(own_key, 2), amount)[rank].astype(jnp.int32)


def bell_draw(rng, extent, scale, bound, shards=(), kind=jnp.bfloat16):
    entries = jax.random.normal(rng, extent, jnp.float32) * scale
    if len(shards) > 0:
        entries = shard_levels(rng, extent, shards, -0.22, 0.18) * entries
    return jnp.clip(entries, min=-bound, max=bound).astype(kind)


def setup_inputs(seed: int = 0) -> dict:
    key_list = jax.random.split(jax.random.key(seed), 11)
    return {
        "left_table": bell_draw(key_list[0], (ENTITIES, EMBED_WIDTH), 0.3, 2.0, ((0, 32),), jnp.float32),
        "left_state": jnp.clip(jnp.exp(math.log(0.5) - 2.3025851 * jax.random.uniform(key_list[1], (ENTITIES,), jnp.float32) ** shard_levels(key_list[1], (ENTITIES,), ((0, 32),), -0.2, 0.2)), 0.05, 0.5),
        "right_table": bell_draw(key_list[2], (ENTITIES, EMBED_WIDTH), 0.3, 2.0, ((0, 32),), jnp.float32),
        "right_state": jnp.clip(jnp.exp(math.log(0.5) - 2.3025851 * jax.random.uniform(key_list[3], (ENTITIES,), jnp.float32) ** shard_levels(key_list[3], (ENTITIES,), ((0, 32),), -0.2, 0.2)), 0.05, 0.5),
        "relation_table": bell_draw(key_list[4], (NREL, EMBED_WIDTH), 1.0, 6.0, (), jnp.float32),
        "relation_state": jnp.clip(jnp.exp(jax.random.uniform(key_list[5], (NREL,), jnp.float32, math.log(0.05), math.log(0.5))), 0.05, 0.5),
        "source_ids": with_ends(jax.random.randint(key_list[6], (N_LEFT, N_RIGHT, EDGES), 0, LEFT_ROWS), jax.random.fold_in(key_list[6], 1), 0, LEFT_ROWS - 1).astype(jnp.int32),
        "target_ids": with_ends(jax.random.randint(key_list[7], (N_LEFT, N_RIGHT, EDGES), 0, RIGHT_ROWS), jax.random.fold_in(key_list[7], 1), 0, RIGHT_ROWS - 1).astype(jnp.int32),
        "relation_ids": with_ends(skewed_ids(key_list[8], (N_LEFT, N_RIGHT, EDGES), NREL, 2), jax.random.fold_in(key_list[8], 3), 0, NREL - 1).astype(jnp.int32),
        "negative_ids": with_ends(jax.random.randint(key_list[9], (N_LEFT, N_RIGHT, GROUPS, NEG), 0, RIGHT_ROWS), jax.random.fold_in(key_list[9], 1), 0, RIGHT_ROWS - 1).astype(jnp.int32),
    }


LEARN_RATE = 0.1
NEG_WEIGHT = 0.03125

def complex_product(first, second):
    half_width = first.shape[-1] // 2
    a_re, a_im = (first[..., :half_width], first[..., half_width:])
    b_re, b_im = (second[..., :half_width], second[..., half_width:])
    return jnp.concatenate([a_re * b_re - a_im * b_im, a_re * b_im + a_im * b_re], axis=-1)

def complex_back(grad, other):
    half_width = grad.shape[-1] // 2
    g_re, g_im = (grad[..., :half_width], grad[..., half_width:])
    o_re, o_im = (other[..., :half_width], other[..., half_width:])
    return jnp.concatenate([g_re * o_re + g_im * o_im, g_im * o_re - g_re * o_im], axis=-1)

def bucket_grads(left_part, right_part, relation_bf, source, target, relation, negative):
    source_emb = left_part[source].astype(jnp.float32)
    target_embedding = right_part[target].astype(jnp.float32)
    relation_emb = relation_bf[relation].astype(jnp.float32)
    query = complex_product(source_emb, relation_emb)
    positive = lax.optimization_barrier(jnp.sum(query * target_embedding, axis=-1))
    query_bf = query.astype(jnp.bfloat16)
    groups = negative.shape[0]
    query_block_rows = query_bf.reshape(groups, -1, EMBED_WIDTH).astype(jnp.float32)
    negative_rows = right_part[negative].astype(jnp.float32)
    score_matrix = jnp.einsum('wet,wjt->wej', query_block_rows, negative_rows)
    positive_score_grad = -jax.nn.sigmoid(-positive)
    negative_score_grad = (NEG_WEIGHT * jax.nn.sigmoid(score_matrix)).astype(jnp.bfloat16).astype(jnp.float32)
    query_gradient = positive_score_grad[:, None] * target_embedding + jnp.einsum('fjs,fsh->fjh', negative_score_grad, negative_rows).reshape(-1, EMBED_WIDTH)
    negative_embedding_grad = jnp.einsum('fre,frl->fel', negative_score_grad, query_block_rows).astype(jnp.bfloat16)
    target_grad = (positive_score_grad[:, None] * query).astype(jnp.bfloat16)
    source_grad = complex_back(query_gradient, relation_emb).astype(jnp.bfloat16)
    relation_grad = complex_back(query_gradient, source_emb).astype(jnp.bfloat16)
    left_term = jnp.zeros((left_part.shape[0], EMBED_WIDTH), jnp.float32).at[source].add(source_grad.astype(jnp.float32))
    all_ids = jnp.concatenate([target, negative.reshape(-1)])
    all_grads = jnp.concatenate([target_grad, negative_embedding_grad.reshape(-1, EMBED_WIDTH)], axis=0).astype(jnp.float32)
    right_term = jnp.zeros((right_part.shape[0], EMBED_WIDTH), jnp.float32).at[all_ids].add(all_grads)
    relation_term = jnp.zeros((NREL, EMBED_WIDTH), jnp.float32).at[relation].add(relation_grad.astype(jnp.float32))
    return (left_term, right_term, relation_term)

def adagrad(table, state, grad):
    state_new = state + lax.optimization_barrier(jnp.mean(grad * grad, axis=-1))
    return (table - LEARN_RATE * grad / jnp.sqrt(state_new)[:, None], state_new)

def reference(left_table, left_state, right_table, right_state, relation_table, relation_state, source_ids, target_ids, relation_ids, negative_ids):
    left_bf = left_table.astype(jnp.bfloat16).reshape(N_LEFT, N_RIGHT * ROWS, EMBED_WIDTH)
    right_bf = right_table.astype(jnp.bfloat16).reshape(N_LEFT, N_RIGHT, ROWS, EMBED_WIDTH)
    right_bf = right_bf.transpose(1, 0, 2, 3).reshape(N_RIGHT, N_LEFT * ROWS, EMBED_WIDTH)
    relation_bf = relation_table.astype(jnp.bfloat16)

    def visit(carry, index):
        left_acc, right_acc, relation_acc = carry
        row_index = index // N_RIGHT
        column = index % N_RIGHT
        partner = (column + N_RIGHT - 1) % N_RIGHT
        terms = bucket_grads(left_bf[row_index], right_bf[partner], relation_bf, source_ids[row_index, column], target_ids[row_index, column], relation_ids[row_index, column], negative_ids[row_index, column])
        return ((left_acc.at[row_index].add(terms[0]), right_acc.at[partner].add(terms[1]), relation_acc + terms[2]), None)
    start_carry = (jnp.zeros((N_LEFT, N_RIGHT * ROWS, EMBED_WIDTH), jnp.float32), jnp.zeros((N_RIGHT, N_LEFT * ROWS, EMBED_WIDTH), jnp.float32), jnp.zeros((NREL, EMBED_WIDTH), jnp.float32))
    (left_grad, right_grad, relation_grad), _ = lax.scan(visit, start_carry, jnp.arange(N_LEFT * N_RIGHT, dtype=jnp.int32))
    left_new, left_state_new = adagrad(left_table, left_state, left_grad.reshape(-1, EMBED_WIDTH))
    right_grad = right_grad.reshape(N_RIGHT, N_LEFT, ROWS, EMBED_WIDTH).transpose(1, 0, 2, 3).reshape(-1, EMBED_WIDTH)
    right_upd, right_state_upd = adagrad(right_table, right_state, right_grad)
    right_new = jnp.roll(right_upd.reshape(N_LEFT, N_RIGHT, ROWS, EMBED_WIDTH), 1, axis=1).reshape(-1, EMBED_WIDTH)
    right_state_new = jnp.roll(right_state_upd.reshape(N_LEFT, N_RIGHT, ROWS), 1, axis=1).reshape(-1)
    relation_new, relation_state_new = adagrad(relation_table, relation_state, relation_grad)
    return (left_new, left_state_new, right_new, right_state_new, relation_new, relation_state_new)
```

```python
import jax
import jax.numpy as jnp
from jax import lax
from jax.sharding import PartitionSpec as P

LEARN_RATE = 0.1
NEG_WEIGHT = 0.03125
BF = jnp.bfloat16
F32 = jnp.float32


def dot(a, b, a_dim, b_dim):
    return lax.dot_general(a, b, (((a_dim,), (b_dim,)), ((), ())), preferred_element_type=F32)


def complex_product(a, b):
    half = a.shape[0] // 2
    a_re, a_im, b_re, b_im = a[:half], a[half:], b[:half], b[half:]
    return jnp.concatenate([a_re * b_re - a_im * b_im, a_re * b_im + a_im * b_re], axis=0)


def complex_back(grad, other):
    half = grad.shape[0] // 2
    g_re, g_im, o_re, o_im = grad[:half], grad[half:], other[:half], other[half:]
    return jnp.concatenate([g_re * o_re + g_im * o_im, g_im * o_re - g_re * o_im], axis=0)


def adagrad(table, state, grad):
    state_new = state + jnp.mean(grad * grad, axis=0)
    return table - LEARN_RATE * grad * lax.rsqrt(state_new)[None, :], state_new


def one_hot(ids, count):
    return (jnp.arange(count, dtype=jnp.int32)[:, None] == ids[None, :]).astype(BF)


def build(mesh):
    n_left, n_right = mesh.shape["left"], mesh.shape["right"]
    inner = 2 if n_left % 2 == 0 else 1
    outer = n_left // inner

    def send_left(value, d_outer, d_inner):
        perm = []
        for i in range(n_left):
            o, n = i // inner, i % inner
            perm.append((i, (o + d_outer) % outer * inner + (n + d_inner) % inner))
        return lax.ppermute(value, "left", perm)

    def send_right(value, by):
        return lax.ppermute(value, "right", [(i, (i + by) % n_right) for i in range(n_right)])

    def send_both(value, d_outer, d_right):
        perm = []
        for i in range(n_left):
            for r in range(n_right):
                o, n = i // inner, i % inner
                to = (o + d_outer) % outer * inner + n
                perm.append((i * n_right + r, to * n_right + (r + d_right) % n_right))
        return lax.ppermute(value, ("left", "right"), perm)

    def per_device(
        left_table, left_state, right_table, right_state, relation_table, relation_state,
        source_ids, target_ids, relation_ids, negative_ids,
    ):
        rows = left_table.shape[0]
        width = left_table.shape[1]
        left_t, right_t, relation_t = left_table.T, right_table.T, relation_table.T
        nrel = relation_t.shape[1]
        here_l, here_r = lax.axis_index("left"), lax.axis_index("right")
        here_o, here_n = here_l // inner, here_l % inner
        source = source_ids.reshape(-1)
        target = target_ids.reshape(-1)
        relation = relation_ids.reshape(-1)
        negative = negative_ids.reshape(negative_ids.shape[2], negative_ids.shape[3])
        groups = negative.shape[0]

        right_bf = right_t.astype(BF)
        left_bf = left_t.astype(BF)
        near = [send_both(right_bf, k, 1) for k in range(outer)]
        left_blocks = [left_bf] + [send_right(left_bf, k) for k in range(1, n_right)]
        moved_t, moved_state = send_right((right_t, right_state), 1)
        right_blocks = list(near)
        for n in range(1, inner):
            right_blocks += [send_left(b, 0, n) for b in near]
        left_part = jnp.concatenate(left_blocks, axis=1)

        def local_left(ids):
            return (here_r - ids // rows) % n_right * rows + ids % rows

        def local_right(ids):
            block = ids // rows
            return ((here_n - block % inner) % inner * outer + (here_o - block // inner) % outer) * rows + ids % rows

        source = local_left(source)
        target = local_right(target)
        negative = local_right(negative)

        n_rows = n_left * rows
        counts = [
            jnp.sum((jnp.arange(n_rows, dtype=jnp.int32)[:, None] == negative[c][None, :]).astype(F32), axis=1)
            for c in range(groups)
        ]
        source_hot = one_hot(source, n_right * rows)
        relation_hot = one_hot(relation, nrel)
        source_emb = dot(left_part, source_hot, 1, 0)
        relation_emb = dot(relation_t.astype(BF), relation_hot, 1, 0)
        query = complex_product(source_emb, relation_emb)
        query_bf = query.astype(BF)

        right_part = jnp.concatenate(right_blocks, axis=1)
        scores = dot(right_part, query_bf, 0, 0)
        hit = jnp.arange(n_rows, dtype=jnp.int32)[:, None] == target[None, :]
        edges = scores.shape[1]
        weight = jnp.concatenate(
            [jnp.broadcast_to((NEG_WEIGHT * c)[:, None], (n_rows, edges // groups)) for c in counts], axis=1
        )
        grad_m = (weight * jax.nn.sigmoid(scores) - jnp.where(hit, jax.nn.sigmoid(-scores), 0.0)).astype(BF)
        right_grad = dot(query_bf, grad_m, 1, 1)
        if inner > 1:
            far = right_grad[:, outer * rows:].astype(BF)
            mine = right_grad[:, : outer * rows]
            mine = mine + send_left(far, 0, 1).astype(F32)
        else:
            mine = right_grad
        mine_bf = mine.astype(BF)
        right_sum = mine[:, :rows]
        for k in range(1, outer):
            right_sum = right_sum + send_left(mine_bf[:, k * rows:(k + 1) * rows], -k, 0).astype(F32)

        query_grad = dot(right_part, grad_m, 1, 0)
        relation_grad = complex_back(query_grad, source_emb).astype(BF)
        relation_term = dot(relation_hot, relation_grad, 1, 1)
        source_grad = complex_back(query_grad, relation_emb).astype(BF)
        left_grad = dot(source_grad, source_hot, 1, 1)
        left_sum = left_grad[:, :rows]
        left_grad_bf = left_grad.astype(BF)
        for k in range(1, n_right):
            left_sum = left_sum + send_right(left_grad_bf[:, k * rows:(k + 1) * rows], -k).astype(F32)

        rel_rows = nrel // n_left
        pieces = relation_term.reshape(n_left, rel_rows, width)
        pieces_bf = pieces.astype(BF)

        def left_shift(value, by):
            return lax.ppermute(value, "left", [(i, (i + by) % n_left) for i in range(n_left)])

        total = lax.dynamic_index_in_dim(pieces, here_l, 0, keepdims=False)
        for k in range(1, n_left):
            piece = lax.dynamic_index_in_dim(pieces_bf, (here_l + k) % n_left, 0, keepdims=False)
            total = total + left_shift(piece, k).astype(F32)
        total_bf = total.astype(BF)
        parts = [total_bf] + [send_right(total_bf, k) for k in range(1, n_right)]
        stack = jnp.stack(parts)
        order = (here_r - jnp.arange(n_right)) % n_right
        summed = jnp.sum(jnp.take(stack, order, axis=0).astype(F32), axis=0).astype(BF)
        got = [summed] + [left_shift(summed, k) for k in range(1, n_left)]
        where = (here_l - jnp.arange(n_left)) % n_left
        relation_total = jnp.take(jnp.stack(got), where, axis=0).reshape(nrel, width).astype(F32)

        left_new, left_state_new = adagrad(left_t, left_state, left_sum)
        right_new, right_state_new = adagrad(moved_t, moved_state, right_sum)
        relation_new, relation_state_new = adagrad(relation_t, relation_state, relation_total.T)
        return (left_new.T, left_state_new, right_new.T, right_state_new, relation_new.T, relation_state_new)

    return per_device


def solution(mesh):
    rows = P(("left", "right"), None)
    vector = P(("left", "right"))
    ids = P("left", "right", None)
    return jax.shard_map(
        build(mesh),
        mesh=mesh,
        in_specs=(rows, vector, rows, vector, P(), P(), ids, ids, ids, P("left", "right", None, None)),
        out_specs=(rows, vector, rows, vector, P(), P()),
        check_vma=False,
    )
```

```python
import jax
import jax.numpy as jnp
from jax import lax
from jax.sharding import PartitionSpec as P

LEARN_RATE = 0.1
NEG_WEIGHT = 0.03125
BF = jnp.bfloat16
F32 = jnp.float32


def dot(a, b, a_dim, b_dim):
    return lax.dot_general(a, b, (((a_dim,), (b_dim,)), ((), ())), preferred_element_type=F32)


def complex_product(a, b):
    half = a.shape[0] // 2
    a_re, a_im, b_re, b_im = a[:half], a[half:], b[:half], b[half:]
    return jnp.concatenate([a_re * b_re - a_im * b_im, a_re * b_im + a_im * b_re], axis=0)


def complex_back(grad, other):
    half = grad.shape[0] // 2
    g_re, g_im, o_re, o_im = grad[:half], grad[half:], other[:half], other[half:]
    return jnp.concatenate([g_re * o_re + g_im * o_im, g_im * o_re - g_re * o_im], axis=0)


def adagrad(table, state, grad):
    state_new = state + jnp.mean(grad * grad, axis=0)
    return table - LEARN_RATE * grad * lax.rsqrt(state_new)[None, :], state_new


def one_hot(ids, count):
    return (jnp.arange(count, dtype=jnp.int32)[:, None] == ids[None, :]).astype(BF)


def build(mesh):
    n_left, n_right = mesh.shape["left"], mesh.shape["right"]
    for count in (n_left, n_right):
        assert count & (count - 1) == 0 and count > 1
    outer = n_left // 2
    far_right = n_right // 2

    def swap_left(value, by):
        return lax.ppermute(value, "left", [(i, i ^ by) for i in range(n_left)])

    def swap_right(value, by):
        return lax.ppermute(value, "right", [(i, i ^ by) for i in range(n_right)])

    def next_column(value, by):
        perm = []
        for i in range(n_left):
            for r in range(n_right):
                perm.append((i * n_right + r, (i ^ by) * n_right + (r + 1) % n_right))
        return lax.ppermute(value, ("left", "right"), perm)

    def tree_sum(values):
        while len(values) > 1:
            values = [values[i] + values[i + 1] for i in range(0, len(values), 2)]
        return values[0]

    def per_device(
        left_table, left_state, right_table, right_state, relation_table, relation_state,
        source_ids, target_ids, relation_ids, negative_ids,
    ):
        rows = left_table.shape[0]
        width = left_table.shape[1]
        left_t, right_t, relation_t = left_table.T, right_table.T, relation_table.T
        nrel = relation_t.shape[1]
        here_l, here_r = lax.axis_index("left"), lax.axis_index("right")
        source = source_ids.reshape(-1)
        target = target_ids.reshape(-1)
        relation = relation_ids.reshape(-1)
        negative = negative_ids.reshape(negative_ids.shape[2], negative_ids.shape[3])
        groups = negative.shape[0]

        right_bf = right_t.astype(BF)
        near = {k: next_column(right_bf, 2 * k) for k in sorted(range(1, outer), key=lambda k: -k)}
        other = {0: next_column(right_bf, 1)}
        left_bf = left_t.astype(BF)
        half_left = [left_bf] + [swap_right(left_bf, 2 * k) for k in range(1, far_right)]
        half_left = jnp.concatenate(half_left, axis=1)
        moved = next_column(jnp.concatenate([right_t, right_state[None, :]], axis=0), 0)
        moved_t, moved_state = moved[:width], moved[width]
        near[0] = moved_t.astype(BF)
        left_part = jnp.concatenate([half_left, swap_right(half_left, 1)], axis=1)
        for k in range(1, outer):
            other[k] = swap_left(near[k], 1)
        right_blocks = [near[k] for k in range(outer)] + [other[k] for k in range(outer)]

        def local(ids, here, half):
            block = (ids // rows) ^ here
            return (block % 2 * half + block // 2) * rows + ids % rows

        source = local(source, here_r, far_right)
        target = local(target, here_l, outer)
        negative = local(negative, here_l, outer)

        n_rows = n_left * rows
        counts = [
            jnp.sum((jnp.arange(n_rows, dtype=jnp.int32)[:, None] == negative[c][None, :]).astype(F32), axis=1)
            for c in range(groups)
        ]
        source_hot = one_hot(source, n_right * rows)
        relation_hot = one_hot(relation, nrel)
        source_emb = dot(left_part, source_hot, 1, 0)
        relation_emb = dot(relation_t.astype(BF), relation_hot, 1, 0)
        query = complex_product(source_emb, relation_emb)
        query_bf = query.astype(BF)

        right_part = jnp.concatenate(right_blocks, axis=1)
        scores = dot(right_part, query_bf, 0, 0)
        hit = jnp.arange(n_rows, dtype=jnp.int32)[:, None] == target[None, :]
        edges = scores.shape[1]
        weight = jnp.concatenate(
            [jnp.broadcast_to((NEG_WEIGHT * c)[:, None], (n_rows, edges // groups)) for c in counts], axis=1
        )
        grad_m = (weight * jax.nn.sigmoid(scores) - jnp.where(hit, jax.nn.sigmoid(-scores), 0.0)).astype(BF)

        half = outer * rows
        cut = half // 2
        far = dot(query_bf, grad_m[half:], 1, 1).astype(BF)
        got_hi = swap_left(far[:, cut:], 1)
        got_lo = swap_left(far[:, :cut], 1)
        mine = dot(query_bf, grad_m[:half], 1, 1)
        hi = mine[:, cut:] + got_hi.astype(F32)
        lo = mine[:, :cut] + got_lo.astype(F32)
        hi_bf, lo_bf = hi.astype(BF), lo.astype(BF)
        right_sum = lo[:, :rows]
        for k in range(outer - 1, 0, -1):
            at = k * rows
            piece = lo_bf[:, at:at + rows] if at < cut else hi_bf[:, at - cut:at - cut + rows]
            right_sum = right_sum + swap_left(piece, 2 * k).astype(F32)

        query_grad = dot(right_part, grad_m, 1, 0)
        relation_grad = complex_back(query_grad, source_emb).astype(BF)
        relation_term = dot(relation_grad, relation_hot, 1, 1)
        source_grad = complex_back(query_grad, relation_emb).astype(BF)
        left_grad = dot(source_grad, source_hot, 1, 1)

        order = [k // 2 + k % 2 * far_right for k in range(n_right)]
        lanes = nrel // 2
        tall = jnp.concatenate([relation_term[:, :lanes], relation_term[:, lanes:]], axis=0)
        pieces = tall.astype(BF).reshape(n_right, -1, lanes)
        piece_rows = pieces.shape[1]
        left_bf_grad = left_grad.astype(BF)
        left_sum = left_grad[:, :rows]
        got = [lax.dynamic_index_in_dim(pieces, here_r, 0, keepdims=False).astype(F32)]
        for k in range(1, n_right):
            block = left_bf_grad[:, order[k] * rows:(order[k] + 1) * rows]
            piece = lax.dynamic_index_in_dim(pieces, here_r ^ k, 0, keepdims=False)
            arrived = swap_right(jnp.concatenate([block, piece], axis=0), k)
            left_sum = left_sum + arrived[:width].astype(F32)
            got.append(arrived[width:].astype(F32))
        relation_piece = tree_sum(got).astype(BF)
        relation_piece = (relation_piece.astype(F32) + swap_left(relation_piece, 1).astype(F32)).astype(BF)
        got = [relation_piece.astype(F32)]
        for k in range(1, outer):
            got.append(swap_left(relation_piece, 2 * k).astype(F32))
        relation_piece = tree_sum(got).astype(BF)
        got = [relation_piece] + [swap_right(relation_piece, k) for k in range(1, n_right)]
        where = here_r ^ jnp.arange(n_right)
        tall = jnp.take(jnp.stack(got), where, axis=0).reshape(-1, lanes).astype(F32)
        relation_total = jnp.concatenate([tall[:width], tall[width:]], axis=1)

        left_new, left_state_new = adagrad(left_t, left_state, left_sum)
        right_new, right_state_new = adagrad(moved_t, moved_state, right_sum)
        relation_new, relation_state_new = adagrad(relation_t, relation_state, relation_total)
        return (left_new.T, left_state_new, right_new.T, right_state_new, relation_new.T, relation_state_new)

    return per_device


def solution(mesh):
    rows = P(("left", "right"), None)
    vector = P(("left", "right"))
    ids = P("left", "right", None)
    return jax.shard_map(
        build(mesh),
        mesh=mesh,
        in_specs=(rows, vector, rows, vector, P(), P(), ids, ids, ids, P("left", "right", None, None)),
        out_specs=(rows, vector, rows, vector, P(), P()),
        check_vma=False,
    )
```

```python
import functools

import jax
import jax.numpy as jnp
from jax import lax
from jax.experimental import pallas as pl
from jax.experimental.pallas import tpu as pltpu
from jax.sharding import PartitionSpec as P

LEARN_RATE = 0.1
NEG_WEIGHT = 0.03125
BF = jnp.bfloat16
F32 = jnp.float32
VMEM_LIMIT = 32 * 1024 * 1024
LANES = 128


def dot(a, b, a_dim, b_dim):
    return lax.dot_general(a, b, (((a_dim,), (b_dim,)), ((), ())), preferred_element_type=F32)


def hot(ids, count):
    spot = lax.broadcasted_iota(jnp.int32, (count, ids.shape[1]), 0)
    return jnp.where(spot == ids, 1.0, 0.0).astype(BF)


def step_of(size, most=256):
    return most if size % most == 0 else size


def call(body, out_shape, flops, scratch=(), here=None):
    def run(*args):
        moved = sum(a.size * a.dtype.itemsize for a in args)
        specs = [pl.BlockSpec(memory_space=pltpu.VMEM)] * len(args)
        if here is not None:
            specs.append(pl.BlockSpec(memory_space=pltpu.SMEM))
            args = (*args, here)
        return pl.pallas_call(
            body,
            out_shape=out_shape,
            in_specs=specs,
            scratch_shapes=list(scratch),
            compiler_params=pltpu.CompilerParams(vmem_limit_bytes=VMEM_LIMIT),
            cost_estimate=pl.CostEstimate(flops=flops, bytes_accessed=moved, transcendentals=0),
        )(*args)

    return run


def shape(*dims, dtype=F32):
    return jax.ShapeDtypeStruct(dims, dtype)


def count_body(ids_ref, out_ref):
    for g in range(out_ref.shape[0]):
        ids = ids_ref[g:g + 1, :]
        for at in range(0, out_ref.shape[1], LANES):
            spot = lax.broadcasted_iota(jnp.int32, (LANES, ids.shape[1]), 0) + at
            total = jnp.sum(jnp.where(spot == ids, NEG_WEIGHT, 0.0), axis=1, keepdims=True)
            out_ref[g, at:at + LANES, :] = jnp.broadcast_to(total, (LANES, LANES))


def query_body(near_ref, sibling_ref, relation_ref, source_ref, kind_ref, s_ref, o_ref, q_ref):
    relation = relation_ref[...].astype(BF)
    half_rows = near_ref.shape[1]
    half = s_ref.shape[0] // 2
    edges = s_ref.shape[1]
    step = step_of(edges)
    for at in range(0, edges, step):
        cols = slice(at, at + step)
        pick = hot(source_ref[:, cols], 2 * half_rows)
        s = dot(near_ref[...], pick[:half_rows], 1, 0) + dot(sibling_ref[...], pick[half_rows:], 1, 0)
        o = dot(relation, hot(kind_ref[:, cols], relation.shape[1]), 1, 0)
        s_ref[:, cols] = s.astype(BF)
        o_ref[:, cols] = o.astype(BF)
        s_re, s_im, o_re, o_im = s[:half], s[half:], o[:half], o[half:]
        q = jnp.concatenate([s_re * o_re - s_im * o_im, s_re * o_im + s_im * o_re], axis=0)
        q_ref[:, cols] = q.astype(BF)


def grad_matrix(rows_ref, q_ref, weight_ref, target_ref, m_ref, base):
    count = rows_ref.shape[1]
    rows_t = rows_ref[...].T
    edges = q_ref.shape[1]
    groups = weight_ref.shape[0]
    step = step_of(edges // groups)
    for at in range(0, edges, step):
        cols = slice(at, at + step)
        scores = dot(rows_t, q_ref[:, cols], 1, 0)
        spot = lax.broadcasted_iota(jnp.int32, (count, step), 0) + base
        h = jnp.where(spot == target_ref[:, cols], 1.0, 0.0)
        w = weight_ref[at // (edges // groups), base:base + count, :]
        w = jnp.concatenate([w] * (step // LANES), axis=1)
        m = (w + h) * (0.5 * jnp.tanh(0.5 * scores) + 0.5) - h
        m_ref[:, cols] = m.astype(BF)


def near_body(blocks, *refs):
    block_refs, refs = refs[:blocks], refs[blocks:]
    q_ref, weight_ref, target_ref, table_ref, state_ref, right_ref, qg_ref, pack_ref, rows_ref, m_ref = refs
    for k, ref in enumerate(block_refs):
        rows_ref[:, k * LANES:(k + 1) * LANES] = ref[...]
    grad_matrix(rows_ref, q_ref, weight_ref, target_ref, m_ref, 0)
    right_ref[...] = dot(q_ref[...], m_ref[...], 1, 1)
    qg_ref[...] = dot(rows_ref[...], m_ref[...], 1, 0)
    width = table_ref.shape[0]
    pack_ref[:width, :] = table_ref[...]
    pack_ref[width:, :] = jnp.broadcast_to(state_ref[...], (pack_ref.shape[0] - width, LANES))


def far_body(blocks, *refs):
    block_refs, refs = refs[:blocks], refs[blocks:]
    q_ref, weight_ref, target_ref, m_ref, hi_ref, lo_ref, rows_ref = refs
    for k, ref in enumerate(block_refs):
        rows_ref[:, k * LANES:(k + 1) * LANES] = ref[...]
    count = rows_ref.shape[1]
    grad_matrix(rows_ref, q_ref, weight_ref, target_ref, m_ref, count)
    far = dot(q_ref[...], m_ref[...], 1, 1).astype(BF)
    hi_ref[...] = far[:, count // 2:]
    lo_ref[...] = far[:, :count // 2]


def back_body(blocks, pieces, *refs):
    block_refs, refs = refs[:blocks], refs[blocks:]
    m_ref, qg_ref, s_ref, o_ref, source_ref, kind_ref, here_ref, near_ref, far_ref = refs[:9]
    piece_refs, refs = refs[9:9 + pieces], refs[9 + pieces:]
    rows_ref, left_ref, kinds_ref, tall_ref = refs
    for k, ref in enumerate(block_refs):
        rows_ref[:, k * LANES:(k + 1) * LANES] = ref[...]
    width, edges = qg_ref.shape
    half = width // 2
    step = step_of(edges)
    for at in range(0, edges, step):
        cols = slice(at, at + step)
        g = qg_ref[:, cols] + dot(rows_ref[...], m_ref[:, cols], 1, 0)
        s = s_ref[:, cols].astype(F32)
        o = o_ref[:, cols].astype(F32)
        g_re, g_im = g[:half], g[half:]
        s_re, s_im, o_re, o_im = s[:half], s[half:], o[:half], o[half:]
        by_kind = jnp.concatenate([g_re * s_re + g_im * s_im, g_im * s_re - g_re * s_im], axis=0).astype(BF)
        by_source = jnp.concatenate([g_re * o_re + g_im * o_im, g_im * o_re - g_re * o_im], axis=0).astype(BF)
        kinds = dot(by_kind, hot(kind_ref[:, cols], kinds_ref.shape[1]), 1, 1)
        left = dot(by_source, hot(source_ref[:, cols], left_ref.shape[1]), 1, 1)
        if at == 0:
            kinds_ref[...] = kinds
            left_ref[...] = left
        else:
            kinds_ref[...] += kinds
            left_ref[...] += left
    cut = left_ref.shape[1] // 2
    near_ref[...] = left_ref[:, :cut]
    far_ref[...] = left_ref[:, cut:].astype(BF)
    parts = kinds_ref.shape[1] // LANES
    for j in range(parts):
        tall_ref[j * width:(j + 1) * width, :] = kinds_ref[:, j * LANES:(j + 1) * LANES]
    rest = tall_ref.shape[0] - parts * width
    if rest:
        tall_ref[parts * width:, :] = jnp.zeros((rest, LANES), F32)
    here = here_ref[0]
    size = tall_ref.shape[0] // pieces
    for k, ref in enumerate(piece_refs):
        start = pl.multiple_of((here ^ k) * size, 16)
        ref[...] = tall_ref[pl.ds(start, size), :].astype(BF)


def relation_body(pieces, *refs):
    piece_refs, refs = refs[:pieces], refs[pieces:]
    table_ref, state_ref, here_ref, new_ref, state_new_ref, tall_ref = refs
    here = here_ref[0]
    size = tall_ref.shape[0] // pieces
    for k, ref in enumerate(piece_refs):
        start = pl.multiple_of((here ^ k) * size, 16)
        tall_ref[pl.ds(start, size), :] = ref[...].astype(F32)
    width, count = table_ref.shape
    for j in range(count // LANES):
        cols = slice(j * LANES, (j + 1) * LANES)
        g = tall_ref[j * width:(j + 1) * width, :]
        state = state_ref[:, cols] + jnp.sum(g * g, axis=0, keepdims=True) * (1.0 / width)
        state_new_ref[:, cols] = state
        new_ref[:, cols] = table_ref[:, cols] - g * (LEARN_RATE * lax.rsqrt(state))


def adagrad(table, state, grad):
    state_new = state + jnp.mean(grad * grad, axis=0)
    return table - LEARN_RATE * grad * lax.rsqrt(state_new)[None, :], state_new


def build(mesh):
    n_left, n_right = mesh.shape["left"], mesh.shape["right"]
    for count in (n_left, n_right):
        assert count & (count - 1) == 0 and count > 3
    outer = n_left // 2
    far_right = n_right // 2

    def swap_left(value, by):
        return lax.ppermute(value, "left", [(i, i ^ by) for i in range(n_left)])

    def swap_right(value, by):
        return lax.ppermute(value, "right", [(i, i ^ by) for i in range(n_right)])

    def next_column(value, by):
        perm = []
        for i in range(n_left):
            for r in range(n_right):
                perm.append((i * n_right + r, (i ^ by) * n_right + (r + 1) % n_right))
        return lax.ppermute(value, ("left", "right"), perm)

    def per_device(
        left_table, left_state, right_table, right_state, relation_table, relation_state,
        source_ids, target_ids, relation_ids, negative_ids,
    ):
        rows = left_table.shape[0]
        width = left_table.shape[1]
        left_t, right_t, relation_t = left_table.T, right_table.T, relation_table.T
        nrel = relation_t.shape[1]
        here_l, here_r = lax.axis_index("left"), lax.axis_index("right")
        me = here_r.astype(jnp.int32).reshape(1)
        source = source_ids.reshape(1, -1)
        target = target_ids.reshape(1, -1)
        kind = relation_ids.reshape(1, -1)
        negative = negative_ids.reshape(negative_ids.shape[2], negative_ids.shape[3])
        groups = negative.shape[0]
        edges = source.shape[1]
        n_rows = n_left * rows
        half = outer * rows

        right_bf = right_t.astype(BF)
        near = {k: next_column(right_bf, 2 * k) for k in range(outer - 1, -1, -1)}
        left_bf = left_t.astype(BF)
        half_left = [left_bf] + [swap_right(left_bf, 2 * k) for k in range(1, far_right)]
        half_left = jnp.concatenate(half_left, axis=1)
        sibling_left = swap_right(half_left, 1)
        other = {k: swap_left(near[k], 1) for k in range(outer)}
        near = [near[k] for k in range(outer)]
        other = [other[k] for k in range(outer)]

        def local(ids, here, half):
            block = (ids // rows) ^ here
            return (block % 2 * half + block // 2) * rows + ids % rows

        source = local(source, here_r, far_right)
        target = local(target, here_l, outer)
        negative = local(negative, here_l, outer)

        flop = 2 * width * edges
        weight = call(count_body, shape(groups, n_rows, LANES), 4 * n_rows * edges)(negative)
        table_bf = shape(width, edges, dtype=BF)
        s, o, q = call(query_body, (table_bf, table_bf, table_bf), flop * (n_right * rows + nrel))(
            half_left, sibling_left, relation_t, source, kind
        )
        part = pltpu.VMEM((width, half), BF)
        right_near, qg_near, pack = call(
            functools.partial(near_body, outer),
            (shape(width, half), shape(width, edges), shape(width + 8, rows)),
            3 * flop * half,
            [part, pltpu.VMEM((half, edges), BF)],
        )(*near, q, weight, target, right_t, right_state[None, :])
        moved = next_column(pack, 0)
        chunk = shape(width, half // 2, dtype=BF)
        m, far_hi, far_lo = call(
            functools.partial(far_body, outer), (shape(half, edges, dtype=BF), chunk, chunk), 2 * flop * half, [part]
        )(*other, q, weight, target)
        got_hi = swap_left(far_hi, 1)
        got_lo = swap_left(far_lo, 1)
        tall = nrel // LANES * width
        size = -(-tall // (n_right * 16)) * 16
        piece = shape(size, LANES, dtype=BF)
        left_rows = n_right * rows
        left_near, left_far, *pieces = call(
            functools.partial(back_body, outer, n_right),
            (shape(width, left_rows // 2), shape(width, left_rows // 2, dtype=BF)) + (piece,) * n_right,
            flop * (half + nrel + left_rows),
            [part, pltpu.VMEM((width, left_rows), F32), pltpu.VMEM((width, nrel), F32),
             pltpu.VMEM((size * n_right, LANES), F32)],
            me,
        )(*other, m, qg_near, s, o, source, kind)

        got = [pieces[0]] + [swap_right(pieces[k], k) for k in range(1, n_right)]
        got = [g.astype(F32) for g in got]
        while len(got) > 1:
            got = [got[i] + got[i + 1] for i in range(0, len(got), 2)]
        mine = got[0].astype(BF)
        bit = 2
        bits = []
        while bit < n_left:
            bits.append(bit)
            bit *= 2
        for bit in bits + [1]:
            mine = (mine.astype(F32) + swap_left(mine, bit).astype(F32)).astype(BF)
        pieces = [mine] + [swap_right(mine, k) for k in range(1, n_right)]

        cut = half // 2
        hi = right_near[:, cut:] + got_hi.astype(F32)
        lo = right_near[:, :cut] + got_lo.astype(F32)
        hi_bf, lo_bf = hi.astype(BF), lo.astype(BF)
        right_sum = lo[:, :rows]
        for k in range(outer - 1, 0, -1):
            at = k * rows
            block = lo_bf[:, at:at + rows] if at < cut else hi_bf[:, at - cut:at - cut + rows]
            right_sum = right_sum + swap_left(block, 2 * k).astype(F32)

        left_near = left_near + swap_right(left_far, 1).astype(F32)
        left_bf_sum = left_near.astype(BF)
        left_sum = left_near[:, :rows]
        for k in range(1, far_right):
            left_sum = left_sum + swap_right(left_bf_sum[:, k * rows:(k + 1) * rows], 2 * k).astype(F32)

        left_new, left_state_new = adagrad(left_t, left_state, left_sum)
        right_new, right_state_new = adagrad(moved[:width], moved[width], right_sum)
        relation_new, relation_state_new = call(
            functools.partial(relation_body, n_right),
            (shape(width, nrel), shape(1, nrel)),
            8 * width * nrel,
            [pltpu.VMEM((size * n_right, LANES), F32)],
            me,
        )(*pieces, relation_t, relation_state[None, :])
        return (
            left_new.T, left_state_new, right_new.T, right_state_new, relation_new.T, relation_state_new.reshape(-1),
        )

    return per_device


def solution(mesh):
    rows = P(("left", "right"), None)
    vector = P(("left", "right"))
    ids = P("left", "right", None)
    return jax.shard_map(
        build(mesh),
        mesh=mesh,
        in_specs=(rows, vector, rows, vector, P(), P(), ids, ids, ids, P("left", "right", None, None)),
        out_specs=(rows, vector, rows, vector, P(), P()),
        check_vma=False,
    )
```

```python
import functools

import jax
import jax.numpy as jnp
from jax import lax
from jax.experimental import pallas as pl
from jax.experimental.pallas import tpu as pltpu
from jax.sharding import PartitionSpec as P

LEARN_RATE = 0.1
NEG_WEIGHT = 0.03125
BF = jnp.bfloat16
F32 = jnp.float32
VMEM_LIMIT = 32 * 1024 * 1024
LANES = 128


def dot(a, b, a_dim, b_dim):
    return lax.dot_general(a, b, (((a_dim,), (b_dim,)), ((), ())), preferred_element_type=F32)


def hot(ids, count):
    spot = lax.broadcasted_iota(jnp.int32, (count, ids.shape[1]), 0)
    return jnp.where(spot == ids, 1.0, 0.0).astype(BF)


def step_of(size, most=256):
    return most if size % most == 0 else size


def call(body, out_shape, flops, scratch=(), here=None, after=()):
    def run(*args):
        moved = sum(a.size * a.dtype.itemsize for a in args)
        specs = [pl.BlockSpec(memory_space=pltpu.VMEM)] * len(args)
        if here is not None:
            specs.append(pl.BlockSpec(memory_space=pltpu.SMEM))
            args = (*args, here)
        inner = body
        if after:
            used = len(args)

            def inner(*refs):
                body(*refs[:used], *refs[used + len(after):])

            specs += [pl.BlockSpec(memory_space=pl.ANY)] * len(after)
            args = (*args, *after)
        return pl.pallas_call(
            inner,
            out_shape=out_shape,
            in_specs=specs,
            scratch_shapes=list(scratch),
            compiler_params=pltpu.CompilerParams(vmem_limit_bytes=VMEM_LIMIT),
            cost_estimate=pl.CostEstimate(flops=flops, bytes_accessed=moved, transcendentals=0),
        )(*args)

    return run


def shape(*dims, dtype=F32):
    return jax.ShapeDtypeStruct(dims, dtype)


def count_body(ids_ref, out_ref):
    for g in range(out_ref.shape[0]):
        ids = ids_ref[g:g + 1, :]
        for at in range(0, out_ref.shape[1], LANES):
            spot = lax.broadcasted_iota(jnp.int32, (LANES, ids.shape[1]), 0) + at
            total = jnp.sum(jnp.where(spot == ids, NEG_WEIGHT, 0.0), axis=1, keepdims=True)
            out_ref[g, at:at + LANES, :] = jnp.broadcast_to(total, (LANES, LANES))


def query_body(near_ref, sibling_ref, relation_ref, source_ref, kind_ref, s_ref, o_ref, q_ref):
    relation = relation_ref[...].astype(BF)
    half_rows = near_ref.shape[1]
    half = s_ref.shape[0] // 2
    edges = s_ref.shape[1]
    step = step_of(edges)
    for at in range(0, edges, step):
        cols = slice(at, at + step)
        pick = hot(source_ref[:, cols], 2 * half_rows)
        s = dot(near_ref[...], pick[:half_rows], 1, 0) + dot(sibling_ref[...], pick[half_rows:], 1, 0)
        o = dot(relation, hot(kind_ref[:, cols], relation.shape[1]), 1, 0)
        s_ref[:, cols] = s.astype(BF)
        o_ref[:, cols] = o.astype(BF)
        s_re, s_im, o_re, o_im = s[:half], s[half:], o[:half], o[half:]
        q = jnp.concatenate([s_re * o_re - s_im * o_im, s_re * o_im + s_im * o_re], axis=0)
        q_ref[:, cols] = q.astype(BF)


def grad_matrix(rows_ref, q_ref, weight_ref, target_ref, m_ref, base):
    count = rows_ref.shape[1]
    rows_t = rows_ref[...].T
    edges = q_ref.shape[1]
    groups = weight_ref.shape[0]
    step = step_of(edges // groups)
    for at in range(0, edges, step):
        cols = slice(at, at + step)
        scores = dot(rows_t, q_ref[:, cols], 1, 0)
        spot = lax.broadcasted_iota(jnp.int32, (count, step), 0) + base
        h = jnp.where(spot == target_ref[:, cols], 1.0, 0.0)
        w = weight_ref[at // (edges // groups), base:base + count, :]
        w = jnp.concatenate([w] * (step // LANES), axis=1)
        m = (w + h) * (0.5 * jnp.tanh(0.5 * scores) + 0.5) - h
        m_ref[:, cols] = m.astype(BF)


def near_body(blocks, *refs):
    block_refs, refs = refs[:blocks], refs[blocks:]
    q_ref, weight_ref, target_ref, table_ref, state_ref, right_ref, qg_ref, pack_ref, rows_ref, m_ref = refs
    for k, ref in enumerate(block_refs):
        rows_ref[:, k * LANES:(k + 1) * LANES] = ref[...]
    grad_matrix(rows_ref, q_ref, weight_ref, target_ref, m_ref, 0)
    right_ref[...] = dot(q_ref[...], m_ref[...], 1, 1)
    qg_ref[...] = dot(rows_ref[...], m_ref[...], 1, 0)
    width = table_ref.shape[0]
    pack_ref[:width, :] = table_ref[...]
    pack_ref[width:, :] = jnp.broadcast_to(state_ref[...], (pack_ref.shape[0] - width, LANES))


def far_body(blocks, *refs):
    block_refs, refs = refs[:blocks], refs[blocks:]
    q_ref, weight_ref, target_ref, m_ref, hi_ref, lo_ref, rows_ref = refs
    for k, ref in enumerate(block_refs):
        rows_ref[:, k * LANES:(k + 1) * LANES] = ref[...]
    count = rows_ref.shape[1]
    grad_matrix(rows_ref, q_ref, weight_ref, target_ref, m_ref, count)
    far = dot(q_ref[...], m_ref[...], 1, 1).astype(BF)
    hi_ref[...] = far[:, count // 2:]
    lo_ref[...] = far[:, :count // 2]


def back_body(blocks, pieces, *refs):
    block_refs, refs = refs[:blocks], refs[blocks:]
    m_ref, qg_ref, s_ref, o_ref, source_ref, kind_ref, here_ref, near_ref, far_ref = refs[:9]
    piece_refs, refs = refs[9:9 + pieces], refs[9 + pieces:]
    rows_ref, left_ref, kinds_ref, tall_ref = refs
    for k, ref in enumerate(block_refs):
        rows_ref[:, k * LANES:(k + 1) * LANES] = ref[...]
    width, edges = qg_ref.shape
    half = width // 2
    step = step_of(edges)
    for at in range(0, edges, step):
        cols = slice(at, at + step)
        g = qg_ref[:, cols] + dot(rows_ref[...], m_ref[:, cols], 1, 0)
        s = s_ref[:, cols].astype(F32)
        o = o_ref[:, cols].astype(F32)
        g_re, g_im = g[:half], g[half:]
        s_re, s_im, o_re, o_im = s[:half], s[half:], o[:half], o[half:]
        by_kind = jnp.concatenate([g_re * s_re + g_im * s_im, g_im * s_re - g_re * s_im], axis=0).astype(BF)
        by_source = jnp.concatenate([g_re * o_re + g_im * o_im, g_im * o_re - g_re * o_im], axis=0).astype(BF)
        kinds = dot(by_kind, hot(kind_ref[:, cols], kinds_ref.shape[1]), 1, 1)
        left = dot(by_source, hot(source_ref[:, cols], left_ref.shape[1]), 1, 1)
        if at == 0:
            kinds_ref[...] = kinds
            left_ref[...] = left
        else:
            kinds_ref[...] += kinds
            left_ref[...] += left
    cut = left_ref.shape[1] // 2
    near_ref[...] = left_ref[:, :cut]
    far_ref[...] = left_ref[:, cut:].astype(BF)
    parts = kinds_ref.shape[1] // LANES
    for j in range(parts):
        tall_ref[j * width:(j + 1) * width, :] = kinds_ref[:, j * LANES:(j + 1) * LANES]
    rest = tall_ref.shape[0] - parts * width
    if rest:
        tall_ref[parts * width:, :] = jnp.zeros((rest, LANES), F32)
    here = here_ref[0]
    size = tall_ref.shape[0] // pieces
    for k, ref in enumerate(piece_refs):
        start = pl.multiple_of((here ^ k) * size, 16)
        ref[...] = tall_ref[pl.ds(start, size), :].astype(BF)


def relation_body(pieces, *refs):
    piece_refs, refs = refs[:pieces], refs[pieces:]
    table_ref, state_ref, here_ref, new_ref, state_new_ref, tall_ref = refs
    here = here_ref[0]
    size = tall_ref.shape[0] // pieces
    for k, ref in enumerate(piece_refs):
        start = pl.multiple_of((here ^ k) * size, 16)
        tall_ref[pl.ds(start, size), :] = ref[...].astype(F32)
    width, count = table_ref.shape
    for j in range(count // LANES):
        cols = slice(j * LANES, (j + 1) * LANES)
        g = tall_ref[j * width:(j + 1) * width, :]
        state = state_ref[:, cols] + jnp.sum(g * g, axis=0, keepdims=True) * (1.0 / width)
        state_new_ref[:, cols] = state
        new_ref[:, cols] = table_ref[:, cols] - g * (LEARN_RATE * lax.rsqrt(state))


def cast_body(in_ref, out_ref):
    out_ref[...] = in_ref[...].astype(BF)


def high_body(blocks, pieces, *refs):
    near_ref, got_ref, refs = refs[0], refs[1], refs[2:]
    piece_refs, refs = refs[:pieces], refs[pieces:]
    block_refs, mine_ref = refs[:blocks], refs[blocks]
    base = near_ref.shape[1] - blocks * LANES
    for k, ref in enumerate(block_refs):
        cols = slice(k * LANES, (k + 1) * LANES)
        ref[...] = (near_ref[:, base + k * LANES:base + (k + 1) * LANES] + got_ref[:, cols].astype(F32)).astype(BF)
    parts = [ref[...].astype(F32) for ref in piece_refs]
    while len(parts) > 1:
        parts = [parts[i] + parts[i + 1] for i in range(0, len(parts), 2)]
    mine_ref[...] = parts[0].astype(BF)


def low_body(blocks, near_ref, got_ref, piece_ref, other_ref, *refs):
    block_refs, (own_ref, mine_ref) = refs[:blocks - 1], refs[blocks - 1:]
    own_ref[...] = near_ref[:, :LANES] + got_ref[:, :LANES].astype(F32)
    for k, ref in enumerate(block_refs):
        cols = slice((k + 1) * LANES, (k + 2) * LANES)
        ref[...] = (near_ref[:, cols] + got_ref[:, cols].astype(F32)).astype(BF)
    mine_ref[...] = (piece_ref[...].astype(F32) + other_ref[...].astype(F32)).astype(BF)


def update_body(parts, own_ref, *refs):
    part_refs, (table_ref, state_ref, new_ref, state_new_ref) = refs[:parts], refs[parts:]
    g = own_ref[...]
    for ref in part_refs:
        g = g + ref[...].astype(F32)
    width = g.shape[0]
    state = state_ref[:1, :] + jnp.sum(g * g, axis=0, keepdims=True) * (1.0 / width)
    state_new_ref[...] = state
    new_ref[...] = table_ref[:width, :] - g * (LEARN_RATE * lax.rsqrt(state))


def build(mesh):
    n_left, n_right = mesh.shape["left"], mesh.shape["right"]
    for count in (n_left, n_right):
        assert count & (count - 1) == 0 and count > 3
    outer = n_left // 2
    far_right = n_right // 2

    def swap_left(value, by):
        return lax.ppermute(value, "left", [(i, i ^ by) for i in range(n_left)])

    def swap_right(value, by):
        return lax.ppermute(value, "right", [(i, i ^ by) for i in range(n_right)])

    def next_column(value, by):
        perm = []
        for i in range(n_left):
            for r in range(n_right):
                perm.append((i * n_right + r, (i ^ by) * n_right + (r + 1) % n_right))
        return lax.ppermute(value, ("left", "right"), perm)

    def per_device(
        left_table, left_state, right_table, right_state, relation_table, relation_state,
        source_ids, target_ids, relation_ids, negative_ids,
    ):
        rows = left_table.shape[0]
        width = left_table.shape[1]
        left_t, right_t, relation_t = left_table.T, right_table.T, relation_table.T
        nrel = relation_t.shape[1]
        here_l, here_r = lax.axis_index("left"), lax.axis_index("right")
        me = here_r.astype(jnp.int32).reshape(1)
        source = source_ids.reshape(1, -1)
        target = target_ids.reshape(1, -1)
        kind = relation_ids.reshape(1, -1)
        negative = negative_ids.reshape(negative_ids.shape[2], negative_ids.shape[3])
        groups = negative.shape[0]
        edges = source.shape[1]
        n_rows = n_left * rows
        half = outer * rows

        one_block = shape(width, rows, dtype=BF)
        right_bf = call(cast_body, one_block, width * rows)(right_t)
        near = {k: next_column(right_bf, 2 * k) for k in range(outer - 1, 0, -1)}
        other = {0: next_column(right_bf, 1)}
        near[0] = next_column(right_bf, 0)
        other[1] = swap_left(near[1], 1)
        left_bf = call(cast_body, one_block, width * rows, after=(near[1], other[0]))(left_t)
        half_left = [left_bf] + [swap_right(left_bf, 2 * k) for k in range(1, far_right)]
        half_left = jnp.concatenate(half_left, axis=1)
        sibling_left = swap_right(half_left, 1)
        for k in range(2, outer):
            other[k] = swap_left(near[k], 1)
        near = [near[k] for k in range(outer)]
        other = [other[k] for k in range(outer)]

        def local(ids, here, half):
            block = (ids // rows) ^ here
            return (block % 2 * half + block // 2) * rows + ids % rows

        source = local(source, here_r, far_right)
        target = local(target, here_l, outer)
        negative = local(negative, here_l, outer)

        flop = 2 * width * edges
        weight = call(count_body, shape(groups, n_rows, LANES), 4 * n_rows * edges)(negative)
        table_bf = shape(width, edges, dtype=BF)
        s, o, q = call(query_body, (table_bf, table_bf, table_bf), flop * (n_right * rows + nrel))(
            half_left, sibling_left, relation_t, source, kind
        )
        part = pltpu.VMEM((width, half), BF)
        right_near, qg_near, pack = call(
            functools.partial(near_body, outer),
            (shape(width, half), shape(width, edges), shape(width + 8, rows)),
            3 * flop * half,
            [part, pltpu.VMEM((half, edges), BF)],
        )(*near, q, weight, target, right_t, right_state[None, :])
        moved = next_column(pack, 0)
        chunk = shape(width, half // 2, dtype=BF)
        m, far_hi, far_lo = call(
            functools.partial(far_body, outer), (shape(half, edges, dtype=BF), chunk, chunk), 2 * flop * half, [part]
        )(*other, q, weight, target)
        got_hi = swap_left(far_hi, 1)
        got_lo = swap_left(far_lo, 1)
        tall = nrel // LANES * width
        size = -(-tall // (n_right * 16)) * 16
        piece = shape(size, LANES, dtype=BF)
        left_rows = n_right * rows
        left_near, left_far, *pieces = call(
            functools.partial(back_body, outer, n_right),
            (shape(width, left_rows // 2), shape(width, left_rows // 2, dtype=BF)) + (piece,) * n_right,
            flop * (half + nrel + left_rows),
            [part, pltpu.VMEM((width, left_rows), F32), pltpu.VMEM((width, nrel), F32),
             pltpu.VMEM((size * n_right, LANES), F32)],
            me,
        )(*other, m, qg_near, s, o, source, kind)

        pieces = [pieces[0]] + [swap_right(pieces[k], k) for k in range(1, n_right)]
        some = outer // 2
        *high, mine = call(
            functools.partial(high_body, some, n_right), (one_block,) * some + (piece,), width * half
        )(right_near, got_hi, *pieces)
        arrived = {some + k: swap_left(block, 2 * (some + k)) for k, block in enumerate(high)}
        *low, own, mine = call(
            functools.partial(low_body, some),
            (one_block,) * (some - 1) + (shape(width, rows), piece),
            width * half,
        )(right_near, got_lo, mine, swap_left(mine, 2))
        for k, block in enumerate(low):
            arrived[k + 1] = swap_left(block, 2 * (k + 1))
        bit = 4
        while bit < n_left:
            mine = (mine.astype(F32) + swap_left(mine, bit).astype(F32)).astype(BF)
            bit *= 2
        mine = (mine.astype(F32) + swap_left(mine, 1).astype(F32)).astype(BF)
        pieces = [mine] + [swap_right(mine, k) for k in range(1, n_right)]

        left_near = left_near + swap_right(left_far, 1).astype(F32)
        left_bf_sum = left_near.astype(BF)
        left_got = [
            swap_right(left_bf_sum[:, k * rows:(k + 1) * rows], 2 * k) for k in range(1, far_right)
        ]

        def update(own, got, table, state):
            return call(
                functools.partial(update_body, len(got)), (shape(width, rows), shape(1, rows)), 8 * width * rows
            )(own, *got, table, state)

        left_new, left_state_new = update(left_near[:, :rows], left_got, left_t, left_state[None, :])
        right_got = [arrived[k] for k in range(1, outer)]
        right_new, right_state_new = update(own, right_got, moved, moved[width:])
        relation_new, relation_state_new = call(
            functools.partial(relation_body, n_right),
            (shape(width, nrel), shape(1, nrel)),
            8 * width * nrel,
            [pltpu.VMEM((size * n_right, LANES), F32)],
            me,
        )(*pieces, relation_t, relation_state[None, :])
        return (
            left_new.T, left_state_new.reshape(-1), right_new.T, right_state_new.reshape(-1),
            relation_new.T, relation_state_new.reshape(-1),
        )

    return per_device


def solution(mesh):
    rows = P(("left", "right"), None)
    vector = P(("left", "right"))
    ids = P("left", "right", None)
    return jax.shard_map(
        build(mesh),
        mesh=mesh,
        in_specs=(rows, vector, rows, vector, P(), P(), ids, ids, ids, P("left", "right", None, None)),
        out_specs=(rows, vector, rows, vector, P(), P()),
        check_vma=False,
    )
```

```python
import functools

import jax
import jax.numpy as jnp
from jax import lax
from jax.experimental import pallas as pl
from jax.experimental.pallas import tpu as pltpu
from jax.sharding import PartitionSpec as P

LEARN_RATE = 0.1
NEG_WEIGHT = 0.03125
BF = jnp.bfloat16
F32 = jnp.float32
VMEM_LIMIT = 32 * 1024 * 1024
LANES = 128


def dot(a, b, a_dim, b_dim):
    return lax.dot_general(a, b, (((a_dim,), (b_dim,)), ((), ())), preferred_element_type=F32)


def hot(ids, count):
    spot = lax.broadcasted_iota(jnp.int32, (count, ids.shape[1]), 0)
    return jnp.where(spot == ids, 1.0, 0.0).astype(BF)


def step_of(size, most=256):
    return most if size % most == 0 else size


def call(body, out_shape, flops, scratch=(), here=None, after=()):
    def run(*args):
        moved = sum(a.size * a.dtype.itemsize for a in args)
        specs = [pl.BlockSpec(memory_space=pltpu.VMEM)] * len(args)
        if here is not None:
            specs.append(pl.BlockSpec(memory_space=pltpu.SMEM))
            args = (*args, here)
        inner = body
        if after:
            used = len(args)

            def inner(*refs):
                body(*refs[:used], *refs[used + len(after):])

            specs += [pl.BlockSpec(memory_space=pl.ANY)] * len(after)
            args = (*args, *after)
        return pl.pallas_call(
            inner,
            out_shape=out_shape,
            in_specs=specs,
            scratch_shapes=list(scratch),
            compiler_params=pltpu.CompilerParams(vmem_limit_bytes=VMEM_LIMIT),
            cost_estimate=pl.CostEstimate(flops=flops, bytes_accessed=moved, transcendentals=0),
        )(*args)

    return run


def shape(*dims, dtype=F32):
    return jax.ShapeDtypeStruct(dims, dtype)


def cast_body(left_ref, right_ref, left_bf_ref, right_bf_ref):
    right_bf_ref[...] = right_ref[...].astype(BF)
    left_bf_ref[...] = left_ref[...].astype(BF)


def count_body(ids_ref, left_ref, out_ref, left_out_ref):
    left_out_ref[...] = left_ref[...]
    for g in range(out_ref.shape[0]):
        ids = ids_ref[g:g + 1, :]
        for at in range(0, out_ref.shape[1], LANES):
            spot = lax.broadcasted_iota(jnp.int32, (LANES, ids.shape[1]), 0) + at
            total = jnp.sum(jnp.where(spot == ids, NEG_WEIGHT, 0.0), axis=1, keepdims=True)
            out_ref[g, at:at + LANES, :] = jnp.broadcast_to(total, (LANES, LANES))


def query_body(near_ref, sibling_ref, relation_ref, source_ref, kind_ref, s_ref, o_ref, q_ref):
    relation = relation_ref[...].astype(BF)
    half_rows = near_ref.shape[1]
    half = s_ref.shape[0] // 2
    edges = s_ref.shape[1]
    step = step_of(edges)
    for at in range(0, edges, step):
        cols = slice(at, at + step)
        pick = hot(source_ref[:, cols], 2 * half_rows)
        s = dot(near_ref[...], pick[:half_rows], 1, 0) + dot(sibling_ref[...], pick[half_rows:], 1, 0)
        o = dot(relation, hot(kind_ref[:, cols], relation.shape[1]), 1, 0)
        s_ref[:, cols] = s.astype(BF)
        o_ref[:, cols] = o.astype(BF)
        s_re, s_im, o_re, o_im = s[:half], s[half:], o[:half], o[half:]
        q = jnp.concatenate([s_re * o_re - s_im * o_im, s_re * o_im + s_im * o_re], axis=0)
        q_ref[:, cols] = q.astype(BF)


def grad_matrix(rows_ref, q_ref, weight_ref, target_ref, m_ref, base):
    count = rows_ref.shape[1]
    rows_t = rows_ref[...].T
    edges = q_ref.shape[1]
    groups = weight_ref.shape[0]
    step = step_of(edges // groups)
    for at in range(0, edges, step):
        cols = slice(at, at + step)
        scores = dot(rows_t, q_ref[:, cols], 1, 0)
        spot = lax.broadcasted_iota(jnp.int32, (count, step), 0) + base
        h = jnp.where(spot == target_ref[:, cols], 1.0, 0.0)
        w = weight_ref[at // (edges // groups), base:base + count, :]
        w = jnp.concatenate([w] * (step // LANES), axis=1)
        m = (w + h) * (0.5 * jnp.tanh(0.5 * scores) + 0.5) - h
        m_ref[:, cols] = m.astype(BF)


def near_body(blocks, *refs):
    block_refs, refs = refs[:blocks], refs[blocks:]
    q_ref, weight_ref, target_ref, right_ref, qg_ref, rows_ref, m_ref = refs
    for k, ref in enumerate(block_refs):
        rows_ref[:, k * LANES:(k + 1) * LANES] = ref[...]
    grad_matrix(rows_ref, q_ref, weight_ref, target_ref, m_ref, 0)
    right_ref[...] = dot(q_ref[...], m_ref[...], 1, 1)
    qg_ref[...] = dot(rows_ref[...], m_ref[...], 1, 0)


def far_body(blocks, *refs):
    block_refs, refs = refs[:blocks], refs[blocks:]
    q_ref, weight_ref, target_ref, m_ref, hi_ref, lo_ref, rows_ref = refs
    for k, ref in enumerate(block_refs):
        rows_ref[:, k * LANES:(k + 1) * LANES] = ref[...]
    count = rows_ref.shape[1]
    grad_matrix(rows_ref, q_ref, weight_ref, target_ref, m_ref, count)
    far = dot(q_ref[...], m_ref[...], 1, 1).astype(BF)
    hi_ref[...] = far[:, count // 2:]
    lo_ref[...] = far[:, :count // 2]


def back_body(blocks, pieces, *refs):
    block_refs, refs = refs[:blocks], refs[blocks:]
    m_ref, qg_ref, s_ref, o_ref, source_ref, kind_ref, here_ref, near_ref = refs[:8]
    piece_refs, refs = refs[8:8 + pieces], refs[8 + pieces:]
    rows_ref, left_ref, kinds_ref, tall_ref = refs
    for k, ref in enumerate(block_refs):
        rows_ref[:, k * LANES:(k + 1) * LANES] = ref[...]
    width, edges = qg_ref.shape
    half = width // 2
    step = step_of(edges)
    for at in range(0, edges, step):
        cols = slice(at, at + step)
        g = qg_ref[:, cols] + dot(rows_ref[...], m_ref[:, cols], 1, 0)
        s = s_ref[:, cols].astype(F32)
        o = o_ref[:, cols].astype(F32)
        g_re, g_im = g[:half], g[half:]
        s_re, s_im, o_re, o_im = s[:half], s[half:], o[:half], o[half:]
        by_kind = jnp.concatenate([g_re * s_re + g_im * s_im, g_im * s_re - g_re * s_im], axis=0).astype(BF)
        by_source = jnp.concatenate([g_re * o_re + g_im * o_im, g_im * o_re - g_re * o_im], axis=0).astype(BF)
        kinds = dot(by_kind, hot(kind_ref[:, cols], kinds_ref.shape[1]), 1, 1)
        left = dot(by_source, hot(source_ref[:, cols], left_ref.shape[1]), 1, 1)
        if at == 0:
            kinds_ref[...] = kinds
            left_ref[...] = left
        else:
            kinds_ref[...] += kinds
            left_ref[...] += left
    cut = left_ref.shape[1] // 2
    near_ref[...] = left_ref[:, :cut]
    parts = kinds_ref.shape[1] // LANES
    for j in range(parts):
        tall_ref[j * width:(j + 1) * width, :] = kinds_ref[:, j * LANES:(j + 1) * LANES]
    rest = tall_ref.shape[0] - parts * width
    if rest:
        tall_ref[parts * width:, :] = jnp.zeros((rest, LANES), F32)
    here = here_ref[0]
    size = tall_ref.shape[0] // pieces
    for k, ref in enumerate(piece_refs):
        start = pl.multiple_of((here ^ k) * size, 16)
        piece = tall_ref[pl.ds(start, size), :].astype(BF)
        if k == 1:
            for j in range(cut // LANES):
                at = cut + j * LANES
                ref[j * width:(j + 1) * width, :] = left_ref[:, at:at + LANES].astype(BF)
            ref[cut // LANES * width:, :] = piece
        else:
            ref[...] = piece


def relation_body(pieces, *refs):
    piece_refs, refs = refs[:pieces], refs[pieces:]
    table_ref, state_ref, here_ref, new_ref, state_new_ref, tall_ref = refs
    here = here_ref[0]
    size = tall_ref.shape[0] // pieces
    for k, ref in enumerate(piece_refs):
        start = pl.multiple_of((here ^ k) * size, 16)
        tall_ref[pl.ds(start, size), :] = ref[...].astype(F32)
    width, count = table_ref.shape
    for j in range(count // LANES):
        cols = slice(j * LANES, (j + 1) * LANES)
        g = tall_ref[j * width:(j + 1) * width, :]
        state = state_ref[:, cols] + jnp.sum(g * g, axis=0, keepdims=True) * (1.0 / width)
        state_new_ref[:, cols] = state
        new_ref[:, cols] = table_ref[:, cols] - g * (LEARN_RATE * lax.rsqrt(state))


def high_body(blocks, pieces, near_ref, got_ref, left_ref, *refs):
    piece_refs, refs = refs[:pieces], refs[pieces:]
    block_refs, mine_ref, left_own_ref, left_refs = refs[:blocks], refs[blocks], refs[blocks + 1], refs[blocks + 2:]
    base = near_ref.shape[1] - blocks * LANES
    for k, ref in enumerate(block_refs):
        cols = slice(k * LANES, (k + 1) * LANES)
        ref[...] = (near_ref[:, base + k * LANES:base + (k + 1) * LANES] + got_ref[:, cols].astype(F32)).astype(BF)
    width = left_ref.shape[0]
    size = mine_ref.shape[0]
    core_ref = piece_refs[1]
    parts = [core_ref[core_ref.shape[0] - size:, :] if k == 1 else ref[...] for k, ref in enumerate(piece_refs)]
    parts = [part.astype(F32) for part in parts]
    while len(parts) > 1:
        parts = [parts[i] + parts[i + 1] for i in range(0, len(parts), 2)]
    mine_ref[...] = parts[0].astype(BF)
    for k in range(left_ref.shape[1] // LANES):
        total = left_ref[:, k * LANES:(k + 1) * LANES] + core_ref[k * width:(k + 1) * width, :].astype(F32)
        if k == 0:
            left_own_ref[...] = total
        else:
            left_refs[k - 1][...] = total.astype(BF)


def low_body(blocks, near_ref, got_ref, piece_ref, other_ref, table_ref, state_ref, *refs):
    block_refs, (own_ref, mine_ref, pack_ref) = refs[:blocks - 1], refs[blocks - 1:]
    mine_ref[...] = (piece_ref[...].astype(F32) + other_ref[...].astype(F32)).astype(BF)
    for k, ref in enumerate(block_refs):
        cols = slice((k + 1) * LANES, (k + 2) * LANES)
        ref[...] = (near_ref[:, cols] + got_ref[:, cols].astype(F32)).astype(BF)
    own_ref[...] = near_ref[:, :LANES] + got_ref[:, :LANES].astype(F32)
    width = table_ref.shape[0]
    pack_ref[:width, :] = table_ref[...]
    pack_ref[width:, :] = jnp.broadcast_to(state_ref[...], (pack_ref.shape[0] - width, LANES))


def sum_body(piece_ref, other_ref, out_ref):
    out_ref[...] = (piece_ref[...].astype(F32) + other_ref[...].astype(F32)).astype(BF)


def update_body(parts, own_ref, *refs):
    part_refs, (table_ref, state_ref, new_ref, state_new_ref) = refs[:parts], refs[parts:]
    g = own_ref[...]
    for ref in part_refs:
        g = g + ref[...].astype(F32)
    width = g.shape[0]
    state = state_ref[:1, :] + jnp.sum(g * g, axis=0, keepdims=True) * (1.0 / width)
    state_new_ref[...] = state
    new_ref[...] = table_ref[:width, :] - g * (LEARN_RATE * lax.rsqrt(state))


def build(mesh):
    n_left, n_right = mesh.shape["left"], mesh.shape["right"]
    for count in (n_left, n_right):
        assert count & (count - 1) == 0 and count > 3
    outer = n_left // 2
    far_right = n_right // 2

    def swap_left(value, by):
        return lax.ppermute(value, "left", [(i, i ^ by) for i in range(n_left)])

    def swap_right(value, by):
        return lax.ppermute(value, "right", [(i, i ^ by) for i in range(n_right)])

    def next_column(value, by):
        perm = []
        for i in range(n_left):
            for r in range(n_right):
                perm.append((i * n_right + r, (i ^ by) * n_right + (r + 1) % n_right))
        return lax.ppermute(value, ("left", "right"), perm)

    def per_device(
        left_table, left_state, right_table, right_state, relation_table, relation_state,
        source_ids, target_ids, relation_ids, negative_ids,
    ):
        rows = left_table.shape[0]
        width = left_table.shape[1]
        left_t, right_t, relation_t = left_table.T, right_table.T, relation_table.T
        nrel = relation_t.shape[1]
        here_l, here_r = lax.axis_index("left"), lax.axis_index("right")
        me = here_r.astype(jnp.int32).reshape(1)
        source = source_ids.reshape(1, -1)
        target = target_ids.reshape(1, -1)
        kind = relation_ids.reshape(1, -1)
        negative = negative_ids.reshape(negative_ids.shape[2], negative_ids.shape[3])
        groups = negative.shape[0]
        edges = source.shape[1]
        n_rows = n_left * rows
        half = outer * rows

        def local(ids, here, half):
            block = (ids // rows) ^ here
            return (block % 2 * half + block // 2) * rows + ids % rows

        source = local(source, here_r, far_right)
        target = local(target, here_l, outer)
        negative = local(negative, here_l, outer)

        flop = 2 * width * edges
        one_block = shape(width, rows, dtype=BF)
        table_bf = shape(width, edges, dtype=BF)

        left_bf, right_bf = call(cast_body, (one_block, one_block), width * rows)(left_t, right_t)
        near = {0: next_column(right_bf, 0)}
        for k in range(outer - 1, 0, -1):
            near[k] = next_column(right_bf, 2 * k)
        other = {0: next_column(right_bf, 1)}
        weight, left_bf = call(
            count_body, (shape(groups, n_rows, LANES), one_block), 4 * n_rows * edges, after=(near[0],)
        )(negative, left_bf)
        half_left = [left_bf] + [swap_right(left_bf, 2 * k) for k in range(1, far_right)]
        half_left = jnp.concatenate(half_left, axis=1)
        sibling_left = swap_right(half_left, 1)
        for k in range(1, outer):
            other[k] = swap_left(near[k], 1)
        near = [near[k] for k in range(outer)]
        other = [other[k] for k in range(outer)]

        s, o, q = call(query_body, (table_bf, table_bf, table_bf), flop * (n_right * rows + nrel))(
            half_left, sibling_left, relation_t, source, kind
        )
        part = pltpu.VMEM((width, half), BF)
        right_near, qg_near = call(
            functools.partial(near_body, outer),
            (shape(width, half), shape(width, edges)),
            3 * flop * half,
            [part, pltpu.VMEM((half, edges), BF)],
        )(*near, q, weight, target)
        chunk = shape(width, half // 2, dtype=BF)
        m, far_hi, far_lo = call(
            functools.partial(far_body, outer),
            (shape(half, edges, dtype=BF), chunk, chunk),
            2 * flop * half,
            [part],
            after=(qg_near,),
        )(*other, q, weight, target)
        got_hi = swap_left(far_hi, 1)
        got_lo = swap_left(far_lo, 1)
        tall = nrel // LANES * width
        size = -(-tall // (n_right * 16)) * 16
        piece = shape(size, LANES, dtype=BF)
        core_piece = shape(far_right * width + size, LANES, dtype=BF)
        left_rows = n_right * rows
        left_near, *pieces = call(
            functools.partial(back_body, outer, n_right),
            (shape(width, left_rows // 2), piece, core_piece) + (piece,) * (n_right - 2),
            flop * (half + nrel + left_rows),
            [part, pltpu.VMEM((width, left_rows), F32), pltpu.VMEM((width, nrel), F32),
             pltpu.VMEM((size * n_right, LANES), F32)],
            me,
        )(*other, m, qg_near, s, o, source, kind)

        pieces = [pieces[0]] + [swap_right(pieces[k], k) for k in range(1, n_right)]
        some = outer // 2
        outs = call(
            functools.partial(high_body, some, n_right),
            (one_block,) * some + (piece, shape(width, rows)) + (one_block,) * (far_right - 1),
            width * half,
        )(right_near, got_hi, left_near, *pieces)
        high, mine, left_own, left_blocks = outs[:some], outs[some], outs[some + 1], outs[some + 2:]
        arrived = {some + k: swap_left(block, 2 * (some + k)) for k, block in enumerate(high)}
        first = swap_left(mine, 2)
        left_got = [swap_right(block, 2 * (k + 1)) for k, block in enumerate(left_blocks)]
        *low, own, mine, pack = call(
            functools.partial(low_body, some),
            (one_block,) * (some - 1) + (shape(width, rows), piece, shape(width + 8, rows)),
            width * half,
            after=tuple(left_got),
        )(right_near, got_lo, mine, first, right_t, right_state[None, :])
        for k, block in enumerate(low):
            arrived[k + 1] = swap_left(block, 2 * (k + 1))
        moved = next_column(pack, 0)
        right_got = [arrived[k] for k in range(1, outer)]
        add = functools.partial(call, sum_body, piece, size * LANES)
        bit = 4
        while bit < n_left:
            mine = add()(mine, swap_left(mine, bit))
            bit *= 2
        mine = add(after=(*right_got, moved))(mine, swap_left(mine, 1))
        pieces = [mine] + [swap_right(mine, k) for k in range(1, n_right)]

        def update(own, got, table, state):
            return call(
                functools.partial(update_body, len(got)), (shape(width, rows), shape(1, rows)), 8 * width * rows
            )(own, *got, table, state)

        left_new, left_state_new = update(left_own, left_got, left_t, left_state[None, :])
        right_new, right_state_new = update(own, right_got, moved, moved[width:])
        relation_new, relation_state_new = call(
            functools.partial(relation_body, n_right),
            (shape(width, nrel), shape(1, nrel)),
            8 * width * nrel,
            [pltpu.VMEM((size * n_right, LANES), F32)],
            me,
        )(*pieces, relation_t, relation_state[None, :])
        return (
            left_new.T, left_state_new.reshape(-1), right_new.T, right_state_new.reshape(-1),
            relation_new.T, relation_state_new.reshape(-1),
        )

    return per_device


def solution(mesh):
    rows = P(("left", "right"), None)
    vector = P(("left", "right"))
    ids = P("left", "right", None)
    return jax.shard_map(
        build(mesh),
        mesh=mesh,
        in_specs=(rows, vector, rows, vector, P(), P(), ids, ids, ids, P("left", "right", None, None)),
        out_specs=(rows, vector, rows, vector, P(), P()),
        check_vma=False,
    )
```

```python
import functools

import jax
import jax.numpy as jnp
from jax import lax
from jax.experimental import pallas as pl
from jax.experimental.pallas import tpu as pltpu
from jax.sharding import PartitionSpec as P

LEARN_RATE = 0.1
NEG_WEIGHT = 0.03125
BF = jnp.bfloat16
F32 = jnp.float32
VMEM_LIMIT = 32 * 1024 * 1024
LANES = 128


def dot(a, b, a_dim, b_dim):
    return lax.dot_general(a, b, (((a_dim,), (b_dim,)), ((), ())), preferred_element_type=F32)


def hot(ids, count):
    spot = lax.broadcasted_iota(jnp.int32, (count, ids.shape[1]), 0)
    return jnp.where(spot == ids, 1.0, 0.0).astype(BF)


def step_of(size, most=256):
    return most if size % most == 0 else size


def call(body, out_shape, scratch=(), here=None, after=()):
    def run(*args):
        specs = [pl.BlockSpec(memory_space=pltpu.VMEM)] * len(args)
        if here is not None:
            specs.append(pl.BlockSpec(memory_space=pltpu.SMEM))
            args = (*args, here)
        inner = body
        if after:
            used = len(args)

            def inner(*refs):
                body(*refs[:used], *refs[used + len(after):])

            specs += [pl.BlockSpec(memory_space=pl.ANY)] * len(after)
            args = (*args, *after)
        return pl.pallas_call(
            inner,
            out_shape=out_shape,
            in_specs=specs,
            scratch_shapes=list(scratch),
            compiler_params=pltpu.CompilerParams(vmem_limit_bytes=VMEM_LIMIT),
            cost_estimate=pl.CostEstimate(flops=0, bytes_accessed=0, transcendentals=0),
        )(*args)

    return run


def shape(*dims, dtype=F32):
    return jax.ShapeDtypeStruct(dims, dtype)


def cast_body(in_ref, out_ref):
    out_ref[...] = in_ref[...].astype(BF)


def count_body(edges, ids_ref, relation_ref, table_ref, state_ref, out_ref, relation_bf_ref, pack_ref):
    groups = out_ref.shape[0]
    slots = (ids_ref.shape[1] - 3 * edges) // groups
    for g in range(groups):
        ids = ids_ref[:, 3 * edges + g * slots:3 * edges + (g + 1) * slots]
        for at in range(0, out_ref.shape[1], LANES):
            spot = lax.broadcasted_iota(jnp.int32, (LANES, slots), 0) + at
            total = jnp.sum(jnp.where(spot == ids, NEG_WEIGHT, 0.0), axis=1, keepdims=True)
            out_ref[g, at:at + LANES, :] = jnp.broadcast_to(total, (LANES, LANES))
    relation_bf_ref[...] = relation_ref[...].astype(BF)
    width = table_ref.shape[0]
    pack_ref[:width, :] = table_ref[...]
    pack_ref[width:, :] = jnp.broadcast_to(state_ref[...], (pack_ref.shape[0] - width, LANES))


def query_body(blocks, *refs):
    near_refs, refs = refs[:blocks], refs[blocks:]
    sibling_ref, relation_ref, ids_ref, s_ref, o_ref, q_ref = refs
    relation = relation_ref[...]
    half = s_ref.shape[0] // 2
    edges = s_ref.shape[1]
    step = step_of(edges)
    near = jnp.concatenate([ref[...] for ref in near_refs], axis=1)
    half_rows = near.shape[1]
    for at in range(0, edges, step):
        cols = slice(at, at + step)
        pick = hot(ids_ref[:, cols], 2 * half_rows)
        s = dot(near, pick[:half_rows], 1, 0) + dot(sibling_ref[...], pick[half_rows:], 1, 0)
        o = dot(relation, hot(ids_ref[:, 2 * edges + at:2 * edges + at + step], relation.shape[1]), 1, 0)
        s_ref[:, cols] = s.astype(BF)
        o_ref[:, cols] = o.astype(BF)
        s_re, s_im, o_re, o_im = s[:half], s[half:], o[:half], o[half:]
        q = jnp.concatenate([s_re * o_re - s_im * o_im, s_re * o_im + s_im * o_re], axis=0)
        q_ref[:, cols] = q.astype(BF)


def grad_matrix(rows_ref, q_ref, weight_ref, ids_ref, m_ref, base):
    count = rows_ref.shape[1]
    rows_t = rows_ref[...].T
    edges = q_ref.shape[1]
    groups = weight_ref.shape[0]
    step = step_of(edges // groups)
    for at in range(0, edges, step):
        cols = slice(at, at + step)
        scores = dot(rows_t, q_ref[:, cols], 1, 0)
        spot = lax.broadcasted_iota(jnp.int32, (count, step), 0) + base
        h = jnp.where(spot == ids_ref[:, edges + at:edges + at + step], 1.0, 0.0)
        w = weight_ref[at // (edges // groups), base:base + count, :]
        w = jnp.concatenate([w] * (step // LANES), axis=1)
        m = (w + h) * (0.5 * jnp.tanh(0.5 * scores) + 0.5) - h
        m_ref[:, cols] = m.astype(BF)


def near_body(blocks, *refs):
    block_refs, refs = refs[:blocks], refs[blocks:]
    q_ref, weight_ref, ids_ref, right_ref, qg_ref, rows_ref, m_ref = refs
    for k, ref in enumerate(block_refs):
        rows_ref[:, k * LANES:(k + 1) * LANES] = ref[...]
    grad_matrix(rows_ref, q_ref, weight_ref, ids_ref, m_ref, 0)
    right_ref[...] = dot(q_ref[...], m_ref[...], 1, 1)
    qg_ref[...] = dot(rows_ref[...], m_ref[...], 1, 0)


def far_body(blocks, *refs):
    block_refs, refs = refs[:blocks], refs[blocks:]
    q_ref, weight_ref, ids_ref, m_ref, hi_ref, lo_ref, rows_ref = refs
    for k, ref in enumerate(block_refs):
        rows_ref[:, k * LANES:(k + 1) * LANES] = ref[...]
    count = rows_ref.shape[1]
    grad_matrix(rows_ref, q_ref, weight_ref, ids_ref, m_ref, count)
    far = dot(q_ref[...], m_ref[...], 1, 1).astype(BF)
    hi_ref[...] = far[:, count // 2:]
    lo_ref[...] = far[:, :count // 2]


def back_body(blocks, pieces, *refs):
    block_refs, refs = refs[:blocks], refs[blocks:]
    m_ref, qg_ref, s_ref, o_ref, ids_ref, here_ref, near_ref = refs[:7]
    piece_refs, refs = refs[7:7 + pieces], refs[7 + pieces:]
    rows_ref, left_ref, kinds_ref, tall_ref = refs
    for k, ref in enumerate(block_refs):
        rows_ref[:, k * LANES:(k + 1) * LANES] = ref[...]
    width, edges = qg_ref.shape
    half = width // 2
    step = step_of(edges)
    for at in range(0, edges, step):
        cols = slice(at, at + step)
        g = qg_ref[:, cols] + dot(rows_ref[...], m_ref[:, cols], 1, 0)
        s = s_ref[:, cols].astype(F32)
        o = o_ref[:, cols].astype(F32)
        g_re, g_im = g[:half], g[half:]
        s_re, s_im, o_re, o_im = s[:half], s[half:], o[:half], o[half:]
        by_kind = jnp.concatenate([g_re * s_re + g_im * s_im, g_im * s_re - g_re * s_im], axis=0).astype(BF)
        by_source = jnp.concatenate([g_re * o_re + g_im * o_im, g_im * o_re - g_re * o_im], axis=0).astype(BF)
        kinds = dot(by_kind, hot(ids_ref[:, 2 * edges + at:2 * edges + at + step], kinds_ref.shape[1]), 1, 1)
        left = dot(by_source, hot(ids_ref[:, cols], left_ref.shape[1]), 1, 1)
        if at == 0:
            kinds_ref[...] = kinds
            left_ref[...] = left
        else:
            kinds_ref[...] += kinds
            left_ref[...] += left
    cut = left_ref.shape[1] // 2
    near_ref[...] = left_ref[:, :cut]
    parts = kinds_ref.shape[1] // LANES
    for j in range(parts):
        tall_ref[j * width:(j + 1) * width, :] = kinds_ref[:, j * LANES:(j + 1) * LANES]
    rest = tall_ref.shape[0] - parts * width
    if rest:
        tall_ref[parts * width:, :] = jnp.zeros((rest, LANES), F32)
    here = here_ref[0]
    size = tall_ref.shape[0] // pieces
    for k, ref in enumerate(piece_refs):
        start = pl.multiple_of((here ^ k) * size, 16)
        piece = tall_ref[pl.ds(start, size), :].astype(BF)
        if k == 1:
            for j in range(cut // LANES):
                at = cut + j * LANES
                ref[j * width:(j + 1) * width, :] = left_ref[:, at:at + LANES].astype(BF)
            ref[cut // LANES * width:, :] = piece
        else:
            ref[...] = piece


def relation_body(pieces, *refs):
    piece_refs, refs = refs[:pieces], refs[pieces:]
    table_ref, state_ref, here_ref, new_ref, state_new_ref, tall_ref = refs
    here = here_ref[0]
    size = tall_ref.shape[0] // pieces
    for k, ref in enumerate(piece_refs):
        start = pl.multiple_of((here ^ k) * size, 16)
        tall_ref[pl.ds(start, size), :] = ref[...].astype(F32)
    width, count = table_ref.shape
    for j in range(count // LANES):
        cols = slice(j * LANES, (j + 1) * LANES)
        g = tall_ref[j * width:(j + 1) * width, :]
        state = state_ref[:, cols] + jnp.sum(g * g, axis=0, keepdims=True) * (1.0 / width)
        state_new_ref[:, cols] = state
        new_ref[:, cols] = table_ref[:, cols] - g * (LEARN_RATE * lax.rsqrt(state))


def high_body(blocks, pieces, near_ref, got_ref, left_ref, *refs):
    piece_refs, refs = refs[:pieces], refs[pieces:]
    block_refs, mine_ref, left_own_ref, left_refs = refs[:blocks], refs[blocks], refs[blocks + 1], refs[blocks + 2:]
    base = near_ref.shape[1] - blocks * LANES
    for k, ref in enumerate(block_refs):
        cols = slice(k * LANES, (k + 1) * LANES)
        ref[...] = (near_ref[:, base + k * LANES:base + (k + 1) * LANES] + got_ref[:, cols].astype(F32)).astype(BF)
    width = left_ref.shape[0]
    size = mine_ref.shape[0]
    core_ref = piece_refs[1]
    parts = [core_ref[core_ref.shape[0] - size:, :] if k == 1 else ref[...] for k, ref in enumerate(piece_refs)]
    parts = [part.astype(F32) for part in parts]
    while len(parts) > 1:
        parts = [parts[i] + parts[i + 1] for i in range(0, len(parts), 2)]
    mine_ref[...] = parts[0].astype(BF)
    for k in range(left_ref.shape[1] // LANES):
        total = left_ref[:, k * LANES:(k + 1) * LANES] + core_ref[k * width:(k + 1) * width, :].astype(F32)
        if k == 0:
            left_own_ref[...] = total
        else:
            left_refs[k - 1][...] = total.astype(BF)


def low_body(blocks, near_ref, got_ref, piece_ref, other_ref, *refs):
    block_refs, mine_ref = refs[:blocks], refs[blocks]
    mine_ref[...] = (piece_ref[...].astype(F32) + other_ref[...].astype(F32)).astype(BF)
    for k, ref in enumerate(block_refs):
        cols = slice(k * LANES, (k + 1) * LANES)
        ref[...] = (near_ref[:, cols] + got_ref[:, cols].astype(F32)).astype(BF)


def sum_body(piece_ref, other_ref, out_ref):
    out_ref[...] = (piece_ref[...].astype(F32) + other_ref[...].astype(F32)).astype(BF)


def update_body(parts, *refs):
    part_refs, (table_ref, state_ref, new_ref, state_new_ref) = refs[:parts], refs[parts:]
    g = part_refs[0][...].astype(F32)
    for ref in part_refs[1:]:
        g = g + ref[...].astype(F32)
    width = g.shape[0]
    state = state_ref[:1, :] + jnp.sum(g * g, axis=0, keepdims=True) * (1.0 / width)
    state_new_ref[...] = state
    new_ref[...] = table_ref[:width, :] - g * (LEARN_RATE * lax.rsqrt(state))


def build(mesh):
    n_left, n_right = mesh.shape["left"], mesh.shape["right"]
    for count in (n_left, n_right):
        assert count & (count - 1) == 0 and count > 3
    outer = n_left // 2
    far_right = n_right // 2

    def swap_left(value, by):
        return lax.ppermute(value, "left", [(i, i ^ by) for i in range(n_left)])

    def swap_right(value, by):
        return lax.ppermute(value, "right", [(i, i ^ by) for i in range(n_right)])

    def next_column(value, by):
        perm = []
        for i in range(n_left):
            for r in range(n_right):
                perm.append((i * n_right + r, (i ^ by) * n_right + (r + 1) % n_right))
        return lax.ppermute(value, ("left", "right"), perm)

    def per_device(
        left_table, left_state, right_table, right_state, relation_table, relation_state,
        source_ids, target_ids, relation_ids, negative_ids,
    ):
        rows = left_table.shape[0]
        width = left_table.shape[1]
        left_t, right_t, relation_t = left_table.T, right_table.T, relation_table.T
        nrel = relation_t.shape[1]
        here_l, here_r = lax.axis_index("left"), lax.axis_index("right")
        me = here_r.astype(jnp.int32).reshape(1)
        edges = source_ids.shape[-1]
        groups = negative_ids.shape[2]
        n_rows = n_left * rows
        half = outer * rows
        one_block = shape(width, rows, dtype=BF)
        table_bf = shape(width, edges, dtype=BF)

        right_bf = call(cast_body, one_block)(right_t)
        near = {k: swap_left(right_bf, 2 * k) for k in range(outer - 1, 0, -1)}
        near[0] = right_bf
        other = {0: swap_left(right_bf, 1)}
        left_bf = call(cast_body, one_block)(left_t)
        half_left = [left_bf] + [swap_right(left_bf, 2 * k) for k in range(1, far_right)]

        def local(ids, here, half):
            block = (ids // rows) ^ here
            return ((block % 2 * half + block // 2) * rows + ids % rows).reshape(-1)

        before_r = (here_r + n_right - 1) % n_right
        ids = [
            local(source_ids, before_r, far_right), local(target_ids, here_l, outer),
            relation_ids.reshape(-1), local(negative_ids, here_l, outer),
        ]
        ids = lax.ppermute(
            jnp.concatenate(ids).reshape(1, -1), "right", [(i, (i - 1) % n_right) for i in range(n_right)]
        )
        sibling_left = swap_right(jnp.concatenate(half_left, axis=1), 1)
        weight, relation_bf, pack = call(
            functools.partial(count_body, edges),
            (shape(groups, n_rows, LANES), shape(width, nrel, dtype=BF), shape(width + 8, rows)),
        )(ids, relation_t, right_t, right_state[None, :])
        for k in range(1, outer):
            other[k] = swap_left(near[k], 1)
        near = [near[k] for k in range(outer)]
        other = [other[k] for k in range(outer)]
        moved = next_column(pack, 0)

        s, o, q = call(functools.partial(query_body, far_right), (table_bf, table_bf, table_bf))(
            *half_left, sibling_left, relation_bf, ids
        )
        part = pltpu.VMEM((width, half), BF)
        right_near, qg_near = call(
            functools.partial(near_body, outer),
            (shape(width, half), shape(width, edges)),
            [part, pltpu.VMEM((half, edges), BF)],
        )(*near, q, weight, ids)
        chunk = shape(width, half // 2, dtype=BF)
        m, far_hi, far_lo = call(
            functools.partial(far_body, outer), (shape(half, edges, dtype=BF), chunk, chunk), [part], after=(qg_near,)
        )(*other, q, weight, ids)
        got_hi = swap_left(far_hi, 1)
        got_lo = swap_left(far_lo, 1)
        tall = nrel // LANES * width
        size = -(-tall // (n_right * 16)) * 16
        piece = shape(size, LANES, dtype=BF)
        core_piece = shape(far_right * width + size, LANES, dtype=BF)
        left_rows = n_right * rows
        left_near, *pieces = call(
            functools.partial(back_body, outer, n_right),
            (shape(width, left_rows // 2), piece, core_piece) + (piece,) * (n_right - 2),
            [part, pltpu.VMEM((width, left_rows), F32), pltpu.VMEM((width, nrel), F32),
             pltpu.VMEM((size * n_right, LANES), F32)],
            me,
            after=(moved,),
        )(*other, m, qg_near, s, o, ids)

        pieces = [pieces[0]] + [swap_right(pieces[k], k) for k in range(1, n_right)]
        some = outer // 2
        outs = call(
            functools.partial(high_body, some, n_right),
            (one_block,) * some + (piece, shape(width, rows)) + (one_block,) * (far_right - 1),
        )(right_near, got_hi, left_near, *pieces)
        high, mine, left_own, left_blocks = outs[:some], outs[some], outs[some + 1], outs[some + 2:]
        right_high = [next_column(block, 2 * (some + k)) for k, block in enumerate(high)]
        first = swap_left(mine, 2)
        left_got = [swap_right(block, 2 * (k + 1)) for k, block in enumerate(left_blocks)]
        *low, mine = call(
            functools.partial(low_body, some), (one_block,) * some + (piece,), after=tuple(left_got)
        )(right_near, got_lo, mine, first)
        right_low = [next_column(block, 2 * k) for k, block in enumerate(low)]
        add = functools.partial(call, sum_body, piece)
        bit = 4
        while bit < n_left:
            mine = add(after=right_high if 2 * bit >= n_left else ())(mine, swap_left(mine, bit))
            bit *= 2
        mine = add(after=right_low)(mine, swap_left(mine, 1))
        pieces = [mine] + [swap_right(mine, k) for k in range(1, n_right)]

        def update(got, table, state):
            return call(functools.partial(update_body, len(got)), (shape(width, rows), shape(1, rows)))(
                *got, table, state
            )

        left_new, left_state_new = update([left_own, *left_got], left_t, left_state[None, :])
        right_new, right_state_new = update([*right_low, *right_high], moved, moved[width:])
        relation_new, relation_state_new = call(
            functools.partial(relation_body, n_right),
            (shape(width, nrel), shape(1, nrel)),
            [pltpu.VMEM((size * n_right, LANES), F32)],
            me,
        )(*pieces, relation_t, relation_state[None, :])
        return (
            left_new.T, left_state_new.reshape(-1), right_new.T, right_state_new.reshape(-1),
            relation_new.T, relation_state_new.reshape(-1),
        )

    return per_device


def solution(mesh):
    rows = P(("left", "right"), None)
    vector = P(("left", "right"))
    ids = P("left", "right", None)
    return jax.shard_map(
        build(mesh),
        mesh=mesh,
        in_specs=(rows, vector, rows, vector, P(), P(), ids, ids, ids, P("left", "right", None, None)),
        out_specs=(rows, vector, rows, vector, P(), P()),
        check_vma=False,
    )
```

```python
import functools

import jax
import jax.numpy as jnp
from jax import lax
from jax.experimental import pallas as pl
from jax.experimental.pallas import tpu as pltpu
from jax.sharding import PartitionSpec as P

LEARN_RATE = 0.1
NEG_WEIGHT = 0.03125
BF = jnp.bfloat16
F32 = jnp.float32
VMEM_LIMIT = 32 * 1024 * 1024
LANES = 128
COST_JOIN = 6e9
COST_UPDATE = 6e9
COST_HIGH = 6e9
COST_LOW = 6e9


def dot(a, b, a_dim, b_dim):
    return lax.dot_general(a, b, (((a_dim,), (b_dim,)), ((), ())), preferred_element_type=F32)


def hot(ids, count):
    spot = lax.broadcasted_iota(jnp.int32, (count, ids.shape[1]), 0)
    return jnp.where(spot == ids, 1.0, 0.0).astype(BF)


def step_of(size, most=256):
    return most if size % most == 0 else size


def call(body, out_shape, scratch=(), here=None, after=(), flops=0):
    def run(*args):
        specs = [pl.BlockSpec(memory_space=pltpu.VMEM)] * len(args)
        if here is not None:
            specs.append(pl.BlockSpec(memory_space=pltpu.SMEM))
            args = (*args, here)
        inner = body
        if after:
            used = len(args)

            def inner(*refs):
                body(*refs[:used], *refs[used + len(after):])

            specs += [pl.BlockSpec(memory_space=pl.ANY)] * len(after)
            args = (*args, *after)
        return pl.pallas_call(
            inner,
            out_shape=out_shape,
            in_specs=specs,
            scratch_shapes=list(scratch),
            compiler_params=pltpu.CompilerParams(vmem_limit_bytes=VMEM_LIMIT),
            cost_estimate=pl.CostEstimate(flops=int(flops), bytes_accessed=0, transcendentals=0),
        )(*args)

    return run


def shape(*dims, dtype=F32):
    return jax.ShapeDtypeStruct(dims, dtype)


def cast_body(in_ref, out_ref):
    out_ref[...] = in_ref[...].astype(BF)


def count_body(far_right, outer, rows, slots, ids_ref, relation_ref, place_ref, out_ref, relation_bf_ref, local_ref):
    def local(ids, here, half):
        block = (ids // rows) ^ here
        return (block % 2 * half + block // 2) * rows + ids % rows

    ids = ids_ref[...]
    local_ref[...] = ids
    local_ref[0:1, :] = local(ids[0:1], place_ref[0], far_right)
    local_ref[1:2, :] = local(ids[1:2], place_ref[1], outer)
    for g in range(out_ref.shape[0]):
        negative = local(ids[3 + g:4 + g, :slots], place_ref[1], outer)
        for at in range(0, out_ref.shape[1], LANES):
            spot = lax.broadcasted_iota(jnp.int32, (LANES, slots), 0) + at
            total = jnp.sum(jnp.where(spot == negative, NEG_WEIGHT, 0.0), axis=1, keepdims=True)
            out_ref[g, at:at + LANES, :] = jnp.broadcast_to(total, (LANES, LANES))
    relation_bf_ref[...] = relation_ref[...].astype(BF)


def pack_body(table_ref, state_ref, pack_ref):
    width = table_ref.shape[0]
    pack_ref[:width, :] = table_ref[...]
    pack_ref[width:, :] = jnp.broadcast_to(state_ref[...], (pack_ref.shape[0] - width, LANES))


def join_body(*refs):
    out_ref = refs[-1]
    at = 0
    for ref in refs[:-1]:
        out_ref[:, at:at + ref.shape[1]] = ref[...]
        at += ref.shape[1]


def query_body(blocks, *refs):
    near_refs, refs = refs[:blocks], refs[blocks:]
    sibling_ref, relation_ref, ids_ref, s_ref, o_ref, q_ref = refs
    relation = relation_ref[...]
    half = s_ref.shape[0] // 2
    edges = s_ref.shape[1]
    step = step_of(edges)
    near = jnp.concatenate([ref[...] for ref in near_refs], axis=1)
    half_rows = near.shape[1]
    for at in range(0, edges, step):
        cols = slice(at, at + step)
        pick = hot(ids_ref[0:1, cols], 2 * half_rows)
        s = dot(near, pick[:half_rows], 1, 0) + dot(sibling_ref[...], pick[half_rows:], 1, 0)
        o = dot(relation, hot(ids_ref[2:3, cols], relation.shape[1]), 1, 0)
        s_ref[:, cols] = s.astype(BF)
        o_ref[:, cols] = o.astype(BF)
        s_re, s_im, o_re, o_im = s[:half], s[half:], o[:half], o[half:]
        q = jnp.concatenate([s_re * o_re - s_im * o_im, s_re * o_im + s_im * o_re], axis=0)
        q_ref[:, cols] = q.astype(BF)


def grad_matrix(rows_ref, q_ref, weight_ref, ids_ref, m_ref, base):
    count = rows_ref.shape[1]
    rows_t = rows_ref[...].T
    edges = q_ref.shape[1]
    groups = weight_ref.shape[0]
    step = step_of(edges // groups)
    for at in range(0, edges, step):
        cols = slice(at, at + step)
        scores = dot(rows_t, q_ref[:, cols], 1, 0)
        spot = lax.broadcasted_iota(jnp.int32, (count, step), 0) + base
        h = jnp.where(spot == ids_ref[1:2, cols], 1.0, 0.0)
        w = weight_ref[at // (edges // groups), base:base + count, :]
        w = jnp.concatenate([w] * (step // LANES), axis=1)
        m = (w + h) * (0.5 * jnp.tanh(0.5 * scores) + 0.5) - h
        m_ref[:, cols] = m.astype(BF)


def near_body(blocks, *refs):
    block_refs, refs = refs[:blocks], refs[blocks:]
    q_ref, weight_ref, ids_ref, right_ref, qg_ref, rows_ref, m_ref = refs
    join_body(*block_refs, rows_ref)
    grad_matrix(rows_ref, q_ref, weight_ref, ids_ref, m_ref, 0)
    right_ref[...] = dot(q_ref[...], m_ref[...], 1, 1)
    qg_ref[...] = dot(rows_ref[...], m_ref[...], 1, 0)


def far_body(blocks, *refs):
    block_refs, refs = refs[:blocks], refs[blocks:]
    q_ref, weight_ref, ids_ref, m_ref, hi_ref, lo_ref, rows_ref = refs
    join_body(*block_refs, rows_ref)
    count = rows_ref.shape[1]
    grad_matrix(rows_ref, q_ref, weight_ref, ids_ref, m_ref, count)
    far = dot(q_ref[...], m_ref[...], 1, 1).astype(BF)
    hi_ref[...] = far[:, count // 2:]
    lo_ref[...] = far[:, :count // 2]


def back_body(blocks, pieces, *refs):
    block_refs, refs = refs[:blocks], refs[blocks:]
    m_ref, qg_ref, s_ref, o_ref, ids_ref, here_ref, near_ref = refs[:7]
    piece_refs, refs = refs[7:7 + pieces], refs[7 + pieces:]
    rows_ref, left_ref, kinds_ref, tall_ref = refs
    join_body(*block_refs, rows_ref)
    width, edges = qg_ref.shape
    half = width // 2
    step = step_of(edges)
    for at in range(0, edges, step):
        cols = slice(at, at + step)
        g = qg_ref[:, cols] + dot(rows_ref[...], m_ref[:, cols], 1, 0)
        s = s_ref[:, cols].astype(F32)
        o = o_ref[:, cols].astype(F32)
        g_re, g_im = g[:half], g[half:]
        s_re, s_im, o_re, o_im = s[:half], s[half:], o[:half], o[half:]
        by_kind = jnp.concatenate([g_re * s_re + g_im * s_im, g_im * s_re - g_re * s_im], axis=0).astype(BF)
        by_source = jnp.concatenate([g_re * o_re + g_im * o_im, g_im * o_re - g_re * o_im], axis=0).astype(BF)
        kinds = dot(by_kind, hot(ids_ref[2:3, cols], kinds_ref.shape[1]), 1, 1)
        left = dot(by_source, hot(ids_ref[0:1, cols], left_ref.shape[1]), 1, 1)
        if at == 0:
            kinds_ref[...] = kinds
            left_ref[...] = left
        else:
            kinds_ref[...] += kinds
            left_ref[...] += left
    cut = left_ref.shape[1] // 2
    near_ref[...] = left_ref[:, :cut]
    parts = kinds_ref.shape[1] // LANES
    for j in range(parts):
        tall_ref[j * width:(j + 1) * width, :] = kinds_ref[:, j * LANES:(j + 1) * LANES]
    rest = tall_ref.shape[0] - parts * width
    if rest:
        tall_ref[parts * width:, :] = jnp.zeros((rest, LANES), F32)
    here = here_ref[0]
    size = tall_ref.shape[0] // pieces
    for k, ref in enumerate(piece_refs):
        start = pl.multiple_of((here ^ k) * size, 16)
        piece = tall_ref[pl.ds(start, size), :].astype(BF)
        if k == 1:
            for j in range(cut // LANES):
                at = cut + j * LANES
                ref[j * width:(j + 1) * width, :] = left_ref[:, at:at + LANES].astype(BF)
            ref[cut // LANES * width:, :] = piece
        else:
            ref[...] = piece


def relation_body(pieces, *refs):
    piece_refs, refs = refs[:pieces], refs[pieces:]
    table_ref, state_ref, here_ref, new_ref, state_new_ref, tall_ref = refs
    here = here_ref[0]
    size = tall_ref.shape[0] // pieces
    for k, ref in enumerate(piece_refs):
        start = pl.multiple_of((here ^ k) * size, 16)
        tall_ref[pl.ds(start, size), :] = ref[...].astype(F32)
    width, count = table_ref.shape
    for j in range(count // LANES):
        cols = slice(j * LANES, (j + 1) * LANES)
        g = tall_ref[j * width:(j + 1) * width, :]
        state = state_ref[:, cols] + jnp.sum(g * g, axis=0, keepdims=True) * (1.0 / width)
        state_new_ref[:, cols] = state
        new_ref[:, cols] = table_ref[:, cols] - g * (LEARN_RATE * lax.rsqrt(state))


def piece_body(pieces, left_ref, *refs):
    piece_refs, refs = refs[:pieces], refs[pieces:]
    mine_ref, left_own_ref, left_refs = refs[0], refs[1], refs[2:]
    width = left_ref.shape[0]
    size = mine_ref.shape[0]
    core_ref = piece_refs[1]
    parts = [core_ref[core_ref.shape[0] - size:, :] if k == 1 else ref[...] for k, ref in enumerate(piece_refs)]
    parts = [part.astype(F32) for part in parts]
    while len(parts) > 1:
        parts = [parts[i] + parts[i + 1] for i in range(0, len(parts), 2)]
    mine_ref[...] = parts[0].astype(BF)
    for k in range(left_ref.shape[1] // LANES):
        total = left_ref[:, k * LANES:(k + 1) * LANES] + core_ref[k * width:(k + 1) * width, :].astype(F32)
        if k == 0:
            left_own_ref[...] = total
        else:
            left_refs[k - 1][...] = total.astype(BF)


def chunk_body(base, near_ref, got_ref, *block_refs):
    for k, ref in enumerate(block_refs):
        cols = slice(k * LANES, (k + 1) * LANES)
        total = near_ref[:, base + k * LANES:base + (k + 1) * LANES] + got_ref[:, cols].astype(F32)
        ref[...] = total.astype(BF)


def sum_body(piece_ref, other_ref, out_ref):
    out_ref[...] = (piece_ref[...].astype(F32) + other_ref[...].astype(F32)).astype(BF)


def update_body(parts, *refs):
    part_refs, (table_ref, state_ref, new_ref, state_new_ref) = refs[:parts], refs[parts:]
    g = part_refs[0][...].astype(F32)
    for ref in part_refs[1:]:
        g = g + ref[...].astype(F32)
    width = g.shape[0]
    state = state_ref[:1, :] + jnp.sum(g * g, axis=0, keepdims=True) * (1.0 / width)
    state_new_ref[...] = state
    new_ref[...] = table_ref[:width, :] - g * (LEARN_RATE * lax.rsqrt(state))


def build(mesh):
    n_left, n_right = mesh.shape["left"], mesh.shape["right"]
    for count in (n_left, n_right):
        assert count & (count - 1) == 0 and count > 3
    outer = n_left // 2
    far_right = n_right // 2

    def swap_left(value, by):
        return lax.ppermute(value, "left", [(i, i ^ by) for i in range(n_left)])

    def swap_right(value, by):
        return lax.ppermute(value, "right", [(i, i ^ by) for i in range(n_right)])

    def next_column(value, by):
        perm = []
        for i in range(n_left):
            for r in range(n_right):
                perm.append((i * n_right + r, (i ^ by) * n_right + (r + 1) % n_right))
        return lax.ppermute(value, ("left", "right"), perm)

    def per_device(
        left_table, left_state, right_table, right_state, relation_table, relation_state,
        source_ids, target_ids, relation_ids, negative_ids,
    ):
        rows = left_table.shape[0]
        width = left_table.shape[1]
        left_t, right_t, relation_t = left_table.T, right_table.T, relation_table.T
        nrel = relation_t.shape[1]
        here_l, here_r = lax.axis_index("left"), lax.axis_index("right")
        me = here_r.astype(jnp.int32).reshape(1)
        edges = source_ids.shape[-1]
        groups = negative_ids.shape[2]
        n_rows = n_left * rows
        half = outer * rows
        one_block = shape(width, rows, dtype=BF)
        table_bf = shape(width, edges, dtype=BF)

        right_bf = call(cast_body, one_block)(right_t)
        near = [right_bf] + [swap_left(right_bf, 2 * k) for k in range(1, outer)]
        other_own = swap_left(right_bf, 1)
        blocks = shape(width, half - rows, dtype=BF)
        joined = call(join_body, blocks, flops=COST_JOIN)(*near[1:])
        other_rest = swap_left(joined, 1)

        ids = [source_ids, target_ids, relation_ids, negative_ids]
        longest = max(i.shape[-1] for i in ids)
        ids = [i.reshape(-1, i.shape[-1]) for i in ids]
        ids = jnp.concatenate([jnp.pad(i, ((0, 0), (0, longest - i.shape[-1]))) for i in ids], axis=0)
        ids = lax.ppermute(ids, "right", [(i, (i - 1) % n_right) for i in range(n_right)])
        left_bf = call(cast_body, one_block, after=(other_own, ids))(left_t)
        half_left = [left_bf] + [swap_right(left_bf, 2 * k) for k in range(1, far_right)]
        sibling_left = swap_right(jnp.concatenate(half_left, axis=1), 1)
        place = jnp.stack([here_r, here_l]).astype(jnp.int32)
        weight, relation_bf, ids = call(
            functools.partial(count_body, far_right, outer, rows, negative_ids.shape[-1]),
            (shape(groups, n_rows, LANES), shape(width, nrel, dtype=BF), shape(*ids.shape, dtype=jnp.int32)),
            here=place,
        )(ids, relation_t)
        moved = next_column(call(pack_body, shape(width + 8, rows), after=(joined,))(right_t, right_state[None, :]), 0)

        s, o, q = call(functools.partial(query_body, far_right), (table_bf, table_bf, table_bf))(
            *half_left, sibling_left, relation_bf, ids
        )
        part = pltpu.VMEM((width, half), BF)
        right_near, qg_near = call(
            functools.partial(near_body, outer),
            (shape(width, half), shape(width, edges)),
            [part, pltpu.VMEM((half, edges), BF)],
        )(*near, q, weight, ids)
        chunk = shape(width, half // 2, dtype=BF)
        m, far_hi, far_lo = call(
            functools.partial(far_body, 2), (shape(half, edges, dtype=BF), chunk, chunk), [part], after=(qg_near,)
        )(other_own, other_rest, q, weight, ids)
        got_hi = swap_left(far_hi, 1)
        got_lo = swap_left(far_lo, 1)
        tall = nrel // LANES * width
        size = -(-tall // (n_right * 16)) * 16
        piece = shape(size, LANES, dtype=BF)
        core_piece = shape(far_right * width + size, LANES, dtype=BF)
        left_rows = n_right * rows
        left_near, *pieces = call(
            functools.partial(back_body, 2, n_right),
            (shape(width, left_rows // 2), piece, core_piece) + (piece,) * (n_right - 2),
            [part, pltpu.VMEM((width, left_rows), F32), pltpu.VMEM((width, nrel), F32),
             pltpu.VMEM((size * n_right, LANES), F32)],
            me,
            after=(moved,),
        )(other_own, other_rest, m, qg_near, s, o, ids)

        some = outer // 2
        outs = (one_block,) * some
        high = call(functools.partial(chunk_body, half // 2), outs, flops=COST_HIGH)(right_near, got_hi)
        low = call(functools.partial(chunk_body, 0), outs, flops=COST_LOW)(right_near, got_lo)
        right_got = [next_column(block, 2 * (some + k)) for k, block in enumerate(high)]
        right_got += [next_column(block, 2 * k) for k, block in enumerate(low)]

        def update(got, table, state, flops=0):
            outs = (shape(width, rows), shape(1, rows))
            return call(functools.partial(update_body, len(got)), outs, flops=flops)(*got, table, state)

        right_new, right_state_new = update(right_got, moved, moved[width:], COST_UPDATE)

        pieces = [pieces[0]] + [swap_right(pieces[k], k) for k in range(1, n_right)]
        mine, left_own, *left_blocks = call(
            functools.partial(piece_body, n_right), (piece, shape(width, rows)) + (one_block,) * (far_right - 1)
        )(left_near, *pieces)
        left_got = [swap_right(block, 2 * (k + 1)) for k, block in enumerate(left_blocks)]
        bit = 2
        while bit < n_left:
            mine = call(sum_body, piece)(mine, swap_left(mine, bit))
            bit *= 2
        mine = call(sum_body, piece, after=(right_state_new,))(mine, swap_left(mine, 1))
        pieces = [mine] + [swap_right(mine, k) for k in range(1, n_right)]
        left_new, left_state_new = update([left_own, *left_got], left_t, left_state[None, :])
        relation_new, relation_state_new = call(
            functools.partial(relation_body, n_right),
            (shape(width, nrel), shape(1, nrel)),
            [pltpu.VMEM((size * n_right, LANES), F32)],
            me,
        )(*pieces, relation_t, relation_state[None, :])
        return (
            left_new.T, left_state_new.reshape(-1), right_new.T, right_state_new.reshape(-1),
            relation_new.T, relation_state_new.reshape(-1),
        )

    return per_device


def solution(mesh):
    rows = P(("left", "right"), None)
    vector = P(("left", "right"))
    ids = P("left", "right", None)
    return jax.shard_map(
        build(mesh),
        mesh=mesh,
        in_specs=(rows, vector, rows, vector, P(), P(), ids, ids, ids, P("left", "right", None, None)),
        out_specs=(rows, vector, rows, vector, P(), P()),
        check_vma=False,
    )
```

```python
import functools

import jax
import jax.numpy as jnp
from jax import lax
from jax.experimental import pallas as pl
from jax.experimental.pallas import tpu as pltpu
from jax.sharding import PartitionSpec as P

LEARN_RATE = 0.1
NEG_WEIGHT = 0.03125
BF = jnp.bfloat16
F32 = jnp.float32
VMEM_LIMIT = 32 * 1024 * 1024
LANES = 128
COST_JOIN = 6e9
COST_UPDATE = 12e9
COST_HIGH = 12e9
COST_LOW = 12e9
COST_SUM = 1e9


def dot(a, b, a_dim, b_dim):
    return lax.dot_general(a, b, (((a_dim,), (b_dim,)), ((), ())), preferred_element_type=F32)


def hot(ids, count):
    spot = lax.broadcasted_iota(jnp.int32, (count, ids.shape[1]), 0)
    return jnp.where(spot == ids, 1.0, 0.0).astype(BF)


def step_of(size, most=256):
    return most if size % most == 0 else size


def call(body, out_shape, scratch=(), here=None, after=(), flops=0, place=pltpu.VMEM):
    def run(*args):
        specs = [pl.BlockSpec(memory_space=place)] * len(args)
        if here is not None:
            specs.append(pl.BlockSpec(memory_space=pltpu.SMEM))
            args = (*args, here)
        inner = body
        if after:
            used = len(args)

            def inner(*refs):
                body(*refs[:used], *refs[used + len(after):])

            specs += [pl.BlockSpec(memory_space=pl.ANY)] * len(after)
            args = (*args, *after)
        return pl.pallas_call(
            inner,
            out_shape=out_shape,
            in_specs=specs,
            scratch_shapes=list(scratch),
            compiler_params=pltpu.CompilerParams(vmem_limit_bytes=VMEM_LIMIT),
            cost_estimate=pl.CostEstimate(flops=int(flops), bytes_accessed=0, transcendentals=0),
        )(*args)

    return run


def shape(*dims, dtype=F32):
    return jax.ShapeDtypeStruct(dims, dtype)


def cast_body(in_ref, out_ref, held_ref, sems):
    rows = held_ref.shape[0] // sems.shape[0]
    copies = []
    for k in range(sems.shape[0]):
        at = slice(k * rows, (k + 1) * rows)
        copies.append(pltpu.make_async_copy(in_ref.at[at], held_ref.at[at], sems.at[k]))
        copies[-1].start()
    for k, copy in enumerate(copies):
        at = slice(k * rows, (k + 1) * rows)
        copy.wait()
        out_ref[at, :] = held_ref[at, :].astype(BF)


def count_body(far_right, outer, rows, slots, ids_ref, relation_ref, place_ref, out_ref, relation_bf_ref, local_ref):
    def local(ids, here, half):
        block = (ids // rows) ^ here
        return (block % 2 * half + block // 2) * rows + ids % rows

    ids = ids_ref[...]
    local_ref[...] = ids
    local_ref[0:1, :] = local(ids[0:1], place_ref[0], far_right)
    local_ref[1:2, :] = local(ids[1:2], place_ref[1], outer)
    for g in range(out_ref.shape[0]):
        negative = local(ids[3 + g:4 + g, :slots], place_ref[1], outer)
        for at in range(0, out_ref.shape[1], LANES):
            spot = lax.broadcasted_iota(jnp.int32, (LANES, slots), 0) + at
            total = jnp.sum(jnp.where(spot == negative, NEG_WEIGHT, 0.0), axis=1, keepdims=True)
            out_ref[g, at:at + LANES, :] = jnp.broadcast_to(total, (LANES, LANES))
    relation_bf_ref[...] = relation_ref[...].astype(BF)


def pack_body(table_ref, state_ref, pack_ref):
    width = table_ref.shape[0]
    pack_ref[:width, :] = table_ref[...]
    pack_ref[width:, :] = jnp.broadcast_to(state_ref[...], (pack_ref.shape[0] - width, LANES))


def join_body(*refs):
    out_ref = refs[-1]
    at = 0
    for ref in refs[:-1]:
        out_ref[:, at:at + ref.shape[1]] = ref[...]
        at += ref.shape[1]


def query_body(blocks, *refs):
    near_refs, refs = refs[:blocks], refs[blocks:]
    sibling_ref, relation_ref, ids_ref, s_ref, o_ref, q_ref = refs
    relation = relation_ref[...]
    half = s_ref.shape[0] // 2
    edges = s_ref.shape[1]
    step = step_of(edges)
    near = jnp.concatenate([ref[...] for ref in near_refs], axis=1)
    half_rows = near.shape[1]
    for at in range(0, edges, step):
        cols = slice(at, at + step)
        pick = hot(ids_ref[0:1, cols], 2 * half_rows)
        s = dot(near, pick[:half_rows], 1, 0) + dot(sibling_ref[...], pick[half_rows:], 1, 0)
        o = dot(relation, hot(ids_ref[2:3, cols], relation.shape[1]), 1, 0)
        s_ref[:, cols] = s.astype(BF)
        o_ref[:, cols] = o.astype(BF)
        s_re, s_im, o_re, o_im = s[:half], s[half:], o[:half], o[half:]
        q = jnp.concatenate([s_re * o_re - s_im * o_im, s_re * o_im + s_im * o_re], axis=0)
        q_ref[:, cols] = q.astype(BF)


def grad_chunk(rows_t, q_ref, weight_ref, ids_ref, base, at, step):
    count = rows_t.shape[0]
    edges = q_ref.shape[1]
    cols = slice(at, at + step)
    scores = dot(rows_t, q_ref[:, cols], 1, 0)
    spot = lax.broadcasted_iota(jnp.int32, (count, step), 0) + base
    h = jnp.where(spot == ids_ref[1:2, cols], 1.0, 0.0)
    w = weight_ref[at // (edges // weight_ref.shape[0]), base:base + count, :]
    w = jnp.concatenate([w] * (step // LANES), axis=1)
    return ((w + h) * (0.5 * jnp.tanh(0.5 * scores) + 0.5) - h).astype(BF)


def complex_back(g, other):
    half = g.shape[0] // 2
    g_re, g_im, o_re, o_im = g[:half], g[half:], other[:half], other[half:]
    return jnp.concatenate([g_re * o_re + g_im * o_im, g_im * o_re - g_re * o_im], axis=0).astype(BF)


def near_body(blocks, *refs):
    block_refs, refs = refs[:blocks], refs[blocks:]
    q_ref, weight_ref, ids_ref, right_ref, qg_ref, rows_ref, m_ref = refs
    join_body(*block_refs, rows_ref)
    rows_t = rows_ref[...].T
    edges = q_ref.shape[1]
    step = step_of(edges // weight_ref.shape[0])
    for at in range(0, edges, step):
        m_ref[:, at:at + step] = grad_chunk(rows_t, q_ref, weight_ref, ids_ref, 0, at, step)
    right_ref[...] = dot(q_ref[...], m_ref[...], 1, 1)
    qg_ref[...] = dot(rows_ref[...], m_ref[...], 1, 0)


def far_body(blocks, pieces, *refs):
    block_refs, refs = refs[:blocks], refs[blocks:]
    q_ref, weight_ref, ids_ref, qg_ref, s_ref, here_ref = refs[:6]
    m_ref, g_ref, mine_ref, theirs_ref, rows_ref, kinds_ref, tall_ref = refs[6:]
    join_body(*block_refs, rows_ref)
    rows_t = rows_ref[...].T
    base = rows_t.shape[0]
    width, edges = qg_ref.shape
    step = step_of(edges // weight_ref.shape[0])
    for at in range(0, edges, step):
        cols = slice(at, at + step)
        m = grad_chunk(rows_t, q_ref, weight_ref, ids_ref, base, at, step)
        m_ref[:, cols] = m
        g = qg_ref[:, cols] + dot(rows_ref[...], m, 1, 0)
        g_ref[:, cols] = g
        by_kind = complex_back(g, s_ref[:, cols].astype(F32))
        kinds = dot(by_kind, hot(ids_ref[2:3, cols], kinds_ref.shape[1]), 1, 1)
        if at == 0:
            kinds_ref[...] = kinds
        else:
            kinds_ref[...] += kinds
    parts = kinds_ref.shape[1] // LANES
    for j in range(parts):
        tall_ref[j * width:(j + 1) * width, :] = kinds_ref[:, j * LANES:(j + 1) * LANES]
    rest = tall_ref.shape[0] - parts * width
    if rest:
        tall_ref[parts * width:, :] = jnp.zeros((rest, LANES), F32)
    here = here_ref[0]
    size = tall_ref.shape[0] // pieces
    for k in range(pieces):
        start = pl.multiple_of((here ^ k) * size, 16)
        piece = tall_ref[pl.ds(start, size), :]
        at = slice(k // 2 * size, (k // 2 + 1) * size)
        if k % 2:
            theirs_ref[at, :] = piece.astype(BF)
        else:
            mine_ref[at, :] = piece


def rest_body(q_ref, m_ref, g_ref, o_ref, ids_ref, hi_ref, lo_ref, near_ref, far_ref, left_ref):
    far = dot(q_ref[...], m_ref[...], 1, 1).astype(BF)
    half = far.shape[1] // 2
    hi_ref[...] = far[:, half:]
    lo_ref[...] = far[:, :half]
    edges = q_ref.shape[1]
    step = step_of(edges)
    for at in range(0, edges, step):
        cols = slice(at, at + step)
        by_source = complex_back(g_ref[:, cols], o_ref[:, cols].astype(F32))
        left = dot(by_source, hot(ids_ref[0:1, cols], left_ref.shape[1]), 1, 1)
        if at == 0:
            left_ref[...] = left
        else:
            left_ref[...] += left
    cut = left_ref.shape[1] // 2
    near_ref[...] = left_ref[:, :cut]
    far_ref[...] = left_ref[:, cut:].astype(BF)


def relation_body(pieces, *refs):
    piece_refs, refs = refs[:pieces // 2], refs[pieces // 2:]
    sibling_ref, table_ref, state_ref, here_ref, new_ref, state_new_ref, tall_ref = refs
    here = here_ref[0]
    size = tall_ref.shape[0] // pieces
    for k in range(pieces):
        start = pl.multiple_of((here ^ k) * size, 16)
        piece = sibling_ref[k // 2 * size:(k // 2 + 1) * size, :] if k % 2 else piece_refs[k // 2][...]
        tall_ref[pl.ds(start, size), :] = piece.astype(F32)
    width, count = table_ref.shape
    for j in range(count // LANES):
        cols = slice(j * LANES, (j + 1) * LANES)
        g = tall_ref[j * width:(j + 1) * width, :]
        state = state_ref[:, cols] + jnp.sum(g * g, axis=0, keepdims=True) * (1.0 / width)
        state_new_ref[:, cols] = state
        new_ref[:, cols] = table_ref[:, cols] - g * (LEARN_RATE * lax.rsqrt(state))


def piece_body(mine_ref, got_ref, own_ref, *other_refs):
    size = own_ref.shape[0]
    for k, ref in enumerate((own_ref, *other_refs)):
        at = slice(k * size, (k + 1) * size)
        ref[...] = (mine_ref[at, :] + got_ref[at, :].astype(F32)).astype(ref.dtype)


def left_body(near_ref, got_ref, own_ref, *other_refs):
    for k, ref in enumerate((own_ref, *other_refs)):
        at = slice(k * LANES, (k + 1) * LANES)
        ref[...] = (near_ref[:, at] + got_ref[:, at].astype(F32)).astype(ref.dtype)


def stack_body(*refs):
    size = refs[0].shape[0]
    for k, ref in enumerate(refs[:-1]):
        refs[-1][k * size:(k + 1) * size, :] = ref[...]


def chunk_body(base, near_ref, got_ref, *block_refs):
    for k, ref in enumerate(block_refs):
        cols = slice(k * LANES, (k + 1) * LANES)
        total = near_ref[:, base + k * LANES:base + (k + 1) * LANES] + got_ref[:, cols].astype(F32)
        ref[...] = total.astype(BF)


def sum_body(*refs):
    total = refs[0][...].astype(F32)
    for ref in refs[1:-1]:
        total = total + ref[...].astype(F32)
    refs[-1][...] = total.astype(BF)


def update_body(parts, *refs):
    part_refs, (table_ref, state_ref, new_ref, state_new_ref) = refs[:parts], refs[parts:]
    g = part_refs[0][...].astype(F32)
    for ref in part_refs[1:]:
        g = g + ref[...].astype(F32)
    width = g.shape[0]
    state = state_ref[state_ref.shape[0] - 1:, :] + jnp.sum(g * g, axis=0, keepdims=True) * (1.0 / width)
    state_new_ref[...] = state
    new_ref[...] = table_ref[:width, :] - g * (LEARN_RATE * lax.rsqrt(state))


def build(mesh):
    n_left, n_right = mesh.shape["left"], mesh.shape["right"]
    for count in (n_left, n_right):
        assert count & (count - 1) == 0 and count > 3
    outer = n_left // 2
    far_right = n_right // 2

    def swap_left(value, by):
        return lax.ppermute(value, "left", [(i, i ^ by) for i in range(n_left)])

    def swap_right(value, by):
        return lax.ppermute(value, "right", [(i, i ^ by) for i in range(n_right)])

    def next_column(value, by):
        perm = []
        for i in range(n_left):
            for r in range(n_right):
                perm.append((i * n_right + r, (i ^ by) * n_right + (r + 1) % n_right))
        return lax.ppermute(value, ("left", "right"), perm)

    def per_device(
        left_table, left_state, right_table, right_state, relation_table, relation_state,
        source_ids, target_ids, relation_ids, negative_ids,
    ):
        rows = left_table.shape[0]
        width = left_table.shape[1]
        left_t, right_t, relation_t = left_table.T, right_table.T, relation_table.T
        nrel = relation_t.shape[1]
        here_l, here_r = lax.axis_index("left"), lax.axis_index("right")
        me = here_r.astype(jnp.int32).reshape(1)
        edges = source_ids.shape[-1]
        groups = negative_ids.shape[2]
        n_rows = n_left * rows
        half = outer * rows
        one_block = shape(width, rows, dtype=BF)
        table_bf = shape(width, edges, dtype=BF)

        def cast(value, after=()):
            parts = 5 if width % 80 == 0 else 1
            scratch = [pltpu.VMEM(value.shape, F32), pltpu.SemaphoreType.DMA((parts,))]
            return call(cast_body, one_block, scratch, after=after, place=pl.ANY)(value)

        right_bf = cast(right_t)
        near = [right_bf] + [swap_left(right_bf, 2 * k) for k in range(1, outer)]
        other_own = swap_left(right_bf, 1)
        blocks = shape(width, half - rows, dtype=BF)
        joined = call(join_body, blocks, flops=COST_JOIN)(*near[1:])
        other_rest = swap_left(joined, 1)

        ids = [source_ids, target_ids, relation_ids, negative_ids]
        longest = max(i.shape[-1] for i in ids)
        ids = [i.reshape(-1, i.shape[-1]) for i in ids]
        ids = jnp.concatenate([jnp.pad(i, ((0, 0), (0, longest - i.shape[-1]))) for i in ids], axis=0)
        ids = lax.ppermute(ids, "right", [(i, (i - 1) % n_right) for i in range(n_right)])
        left_bf = cast(left_t, after=(other_own, ids))
        half_left = [left_bf] + [swap_right(left_bf, 2 * k) for k in range(1, far_right)]
        sibling_left = swap_right(jnp.concatenate(half_left, axis=1), 1)
        place = jnp.stack([here_r, here_l]).astype(jnp.int32)
        weight, relation_bf, ids = call(
            functools.partial(count_body, far_right, outer, rows, negative_ids.shape[-1]),
            (shape(groups, n_rows, LANES), shape(width, nrel, dtype=BF), shape(*ids.shape, dtype=jnp.int32)),
            here=place,
        )(ids, relation_t)
        moved = next_column(call(pack_body, shape(width + 8, rows), after=(joined,))(right_t, right_state[None, :]), 0)

        s, o, q = call(functools.partial(query_body, far_right), (table_bf, table_bf, table_bf))(
            *half_left, sibling_left, relation_bf, ids
        )
        part = pltpu.VMEM((width, half), BF)
        right_near, qg_near = call(
            functools.partial(near_body, outer),
            (shape(width, half), shape(width, edges)),
            [part, pltpu.VMEM((half, edges), BF)],
        )(*near, q, weight, ids)
        chunk = shape(width, half // 2, dtype=BF)
        tall = nrel // LANES * width
        size = -(-tall // (n_right * 16)) * 16
        piece = shape(size, LANES, dtype=BF)
        all_pieces = pltpu.VMEM((size * n_right, LANES), F32)
        m, g, mine, theirs = call(
            functools.partial(far_body, 2, n_right),
            (shape(half, edges, dtype=BF), shape(width, edges), shape(far_right * size, LANES),
             shape(far_right * size, LANES, dtype=BF)),
            [part, pltpu.VMEM((width, nrel), F32), all_pieces],
            me,
            after=(moved,),
        )(other_own, other_rest, q, weight, ids, qg_near, s)
        left_rows = n_right * rows
        left_half = left_rows // 2
        far_hi, far_lo, left_near, left_far = call(
            rest_body,
            (chunk, chunk, shape(width, left_half), shape(width, left_half, dtype=BF)),
            [pltpu.VMEM((width, left_rows), F32)],
        )(q, m, g, o, ids)

        mine, *rest = call(
            piece_body, (shape(size, LANES),) + (piece,) * (far_right - 1), flops=COST_SUM
        )(mine, swap_right(theirs, 1))
        got = [swap_right(p, 2 * (k + 1)) for k, p in enumerate(rest)]
        mine = call(sum_body, piece, flops=COST_SUM)(mine, *got)
        bit = 2
        while bit < n_left:
            mine = call(sum_body, piece, flops=COST_SUM)(mine, swap_left(mine, bit))
            bit *= 2
        mine = call(sum_body, piece, flops=COST_SUM)(mine, swap_left(mine, 1))
        pieces = [mine] + [swap_right(mine, 2 * k) for k in range(1, far_right)]
        sibling = swap_right(call(stack_body, shape(far_right * size, LANES, dtype=BF))(*pieces), 1)

        left_own, *blocks = call(left_body, (shape(width, rows),) + (one_block,) * (far_right - 1))(
            left_near, swap_right(left_far, 1)
        )
        left_got = [swap_right(block, 2 * (k + 1)) for k, block in enumerate(blocks)]

        some = outer // 2
        got_hi = swap_left(far_hi, 1)
        got_lo = swap_left(far_lo, 1)
        outs = (one_block,) * some
        high = call(functools.partial(chunk_body, half // 2), outs, flops=COST_HIGH)(right_near, got_hi)
        low = call(functools.partial(chunk_body, 0), outs, flops=COST_LOW, after=left_got)(right_near, got_lo)
        right_got = [next_column(block, 2 * (some + k)) for k, block in enumerate(high)]
        right_got += [next_column(block, 2 * k) for k, block in enumerate(low)]

        def update(got, table, state, flops=0):
            outs = (shape(width, rows), shape(1, rows))
            return call(functools.partial(update_body, len(got)), outs, flops=flops)(*got, table, state)

        left_new, left_state_new = update([left_own, *left_got], left_t, left_state[None, :])
        right_new, right_state_new = update(right_got, moved, moved, COST_UPDATE)
        relation_new, relation_state_new = call(
            functools.partial(relation_body, n_right), (shape(width, nrel), shape(1, nrel)), [all_pieces], me
        )(*pieces, sibling, relation_t, relation_state[None, :])
        return (
            left_new.T, left_state_new.reshape(-1), right_new.T, right_state_new.reshape(-1),
            relation_new.T, relation_state_new.reshape(-1),
        )

    return per_device


def solution(mesh):
    rows = P(("left", "right"), None)
    vector = P(("left", "right"))
    ids = P("left", "right", None)
    return jax.shard_map(
        build(mesh),
        mesh=mesh,
        in_specs=(rows, vector, rows, vector, P(), P(), ids, ids, ids, P("left", "right", None, None)),
        out_specs=(rows, vector, rows, vector, P(), P()),
        check_vma=False,
    )
```

```python
import functools

import jax
import jax.numpy as jnp
from jax import lax
from jax.experimental import pallas as pl
from jax.experimental.pallas import tpu as pltpu
from jax.sharding import PartitionSpec as P

LEARN_RATE = 0.1
NEG_WEIGHT = 0.03125
BF = jnp.bfloat16
F32 = jnp.float32
VMEM_LIMIT = 32 * 1024 * 1024
LANES = 128
COST_JOIN_LOW = 6e9
COST_JOIN_HIGH = 6e9
COST_ADD = 6e9
COST_HIGH = 12e9
COST_LOW = 6e9
COST_SUM = 1e9
COST_MIDDLE = 6e9


def dot(a, b, a_dim, b_dim):
    return lax.dot_general(a, b, (((a_dim,), (b_dim,)), ((), ())), preferred_element_type=F32)


def hot(ids, count):
    spot = lax.broadcasted_iota(jnp.int32, (count, ids.shape[1]), 0)
    return jnp.where(spot == ids, 1.0, 0.0).astype(BF)


def step_of(size, most=256):
    return most if size % most == 0 else size


def call(body, out_shape, scratch=(), here=None, after=(), flops=0, place=pltpu.VMEM):
    def run(*args):
        specs = [pl.BlockSpec(memory_space=place)] * len(args)
        if here is not None:
            specs.append(pl.BlockSpec(memory_space=pltpu.SMEM))
            args = (*args, here)
        inner = body
        if after:
            used = len(args)

            def inner(*refs):
                body(*refs[:used], *refs[used + len(after):])

            specs += [pl.BlockSpec(memory_space=pl.ANY)] * len(after)
            args = (*args, *after)
        return pl.pallas_call(
            inner,
            out_shape=out_shape,
            in_specs=specs,
            scratch_shapes=list(scratch),
            compiler_params=pltpu.CompilerParams(vmem_limit_bytes=VMEM_LIMIT),
            cost_estimate=pl.CostEstimate(flops=int(flops), bytes_accessed=0, transcendentals=0),
        )(*args)

    return run


def shape(*dims, dtype=F32):
    return jax.ShapeDtypeStruct(dims, dtype)


def cast_body(in_ref, out_ref, held_ref, sems):
    rows = held_ref.shape[0] // sems.shape[0]
    copies = []
    for k in range(sems.shape[0]):
        at = slice(k * rows, (k + 1) * rows)
        copies.append(pltpu.make_async_copy(in_ref.at[at], held_ref.at[at], sems.at[k]))
        copies[-1].start()
    for k, copy in enumerate(copies):
        at = slice(k * rows, (k + 1) * rows)
        copy.wait()
        out_ref[at, :] = held_ref[at, :].astype(BF)


def count_body(far_right, outer, rows, slots, ids_ref, relation_ref, place_ref, out_ref, relation_bf_ref, local_ref):
    def local(ids, here, half):
        block = (ids // rows) ^ here
        return (block % 2 * half + block // 2) * rows + ids % rows

    ids = ids_ref[...]
    local_ref[...] = ids
    local_ref[0:1, :] = local(ids[0:1], place_ref[0], far_right)
    local_ref[1:2, :] = local(ids[1:2], place_ref[1], outer)
    for g in range(out_ref.shape[0]):
        negative = local(ids[3 + g:4 + g, :slots], place_ref[1], outer)
        for at in range(0, out_ref.shape[1], LANES):
            spot = lax.broadcasted_iota(jnp.int32, (LANES, slots), 0) + at
            total = jnp.sum(jnp.where(spot == negative, NEG_WEIGHT, 0.0), axis=1, keepdims=True)
            out_ref[g, at:at + LANES, :] = jnp.broadcast_to(total, (LANES, LANES))
    relation_bf_ref[...] = relation_ref[...].astype(BF)


def pack_body(table_ref, state_ref, pack_ref):
    width = table_ref.shape[0]
    pack_ref[:width, :] = table_ref[...]
    pack_ref[width:, :] = jnp.broadcast_to(state_ref[...], (pack_ref.shape[0] - width, LANES))


def join_body(*refs):
    out_ref = refs[-1]
    at = 0
    for ref in refs[:-1]:
        out_ref[:, at:at + ref.shape[1]] = ref[...]
        at += ref.shape[1]


def query_body(blocks, *refs):
    near_refs, refs = refs[:blocks], refs[blocks:]
    sibling_ref, relation_ref, ids_ref, s_ref, o_ref, q_ref = refs
    relation = relation_ref[...]
    half = s_ref.shape[0] // 2
    edges = s_ref.shape[1]
    step = step_of(edges)
    near = jnp.concatenate([ref[...] for ref in near_refs], axis=1)
    half_rows = near.shape[1]
    for at in range(0, edges, step):
        cols = slice(at, at + step)
        pick = hot(ids_ref[0:1, cols], 2 * half_rows)
        s = dot(near, pick[:half_rows], 1, 0) + dot(sibling_ref[...], pick[half_rows:], 1, 0)
        o = dot(relation, hot(ids_ref[2:3, cols], relation.shape[1]), 1, 0)
        s_ref[:, cols] = s.astype(BF)
        o_ref[:, cols] = o.astype(BF)
        s_re, s_im, o_re, o_im = s[:half], s[half:], o[:half], o[half:]
        q = jnp.concatenate([s_re * o_re - s_im * o_im, s_re * o_im + s_im * o_re], axis=0)
        q_ref[:, cols] = q.astype(BF)


def grad_chunk(rows_t, q_ref, weight_ref, ids_ref, base, at, step):
    count = rows_t.shape[0]
    edges = q_ref.shape[1]
    cols = slice(at, at + step)
    scores = dot(rows_t, q_ref[:, cols], 1, 0)
    spot = lax.broadcasted_iota(jnp.int32, (count, step), 0) + base
    h = jnp.where(spot == ids_ref[1:2, cols], 1.0, 0.0)
    w = weight_ref[at // (edges // weight_ref.shape[0]), base:base + count, :]
    w = jnp.concatenate([w] * (step // LANES), axis=1)
    return ((w + h) * (0.5 * jnp.tanh(0.5 * scores) + 0.5) - h).astype(BF)


def complex_back(g, other):
    half = g.shape[0] // 2
    g_re, g_im, o_re, o_im = g[:half], g[half:], other[:half], other[half:]
    return jnp.concatenate([g_re * o_re + g_im * o_im, g_im * o_re - g_re * o_im], axis=0).astype(BF)


def products(rows_ref, q_ref, weight_ref, ids_ref, m_ref, base):
    rows_t = rows_ref[...].T
    step = step_of(q_ref.shape[1] // weight_ref.shape[0])
    for at in range(0, q_ref.shape[1], step):
        m_ref[:, at:at + step] = grad_chunk(rows_t, q_ref, weight_ref, ids_ref, base, at, step)


def near_body(blocks, *refs):
    block_refs, refs = refs[:blocks], refs[blocks:]
    q_ref, weight_ref, ids_ref, right_ref, qg_ref, rows_ref, m_ref = refs
    join_body(*block_refs, rows_ref)
    products(rows_ref, q_ref, weight_ref, ids_ref, m_ref, 0)
    right_ref[...] = dot(q_ref[...], m_ref[...], 1, 1)
    qg_ref[...] = dot(rows_ref[...], m_ref[...], 1, 0)


def middle_body(base, rows_ref, q_ref, weight_ref, ids_ref, qg_ref, right_ref, qg_out_ref, m_ref):
    products(rows_ref, q_ref, weight_ref, ids_ref, m_ref, base)
    right_ref[...] = dot(q_ref[...], m_ref[...], 1, 1).astype(BF)
    qg_out_ref[...] = qg_ref[...] + dot(rows_ref[...], m_ref[...], 1, 0)


def far_body(
    base, pieces, rows_ref, q_ref, weight_ref, ids_ref, qg_ref, s_ref, here_ref,
    m_ref, g_ref, mine_ref, theirs_ref, kinds_ref, tall_ref,
):
    rows_t = rows_ref[...].T
    width, edges = qg_ref.shape
    step = step_of(edges // weight_ref.shape[0])
    for at in range(0, edges, step):
        cols = slice(at, at + step)
        m = grad_chunk(rows_t, q_ref, weight_ref, ids_ref, base, at, step)
        m_ref[:, cols] = m
        g = qg_ref[:, cols] + dot(rows_ref[...], m, 1, 0)
        g_ref[:, cols] = g
        by_kind = complex_back(g, s_ref[:, cols].astype(F32))
        kinds = dot(by_kind, hot(ids_ref[2:3, cols], kinds_ref.shape[1]), 1, 1)
        if at == 0:
            kinds_ref[...] = kinds
        else:
            kinds_ref[...] += kinds
    parts = kinds_ref.shape[1] // LANES
    for j in range(parts):
        tall_ref[j * width:(j + 1) * width, :] = kinds_ref[:, j * LANES:(j + 1) * LANES]
    rest = tall_ref.shape[0] - parts * width
    if rest:
        tall_ref[parts * width:, :] = jnp.zeros((rest, LANES), F32)
    here = here_ref[0]
    size = tall_ref.shape[0] // pieces
    for k in range(pieces):
        start = pl.multiple_of((here ^ k) * size, 16)
        piece = tall_ref[pl.ds(start, size), :]
        at = slice(k // 2 * size, (k // 2 + 1) * size)
        if k % 2:
            theirs_ref[at, :] = piece.astype(BF)
        else:
            mine_ref[at, :] = piece


def rest_body(q_ref, m_ref, g_ref, o_ref, ids_ref, right_ref, near_ref, far_ref, left_ref):
    right_ref[...] = dot(q_ref[...], m_ref[...], 1, 1).astype(BF)
    edges = q_ref.shape[1]
    step = step_of(edges)
    for at in range(0, edges, step):
        cols = slice(at, at + step)
        by_source = complex_back(g_ref[:, cols], o_ref[:, cols].astype(F32))
        left = dot(by_source, hot(ids_ref[0:1, cols], left_ref.shape[1]), 1, 1)
        if at == 0:
            left_ref[...] = left
        else:
            left_ref[...] += left
    cut = left_ref.shape[1] // 2
    near_ref[...] = left_ref[:, :cut]
    far_ref[...] = left_ref[:, cut:].astype(BF)


def relation_body(pieces, *refs):
    piece_refs, refs = refs[:pieces // 2], refs[pieces // 2:]
    sibling_ref, table_ref, state_ref, here_ref, new_ref, state_new_ref, tall_ref = refs
    here = here_ref[0]
    size = tall_ref.shape[0] // pieces
    for k in range(pieces):
        start = pl.multiple_of((here ^ k) * size, 16)
        piece = sibling_ref[k // 2 * size:(k // 2 + 1) * size, :] if k % 2 else piece_refs[k // 2][...]
        tall_ref[pl.ds(start, size), :] = piece.astype(F32)
    width, count = table_ref.shape
    for j in range(count // LANES):
        cols = slice(j * LANES, (j + 1) * LANES)
        g = tall_ref[j * width:(j + 1) * width, :]
        state = state_ref[:, cols] + jnp.sum(g * g, axis=0, keepdims=True) * (1.0 / width)
        state_new_ref[:, cols] = state
        new_ref[:, cols] = table_ref[:, cols] - g * (LEARN_RATE * lax.rsqrt(state))


def piece_body(mine_ref, got_ref, own_ref, *other_refs):
    size = own_ref.shape[0]
    for k, ref in enumerate((own_ref, *other_refs)):
        at = slice(k * size, (k + 1) * size)
        ref[...] = (mine_ref[at, :] + got_ref[at, :].astype(F32)).astype(ref.dtype)


def left_body(near_ref, got_ref, own_ref, *other_refs):
    for k, ref in enumerate((own_ref, *other_refs)):
        at = slice(k * LANES, (k + 1) * LANES)
        ref[...] = (near_ref[:, at] + got_ref[:, at].astype(F32)).astype(ref.dtype)


def stack_body(*refs):
    size = refs[0].shape[0]
    for k, ref in enumerate(refs[:-1]):
        refs[-1][k * size:(k + 1) * size, :] = ref[...]


def chunk_body(base, near_ref, got_ref, *block_refs):
    for k, ref in enumerate(block_refs):
        cols = slice(k * LANES, (k + 1) * LANES)
        total = near_ref[:, base + k * LANES:base + (k + 1) * LANES] + got_ref[:, cols].astype(F32)
        ref[...] = total.astype(BF)


def sum_body(*refs):
    total = refs[0][...].astype(F32)
    for ref in refs[1:-1]:
        total = total + ref[...].astype(F32)
    refs[-1][...] = total.astype(BF)


def add_body(*refs):
    total = refs[0][...].astype(F32)
    for ref in refs[1:-1]:
        total = total + ref[...].astype(F32)
    refs[-1][...] = total


def update_body(parts, *refs):
    part_refs, (table_ref, state_ref, new_ref, state_new_ref) = refs[:parts], refs[parts:]
    g = part_refs[0][...].astype(F32)
    for ref in part_refs[1:]:
        g = g + ref[...].astype(F32)
    width = g.shape[0]
    state = state_ref[state_ref.shape[0] - 1:, :] + jnp.sum(g * g, axis=0, keepdims=True) * (1.0 / width)
    state_new_ref[...] = state
    new_ref[...] = table_ref[:width, :] - g * (LEARN_RATE * lax.rsqrt(state))


def build(mesh):
    n_left, n_right = mesh.shape["left"], mesh.shape["right"]
    for count in (n_left, n_right):
        assert count & (count - 1) == 0 and count > 3
    outer = n_left // 2
    far_right = n_right // 2

    def swap_left(value, by):
        return lax.ppermute(value, "left", [(i, i ^ by) for i in range(n_left)])

    def swap_right(value, by):
        return lax.ppermute(value, "right", [(i, i ^ by) for i in range(n_right)])

    def next_column(value, by):
        perm = []
        for i in range(n_left):
            for r in range(n_right):
                perm.append((i * n_right + r, (i ^ by) * n_right + (r + 1) % n_right))
        return lax.ppermute(value, ("left", "right"), perm)

    def per_device(
        left_table, left_state, right_table, right_state, relation_table, relation_state,
        source_ids, target_ids, relation_ids, negative_ids,
    ):
        rows = left_table.shape[0]
        width = left_table.shape[1]
        left_t, right_t, relation_t = left_table.T, right_table.T, relation_table.T
        nrel = relation_t.shape[1]
        here_l, here_r = lax.axis_index("left"), lax.axis_index("right")
        me = here_r.astype(jnp.int32).reshape(1)
        edges = source_ids.shape[-1]
        groups = negative_ids.shape[2]
        n_rows = n_left * rows
        half = outer * rows
        one_block = shape(width, rows, dtype=BF)
        table_bf = shape(width, edges, dtype=BF)

        def cast(value, after=()):
            parts = 5 if width % 80 == 0 else 1
            scratch = [pltpu.VMEM(value.shape, F32), pltpu.SemaphoreType.DMA((parts,))]
            return call(cast_body, one_block, scratch, after=after, place=pl.ANY)(value)

        right_bf = cast(right_t)
        near = [right_bf] + [swap_left(right_bf, 2 * k) for k in range(1, outer)]
        some = outer // 2
        cut = some * rows
        chunk = shape(width, cut, dtype=BF)
        joined = call(join_body, chunk, flops=COST_JOIN_LOW)(*near[:some])
        other_low = swap_left(joined, 1)
        joined = call(join_body, chunk, flops=COST_JOIN_HIGH, after=(joined,))(*near[some:])
        other_high = swap_left(joined, 1)

        ids = [source_ids, target_ids, relation_ids, negative_ids]
        longest = max(i.shape[-1] for i in ids)
        ids = [i.reshape(-1, i.shape[-1]) for i in ids]
        ids = jnp.concatenate([jnp.pad(i, ((0, 0), (0, longest - i.shape[-1]))) for i in ids], axis=0)
        ids = lax.ppermute(ids, "right", [(i, (i - 1) % n_right) for i in range(n_right)])
        left_bf = cast(left_t)
        half_left = [left_bf] + [swap_right(left_bf, 2 * k) for k in range(1, far_right)]
        half_joined = call(join_body, shape(width, far_right * rows, dtype=BF), after=(ids,))(*half_left)
        sibling_left = swap_right(half_joined, 1)
        place = jnp.stack([here_r, here_l]).astype(jnp.int32)
        weight, relation_bf, ids = call(
            functools.partial(count_body, far_right, outer, rows, negative_ids.shape[-1]),
            (shape(groups, n_rows, LANES), shape(width, nrel, dtype=BF), shape(*ids.shape, dtype=jnp.int32)),
            here=place,
        )(ids, relation_t)
        moved = next_column(call(pack_body, shape(width + 8, rows), after=(joined,))(right_t, right_state[None, :]), 0)

        s, o, q = call(functools.partial(query_body, far_right), (table_bf, table_bf, table_bf))(
            *half_left, sibling_left, relation_bf, ids
        )
        right_near, qg = call(
            functools.partial(near_body, outer),
            (shape(width, half), shape(width, edges)),
            [pltpu.VMEM((width, half), BF), pltpu.VMEM((half, edges), BF)],
        )(*near, q, weight, ids)
        right_low, qg = call(
            functools.partial(middle_body, half), (chunk, shape(width, edges)), [pltpu.VMEM((cut, edges), BF)],
            flops=COST_MIDDLE,
        )(other_low, q, weight, ids, qg)
        got_low = swap_left(right_low, 1)
        tall = nrel // LANES * width
        size = -(-tall // (n_right * 16)) * 16
        piece = shape(size, LANES, dtype=BF)
        all_pieces = pltpu.VMEM((size * n_right, LANES), F32)
        m, g, mine, theirs = call(
            functools.partial(far_body, half + cut, n_right),
            (shape(cut, edges, dtype=BF), shape(width, edges), shape(far_right * size, LANES),
             shape(far_right * size, LANES, dtype=BF)),
            [pltpu.VMEM((width, nrel), F32), all_pieces],
            me,
            after=(moved,),
        )(other_high, q, weight, ids, qg, s)
        left_rows = n_right * rows
        left_half = left_rows // 2
        right_high, left_near, left_far = call(
            rest_body,
            (chunk, shape(width, left_half), shape(width, left_half, dtype=BF)),
            [pltpu.VMEM((width, left_rows), F32)],
        )(q, m, g, o, ids)

        got_high = swap_left(right_high, 1)
        outs = (one_block,) * some
        low = call(functools.partial(chunk_body, 0), outs, flops=COST_LOW)(right_near, got_low)
        low = [next_column(block, 2 * k) for k, block in enumerate(low)]
        low = call(add_body, shape(width, rows), flops=COST_ADD)(*low)
        high = call(functools.partial(chunk_body, cut), outs, flops=COST_HIGH)(right_near, got_high)
        high = [next_column(block, 2 * (some + k)) for k, block in enumerate(high)]
        high = call(add_body, shape(width, rows), flops=COST_ADD)(*high)

        left_own, *blocks = call(left_body, (shape(width, rows),) + (one_block,) * (far_right - 1))(
            left_near, swap_right(left_far, 1)
        )
        left_got = [swap_right(block, 2 * (k + 1)) for k, block in enumerate(blocks)]

        mine, *rest = call(
            piece_body, (shape(size, LANES),) + (piece,) * (far_right - 1), flops=COST_SUM, after=(got_low, right_high)
        )(mine, swap_right(theirs, 1))
        got = [swap_right(p, 2 * (k + 1)) for k, p in enumerate(rest)]
        mine = call(sum_body, piece, flops=COST_SUM)(mine, *got)
        bit = 2
        while bit < n_left:
            after = (low, left_own, got_high) if bit == 2 else ()
            mine = call(sum_body, piece, flops=COST_SUM, after=after)(mine, swap_left(mine, bit))
            bit *= 2
        mine = call(sum_body, piece, flops=COST_SUM, after=(high, *left_got))(mine, swap_left(mine, 1))
        pieces = [mine] + [swap_right(mine, 2 * k) for k in range(1, far_right)]
        sibling = swap_right(call(stack_body, shape(far_right * size, LANES, dtype=BF))(*pieces), 1)

        def update(got, table, state, flops=0):
            outs = (shape(width, rows), shape(1, rows))
            return call(functools.partial(update_body, len(got)), outs, flops=flops)(*got, table, state)

        left_new, left_state_new = update([left_own, *left_got], left_t, left_state[None, :])
        right_new, right_state_new = update([low, high], moved, moved)
        relation_new, relation_state_new = call(
            functools.partial(relation_body, n_right), (shape(width, nrel), shape(1, nrel)), [all_pieces], me
        )(*pieces, sibling, relation_t, relation_state[None, :])
        return (
            left_new.T, left_state_new.reshape(-1), right_new.T, right_state_new.reshape(-1),
            relation_new.T, relation_state_new.reshape(-1),
        )

    return per_device


def solution(mesh):
    rows = P(("left", "right"), None)
    vector = P(("left", "right"))
    ids = P("left", "right", None)
    return jax.shard_map(
        build(mesh),
        mesh=mesh,
        in_specs=(rows, vector, rows, vector, P(), P(), ids, ids, ids, P("left", "right", None, None)),
        out_specs=(rows, vector, rows, vector, P(), P()),
        check_vma=False,
    )
```

```python
import functools

import jax
import jax.numpy as jnp
from jax import lax
from jax.experimental import pallas as pl
from jax.experimental.pallas import tpu as pltpu
from jax.sharding import PartitionSpec as P

LEARN_RATE = 0.1
NEG_WEIGHT = 0.03125
BF = jnp.bfloat16
F32 = jnp.float32
VMEM_LIMIT = 32 * 1024 * 1024
LANES = 128
COST_JOIN = 6e9
COST_UPDATE = 6e9
COST_SUM = 1e9


def dot(a, b, a_dim, b_dim):
    return lax.dot_general(a, b, (((a_dim,), (b_dim,)), ((), ())), preferred_element_type=F32)


def hot(ids, count):
    spot = lax.broadcasted_iota(jnp.int32, (count, ids.shape[1]), 0)
    return jnp.where(spot == ids, 1.0, 0.0).astype(BF)


def step_of(size, most=256):
    return most if size % most == 0 else size


def call(body, out_shape, scratch=(), here=None, after=(), flops=0, place=pltpu.VMEM):
    def run(*args):
        specs = [pl.BlockSpec(memory_space=place)] * len(args)
        if here is not None:
            specs.append(pl.BlockSpec(memory_space=pltpu.SMEM))
            args = (*args, here)
        inner = body
        if after:
            used = len(args)

            def inner(*refs):
                body(*refs[:used], *refs[used + len(after):])

            specs += [pl.BlockSpec(memory_space=pl.ANY)] * len(after)
            args = (*args, *after)
        return pl.pallas_call(
            inner,
            out_shape=out_shape,
            in_specs=specs,
            scratch_shapes=list(scratch),
            compiler_params=pltpu.CompilerParams(vmem_limit_bytes=VMEM_LIMIT),
            cost_estimate=pl.CostEstimate(flops=int(flops), bytes_accessed=0, transcendentals=0),
        )(*args)

    return run


def shape(*dims, dtype=F32):
    return jax.ShapeDtypeStruct(dims, dtype)


def cast_body(in_ref, out_ref, held_ref, sems):
    rows = held_ref.shape[0] // sems.shape[0]
    copies = []
    for k in range(sems.shape[0]):
        at = slice(k * rows, (k + 1) * rows)
        copies.append(pltpu.make_async_copy(in_ref.at[at], held_ref.at[at], sems.at[k]))
        copies[-1].start()
    for k, copy in enumerate(copies):
        at = slice(k * rows, (k + 1) * rows)
        copy.wait()
        out_ref[at, :] = held_ref[at, :].astype(BF)


def count_body(far_right, outer, rows, slots, ids_ref, relation_ref, place_ref, out_ref, relation_bf_ref, local_ref):
    def local(ids, here, half):
        block = (ids // rows) ^ here
        return (block % 2 * half + block // 2) * rows + ids % rows

    ids = ids_ref[...]
    local_ref[...] = ids
    local_ref[0:1, :] = local(ids[0:1], place_ref[0], far_right)
    local_ref[1:2, :] = local(ids[1:2], place_ref[1], outer)
    for g in range(out_ref.shape[0]):
        negative = local(ids[3 + g:4 + g, :slots], place_ref[1], outer)
        for at in range(0, out_ref.shape[1], LANES):
            spot = lax.broadcasted_iota(jnp.int32, (LANES, slots), 0) + at
            total = jnp.sum(jnp.where(spot == negative, NEG_WEIGHT, 0.0), axis=1, keepdims=True)
            out_ref[g, at:at + LANES, :] = jnp.broadcast_to(total, (LANES, LANES))
    relation_bf_ref[...] = relation_ref[...].astype(BF)


def pack_body(table_ref, state_ref, pack_ref):
    width = table_ref.shape[0]
    pack_ref[:width, :] = table_ref[...]
    pack_ref[width:, :] = jnp.broadcast_to(state_ref[...], (pack_ref.shape[0] - width, LANES))


def join_body(*refs):
    out_ref = refs[-1]
    at = 0
    for ref in refs[:-1]:
        out_ref[:, at:at + ref.shape[1]] = ref[...]
        at += ref.shape[1]


def query_body(blocks, *refs):
    near_refs, refs = refs[:blocks], refs[blocks:]
    sibling_ref, relation_ref, ids_ref, s_ref, o_ref, q_ref = refs
    relation = relation_ref[...]
    half = s_ref.shape[0] // 2
    edges = s_ref.shape[1]
    step = step_of(edges)
    near = jnp.concatenate([ref[...] for ref in near_refs], axis=1)
    half_rows = near.shape[1]
    for at in range(0, edges, step):
        cols = slice(at, at + step)
        pick = hot(ids_ref[0:1, cols], 2 * half_rows)
        s = dot(near, pick[:half_rows], 1, 0) + dot(sibling_ref[...], pick[half_rows:], 1, 0)
        o = dot(relation, hot(ids_ref[2:3, cols], relation.shape[1]), 1, 0)
        s_ref[:, cols] = s.astype(BF)
        o_ref[:, cols] = o.astype(BF)
        s_re, s_im, o_re, o_im = s[:half], s[half:], o[:half], o[half:]
        q = jnp.concatenate([s_re * o_re - s_im * o_im, s_re * o_im + s_im * o_re], axis=0)
        q_ref[:, cols] = q.astype(BF)


def grad_chunk(rows_t, q_ref, weight_ref, ids_ref, base, at, step):
    count = rows_t.shape[0]
    edges = q_ref.shape[1]
    cols = slice(at, at + step)
    scores = dot(rows_t, q_ref[:, cols], 1, 0)
    spot = lax.broadcasted_iota(jnp.int32, (count, step), 0) + base
    h = jnp.where(spot == ids_ref[1:2, cols], 1.0, 0.0)
    w = weight_ref[at // (edges // weight_ref.shape[0]), base:base + count, :]
    w = jnp.concatenate([w] * (step // LANES), axis=1)
    return ((w + h) * (0.5 * jnp.tanh(0.5 * scores) + 0.5) - h).astype(BF)


def complex_back(g, other):
    half = g.shape[0] // 2
    g_re, g_im, o_re, o_im = g[:half], g[half:], other[:half], other[half:]
    return jnp.concatenate([g_re * o_re + g_im * o_im, g_im * o_re - g_re * o_im], axis=0).astype(BF)


def near_body(blocks, *refs):
    block_refs, refs = refs[:blocks], refs[blocks:]
    q_ref, weight_ref, ids_ref, right_ref, qg_ref, rows_ref, m_ref = refs
    join_body(*block_refs, rows_ref)
    rows_t = rows_ref[...].T
    edges = q_ref.shape[1]
    step = step_of(edges // weight_ref.shape[0])
    for at in range(0, edges, step):
        m_ref[:, at:at + step] = grad_chunk(rows_t, q_ref, weight_ref, ids_ref, 0, at, step)
    right_ref[...] = dot(q_ref[...], m_ref[...], 1, 1)
    qg_ref[...] = dot(rows_ref[...], m_ref[...], 1, 0)


def far_body(blocks, pieces, *refs):
    block_refs, refs = refs[:blocks], refs[blocks:]
    q_ref, weight_ref, ids_ref, qg_ref, s_ref, here_ref = refs[:6]
    m_ref, g_ref, mine_ref, theirs_ref, rows_ref, kinds_ref, tall_ref = refs[6:]
    join_body(*block_refs, rows_ref)
    rows_t = rows_ref[...].T
    base = rows_t.shape[0]
    width, edges = qg_ref.shape
    step = step_of(edges // weight_ref.shape[0])
    for at in range(0, edges, step):
        cols = slice(at, at + step)
        m = grad_chunk(rows_t, q_ref, weight_ref, ids_ref, base, at, step)
        m_ref[:, cols] = m
        g = qg_ref[:, cols] + dot(rows_ref[...], m, 1, 0)
        g_ref[:, cols] = g
        by_kind = complex_back(g, s_ref[:, cols].astype(F32))
        kinds = dot(by_kind, hot(ids_ref[2:3, cols], kinds_ref.shape[1]), 1, 1)
        if at == 0:
            kinds_ref[...] = kinds
        else:
            kinds_ref[...] += kinds
    parts = kinds_ref.shape[1] // LANES
    for j in range(parts):
        tall_ref[j * width:(j + 1) * width, :] = kinds_ref[:, j * LANES:(j + 1) * LANES]
    rest = tall_ref.shape[0] - parts * width
    if rest:
        tall_ref[parts * width:, :] = jnp.zeros((rest, LANES), F32)
    here = here_ref[0]
    size = tall_ref.shape[0] // pieces
    for k in range(pieces):
        start = pl.multiple_of((here ^ k) * size, 16)
        piece = tall_ref[pl.ds(start, size), :]
        at = slice(k // 2 * size, (k // 2 + 1) * size)
        if k % 2:
            theirs_ref[at, :] = piece.astype(BF)
        else:
            mine_ref[at, :] = piece


def rest_body(q_ref, m_ref, g_ref, o_ref, ids_ref, right_ref, near_ref, far_ref, left_ref):
    right_ref[...] = dot(q_ref[...], m_ref[...], 1, 1).astype(BF)
    edges = q_ref.shape[1]
    step = step_of(edges)
    for at in range(0, edges, step):
        cols = slice(at, at + step)
        by_source = complex_back(g_ref[:, cols], o_ref[:, cols].astype(F32))
        left = dot(by_source, hot(ids_ref[0:1, cols], left_ref.shape[1]), 1, 1)
        if at == 0:
            left_ref[...] = left
        else:
            left_ref[...] += left
    cut = left_ref.shape[1] // 2
    near_ref[...] = left_ref[:, :cut]
    far_ref[...] = left_ref[:, cut:].astype(BF)


def relation_body(pieces, *refs):
    piece_refs, refs = refs[:pieces // 2], refs[pieces // 2:]
    sibling_ref, table_ref, state_ref, here_ref, new_ref, state_new_ref, tall_ref = refs
    here = here_ref[0]
    size = tall_ref.shape[0] // pieces
    for k in range(pieces):
        start = pl.multiple_of((here ^ k) * size, 16)
        piece = sibling_ref[k // 2 * size:(k // 2 + 1) * size, :] if k % 2 else piece_refs[k // 2][...]
        tall_ref[pl.ds(start, size), :] = piece.astype(F32)
    width, count = table_ref.shape
    for j in range(count // LANES):
        cols = slice(j * LANES, (j + 1) * LANES)
        g = tall_ref[j * width:(j + 1) * width, :]
        state = state_ref[:, cols] + jnp.sum(g * g, axis=0, keepdims=True) * (1.0 / width)
        state_new_ref[:, cols] = state
        new_ref[:, cols] = table_ref[:, cols] - g * (LEARN_RATE * lax.rsqrt(state))


def piece_body(mine_ref, got_ref, own_ref, *other_refs):
    size = own_ref.shape[0]
    for k, ref in enumerate((own_ref, *other_refs)):
        at = slice(k * size, (k + 1) * size)
        ref[...] = (mine_ref[at, :] + got_ref[at, :].astype(F32)).astype(ref.dtype)


def left_body(near_ref, got_ref, own_ref, *other_refs):
    for k, ref in enumerate((own_ref, *other_refs)):
        at = slice(k * LANES, (k + 1) * LANES)
        ref[...] = (near_ref[:, at] + got_ref[:, at].astype(F32)).astype(ref.dtype)


def stack_body(*refs):
    size = refs[0].shape[0]
    for k, ref in enumerate(refs[:-1]):
        refs[-1][k * size:(k + 1) * size, :] = ref[...]


def chunk_body(near_ref, got_ref, *block_refs):
    for k, ref in enumerate(block_refs):
        cols = slice(k * LANES, (k + 1) * LANES)
        ref[...] = (near_ref[:, cols] + got_ref[:, cols].astype(F32)).astype(BF)


def sum_body(*refs):
    total = refs[0][...].astype(F32)
    for ref in refs[1:-1]:
        total = total + ref[...].astype(F32)
    refs[-1][...] = total.astype(BF)


def update_body(parts, *refs):
    part_refs, (table_ref, state_ref, new_ref, state_new_ref) = refs[:parts], refs[parts:]
    g = part_refs[0][...].astype(F32)
    for ref in part_refs[1:]:
        g = g + ref[...].astype(F32)
    width = g.shape[0]
    state = state_ref[state_ref.shape[0] - 1:, :] + jnp.sum(g * g, axis=0, keepdims=True) * (1.0 / width)
    state_new_ref[...] = state
    new_ref[...] = table_ref[:width, :] - g * (LEARN_RATE * lax.rsqrt(state))


def build(mesh):
    n_left, n_right = mesh.shape["left"], mesh.shape["right"]
    for count in (n_left, n_right):
        assert count & (count - 1) == 0 and count > 3
    outer = n_left // 2
    far_right = n_right // 2

    def swap_left(value, by):
        return lax.ppermute(value, "left", [(i, i ^ by) for i in range(n_left)])

    def swap_right(value, by):
        return lax.ppermute(value, "right", [(i, i ^ by) for i in range(n_right)])

    def next_column(value, by):
        perm = []
        for i in range(n_left):
            for r in range(n_right):
                perm.append((i * n_right + r, (i ^ by) * n_right + (r + 1) % n_right))
        return lax.ppermute(value, ("left", "right"), perm)

    def per_device(
        left_table, left_state, right_table, right_state, relation_table, relation_state,
        source_ids, target_ids, relation_ids, negative_ids,
    ):
        rows = left_table.shape[0]
        width = left_table.shape[1]
        left_t, right_t, relation_t = left_table.T, right_table.T, relation_table.T
        nrel = relation_t.shape[1]
        here_l, here_r = lax.axis_index("left"), lax.axis_index("right")
        me = here_r.astype(jnp.int32).reshape(1)
        edges = source_ids.shape[-1]
        groups = negative_ids.shape[2]
        n_rows = n_left * rows
        half = outer * rows
        one_block = shape(width, rows, dtype=BF)
        table_bf = shape(width, edges, dtype=BF)

        def cast(value, after=()):
            parts = 5 if width % 80 == 0 else 1
            scratch = [pltpu.VMEM(value.shape, F32), pltpu.SemaphoreType.DMA((parts,))]
            return call(cast_body, one_block, scratch, after=after, place=pl.ANY)(value)

        right_bf = cast(right_t)
        near = [right_bf] + [swap_left(right_bf, 2 * k) for k in range(1, outer)]
        other_own = swap_left(right_bf, 1)
        blocks = shape(width, half - rows, dtype=BF)
        joined = call(join_body, blocks, flops=COST_JOIN)(*near[1:])
        other_rest = swap_left(joined, 1)

        ids = [source_ids, target_ids, relation_ids, negative_ids]
        longest = max(i.shape[-1] for i in ids)
        ids = [i.reshape(-1, i.shape[-1]) for i in ids]
        ids = jnp.concatenate([jnp.pad(i, ((0, 0), (0, longest - i.shape[-1]))) for i in ids], axis=0)
        ids = lax.ppermute(ids, "right", [(i, (i - 1) % n_right) for i in range(n_right)])
        left_bf = call(join_body, one_block, after=(other_own, ids))(cast(left_t))
        half_left = [left_bf] + [swap_right(left_bf, 2 * k) for k in range(1, far_right)]
        sibling_left = swap_right(jnp.concatenate(half_left, axis=1), 1)
        place = jnp.stack([here_r, here_l]).astype(jnp.int32)
        weight, relation_bf, ids = call(
            functools.partial(count_body, far_right, outer, rows, negative_ids.shape[-1]),
            (shape(groups, n_rows, LANES), shape(width, nrel, dtype=BF), shape(*ids.shape, dtype=jnp.int32)),
            here=place,
        )(ids, relation_t)
        moved = next_column(call(pack_body, shape(width + 8, rows), after=(joined,))(right_t, right_state[None, :]), 0)

        s, o, q = call(functools.partial(query_body, far_right), (table_bf, table_bf, table_bf))(
            *half_left, sibling_left, relation_bf, ids
        )
        part = pltpu.VMEM((width, half), BF)
        right_near, qg_near = call(
            functools.partial(near_body, outer),
            (shape(width, half), shape(width, edges)),
            [part, pltpu.VMEM((half, edges), BF)],
        )(*near, q, weight, ids)
        tall = nrel // LANES * width
        size = -(-tall // (n_right * 16)) * 16
        piece = shape(size, LANES, dtype=BF)
        all_pieces = pltpu.VMEM((size * n_right, LANES), F32)
        m, g, mine, theirs = call(
            functools.partial(far_body, 2, n_right),
            (shape(half, edges, dtype=BF), shape(width, edges), shape(far_right * size, LANES),
             shape(far_right * size, LANES, dtype=BF)),
            [part, pltpu.VMEM((width, nrel), F32), all_pieces],
            me,
            after=(moved,),
        )(other_own, other_rest, q, weight, ids, qg_near, s)
        left_rows = n_right * rows
        left_half = left_rows // 2
        right_far, left_near, left_far = call(
            rest_body,
            (shape(width, half, dtype=BF), shape(width, left_half), shape(width, left_half, dtype=BF)),
            [pltpu.VMEM((width, left_rows), F32)],
        )(q, m, g, o, ids)

        left_own, *blocks = call(left_body, (shape(width, rows),) + (one_block,) * (far_right - 1))(
            left_near, swap_right(left_far, 1)
        )
        left_got = [swap_right(block, 2 * (k + 1)) for k, block in enumerate(blocks)]

        mine, *rest = call(
            piece_body, (shape(size, LANES),) + (piece,) * (far_right - 1), flops=COST_SUM, after=(right_far,)
        )(mine, swap_right(theirs, 1))
        got = [swap_right(p, 2 * (k + 1)) for k, p in enumerate(rest)]
        mine = call(sum_body, piece, flops=COST_SUM)(mine, *got)
        bit = 2
        while bit < n_left:
            mine = call(sum_body, piece, flops=COST_SUM)(mine, swap_left(mine, bit))
            bit *= 2
        right_got = swap_left(right_far, 1)
        blocks = call(chunk_body, (one_block,) * outer, after=(*left_got, mine))(right_near, right_got)
        right_got = [next_column(block, 2 * k) for k, block in enumerate(blocks)]

        mine = call(sum_body, piece, flops=COST_SUM)(mine, swap_left(mine, 1))
        pieces = [mine] + [swap_right(mine, 2 * k) for k in range(1, far_right)]
        sibling = swap_right(call(stack_body, shape(far_right * size, LANES, dtype=BF))(*pieces), 1)

        def update(got, table, state, flops=0):
            outs = (shape(width, rows), shape(1, rows))
            return call(functools.partial(update_body, len(got)), outs, flops=flops)(*got, table, state)

        left_new, left_state_new = update([left_own, *left_got], left_t, left_state[None, :])
        right_new, right_state_new = update(right_got, moved, moved, COST_UPDATE)
        relation_new, relation_state_new = call(
            functools.partial(relation_body, n_right),
            (shape(width, nrel), shape(1, nrel)),
            [all_pieces],
            me,
            after=(right_state_new,),
        )(*pieces, sibling, relation_t, relation_state[None, :])
        return (
            left_new.T, left_state_new.reshape(-1), right_new.T, right_state_new.reshape(-1),
            relation_new.T, relation_state_new.reshape(-1),
        )

    return per_device


def solution(mesh):
    rows = P(("left", "right"), None)
    vector = P(("left", "right"))
    ids = P("left", "right", None)
    return jax.shard_map(
        build(mesh),
        mesh=mesh,
        in_specs=(rows, vector, rows, vector, P(), P(), ids, ids, ids, P("left", "right", None, None)),
        out_specs=(rows, vector, rows, vector, P(), P()),
        check_vma=False,
    )
```

```python
import functools

import jax
import jax.numpy as jnp
from jax import lax
from jax.experimental import pallas as pl
from jax.experimental.pallas import tpu as pltpu
from jax.sharding import PartitionSpec as P

LEARN_RATE = 0.1
NEG_WEIGHT = 0.03125
BF = jnp.bfloat16
F32 = jnp.float32
VMEM_LIMIT = 32 * 1024 * 1024
LANES = 128
COST_JOIN = 6e9
COST_UPDATE = 0
COST_SUM = 1e9


def dot(a, b, a_dim, b_dim):
    return lax.dot_general(a, b, (((a_dim,), (b_dim,)), ((), ())), preferred_element_type=F32)


def hot(ids, count):
    spot = lax.broadcasted_iota(jnp.int32, (count, ids.shape[1]), 0)
    return jnp.where(spot == ids, 1.0, 0.0).astype(BF)


def step_of(size, most=256):
    return most if size % most == 0 else size


def call(body, out_shape, scratch=(), here=None, after=(), flops=0, place=pltpu.VMEM):
    def run(*args):
        specs = [pl.BlockSpec(memory_space=place)] * len(args)
        if here is not None:
            specs.append(pl.BlockSpec(memory_space=pltpu.SMEM))
            args = (*args, here)
        inner = body
        if after:
            used = len(args)

            def inner(*refs):
                body(*refs[:used], *refs[used + len(after):])

            specs += [pl.BlockSpec(memory_space=pl.ANY)] * len(after)
            args = (*args, *after)
        return pl.pallas_call(
            inner,
            out_shape=out_shape,
            in_specs=specs,
            scratch_shapes=list(scratch),
            compiler_params=pltpu.CompilerParams(vmem_limit_bytes=VMEM_LIMIT),
            cost_estimate=pl.CostEstimate(flops=int(flops), bytes_accessed=0, transcendentals=0),
        )(*args)

    return run


def shape(*dims, dtype=F32):
    return jax.ShapeDtypeStruct(dims, dtype)


def cast_body(in_ref, out_ref, held_ref, sems):
    rows = held_ref.shape[0] // sems.shape[0]
    copies = []
    for k in range(sems.shape[0]):
        at = slice(k * rows, (k + 1) * rows)
        copies.append(pltpu.make_async_copy(in_ref.at[at], held_ref.at[at], sems.at[k]))
        copies[-1].start()
    for k, copy in enumerate(copies):
        at = slice(k * rows, (k + 1) * rows)
        copy.wait()
        out_ref[at, :] = held_ref[at, :].astype(BF)


def count_body(far_right, outer, rows, slots, ids_ref, relation_ref, place_ref, out_ref, relation_bf_ref, local_ref):
    def local(ids, here, half):
        block = (ids // rows) ^ here
        return (block % 2 * half + block // 2) * rows + ids % rows

    ids = ids_ref[...]
    local_ref[...] = ids
    local_ref[0:1, :] = local(ids[0:1], place_ref[0], far_right)
    local_ref[1:2, :] = local(ids[1:2], place_ref[1], outer)
    for g in range(out_ref.shape[0]):
        negative = local(ids[3 + g:4 + g, :slots], place_ref[1], outer)
        for at in range(0, out_ref.shape[1], LANES):
            spot = lax.broadcasted_iota(jnp.int32, (LANES, slots), 0) + at
            total = jnp.sum(jnp.where(spot == negative, NEG_WEIGHT, 0.0), axis=1, keepdims=True)
            out_ref[g, at:at + LANES, :] = jnp.broadcast_to(total, (LANES, LANES))
    relation_bf_ref[...] = relation_ref[...].astype(BF)


def pack_body(table_ref, state_ref, pack_ref):
    width = table_ref.shape[0]
    pack_ref[:width, :] = table_ref[...]
    pack_ref[width:, :] = jnp.broadcast_to(state_ref[...], (pack_ref.shape[0] - width, LANES))


def join_body(*refs):
    out_ref = refs[-1]
    at = 0
    for ref in refs[:-1]:
        out_ref[:, at:at + ref.shape[1]] = ref[...]
        at += ref.shape[1]


def query_body(blocks, *refs):
    near_refs, refs = refs[:blocks], refs[blocks:]
    sibling_ref, relation_ref, ids_ref, s_ref, o_ref, q_ref = refs
    relation = relation_ref[...]
    half = s_ref.shape[0] // 2
    edges = s_ref.shape[1]
    step = step_of(edges)
    near = jnp.concatenate([ref[...] for ref in near_refs], axis=1)
    half_rows = near.shape[1]
    for at in range(0, edges, step):
        cols = slice(at, at + step)
        pick = hot(ids_ref[0:1, cols], 2 * half_rows)
        s = dot(near, pick[:half_rows], 1, 0) + dot(sibling_ref[...], pick[half_rows:], 1, 0)
        o = dot(relation, hot(ids_ref[2:3, cols], relation.shape[1]), 1, 0)
        s_ref[:, cols] = s.astype(BF)
        o_ref[:, cols] = o.astype(BF)
        s_re, s_im, o_re, o_im = s[:half], s[half:], o[:half], o[half:]
        q = jnp.concatenate([s_re * o_re - s_im * o_im, s_re * o_im + s_im * o_re], axis=0)
        q_ref[:, cols] = q.astype(BF)


def grad_chunk(rows_t, q_ref, weight_ref, ids_ref, base, at, step):
    count = rows_t.shape[0]
    edges = q_ref.shape[1]
    cols = slice(at, at + step)
    scores = dot(rows_t, q_ref[:, cols], 1, 0)
    spot = lax.broadcasted_iota(jnp.int32, (count, step), 0) + base
    h = jnp.where(spot == ids_ref[1:2, cols], 1.0, 0.0)
    w = weight_ref[at // (edges // weight_ref.shape[0]), base:base + count, :]
    w = jnp.concatenate([w] * (step // LANES), axis=1)
    return ((w + h) * (0.5 * jnp.tanh(0.5 * scores) + 0.5) - h).astype(BF)


def complex_back(g, other):
    half = g.shape[0] // 2
    g_re, g_im, o_re, o_im = g[:half], g[half:], other[:half], other[half:]
    return jnp.concatenate([g_re * o_re + g_im * o_im, g_im * o_re - g_re * o_im], axis=0).astype(BF)


def near_body(blocks, *refs):
    block_refs, refs = refs[:blocks], refs[blocks:]
    q_ref, weight_ref, ids_ref, right_ref, qg_ref, rows_ref, m_ref = refs
    join_body(*block_refs, rows_ref)
    rows_t = rows_ref[...].T
    edges = q_ref.shape[1]
    step = step_of(edges // weight_ref.shape[0])
    for at in range(0, edges, step):
        m_ref[:, at:at + step] = grad_chunk(rows_t, q_ref, weight_ref, ids_ref, 0, at, step)
    right_ref[...] = dot(q_ref[...], m_ref[...], 1, 1).astype(BF)
    qg_ref[...] = dot(rows_ref[...], m_ref[...], 1, 0)


def far_body(blocks, pieces, *refs):
    block_refs, refs = refs[:blocks], refs[blocks:]
    q_ref, weight_ref, ids_ref, qg_ref, s_ref, here_ref = refs[:6]
    m_ref, g_ref, mine_ref, theirs_ref, rows_ref, kinds_ref, tall_ref = refs[6:]
    join_body(*block_refs, rows_ref)
    rows_t = rows_ref[...].T
    base = rows_t.shape[0]
    width, edges = qg_ref.shape
    step = step_of(edges // weight_ref.shape[0])
    for at in range(0, edges, step):
        cols = slice(at, at + step)
        m = grad_chunk(rows_t, q_ref, weight_ref, ids_ref, base, at, step)
        m_ref[:, cols] = m
        g = qg_ref[:, cols] + dot(rows_ref[...], m, 1, 0)
        g_ref[:, cols] = g
        by_kind = complex_back(g, s_ref[:, cols].astype(F32))
        kinds = dot(by_kind, hot(ids_ref[2:3, cols], kinds_ref.shape[1]), 1, 1)
        if at == 0:
            kinds_ref[...] = kinds
        else:
            kinds_ref[...] += kinds
    parts = kinds_ref.shape[1] // LANES
    for j in range(parts):
        tall_ref[j * width:(j + 1) * width, :] = kinds_ref[:, j * LANES:(j + 1) * LANES]
    rest = tall_ref.shape[0] - parts * width
    if rest:
        tall_ref[parts * width:, :] = jnp.zeros((rest, LANES), F32)
    here = here_ref[0]
    size = tall_ref.shape[0] // pieces
    for k in range(pieces):
        start = pl.multiple_of((here ^ k) * size, 16)
        piece = tall_ref[pl.ds(start, size), :]
        at = slice(k // 2 * size, (k // 2 + 1) * size)
        if k % 2:
            theirs_ref[at, :] = piece.astype(BF)
        else:
            mine_ref[at, :] = piece


def rest_body(q_ref, m_ref, g_ref, o_ref, ids_ref, right_ref, near_ref, far_ref, left_ref):
    right_ref[...] = dot(q_ref[...], m_ref[...], 1, 1).astype(BF)
    edges = q_ref.shape[1]
    step = step_of(edges)
    for at in range(0, edges, step):
        cols = slice(at, at + step)
        by_source = complex_back(g_ref[:, cols], o_ref[:, cols].astype(F32))
        left = dot(by_source, hot(ids_ref[0:1, cols], left_ref.shape[1]), 1, 1)
        if at == 0:
            left_ref[...] = left
        else:
            left_ref[...] += left
    cut = left_ref.shape[1] // 2
    near_ref[...] = left_ref[:, :cut]
    far_ref[...] = left_ref[:, cut:].astype(BF)


def relation_body(pieces, *refs):
    piece_refs, refs = refs[:pieces // 2], refs[pieces // 2:]
    sibling_ref, table_ref, state_ref, here_ref, new_ref, state_new_ref, tall_ref = refs
    here = here_ref[0]
    size = tall_ref.shape[0] // pieces
    for k in range(pieces):
        start = pl.multiple_of((here ^ k) * size, 16)
        piece = sibling_ref[k // 2 * size:(k // 2 + 1) * size, :] if k % 2 else piece_refs[k // 2][...]
        tall_ref[pl.ds(start, size), :] = piece.astype(F32)
    width, count = table_ref.shape
    for j in range(count // LANES):
        cols = slice(j * LANES, (j + 1) * LANES)
        g = tall_ref[j * width:(j + 1) * width, :]
        state = state_ref[:, cols] + jnp.sum(g * g, axis=0, keepdims=True) * (1.0 / width)
        state_new_ref[:, cols] = state
        new_ref[:, cols] = table_ref[:, cols] - g * (LEARN_RATE * lax.rsqrt(state))


def piece_body(mine_ref, got_ref, own_ref, *other_refs):
    size = own_ref.shape[0]
    for k, ref in enumerate((own_ref, *other_refs)):
        at = slice(k * size, (k + 1) * size)
        ref[...] = (mine_ref[at, :] + got_ref[at, :].astype(F32)).astype(ref.dtype)


def left_body(near_ref, got_ref, own_ref, *other_refs):
    for k, ref in enumerate((own_ref, *other_refs)):
        at = slice(k * LANES, (k + 1) * LANES)
        ref[...] = (near_ref[:, at] + got_ref[:, at].astype(F32)).astype(ref.dtype)


def stack_body(*refs):
    size = refs[0].shape[0]
    for k, ref in enumerate(refs[:-1]):
        refs[-1][k * size:(k + 1) * size, :] = ref[...]


def block_body(k, near_ref, got_ref, block_ref):
    cols = slice(k * LANES, (k + 1) * LANES)
    block_ref[...] = (near_ref[:, cols].astype(F32) + got_ref[:, cols].astype(F32)).astype(block_ref.dtype)


def sum_body(*refs):
    total = refs[0][...].astype(F32)
    for ref in refs[1:-1]:
        total = total + ref[...].astype(F32)
    refs[-1][...] = total.astype(BF)


def update_body(parts, *refs):
    part_refs, (table_ref, state_ref, new_ref, state_new_ref) = refs[:parts], refs[parts:]
    g = part_refs[0][...].astype(F32)
    for ref in part_refs[1:]:
        g = g + ref[...].astype(F32)
    width = g.shape[0]
    state = state_ref[state_ref.shape[0] - 1:, :] + jnp.sum(g * g, axis=0, keepdims=True) * (1.0 / width)
    state_new_ref[...] = state
    new_ref[...] = table_ref[:width, :] - g * (LEARN_RATE * lax.rsqrt(state))


def build(mesh):
    n_left, n_right = mesh.shape["left"], mesh.shape["right"]
    for count in (n_left, n_right):
        assert count & (count - 1) == 0 and count > 3
    outer = n_left // 2
    far_right = n_right // 2

    def swap_left(value, by):
        return lax.ppermute(value, "left", [(i, i ^ by) for i in range(n_left)])

    def swap_right(value, by):
        return lax.ppermute(value, "right", [(i, i ^ by) for i in range(n_right)])

    def next_column(value, by):
        perm = []
        for i in range(n_left):
            for r in range(n_right):
                perm.append((i * n_right + r, (i ^ by) * n_right + (r + 1) % n_right))
        return lax.ppermute(value, ("left", "right"), perm)

    def per_device(
        left_table, left_state, right_table, right_state, relation_table, relation_state,
        source_ids, target_ids, relation_ids, negative_ids,
    ):
        rows = left_table.shape[0]
        width = left_table.shape[1]
        left_t, right_t, relation_t = left_table.T, right_table.T, relation_table.T
        nrel = relation_t.shape[1]
        here_l, here_r = lax.axis_index("left"), lax.axis_index("right")
        me = here_r.astype(jnp.int32).reshape(1)
        edges = source_ids.shape[-1]
        groups = negative_ids.shape[2]
        n_rows = n_left * rows
        half = outer * rows
        one_block = shape(width, rows, dtype=BF)
        table_bf = shape(width, edges, dtype=BF)

        def cast(value, after=()):
            parts = 5 if width % 80 == 0 else 1
            scratch = [pltpu.VMEM(value.shape, F32), pltpu.SemaphoreType.DMA((parts,))]
            return call(cast_body, one_block, scratch, after=after, place=pl.ANY)(value)

        right_bf = right_t.astype(BF)
        near = [next_column(right_bf, 2 * k) for k in range(outer)]
        other_own = next_column(right_bf, 1)

        ids = [source_ids, target_ids, relation_ids, negative_ids]
        longest = max(i.shape[-1] for i in ids)
        ids = [i.reshape(-1, i.shape[-1]) for i in ids]
        ids = jnp.concatenate([jnp.pad(i, ((0, 0), (0, longest - i.shape[-1]))) for i in ids], axis=0)
        place = jnp.stack([here_r, here_l]).astype(jnp.int32)
        weight, relation_bf, ids = call(
            functools.partial(count_body, far_right, outer, rows, negative_ids.shape[-1]),
            (shape(groups, n_rows, LANES), shape(width, nrel, dtype=BF), shape(*ids.shape, dtype=jnp.int32)),
            here=place,
        )(ids, relation_t)

        blocks = shape(width, half - rows, dtype=BF)
        joined = call(join_body, blocks, flops=COST_JOIN, after=(weight,))(*near[1:])
        other_rest = swap_left(joined, 1)
        left_bf = call(join_body, one_block, after=(other_own, near[0]))(cast(left_t))
        half_left = [left_bf] + [swap_right(left_bf, 2 * k) for k in range(1, far_right)]
        sibling_left = swap_right(jnp.concatenate(half_left, axis=1), 1)
        moved = next_column(call(pack_body, shape(width + 8, rows), after=(joined,))(right_t, right_state[None, :]), 0)

        s, o, q = call(functools.partial(query_body, far_right), (table_bf, table_bf, table_bf))(
            *half_left, sibling_left, relation_bf, ids
        )
        part = pltpu.VMEM((width, half), BF)
        right_near, qg_near = call(
            functools.partial(near_body, outer),
            (shape(width, half, dtype=BF), shape(width, edges)),
            [part, pltpu.VMEM((half, edges), BF)],
        )(*near, q, weight, ids)
        tall = nrel // LANES * width
        size = -(-tall // (n_right * 16)) * 16
        piece = shape(size, LANES, dtype=BF)
        all_pieces = pltpu.VMEM((size * n_right, LANES), F32)
        m, g, mine, theirs = call(
            functools.partial(far_body, 2, n_right),
            (shape(half, edges, dtype=BF), shape(width, edges), shape(far_right * size, LANES),
             shape(far_right * size, LANES, dtype=BF)),
            [part, pltpu.VMEM((width, nrel), F32), all_pieces],
            me,
            after=(moved,),
        )(other_own, other_rest, q, weight, ids, qg_near, s)
        left_rows = n_right * rows
        left_half = left_rows // 2
        right_far, left_near, left_far = call(
            rest_body,
            (shape(width, half, dtype=BF), shape(width, left_half), shape(width, left_half, dtype=BF)),
            [pltpu.VMEM((width, left_rows), F32)],
        )(q, m, g, o, ids)

        left_own, *blocks = call(left_body, (shape(width, rows),) + (one_block,) * (far_right - 1))(
            left_near, swap_right(left_far, 1)
        )
        left_got = [swap_right(block, 2 * (k + 1)) for k, block in enumerate(blocks)]

        mine, *rest = call(
            piece_body, (shape(size, LANES),) + (piece,) * (far_right - 1), flops=COST_SUM, after=(right_far,)
        )(mine, swap_right(theirs, 1))
        got = [swap_right(p, 2 * (k + 1)) for k, p in enumerate(rest)]
        mine = call(sum_body, piece, flops=COST_SUM)(mine, *got)

        far_got = swap_left(right_far, 1)

        def block(k, dtype=BF, after=()):
            body = functools.partial(block_body, k)
            return call(body, shape(width, rows, dtype=dtype), after=after)(right_near, far_got)

        bits = [1 << b for b in range(1, n_left.bit_length() - 1)] + [1]
        arrived = {step: [] for step in range(len(bits))}
        for step, bit in enumerate(bits):
            after = arrived[0] if step == len(bits) - 1 else ()
            mine = call(sum_body, piece, flops=COST_SUM, after=after)(mine, swap_left(mine, bit))
            for k in range(outer - 1, 0, -1):
                if (outer - 1 - k) * len(bits) // (outer - 1) == step:
                    arrived[step].append(swap_left(block(k, after=(mine,)), 2 * k))
        right_got = [block(0, F32)] + [a for step in arrived.values() for a in step]

        pieces = [mine] + [swap_right(mine, 2 * k) for k in range(1, far_right)]
        stacked = call(stack_body, shape(far_right * size, LANES, dtype=BF), after=arrived[1])(*pieces)
        sibling = swap_right(stacked, 1)

        def update(got, table, state, flops=0):
            outs = (shape(width, rows), shape(1, rows))
            return call(functools.partial(update_body, len(got)), outs, flops=flops)(*got, table, state)

        left_new, left_state_new = update([left_own, *left_got], left_t, left_state[None, :])
        right_new, right_state_new = update(right_got, moved, moved, COST_UPDATE)
        relation_new, relation_state_new = call(
            functools.partial(relation_body, n_right),
            (shape(width, nrel), shape(1, nrel)),
            [all_pieces],
            me,
            after=(right_state_new,),
        )(*pieces, sibling, relation_t, relation_state[None, :])
        return (
            left_new.T, left_state_new.reshape(-1), right_new.T, right_state_new.reshape(-1),
            relation_new.T, relation_state_new.reshape(-1),
        )

    return per_device


def solution(mesh):
    rows = P(("left", "right"), None)
    vector = P(("left", "right"))
    ids = P("left", "right", None)
    return jax.shard_map(
        build(mesh),
        mesh=mesh,
        in_specs=(rows, vector, rows, vector, P(), P(), ids, ids, ids, P("left", "right", None, None)),
        out_specs=(rows, vector, rows, vector, P(), P()),
        check_vma=False,
    )
```

```python
import functools

import jax
import jax.numpy as jnp
from jax import lax
from jax.experimental import pallas as pl
from jax.experimental.pallas import tpu as pltpu
from jax.sharding import PartitionSpec as P

LEARN_RATE = 0.1
NEG_WEIGHT = 0.03125
BF = jnp.bfloat16
F32 = jnp.float32
VMEM_LIMIT = 32 * 1024 * 1024
LANES = 128
COST_JOIN = 6e9
COST_UPDATE = 6e9
COST_CHUNK = 12e9


def dot(a, b, a_dim, b_dim):
    return lax.dot_general(a, b, (((a_dim,), (b_dim,)), ((), ())), preferred_element_type=F32)


def hot(ids, count):
    spot = lax.broadcasted_iota(jnp.int32, (count, ids.shape[1]), 0)
    return jnp.where(spot == ids, 1.0, 0.0).astype(BF)


def step_of(size, most=256):
    return most if size % most == 0 else size


def call(body, out_shape, scratch=(), here=None, after=(), flops=0, place=pltpu.VMEM):
    def run(*args):
        specs = [pl.BlockSpec(memory_space=place)] * len(args)
        if here is not None:
            specs.append(pl.BlockSpec(memory_space=pltpu.SMEM))
            args = (*args, here)
        inner = body
        if after:
            used = len(args)

            def inner(*refs):
                body(*refs[:used], *refs[used + len(after):])

            specs += [pl.BlockSpec(memory_space=pl.ANY)] * len(after)
            args = (*args, *after)
        return pl.pallas_call(
            inner,
            out_shape=out_shape,
            in_specs=specs,
            scratch_shapes=list(scratch),
            compiler_params=pltpu.CompilerParams(vmem_limit_bytes=VMEM_LIMIT),
            cost_estimate=pl.CostEstimate(flops=int(flops), bytes_accessed=0, transcendentals=0),
        )(*args)

    return run


def shape(*dims, dtype=F32):
    return jax.ShapeDtypeStruct(dims, dtype)


def cast_body(in_ref, out_ref, held_ref, sems):
    rows = held_ref.shape[0] // sems.shape[0]
    copies = []
    for k in range(sems.shape[0]):
        at = slice(k * rows, (k + 1) * rows)
        copies.append(pltpu.make_async_copy(in_ref.at[at], held_ref.at[at], sems.at[k]))
        copies[-1].start()
    for k, copy in enumerate(copies):
        at = slice(k * rows, (k + 1) * rows)
        copy.wait()
        out_ref[at, :] = held_ref[at, :].astype(BF)


def count_body(far_right, outer, rows, slots, ids_ref, relation_ref, place_ref, out_ref, relation_bf_ref, local_ref):
    def local(ids, here, half):
        block = (ids // rows) ^ here
        return (block % 2 * half + block // 2) * rows + ids % rows

    ids = ids_ref[...]
    local_ref[...] = ids
    local_ref[0:1, :] = local(ids[0:1], place_ref[0], far_right)
    local_ref[1:2, :] = local(ids[1:2], place_ref[1], outer)
    for g in range(out_ref.shape[0]):
        negative = local(ids[3 + g:4 + g, :slots], place_ref[1], outer)
        for at in range(0, out_ref.shape[1], LANES):
            spot = lax.broadcasted_iota(jnp.int32, (LANES, slots), 0) + at
            total = jnp.sum(jnp.where(spot == negative, NEG_WEIGHT, 0.0), axis=1, keepdims=True)
            out_ref[g, at:at + LANES, :] = jnp.broadcast_to(total, (LANES, LANES))
    relation_bf_ref[...] = relation_ref[...].astype(BF)


def pack_body(table_ref, state_ref, pack_ref):
    width = table_ref.shape[0]
    pack_ref[:width, :] = table_ref[...]
    pack_ref[width:, :] = jnp.broadcast_to(state_ref[...], (pack_ref.shape[0] - width, LANES))


def join_body(*refs):
    out_ref = refs[-1]
    at = 0
    for ref in refs[:-1]:
        out_ref[:, at:at + ref.shape[1]] = ref[...]
        at += ref.shape[1]


def query_body(blocks, *refs):
    near_refs, refs = refs[:blocks], refs[blocks:]
    sibling_ref, relation_ref, ids_ref, s_ref, o_ref, q_ref = refs
    relation = relation_ref[...]
    half = s_ref.shape[0] // 2
    edges = s_ref.shape[1]
    step = step_of(edges)
    near = jnp.concatenate([ref[...] for ref in near_refs], axis=1)
    half_rows = near.shape[1]
    for at in range(0, edges, step):
        cols = slice(at, at + step)
        pick = hot(ids_ref[0:1, cols], 2 * half_rows)
        s = dot(near, pick[:half_rows], 1, 0) + dot(sibling_ref[...], pick[half_rows:], 1, 0)
        o = dot(relation, hot(ids_ref[2:3, cols], relation.shape[1]), 1, 0)
        s_ref[:, cols] = s.astype(BF)
        o_ref[:, cols] = o.astype(BF)
        s_re, s_im, o_re, o_im = s[:half], s[half:], o[:half], o[half:]
        q = jnp.concatenate([s_re * o_re - s_im * o_im, s_re * o_im + s_im * o_re], axis=0)
        q_ref[:, cols] = q.astype(BF)


def grad_chunk(rows_t, q_ref, weight_ref, ids_ref, base, at, step):
    count = rows_t.shape[0]
    edges = q_ref.shape[1]
    cols = slice(at, at + step)
    scores = dot(rows_t, q_ref[:, cols], 1, 0)
    spot = lax.broadcasted_iota(jnp.int32, (count, step), 0) + base
    h = jnp.where(spot == ids_ref[1:2, cols], 1.0, 0.0)
    w = weight_ref[at // (edges // weight_ref.shape[0]), base:base + count, :]
    w = jnp.concatenate([w] * (step // LANES), axis=1)
    return ((w + h) * (0.5 * jnp.tanh(0.5 * scores) + 0.5) - h).astype(BF)


def complex_back(g, other):
    half = g.shape[0] // 2
    g_re, g_im, o_re, o_im = g[:half], g[half:], other[:half], other[half:]
    return jnp.concatenate([g_re * o_re + g_im * o_im, g_im * o_re - g_re * o_im], axis=0).astype(BF)


def near_body(blocks, *refs):
    block_refs, refs = refs[:blocks], refs[blocks:]
    q_ref, weight_ref, ids_ref, right_ref, qg_ref, rows_ref, m_ref = refs
    join_body(*block_refs, rows_ref)
    rows_t = rows_ref[...].T
    edges = q_ref.shape[1]
    step = step_of(edges // weight_ref.shape[0])
    for at in range(0, edges, step):
        m_ref[:, at:at + step] = grad_chunk(rows_t, q_ref, weight_ref, ids_ref, 0, at, step)
    right_ref[...] = dot(q_ref[...], m_ref[...], 1, 1)
    qg_ref[...] = dot(rows_ref[...], m_ref[...], 1, 0)


def far_body(blocks, *refs):
    block_refs, refs = refs[:blocks], refs[blocks:]
    q_ref, weight_ref, ids_ref, m_ref, right_ref, rows_ref = refs
    join_body(*block_refs, rows_ref)
    rows_t = rows_ref[...].T
    base = rows_t.shape[0]
    step = step_of(q_ref.shape[1] // weight_ref.shape[0])
    for at in range(0, q_ref.shape[1], step):
        m_ref[:, at:at + step] = grad_chunk(rows_t, q_ref, weight_ref, ids_ref, base, at, step)
    right_ref[...] = dot(q_ref[...], m_ref[...], 1, 1).astype(BF)


def back_body(blocks, *refs):
    block_refs, refs = refs[:blocks], refs[blocks:]
    m_ref, qg_ref, s_ref, ids_ref, g_ref, tall_ref, rows_ref, kinds_ref = refs
    join_body(*block_refs, rows_ref)
    width, edges = qg_ref.shape
    step = step_of(edges)
    for at in range(0, edges, step):
        cols = slice(at, at + step)
        g = qg_ref[:, cols] + dot(rows_ref[...], m_ref[:, cols], 1, 0)
        g_ref[:, cols] = g
        by_kind = complex_back(g, s_ref[:, cols].astype(F32))
        kinds = dot(by_kind, hot(ids_ref[2:3, cols], kinds_ref.shape[1]), 1, 1)
        if at == 0:
            kinds_ref[...] = kinds
        else:
            kinds_ref[...] += kinds
    parts = kinds_ref.shape[1] // LANES
    for j in range(parts):
        tall_ref[j * width:(j + 1) * width, :] = kinds_ref[:, j * LANES:(j + 1) * LANES].astype(BF)
    rest = tall_ref.shape[0] - parts * width
    if rest:
        tall_ref[parts * width:, :] = jnp.zeros((rest, LANES), BF)


def source_body(g_ref, o_ref, ids_ref, near_ref, far_ref, left_ref):
    edges = g_ref.shape[1]
    step = step_of(edges)
    for at in range(0, edges, step):
        cols = slice(at, at + step)
        by_source = complex_back(g_ref[:, cols], o_ref[:, cols].astype(F32))
        left = dot(by_source, hot(ids_ref[0:1, cols], left_ref.shape[1]), 1, 1)
        if at == 0:
            left_ref[...] = left
        else:
            left_ref[...] += left
    cut = left_ref.shape[1] // 2
    near_ref[...] = left_ref[:, :cut]
    far_ref[...] = left_ref[:, cut:].astype(BF)


def relation_body(tall_ref, table_ref, state_ref, new_ref, state_new_ref):
    width, count = table_ref.shape
    for j in range(count // LANES):
        cols = slice(j * LANES, (j + 1) * LANES)
        g = tall_ref[j * width:(j + 1) * width, :].astype(F32)
        state = state_ref[:, cols] + jnp.sum(g * g, axis=0, keepdims=True) * (1.0 / width)
        state_new_ref[:, cols] = state
        new_ref[:, cols] = table_ref[:, cols] - g * (LEARN_RATE * lax.rsqrt(state))


def pieces_body(pieces_ref, out_ref):
    total = jnp.sum(pieces_ref[...].astype(F32), axis=0).astype(BF)
    for k in range(out_ref.shape[0]):
        out_ref[k] = total


def left_body(near_ref, got_ref, own_ref, *other_refs):
    for k, ref in enumerate((own_ref, *other_refs)):
        at = slice(k * LANES, (k + 1) * LANES)
        ref[...] = (near_ref[:, at] + got_ref[:, at].astype(F32)).astype(ref.dtype)


def chunk_body(near_ref, got_ref, *block_refs):
    for k, ref in enumerate(block_refs):
        cols = slice(k * LANES, (k + 1) * LANES)
        ref[...] = (near_ref[:, cols] + got_ref[:, cols].astype(F32)).astype(BF)


def update_body(parts, *refs):
    part_refs, (table_ref, state_ref, new_ref, state_new_ref) = refs[:parts], refs[parts:]
    g = part_refs[0][...].astype(F32)
    for ref in part_refs[1:]:
        g = g + ref[...].astype(F32)
    width = g.shape[0]
    state = state_ref[state_ref.shape[0] - 1:, :] + jnp.sum(g * g, axis=0, keepdims=True) * (1.0 / width)
    state_new_ref[...] = state
    new_ref[...] = table_ref[:width, :] - g * (LEARN_RATE * lax.rsqrt(state))


def build(mesh):
    n_left, n_right = mesh.shape["left"], mesh.shape["right"]
    for count in (n_left, n_right):
        assert count & (count - 1) == 0 and count > 3
    outer = n_left // 2
    far_right = n_right // 2

    def swap_left(value, by):
        return lax.ppermute(value, "left", [(i, i ^ by) for i in range(n_left)])

    def swap_right(value, by):
        return lax.ppermute(value, "right", [(i, i ^ by) for i in range(n_right)])

    def next_column(value, by):
        perm = []
        for i in range(n_left):
            for r in range(n_right):
                perm.append((i * n_right + r, (i ^ by) * n_right + (r + 1) % n_right))
        return lax.ppermute(value, ("left", "right"), perm)

    def per_device(
        left_table, left_state, right_table, right_state, relation_table, relation_state,
        source_ids, target_ids, relation_ids, negative_ids,
    ):
        rows = left_table.shape[0]
        width = left_table.shape[1]
        left_t, right_t, relation_t = left_table.T, right_table.T, relation_table.T
        nrel = relation_t.shape[1]
        here_l, here_r = lax.axis_index("left"), lax.axis_index("right")
        edges = source_ids.shape[-1]
        groups = negative_ids.shape[2]
        n_rows = n_left * rows
        half = outer * rows
        one_block = shape(width, rows, dtype=BF)
        table_bf = shape(width, edges, dtype=BF)

        def cast(value, after=()):
            parts = 5 if width % 80 == 0 else 1
            scratch = [pltpu.VMEM(value.shape, F32), pltpu.SemaphoreType.DMA((parts,))]
            return call(cast_body, one_block, scratch, after=after, place=pl.ANY)(value)

        right_bf = cast(right_t)
        near = [right_bf] + [swap_left(right_bf, 2 * k) for k in range(1, outer)]
        other_own = swap_left(right_bf, 1)
        blocks = shape(width, half - rows, dtype=BF)
        joined = call(join_body, blocks, flops=COST_JOIN)(*near[1:])
        other_rest = swap_left(joined, 1)

        ids = [source_ids, target_ids, relation_ids, negative_ids]
        longest = max(i.shape[-1] for i in ids)
        ids = [i.reshape(-1, i.shape[-1]) for i in ids]
        ids = jnp.concatenate([jnp.pad(i, ((0, 0), (0, longest - i.shape[-1]))) for i in ids], axis=0)
        ids = lax.ppermute(ids, "right", [(i, (i - 1) % n_right) for i in range(n_right)])
        left_bf = call(join_body, one_block, after=(other_own, ids))(cast(left_t))
        half_left = [left_bf] + [swap_right(left_bf, 2 * k) for k in range(1, far_right)]
        sibling_left = swap_right(jnp.concatenate(half_left, axis=1), 1)
        place = jnp.stack([here_r, here_l]).astype(jnp.int32)
        weight, relation_bf, ids = call(
            functools.partial(count_body, far_right, outer, rows, negative_ids.shape[-1]),
            (shape(groups, n_rows, LANES), shape(width, nrel, dtype=BF), shape(*ids.shape, dtype=jnp.int32)),
            here=place,
        )(ids, relation_t)
        moved = next_column(call(pack_body, shape(width + 8, rows), after=(joined,))(right_t, right_state[None, :]), 0)

        s, o, q = call(functools.partial(query_body, far_right), (table_bf, table_bf, table_bf))(
            *half_left, sibling_left, relation_bf, ids
        )
        part = pltpu.VMEM((width, half), BF)
        right_near, qg_near = call(
            functools.partial(near_body, outer),
            (shape(width, half), shape(width, edges)),
            [part, pltpu.VMEM((half, edges), BF)],
        )(*near, q, weight, ids)
        m, right_far = call(
            functools.partial(far_body, 2), (shape(half, edges, dtype=BF), shape(width, half, dtype=BF)), [part],
            after=(qg_near, moved),
        )(other_own, other_rest, q, weight, ids)
        right_got = swap_left(right_far, 1)

        devices = n_left * n_right
        tall = nrel // LANES * width
        size = -(-tall // (devices * 16)) * 16
        left_rows = n_right * rows
        left_half = left_rows // 2
        g, kinds = call(
            functools.partial(back_body, 2),
            (shape(width, edges), shape(devices * size, LANES, dtype=BF)),
            [part, pltpu.VMEM((width, nrel), F32)],
        )(other_own, other_rest, m, qg_near, s, ids)

        def exchange(value):
            return lax.all_to_all(value, ("left", "right"), 0, 0, tiled=True)

        pieces = shape(devices, size, LANES, dtype=BF)
        kinds = exchange(kinds.reshape(devices, size, LANES))
        left_near, left_far = call(
            source_body,
            (shape(width, left_half), shape(width, left_half, dtype=BF)),
            [pltpu.VMEM((width, left_rows), F32)],
            after=(kinds,),
        )(g, o, ids)
        left_own, *halves = call(left_body, (shape(width, rows),) + (one_block,) * (far_right - 1))(
            left_near, swap_right(left_far, 1)
        )
        left_got = [swap_right(block, 2 * (k + 1)) for k, block in enumerate(halves)]

        blocks = call(chunk_body, (one_block,) * outer, after=(kinds,), flops=COST_CHUNK)(right_near, right_got)
        kinds = call(pieces_body, pieces, after=(blocks[0],))(kinds)
        right_got = [next_column(block, 2 * k) for k, block in enumerate(blocks)]
        kinds = exchange(kinds).reshape(devices * size, LANES)

        def update(got, table, state, flops=0):
            outs = (shape(width, rows), shape(1, rows))
            return call(functools.partial(update_body, len(got)), outs, flops=flops)(*got, table, state)

        left_new, left_state_new = update([left_own, *left_got], left_t, left_state[None, :])
        right_new, right_state_new = update(right_got, moved, moved, COST_UPDATE)
        relation_new, relation_state_new = call(relation_body, (shape(width, nrel), shape(1, nrel)))(
            kinds, relation_t, relation_state[None, :]
        )
        return (
            left_new.T, left_state_new.reshape(-1), right_new.T, right_state_new.reshape(-1),
            relation_new.T, relation_state_new.reshape(-1),
        )

    return per_device


def solution(mesh):
    rows = P(("left", "right"), None)
    vector = P(("left", "right"))
    ids = P("left", "right", None)
    return jax.shard_map(
        build(mesh),
        mesh=mesh,
        in_specs=(rows, vector, rows, vector, P(), P(), ids, ids, ids, P("left", "right", None, None)),
        out_specs=(rows, vector, rows, vector, P(), P()),
        check_vma=False,
    )
```

```python
import functools

import jax
import jax.numpy as jnp
from jax import lax
from jax.experimental import pallas as pl
from jax.experimental.pallas import tpu as pltpu
from jax.sharding import PartitionSpec as P

LEARN_RATE = 0.1
NEG_WEIGHT = 0.03125
BF = jnp.bfloat16
F32 = jnp.float32
VMEM_LIMIT = 32 * 1024 * 1024
LANES = 128
COST_JOIN_LOW = 6e9
COST_JOIN_HIGH = 6e9
COST_UPDATE = 12e9
COST_HIGH = 12e9
COST_LOW = 12e9
COST_SUM = 1e9
COST_MIDDLE = 6e9


def dot(a, b, a_dim, b_dim):
    return lax.dot_general(a, b, (((a_dim,), (b_dim,)), ((), ())), preferred_element_type=F32)


def hot(ids, count):
    spot = lax.broadcasted_iota(jnp.int32, (count, ids.shape[1]), 0)
    return jnp.where(spot == ids, 1.0, 0.0).astype(BF)


def step_of(size, most=256):
    return most if size % most == 0 else size


def call(body, out_shape, scratch=(), here=None, after=(), flops=0, place=pltpu.VMEM):
    def run(*args):
        specs = [pl.BlockSpec(memory_space=place)] * len(args)
        if here is not None:
            specs.append(pl.BlockSpec(memory_space=pltpu.SMEM))
            args = (*args, here)
        inner = body
        if after:
            used = len(args)

            def inner(*refs):
                body(*refs[:used], *refs[used + len(after):])

            specs += [pl.BlockSpec(memory_space=pl.ANY)] * len(after)
            args = (*args, *after)
        return pl.pallas_call(
            inner,
            out_shape=out_shape,
            in_specs=specs,
            scratch_shapes=list(scratch),
            compiler_params=pltpu.CompilerParams(vmem_limit_bytes=VMEM_LIMIT),
            cost_estimate=pl.CostEstimate(flops=int(flops), bytes_accessed=0, transcendentals=0),
        )(*args)

    return run


def shape(*dims, dtype=F32):
    return jax.ShapeDtypeStruct(dims, dtype)


def cast_body(in_ref, out_ref, held_ref, sems):
    rows = held_ref.shape[0] // sems.shape[0]
    copies = []
    for k in range(sems.shape[0]):
        at = slice(k * rows, (k + 1) * rows)
        copies.append(pltpu.make_async_copy(in_ref.at[at], held_ref.at[at], sems.at[k]))
        copies[-1].start()
    for k, copy in enumerate(copies):
        at = slice(k * rows, (k + 1) * rows)
        copy.wait()
        out_ref[at, :] = held_ref[at, :].astype(BF)


def count_body(far_right, outer, rows, slots, ids_ref, relation_ref, place_ref, out_ref, relation_bf_ref, local_ref):
    def local(ids, here, half):
        block = (ids // rows) ^ here
        return (block % 2 * half + block // 2) * rows + ids % rows

    ids = ids_ref[...]
    local_ref[...] = ids
    local_ref[0:1, :] = local(ids[0:1], place_ref[0], far_right)
    local_ref[1:2, :] = local(ids[1:2], place_ref[1], outer)
    for g in range(out_ref.shape[0]):
        negative = local(ids[3 + g:4 + g, :slots], place_ref[1], outer)
        for at in range(0, out_ref.shape[1], LANES):
            spot = lax.broadcasted_iota(jnp.int32, (LANES, slots), 0) + at
            total = jnp.sum(jnp.where(spot == negative, NEG_WEIGHT, 0.0), axis=1, keepdims=True)
            out_ref[g, at:at + LANES, :] = jnp.broadcast_to(total, (LANES, LANES))
    relation_bf_ref[...] = relation_ref[...].astype(BF)


def pack_body(table_ref, state_ref, pack_ref):
    width = table_ref.shape[0]
    pack_ref[:width, :] = table_ref[...]
    pack_ref[width:, :] = jnp.broadcast_to(state_ref[...], (pack_ref.shape[0] - width, LANES))


def join_body(*refs):
    out_ref = refs[-1]
    at = 0
    for ref in refs[:-1]:
        out_ref[:, at:at + ref.shape[1]] = ref[...]
        at += ref.shape[1]


def query_body(blocks, *refs):
    near_refs, refs = refs[:blocks], refs[blocks:]
    sibling_ref, relation_ref, ids_ref, s_ref, o_ref, q_ref = refs
    relation = relation_ref[...]
    half = s_ref.shape[0] // 2
    edges = s_ref.shape[1]
    step = step_of(edges)
    near = jnp.concatenate([ref[...] for ref in near_refs], axis=1)
    half_rows = near.shape[1]
    for at in range(0, edges, step):
        cols = slice(at, at + step)
        pick = hot(ids_ref[0:1, cols], 2 * half_rows)
        s = dot(near, pick[:half_rows], 1, 0) + dot(sibling_ref[...], pick[half_rows:], 1, 0)
        o = dot(relation, hot(ids_ref[2:3, cols], relation.shape[1]), 1, 0)
        s_ref[:, cols] = s.astype(BF)
        o_ref[:, cols] = o.astype(BF)
        s_re, s_im, o_re, o_im = s[:half], s[half:], o[:half], o[half:]
        q = jnp.concatenate([s_re * o_re - s_im * o_im, s_re * o_im + s_im * o_re], axis=0)
        q_ref[:, cols] = q.astype(BF)


def grad_chunk(rows_t, q_ref, weight_ref, ids_ref, base, at, step):
    count = rows_t.shape[0]
    edges = q_ref.shape[1]
    cols = slice(at, at + step)
    scores = dot(rows_t, q_ref[:, cols], 1, 0)
    spot = lax.broadcasted_iota(jnp.int32, (count, step), 0) + base
    h = jnp.where(spot == ids_ref[1:2, cols], 1.0, 0.0)
    w = weight_ref[at // (edges // weight_ref.shape[0]), base:base + count, :]
    w = jnp.concatenate([w] * (step // LANES), axis=1)
    return ((w + h) * (0.5 * jnp.tanh(0.5 * scores) + 0.5) - h).astype(BF)


def complex_back(g, other):
    half = g.shape[0] // 2
    g_re, g_im, o_re, o_im = g[:half], g[half:], other[:half], other[half:]
    return jnp.concatenate([g_re * o_re + g_im * o_im, g_im * o_re - g_re * o_im], axis=0).astype(BF)


def products(rows_ref, q_ref, weight_ref, ids_ref, m_ref, base):
    rows_t = rows_ref[...].T
    step = step_of(q_ref.shape[1] // weight_ref.shape[0])
    for at in range(0, q_ref.shape[1], step):
        m_ref[:, at:at + step] = grad_chunk(rows_t, q_ref, weight_ref, ids_ref, base, at, step)


def near_body(blocks, *refs):
    block_refs, refs = refs[:blocks], refs[blocks:]
    q_ref, weight_ref, ids_ref, right_ref, qg_ref, rows_ref, m_ref = refs
    join_body(*block_refs, rows_ref)
    products(rows_ref, q_ref, weight_ref, ids_ref, m_ref, 0)
    right_ref[...] = dot(q_ref[...], m_ref[...], 1, 1)
    qg_ref[...] = dot(rows_ref[...], m_ref[...], 1, 0)


def middle_body(base, rows_ref, q_ref, weight_ref, ids_ref, qg_ref, right_ref, qg_out_ref, m_ref):
    products(rows_ref, q_ref, weight_ref, ids_ref, m_ref, base)
    right_ref[...] = dot(q_ref[...], m_ref[...], 1, 1).astype(BF)
    qg_out_ref[...] = qg_ref[...] + dot(rows_ref[...], m_ref[...], 1, 0)


def far_body(
    base, pieces, rows_ref, q_ref, weight_ref, ids_ref, qg_ref, s_ref, here_ref,
    m_ref, g_ref, mine_ref, theirs_ref, kinds_ref, tall_ref,
):
    rows_t = rows_ref[...].T
    width, edges = qg_ref.shape
    step = step_of(edges // weight_ref.shape[0])
    for at in range(0, edges, step):
        cols = slice(at, at + step)
        m = grad_chunk(rows_t, q_ref, weight_ref, ids_ref, base, at, step)
        m_ref[:, cols] = m
        g = qg_ref[:, cols] + dot(rows_ref[...], m, 1, 0)
        g_ref[:, cols] = g
        by_kind = complex_back(g, s_ref[:, cols].astype(F32))
        kinds = dot(by_kind, hot(ids_ref[2:3, cols], kinds_ref.shape[1]), 1, 1)
        if at == 0:
            kinds_ref[...] = kinds
        else:
            kinds_ref[...] += kinds
    parts = kinds_ref.shape[1] // LANES
    for j in range(parts):
        tall_ref[j * width:(j + 1) * width, :] = kinds_ref[:, j * LANES:(j + 1) * LANES]
    rest = tall_ref.shape[0] - parts * width
    if rest:
        tall_ref[parts * width:, :] = jnp.zeros((rest, LANES), F32)
    here = here_ref[0]
    size = tall_ref.shape[0] // pieces
    for k in range(pieces):
        start = pl.multiple_of((here ^ k) * size, 16)
        piece = tall_ref[pl.ds(start, size), :]
        at = slice(k // 2 * size, (k // 2 + 1) * size)
        if k % 2:
            theirs_ref[at, :] = piece.astype(BF)
        else:
            mine_ref[at, :] = piece


def rest_body(q_ref, m_ref, g_ref, o_ref, ids_ref, low_ref, right_ref, low_out_ref, near_ref, far_ref, left_ref):
    low_out_ref[...] = low_ref[...]
    right_ref[...] = dot(q_ref[...], m_ref[...], 1, 1).astype(BF)
    edges = q_ref.shape[1]
    step = step_of(edges)
    for at in range(0, edges, step):
        cols = slice(at, at + step)
        by_source = complex_back(g_ref[:, cols], o_ref[:, cols].astype(F32))
        left = dot(by_source, hot(ids_ref[0:1, cols], left_ref.shape[1]), 1, 1)
        if at == 0:
            left_ref[...] = left
        else:
            left_ref[...] += left
    cut = left_ref.shape[1] // 2
    near_ref[...] = left_ref[:, :cut]
    far_ref[...] = left_ref[:, cut:].astype(BF)


def relation_body(pieces, *refs):
    piece_refs, refs = refs[:pieces // 2], refs[pieces // 2:]
    sibling_ref, table_ref, state_ref, here_ref, new_ref, state_new_ref, tall_ref = refs
    here = here_ref[0]
    size = tall_ref.shape[0] // pieces
    for k in range(pieces):
        start = pl.multiple_of((here ^ k) * size, 16)
        piece = sibling_ref[k // 2 * size:(k // 2 + 1) * size, :] if k % 2 else piece_refs[k // 2][...]
        tall_ref[pl.ds(start, size), :] = piece.astype(F32)
    width, count = table_ref.shape
    for j in range(count // LANES):
        cols = slice(j * LANES, (j + 1) * LANES)
        g = tall_ref[j * width:(j + 1) * width, :]
        state = state_ref[:, cols] + jnp.sum(g * g, axis=0, keepdims=True) * (1.0 / width)
        state_new_ref[:, cols] = state
        new_ref[:, cols] = table_ref[:, cols] - g * (LEARN_RATE * lax.rsqrt(state))


def piece_body(mine_ref, got_ref, own_ref, *other_refs):
    size = own_ref.shape[0]
    for k, ref in enumerate((own_ref, *other_refs)):
        at = slice(k * size, (k + 1) * size)
        ref[...] = (mine_ref[at, :] + got_ref[at, :].astype(F32)).astype(ref.dtype)


def left_body(near_ref, got_ref, own_ref, *other_refs):
    for k, ref in enumerate((own_ref, *other_refs)):
        at = slice(k * LANES, (k + 1) * LANES)
        ref[...] = (near_ref[:, at] + got_ref[:, at].astype(F32)).astype(ref.dtype)


def stack_body(*refs):
    size = refs[0].shape[0]
    for k, ref in enumerate(refs[:-1]):
        refs[-1][k * size:(k + 1) * size, :] = ref[...]


def chunk_body(base, near_ref, got_ref, *block_refs):
    for k, ref in enumerate(block_refs):
        cols = slice(k * LANES, (k + 1) * LANES)
        total = near_ref[:, base + k * LANES:base + (k + 1) * LANES] + got_ref[:, cols].astype(F32)
        ref[...] = total.astype(BF)


def sum_body(*refs):
    total = refs[0][...].astype(F32)
    for ref in refs[1:-1]:
        total = total + ref[...].astype(F32)
    refs[-1][...] = total.astype(BF)


def update_body(parts, *refs):
    part_refs, (table_ref, state_ref, new_ref, state_new_ref) = refs[:parts], refs[parts:]
    g = part_refs[0][...].astype(F32)
    for ref in part_refs[1:]:
        g = g + ref[...].astype(F32)
    width = g.shape[0]
    state = state_ref[state_ref.shape[0] - 1:, :] + jnp.sum(g * g, axis=0, keepdims=True) * (1.0 / width)
    state_new_ref[...] = state
    new_ref[...] = table_ref[:width, :] - g * (LEARN_RATE * lax.rsqrt(state))


def build(mesh):
    n_left, n_right = mesh.shape["left"], mesh.shape["right"]
    for count in (n_left, n_right):
        assert count & (count - 1) == 0 and count > 3
    outer = n_left // 2
    far_right = n_right // 2

    def swap_left(value, by):
        return lax.ppermute(value, "left", [(i, i ^ by) for i in range(n_left)])

    def swap_right(value, by):
        return lax.ppermute(value, "right", [(i, i ^ by) for i in range(n_right)])

    def next_column(value, by):
        perm = []
        for i in range(n_left):
            for r in range(n_right):
                perm.append((i * n_right + r, (i ^ by) * n_right + (r + 1) % n_right))
        return lax.ppermute(value, ("left", "right"), perm)

    def per_device(
        left_table, left_state, right_table, right_state, relation_table, relation_state,
        source_ids, target_ids, relation_ids, negative_ids,
    ):
        rows = left_table.shape[0]
        width = left_table.shape[1]
        left_t, right_t, relation_t = left_table.T, right_table.T, relation_table.T
        nrel = relation_t.shape[1]
        here_l, here_r = lax.axis_index("left"), lax.axis_index("right")
        me = here_r.astype(jnp.int32).reshape(1)
        edges = source_ids.shape[-1]
        groups = negative_ids.shape[2]
        n_rows = n_left * rows
        half = outer * rows
        one_block = shape(width, rows, dtype=BF)
        table_bf = shape(width, edges, dtype=BF)

        def cast(value, after=()):
            parts = 5 if width % 80 == 0 else 1
            scratch = [pltpu.VMEM(value.shape, F32), pltpu.SemaphoreType.DMA((parts,))]
            return call(cast_body, one_block, scratch, after=after, place=pl.ANY)(value)

        right_bf = right_t.astype(BF)
        near = [right_bf] + [swap_left(right_bf, 2 * k) for k in range(1, outer)]
        some = outer // 2
        cut = some * rows
        chunk = shape(width, cut, dtype=BF)
        joined_low = call(join_body, chunk, flops=COST_JOIN_LOW)(*near[:some])
        other_low = call(join_body, chunk, flops=COST_MIDDLE)(swap_left(joined_low, 1))

        ids = [source_ids, target_ids, relation_ids, negative_ids]
        longest = max(i.shape[-1] for i in ids)
        ids = [i.reshape(-1, i.shape[-1]) for i in ids]
        ids = jnp.concatenate([jnp.pad(i, ((0, 0), (0, longest - i.shape[-1]))) for i in ids], axis=0)
        ids = lax.ppermute(ids, "right", [(i, (i - 1) % n_right) for i in range(n_right)])
        left_bf = cast(left_t)
        half_left = [left_bf] + [swap_right(left_bf, 2 * k) for k in range(1, far_right)]
        place = jnp.stack([here_r, here_l]).astype(jnp.int32)
        weight, relation_bf, ids = call(
            functools.partial(count_body, far_right, outer, rows, negative_ids.shape[-1]),
            (shape(groups, n_rows, LANES), shape(width, nrel, dtype=BF), shape(*ids.shape, dtype=jnp.int32)),
            here=place,
            after=(joined_low,),
        )(ids, relation_t)
        joined = call(join_body, chunk, flops=COST_JOIN_HIGH, after=(weight,))(*near[some:])
        other_high = swap_left(joined, 1)
        half_joined = call(join_body, shape(width, far_right * rows, dtype=BF), after=(joined,))(*half_left)
        sibling_left = swap_right(half_joined, 1)
        moved = next_column(call(pack_body, shape(width + 8, rows), after=(joined,))(right_t, right_state[None, :]), 0)

        s, o, q = call(functools.partial(query_body, far_right), (table_bf, table_bf, table_bf))(
            *half_left, sibling_left, relation_bf, ids
        )
        right_near, qg = call(
            functools.partial(near_body, outer),
            (shape(width, half), shape(width, edges)),
            [pltpu.VMEM((width, half), BF), pltpu.VMEM((half, edges), BF)],
        )(*near, q, weight, ids)
        right_low, qg = call(
            functools.partial(middle_body, half), (chunk, shape(width, edges)), [pltpu.VMEM((cut, edges), BF)],
        )(other_low, q, weight, ids, qg)
        tall = nrel // LANES * width
        size = -(-tall // (n_right * 16)) * 16
        piece = shape(size, LANES, dtype=BF)
        all_pieces = pltpu.VMEM((size * n_right, LANES), F32)
        m, g, mine, theirs = call(
            functools.partial(far_body, half + cut, n_right),
            (shape(cut, edges, dtype=BF), shape(width, edges), shape(far_right * size, LANES),
             shape(far_right * size, LANES, dtype=BF)),
            [pltpu.VMEM((width, nrel), F32), all_pieces],
            me,
            after=(moved,),
        )(other_high, q, weight, ids, qg, s)
        left_rows = n_right * rows
        left_half = left_rows // 2
        right_high, right_low, left_near, left_far = call(
            rest_body,
            (chunk, chunk, shape(width, left_half), shape(width, left_half, dtype=BF)),
            [pltpu.VMEM((width, left_rows), F32)],
        )(q, m, g, o, ids, right_low)

        mine, *rest = call(
            piece_body, (shape(size, LANES),) + (piece,) * (far_right - 1), flops=COST_SUM
        )(mine, swap_right(theirs, 1))
        got = [swap_right(p, 2 * (k + 1)) for k, p in enumerate(rest)]
        mine = call(sum_body, piece, flops=COST_SUM)(mine, *got)
        bit = 2
        while bit < n_left:
            mine = call(sum_body, piece, flops=COST_SUM)(mine, swap_left(mine, bit))
            bit *= 2
        mine = call(sum_body, piece, flops=COST_SUM)(mine, swap_left(mine, 1))
        pieces = [mine] + [swap_right(mine, 2 * k) for k in range(1, far_right)]
        sibling = swap_right(call(stack_body, shape(far_right * size, LANES, dtype=BF))(*pieces), 1)

        left_own, *blocks = call(left_body, (shape(width, rows),) + (one_block,) * (far_right - 1))(
            left_near, swap_right(left_far, 1)
        )
        left_got = [swap_right(block, 2 * (k + 1)) for k, block in enumerate(blocks)]

        got_low = swap_left(right_low, 1)
        got_high = swap_left(right_high, 1)
        outs = (one_block,) * some
        high = call(functools.partial(chunk_body, cut), outs, flops=COST_HIGH)(right_near, got_high)
        low = call(functools.partial(chunk_body, 0), outs, flops=COST_LOW, after=left_got)(right_near, got_low)
        right_got = [next_column(block, 2 * (some + k)) for k, block in enumerate(high)]
        right_got += [next_column(block, 2 * k) for k, block in enumerate(low)]

        def update(got, table, state, flops=0):
            outs = (shape(width, rows), shape(1, rows))
            return call(functools.partial(update_body, len(got)), outs, flops=flops)(*got, table, state)

        left_new, left_state_new = update([left_own, *left_got], left_t, left_state[None, :])
        right_new, right_state_new = update(right_got, moved, moved, COST_UPDATE)
        relation_new, relation_state_new = call(
            functools.partial(relation_body, n_right), (shape(width, nrel), shape(1, nrel)), [all_pieces], me
        )(*pieces, sibling, relation_t, relation_state[None, :])
        return (
            left_new.T, left_state_new.reshape(-1), right_new.T, right_state_new.reshape(-1),
            relation_new.T, relation_state_new.reshape(-1),
        )

    return per_device


def solution(mesh):
    rows = P(("left", "right"), None)
    vector = P(("left", "right"))
    ids = P("left", "right", None)
    return jax.shard_map(
        build(mesh),
        mesh=mesh,
        in_specs=(rows, vector, rows, vector, P(), P(), ids, ids, ids, P("left", "right", None, None)),
        out_specs=(rows, vector, rows, vector, P(), P()),
        check_vma=False,
    )
```

```python
import functools

import jax
import jax.numpy as jnp
from jax import lax
from jax.experimental import pallas as pl
from jax.experimental.pallas import tpu as pltpu
from jax.sharding import PartitionSpec as P

LEARN_RATE = 0.1
NEG_WEIGHT = 0.03125
BF = jnp.bfloat16
F32 = jnp.float32
VMEM_LIMIT = 32 * 1024 * 1024
LANES = 128
COST_JOIN_LOW = 6e9
COST_JOIN_HIGH = 6e9
COST_UPDATE = 6e9
COST_CHUNK = 12e9
COST_SUM = 1e9
COST_MIDDLE = 6e9
COST_QUERY = 6e9


def dot(a, b, a_dim, b_dim):
    return lax.dot_general(a, b, (((a_dim,), (b_dim,)), ((), ())), preferred_element_type=F32)


def hot(ids, count):
    spot = lax.broadcasted_iota(jnp.int32, (count, ids.shape[1]), 0)
    return jnp.where(spot == ids, 1.0, 0.0).astype(BF)


def step_of(size, most=256):
    return most if size % most == 0 else size


def call(body, out_shape, scratch=(), here=None, after=(), flops=0, place=pltpu.VMEM):
    def run(*args):
        specs = [pl.BlockSpec(memory_space=place)] * len(args)
        if here is not None:
            specs.append(pl.BlockSpec(memory_space=pltpu.SMEM))
            args = (*args, here)
        inner = body
        if after:
            used = len(args)

            def inner(*refs):
                body(*refs[:used], *refs[used + len(after):])

            specs += [pl.BlockSpec(memory_space=pl.ANY)] * len(after)
            args = (*args, *after)
        return pl.pallas_call(
            inner,
            out_shape=out_shape,
            in_specs=specs,
            scratch_shapes=list(scratch),
            compiler_params=pltpu.CompilerParams(vmem_limit_bytes=VMEM_LIMIT),
            cost_estimate=pl.CostEstimate(flops=int(flops), bytes_accessed=0, transcendentals=0),
        )(*args)

    return run


def shape(*dims, dtype=F32):
    return jax.ShapeDtypeStruct(dims, dtype)


def cast_body(in_ref, out_ref, held_ref, sems):
    rows = held_ref.shape[0] // sems.shape[0]
    copies = []
    for k in range(sems.shape[0]):
        at = slice(k * rows, (k + 1) * rows)
        copies.append(pltpu.make_async_copy(in_ref.at[at], held_ref.at[at], sems.at[k]))
        copies[-1].start()
    for k, copy in enumerate(copies):
        at = slice(k * rows, (k + 1) * rows)
        copy.wait()
        out_ref[at, :] = held_ref[at, :].astype(BF)


def count_body(far_right, outer, rows, slots, ids_ref, relation_ref, place_ref, out_ref, relation_bf_ref, local_ref):
    def local(ids, here, half):
        block = (ids // rows) ^ here
        return (block % 2 * half + block // 2) * rows + ids % rows

    ids = ids_ref[...]
    local_ref[...] = ids
    local_ref[0:1, :] = local(ids[0:1], place_ref[0], far_right)
    local_ref[1:2, :] = local(ids[1:2], place_ref[1], outer)
    for g in range(out_ref.shape[0]):
        negative = local(ids[3 + g:4 + g, :slots], place_ref[1], outer)
        for at in range(0, out_ref.shape[1], LANES):
            spot = lax.broadcasted_iota(jnp.int32, (LANES, slots), 0) + at
            total = jnp.sum(jnp.where(spot == negative, NEG_WEIGHT, 0.0), axis=1, keepdims=True)
            out_ref[g, at:at + LANES, :] = jnp.broadcast_to(total, (LANES, LANES))
    relation_bf_ref[...] = relation_ref[...].astype(BF)


def pack_body(table_ref, state_ref, pack_ref):
    width = table_ref.shape[0]
    pack_ref[:width, :] = table_ref[...]
    pack_ref[width:, :] = jnp.broadcast_to(state_ref[...], (pack_ref.shape[0] - width, LANES))


def join_body(*refs):
    out_ref = refs[-1]
    at = 0
    for ref in refs[:-1]:
        out_ref[:, at:at + ref.shape[1]] = ref[...]
        at += ref.shape[1]


def query_body(blocks, *refs):
    near_refs, refs = refs[:blocks], refs[blocks:]
    sibling_ref, relation_ref, ids_ref, s_ref, o_ref, q_ref = refs
    relation = relation_ref[...]
    half = s_ref.shape[0] // 2
    edges = s_ref.shape[1]
    step = step_of(edges)
    near = jnp.concatenate([ref[...] for ref in near_refs], axis=1)
    half_rows = near.shape[1]
    for at in range(0, edges, step):
        cols = slice(at, at + step)
        pick = hot(ids_ref[0:1, cols], 2 * half_rows)
        s = dot(near, pick[:half_rows], 1, 0) + dot(sibling_ref[...], pick[half_rows:], 1, 0)
        o = dot(relation, hot(ids_ref[2:3, cols], relation.shape[1]), 1, 0)
        s_ref[:, cols] = s.astype(BF)
        o_ref[:, cols] = o.astype(BF)
        s_re, s_im, o_re, o_im = s[:half], s[half:], o[:half], o[half:]
        q = jnp.concatenate([s_re * o_re - s_im * o_im, s_re * o_im + s_im * o_re], axis=0)
        q_ref[:, cols] = q.astype(BF)


def grad_chunk(rows_t, q_ref, weight_ref, ids_ref, base, at, step):
    count = rows_t.shape[0]
    edges = q_ref.shape[1]
    cols = slice(at, at + step)
    scores = dot(rows_t, q_ref[:, cols], 1, 0)
    spot = lax.broadcasted_iota(jnp.int32, (count, step), 0) + base
    h = jnp.where(spot == ids_ref[1:2, cols], 1.0, 0.0)
    w = weight_ref[at // (edges // weight_ref.shape[0]), base:base + count, :]
    w = jnp.concatenate([w] * (step // LANES), axis=1)
    return ((w + h) * (0.5 * jnp.tanh(0.5 * scores) + 0.5) - h).astype(BF)


def complex_back(g, other):
    half = g.shape[0] // 2
    g_re, g_im, o_re, o_im = g[:half], g[half:], other[:half], other[half:]
    return jnp.concatenate([g_re * o_re + g_im * o_im, g_im * o_re - g_re * o_im], axis=0).astype(BF)


def products(rows_ref, q_ref, weight_ref, ids_ref, m_ref, base):
    rows_t = rows_ref[...].T
    step = step_of(q_ref.shape[1] // weight_ref.shape[0])
    for at in range(0, q_ref.shape[1], step):
        m_ref[:, at:at + step] = grad_chunk(rows_t, q_ref, weight_ref, ids_ref, base, at, step)


def near_body(blocks, *refs):
    block_refs, refs = refs[:blocks], refs[blocks:]
    q_ref, weight_ref, ids_ref, right_ref, qg_ref, rows_ref, m_ref = refs
    join_body(*block_refs, rows_ref)
    products(rows_ref, q_ref, weight_ref, ids_ref, m_ref, 0)
    right_ref[...] = dot(q_ref[...], m_ref[...], 1, 1)
    qg_ref[...] = dot(rows_ref[...], m_ref[...], 1, 0)


def middle_body(base, rows_ref, q_ref, weight_ref, ids_ref, qg_ref, right_ref, qg_out_ref, m_ref):
    products(rows_ref, q_ref, weight_ref, ids_ref, m_ref, base)
    right_ref[...] = dot(q_ref[...], m_ref[...], 1, 1).astype(BF)
    qg_out_ref[...] = qg_ref[...] + dot(rows_ref[...], m_ref[...], 1, 0)


def far_body(
    base, pieces, rows_ref, q_ref, weight_ref, ids_ref, qg_ref, s_ref, here_ref,
    m_ref, g_ref, mine_ref, theirs_ref, kinds_ref, tall_ref,
):
    rows_t = rows_ref[...].T
    width, edges = qg_ref.shape
    step = step_of(edges // weight_ref.shape[0])
    for at in range(0, edges, step):
        cols = slice(at, at + step)
        m = grad_chunk(rows_t, q_ref, weight_ref, ids_ref, base, at, step)
        m_ref[:, cols] = m
        g = qg_ref[:, cols] + dot(rows_ref[...], m, 1, 0)
        g_ref[:, cols] = g
        by_kind = complex_back(g, s_ref[:, cols].astype(F32))
        kinds = dot(by_kind, hot(ids_ref[2:3, cols], kinds_ref.shape[1]), 1, 1)
        if at == 0:
            kinds_ref[...] = kinds
        else:
            kinds_ref[...] += kinds
    parts = kinds_ref.shape[1] // LANES
    for j in range(parts):
        tall_ref[j * width:(j + 1) * width, :] = kinds_ref[:, j * LANES:(j + 1) * LANES]
    rest = tall_ref.shape[0] - parts * width
    if rest:
        tall_ref[parts * width:, :] = jnp.zeros((rest, LANES), F32)
    here = here_ref[0]
    size = tall_ref.shape[0] // pieces
    for k in range(pieces):
        start = pl.multiple_of((here ^ k) * size, 16)
        piece = tall_ref[pl.ds(start, size), :]
        at = slice(k // 2 * size, (k // 2 + 1) * size)
        if k % 2:
            theirs_ref[at, :] = piece.astype(BF)
        else:
            mine_ref[at, :] = piece


def rest_body(q_ref, m_ref, g_ref, o_ref, ids_ref, low_ref, right_ref, near_ref, far_ref, left_ref):
    cut = low_ref.shape[1]
    right_ref[:, :cut] = low_ref[...]
    right_ref[:, cut:] = dot(q_ref[...], m_ref[...], 1, 1).astype(BF)
    edges = q_ref.shape[1]
    step = step_of(edges)
    for at in range(0, edges, step):
        cols = slice(at, at + step)
        by_source = complex_back(g_ref[:, cols], o_ref[:, cols].astype(F32))
        left = dot(by_source, hot(ids_ref[0:1, cols], left_ref.shape[1]), 1, 1)
        if at == 0:
            left_ref[...] = left
        else:
            left_ref[...] += left
    cut = left_ref.shape[1] // 2
    near_ref[...] = left_ref[:, :cut]
    far_ref[...] = left_ref[:, cut:].astype(BF)


def relation_body(pieces, *refs):
    piece_refs, refs = refs[:pieces // 2], refs[pieces // 2:]
    sibling_ref, table_ref, state_ref, here_ref, new_ref, state_new_ref, tall_ref = refs
    here = here_ref[0]
    size = tall_ref.shape[0] // pieces
    for k in range(pieces):
        start = pl.multiple_of((here ^ k) * size, 16)
        piece = sibling_ref[k // 2 * size:(k // 2 + 1) * size, :] if k % 2 else piece_refs[k // 2][...]
        tall_ref[pl.ds(start, size), :] = piece.astype(F32)
    width, count = table_ref.shape
    for j in range(count // LANES):
        cols = slice(j * LANES, (j + 1) * LANES)
        g = tall_ref[j * width:(j + 1) * width, :]
        state = state_ref[:, cols] + jnp.sum(g * g, axis=0, keepdims=True) * (1.0 / width)
        state_new_ref[:, cols] = state
        new_ref[:, cols] = table_ref[:, cols] - g * (LEARN_RATE * lax.rsqrt(state))


def piece_body(mine_ref, got_ref, own_ref, *other_refs):
    size = own_ref.shape[0]
    for k, ref in enumerate((own_ref, *other_refs)):
        at = slice(k * size, (k + 1) * size)
        ref[...] = (mine_ref[at, :] + got_ref[at, :].astype(F32)).astype(ref.dtype)


def left_body(near_ref, got_ref, own_ref, *other_refs):
    for k, ref in enumerate((own_ref, *other_refs)):
        at = slice(k * LANES, (k + 1) * LANES)
        ref[...] = (near_ref[:, at] + got_ref[:, at].astype(F32)).astype(ref.dtype)


def stack_body(*refs):
    size = refs[0].shape[0]
    for k, ref in enumerate(refs[:-1]):
        refs[-1][k * size:(k + 1) * size, :] = ref[...]


def chunk_body(near_ref, got_ref, *block_refs):
    for k, ref in enumerate(block_refs):
        cols = slice(k * LANES, (k + 1) * LANES)
        ref[...] = (near_ref[:, cols] + got_ref[:, cols].astype(F32)).astype(BF)


def sum_body(*refs):
    total = refs[0][...].astype(F32)
    for ref in refs[1:-1]:
        total = total + ref[...].astype(F32)
    refs[-1][...] = total.astype(BF)


def update_body(parts, *refs):
    part_refs, (table_ref, state_ref, new_ref, state_new_ref) = refs[:parts], refs[parts:]
    g = part_refs[0][...].astype(F32)
    for ref in part_refs[1:]:
        g = g + ref[...].astype(F32)
    width = g.shape[0]
    state = state_ref[state_ref.shape[0] - 1:, :] + jnp.sum(g * g, axis=0, keepdims=True) * (1.0 / width)
    state_new_ref[...] = state
    new_ref[...] = table_ref[:width, :] - g * (LEARN_RATE * lax.rsqrt(state))


def build(mesh):
    n_left, n_right = mesh.shape["left"], mesh.shape["right"]
    for count in (n_left, n_right):
        assert count & (count - 1) == 0 and count > 3
    outer = n_left // 2
    far_right = n_right // 2

    def swap_left(value, by):
        return lax.ppermute(value, "left", [(i, i ^ by) for i in range(n_left)])

    def swap_right(value, by):
        return lax.ppermute(value, "right", [(i, i ^ by) for i in range(n_right)])

    def next_column(value, by):
        perm = []
        for i in range(n_left):
            for r in range(n_right):
                perm.append((i * n_right + r, (i ^ by) * n_right + (r + 1) % n_right))
        return lax.ppermute(value, ("left", "right"), perm)

    def per_device(
        left_table, left_state, right_table, right_state, relation_table, relation_state,
        source_ids, target_ids, relation_ids, negative_ids,
    ):
        rows = left_table.shape[0]
        width = left_table.shape[1]
        left_t, right_t, relation_t = left_table.T, right_table.T, relation_table.T
        nrel = relation_t.shape[1]
        here_l, here_r = lax.axis_index("left"), lax.axis_index("right")
        me = here_r.astype(jnp.int32).reshape(1)
        edges = source_ids.shape[-1]
        groups = negative_ids.shape[2]
        n_rows = n_left * rows
        half = outer * rows
        one_block = shape(width, rows, dtype=BF)
        table_bf = shape(width, edges, dtype=BF)

        def cast(value, after=()):
            parts = 5 if width % 80 == 0 else 1
            scratch = [pltpu.VMEM(value.shape, F32), pltpu.SemaphoreType.DMA((parts,))]
            return call(cast_body, one_block, scratch, after=after, place=pl.ANY)(value)

        right_bf = right_t.astype(BF)
        near = [right_bf] + [swap_left(right_bf, 2 * k) for k in range(1, outer)]
        some = outer // 2
        cut = some * rows
        chunk = shape(width, cut, dtype=BF)
        joined_low = call(join_body, chunk, flops=COST_JOIN_LOW)(*near[:some])
        other_low = call(join_body, chunk, flops=COST_MIDDLE)(swap_left(joined_low, 1))

        ids = [source_ids, target_ids, relation_ids, negative_ids]
        longest = max(i.shape[-1] for i in ids)
        ids = [i.reshape(-1, i.shape[-1]) for i in ids]
        ids = jnp.concatenate([jnp.pad(i, ((0, 0), (0, longest - i.shape[-1]))) for i in ids], axis=0)
        ids = lax.ppermute(ids, "right", [(i, (i - 1) % n_right) for i in range(n_right)])
        left_bf = cast(left_t)
        half_left = [left_bf] + [swap_right(left_bf, 2 * k) for k in range(1, far_right)]
        place = jnp.stack([here_r, here_l]).astype(jnp.int32)
        weight, relation_bf, ids = call(
            functools.partial(count_body, far_right, outer, rows, negative_ids.shape[-1]),
            (shape(groups, n_rows, LANES), shape(width, nrel, dtype=BF), shape(*ids.shape, dtype=jnp.int32)),
            here=place,
            after=(joined_low,),
        )(ids, relation_t)
        half_joined = call(join_body, shape(width, far_right * rows, dtype=BF), after=(weight,))(*half_left)
        joined = call(join_body, chunk, flops=COST_JOIN_HIGH, after=(half_joined,))(*near[some:])
        other_high = swap_left(joined, 1)
        sibling_left = swap_right(half_joined, 1)
        moved = next_column(call(pack_body, shape(width + 8, rows), after=(joined,))(right_t, right_state[None, :]), 0)

        s, o, q = call(functools.partial(query_body, far_right), (table_bf, table_bf, table_bf), flops=COST_QUERY)(
            *half_left, sibling_left, relation_bf, ids
        )
        right_near, qg = call(
            functools.partial(near_body, outer),
            (shape(width, half), shape(width, edges)),
            [pltpu.VMEM((width, half), BF), pltpu.VMEM((half, edges), BF)],
        )(*near, q, weight, ids)
        right_low, qg = call(
            functools.partial(middle_body, half), (chunk, shape(width, edges)), [pltpu.VMEM((cut, edges), BF)],
        )(other_low, q, weight, ids, qg)
        tall = nrel // LANES * width
        size = -(-tall // (n_right * 16)) * 16
        piece = shape(size, LANES, dtype=BF)
        all_pieces = pltpu.VMEM((size * n_right, LANES), F32)
        m, g, mine, theirs = call(
            functools.partial(far_body, half + cut, n_right),
            (shape(cut, edges, dtype=BF), shape(width, edges), shape(far_right * size, LANES),
             shape(far_right * size, LANES, dtype=BF)),
            [pltpu.VMEM((width, nrel), F32), all_pieces],
            me,
            after=(moved,),
        )(other_high, q, weight, ids, qg, s)
        left_rows = n_right * rows
        left_half = left_rows // 2
        right_far, left_near, left_far = call(
            rest_body,
            (shape(width, half, dtype=BF), shape(width, left_half), shape(width, left_half, dtype=BF)),
            [pltpu.VMEM((width, left_rows), F32)],
        )(q, m, g, o, ids, right_low)

        right_got = swap_left(right_far, 1)

        mine, *rest = call(
            piece_body, (shape(size, LANES),) + (piece,) * (far_right - 1), flops=COST_SUM, after=(right_far,)
        )(mine, swap_right(theirs, 1))
        got = [swap_right(p, 2 * (k + 1)) for k, p in enumerate(rest)]
        mine = call(sum_body, piece, flops=COST_SUM)(mine, *got)
        bit = 2
        while bit < n_left:
            after = (right_got,) if 2 * bit == n_left else ()
            mine = call(sum_body, piece, flops=COST_SUM, after=after)(mine, swap_left(mine, bit))
            bit *= 2
        over_z = mine
        mine = call(sum_body, piece, flops=COST_SUM)(mine, swap_left(mine, 1))
        pieces = [mine] + [swap_right(mine, 2 * k) for k in range(1, far_right)]
        sibling = swap_right(call(stack_body, shape(far_right * size, LANES, dtype=BF))(*pieces), 1)

        left_own, *blocks = call(left_body, (shape(width, rows),) + (one_block,) * (far_right - 1))(
            left_near, swap_right(left_far, 1)
        )
        left_got = [swap_right(block, 2 * (k + 1)) for k, block in enumerate(blocks)]

        blocks = call(chunk_body, (one_block,) * outer, flops=COST_CHUNK, after=(over_z, *left_got))(
            right_near, right_got
        )
        right_got = [next_column(blocks[k], 2 * k) for k in range(outer - 1, -1, -1)]

        def update(got, table, state, flops=0):
            outs = (shape(width, rows), shape(1, rows))
            return call(functools.partial(update_body, len(got)), outs, flops=flops)(*got, table, state)

        left_new, left_state_new = update([left_own, *left_got], left_t, left_state[None, :])
        right_new, right_state_new = update(right_got, moved, moved, COST_UPDATE)
        relation_new, relation_state_new = call(
            functools.partial(relation_body, n_right), (shape(width, nrel), shape(1, nrel)), [all_pieces], me
        )(*pieces, sibling, relation_t, relation_state[None, :])
        return (
            left_new.T, left_state_new.reshape(-1), right_new.T, right_state_new.reshape(-1),
            relation_new.T, relation_state_new.reshape(-1),
        )

    return per_device


def solution(mesh):
    rows = P(("left", "right"), None)
    vector = P(("left", "right"))
    ids = P("left", "right", None)
    return jax.shard_map(
        build(mesh),
        mesh=mesh,
        in_specs=(rows, vector, rows, vector, P(), P(), ids, ids, ids, P("left", "right", None, None)),
        out_specs=(rows, vector, rows, vector, P(), P()),
        check_vma=False,
    )
```

```python
import functools

import jax
import jax.numpy as jnp
from jax import lax
from jax.experimental import pallas as pl
from jax.experimental.pallas import tpu as pltpu
from jax.sharding import PartitionSpec as P

LEARN_RATE = 0.1
NEG_WEIGHT = 0.03125
BF = jnp.bfloat16
F32 = jnp.float32
VMEM_LIMIT = 32 * 1024 * 1024
LANES = 128
COST_JOIN_LOW = 6e9
COST_JOIN_HIGH = 6e9
COST_UPDATE = 12e9
COST_HIGH = 12e9
COST_LOW = 12e9
COST_SUM = 1e9
COST_MIDDLE = 6e9
COST_QUERY = 6e9


def dot(a, b, a_dim, b_dim):
    return lax.dot_general(a, b, (((a_dim,), (b_dim,)), ((), ())), preferred_element_type=F32)


def hot(ids, count):
    spot = lax.broadcasted_iota(jnp.int32, (count, ids.shape[1]), 0)
    return jnp.where(spot == ids, 1.0, 0.0).astype(BF)


def step_of(size, most=256):
    return most if size % most == 0 else size


def call(body, out_shape, scratch=(), here=None, after=(), flops=0, place=pltpu.VMEM):
    def run(*args):
        specs = [pl.BlockSpec(memory_space=place)] * len(args)
        if here is not None:
            specs.append(pl.BlockSpec(memory_space=pltpu.SMEM))
            args = (*args, here)
        inner = body
        if after:
            used = len(args)

            def inner(*refs):
                body(*refs[:used], *refs[used + len(after):])

            specs += [pl.BlockSpec(memory_space=pl.ANY)] * len(after)
            args = (*args, *after)
        return pl.pallas_call(
            inner,
            out_shape=out_shape,
            in_specs=specs,
            scratch_shapes=list(scratch),
            compiler_params=pltpu.CompilerParams(vmem_limit_bytes=VMEM_LIMIT),
            cost_estimate=pl.CostEstimate(flops=int(flops), bytes_accessed=0, transcendentals=0),
        )(*args)

    return run


def shape(*dims, dtype=F32):
    return jax.ShapeDtypeStruct(dims, dtype)


def cast_body(in_ref, out_ref, held_ref, sems):
    rows = held_ref.shape[0] // sems.shape[0]
    copies = []
    for k in range(sems.shape[0]):
        at = slice(k * rows, (k + 1) * rows)
        copies.append(pltpu.make_async_copy(in_ref.at[at], held_ref.at[at], sems.at[k]))
        copies[-1].start()
    for k, copy in enumerate(copies):
        at = slice(k * rows, (k + 1) * rows)
        copy.wait()
        out_ref[at, :] = held_ref[at, :].astype(BF)


def count_body(far_right, outer, rows, slots, ids_ref, relation_ref, place_ref, out_ref, relation_bf_ref, local_ref):
    def local(ids, here, half):
        block = (ids // rows) ^ here
        return (block % 2 * half + block // 2) * rows + ids % rows

    ids = ids_ref[...]
    local_ref[...] = ids
    local_ref[0:1, :] = local(ids[0:1], place_ref[0], far_right)
    local_ref[1:2, :] = local(ids[1:2], place_ref[1], outer)
    for g in range(out_ref.shape[0]):
        negative = local(ids[3 + g:4 + g, :slots], place_ref[1], outer)
        for at in range(0, out_ref.shape[1], LANES):
            spot = lax.broadcasted_iota(jnp.int32, (LANES, slots), 0) + at
            total = jnp.sum(jnp.where(spot == negative, NEG_WEIGHT, 0.0), axis=1, keepdims=True)
            out_ref[g, at:at + LANES, :] = jnp.broadcast_to(total, (LANES, LANES))
    relation_bf_ref[...] = relation_ref[...].astype(BF)


def pack_body(table_ref, state_ref, pack_ref):
    width = table_ref.shape[0]
    pack_ref[:width, :] = table_ref[...]
    pack_ref[width:, :] = jnp.broadcast_to(state_ref[...], (pack_ref.shape[0] - width, LANES))


def join_body(*refs):
    out_ref = refs[-1]
    at = 0
    for ref in refs[:-1]:
        out_ref[:, at:at + ref.shape[1]] = ref[...]
        at += ref.shape[1]


def query_body(blocks, *refs):
    near_refs, refs = refs[:blocks], refs[blocks:]
    sibling_ref, relation_ref, ids_ref, s_ref, o_ref, q_ref = refs
    relation = relation_ref[...]
    half = s_ref.shape[0] // 2
    edges = s_ref.shape[1]
    step = step_of(edges)
    near = jnp.concatenate([ref[...] for ref in near_refs], axis=1)
    half_rows = near.shape[1]
    for at in range(0, edges, step):
        cols = slice(at, at + step)
        pick = hot(ids_ref[0:1, cols], 2 * half_rows)
        s = dot(near, pick[:half_rows], 1, 0) + dot(sibling_ref[...], pick[half_rows:], 1, 0)
        o = dot(relation, hot(ids_ref[2:3, cols], relation.shape[1]), 1, 0)
        s_ref[:, cols] = s.astype(BF)
        o_ref[:, cols] = o.astype(BF)
        s_re, s_im, o_re, o_im = s[:half], s[half:], o[:half], o[half:]
        q = jnp.concatenate([s_re * o_re - s_im * o_im, s_re * o_im + s_im * o_re], axis=0)
        q_ref[:, cols] = q.astype(BF)


def grad_chunk(rows_t, q_ref, weight_ref, ids_ref, base, at, step):
    count = rows_t.shape[0]
    edges = q_ref.shape[1]
    cols = slice(at, at + step)
    scores = dot(rows_t, q_ref[:, cols], 1, 0)
    spot = lax.broadcasted_iota(jnp.int32, (count, step), 0) + base
    h = jnp.where(spot == ids_ref[1:2, cols], 1.0, 0.0)
    w = weight_ref[at // (edges // weight_ref.shape[0]), base:base + count, :]
    w = jnp.concatenate([w] * (step // LANES), axis=1)
    return ((w + h) * (0.5 * jnp.tanh(0.5 * scores) + 0.5) - h).astype(BF)


def complex_back(g, other):
    half = g.shape[0] // 2
    g_re, g_im, o_re, o_im = g[:half], g[half:], other[:half], other[half:]
    return jnp.concatenate([g_re * o_re + g_im * o_im, g_im * o_re - g_re * o_im], axis=0).astype(BF)


def products(rows_ref, q_ref, weight_ref, ids_ref, m_ref, base):
    rows_t = rows_ref[...].T
    step = step_of(q_ref.shape[1] // weight_ref.shape[0])
    for at in range(0, q_ref.shape[1], step):
        m_ref[:, at:at + step] = grad_chunk(rows_t, q_ref, weight_ref, ids_ref, base, at, step)


def near_body(blocks, *refs):
    block_refs, refs = refs[:blocks], refs[blocks:]
    q_ref, weight_ref, ids_ref, right_ref, qg_ref, rows_ref, m_ref = refs
    join_body(*block_refs, rows_ref)
    products(rows_ref, q_ref, weight_ref, ids_ref, m_ref, 0)
    right_ref[...] = dot(q_ref[...], m_ref[...], 1, 1)
    qg_ref[...] = dot(rows_ref[...], m_ref[...], 1, 0)


def middle_body(base, rows_ref, q_ref, weight_ref, ids_ref, qg_ref, right_ref, qg_out_ref, m_ref):
    products(rows_ref, q_ref, weight_ref, ids_ref, m_ref, base)
    right_ref[...] = dot(q_ref[...], m_ref[...], 1, 1).astype(BF)
    qg_out_ref[...] = qg_ref[...] + dot(rows_ref[...], m_ref[...], 1, 0)


def far_body(
    base, pieces, rows_ref, q_ref, weight_ref, ids_ref, qg_ref, s_ref, here_ref,
    m_ref, g_ref, mine_ref, theirs_ref, kinds_ref, tall_ref,
):
    rows_t = rows_ref[...].T
    width, edges = qg_ref.shape
    step = step_of(edges // weight_ref.shape[0])
    for at in range(0, edges, step):
        cols = slice(at, at + step)
        m = grad_chunk(rows_t, q_ref, weight_ref, ids_ref, base, at, step)
        m_ref[:, cols] = m
        g = qg_ref[:, cols] + dot(rows_ref[...], m, 1, 0)
        g_ref[:, cols] = g
        by_kind = complex_back(g, s_ref[:, cols].astype(F32))
        kinds = dot(by_kind, hot(ids_ref[2:3, cols], kinds_ref.shape[1]), 1, 1)
        if at == 0:
            kinds_ref[...] = kinds
        else:
            kinds_ref[...] += kinds
    parts = kinds_ref.shape[1] // LANES
    for j in range(parts):
        tall_ref[j * width:(j + 1) * width, :] = kinds_ref[:, j * LANES:(j + 1) * LANES]
    rest = tall_ref.shape[0] - parts * width
    if rest:
        tall_ref[parts * width:, :] = jnp.zeros((rest, LANES), F32)
    here = here_ref[0]
    size = tall_ref.shape[0] // pieces
    for k in range(pieces):
        start = pl.multiple_of((here ^ k) * size, 16)
        piece = tall_ref[pl.ds(start, size), :]
        at = slice(k // 2 * size, (k // 2 + 1) * size)
        if k % 2:
            theirs_ref[at, :] = piece.astype(BF)
        else:
            mine_ref[at, :] = piece


def rest_body(m_ref, q_ref, g_ref, o_ref, ids_ref, low_ref, right_ref, low_out_ref, near_ref, far_ref, left_ref):
    low_out_ref[...] = low_ref[...]
    right_ref[...] = dot(q_ref[...], m_ref[...], 1, 1).astype(BF)
    edges = q_ref.shape[1]
    step = step_of(edges)
    for at in range(0, edges, step):
        cols = slice(at, at + step)
        by_source = complex_back(g_ref[:, cols], o_ref[:, cols].astype(F32))
        left = dot(by_source, hot(ids_ref[0:1, cols], left_ref.shape[1]), 1, 1)
        if at == 0:
            left_ref[...] = left
        else:
            left_ref[...] += left
    cut = left_ref.shape[1] // 2
    near_ref[...] = left_ref[:, :cut]
    far_ref[...] = left_ref[:, cut:].astype(BF)


def relation_body(pieces, *refs):
    piece_refs, refs = refs[:pieces // 2], refs[pieces // 2:]
    sibling_ref, table_ref, state_ref, here_ref, new_ref, state_new_ref, tall_ref = refs
    here = here_ref[0]
    size = tall_ref.shape[0] // pieces
    for k in range(pieces):
        start = pl.multiple_of((here ^ k) * size, 16)
        piece = sibling_ref[k // 2 * size:(k // 2 + 1) * size, :] if k % 2 else piece_refs[k // 2][...]
        tall_ref[pl.ds(start, size), :] = piece.astype(F32)
    width, count = table_ref.shape
    for j in range(count // LANES):
        cols = slice(j * LANES, (j + 1) * LANES)
        g = tall_ref[j * width:(j + 1) * width, :]
        state = state_ref[:, cols] + jnp.sum(g * g, axis=0, keepdims=True) * (1.0 / width)
        state_new_ref[:, cols] = state
        new_ref[:, cols] = table_ref[:, cols] - g * (LEARN_RATE * lax.rsqrt(state))


def piece_body(mine_ref, got_ref, own_ref, *other_refs):
    size = own_ref.shape[0]
    for k, ref in enumerate((own_ref, *other_refs)):
        at = slice(k * size, (k + 1) * size)
        ref[...] = (mine_ref[at, :] + got_ref[at, :].astype(F32)).astype(ref.dtype)


def left_body(near_ref, got_ref, own_ref, *other_refs):
    for k, ref in enumerate((own_ref, *other_refs)):
        at = slice(k * LANES, (k + 1) * LANES)
        ref[...] = (near_ref[:, at] + got_ref[:, at].astype(F32)).astype(ref.dtype)


def stack_body(*refs):
    size = refs[0].shape[0]
    for k, ref in enumerate(refs[:-1]):
        refs[-1][k * size:(k + 1) * size, :] = ref[...]


def chunk_body(base, near_ref, got_ref, *block_refs):
    for k, ref in enumerate(block_refs):
        cols = slice(k * LANES, (k + 1) * LANES)
        total = near_ref[:, base + k * LANES:base + (k + 1) * LANES] + got_ref[:, cols].astype(F32)
        ref[...] = total.astype(BF)


def sum_body(*refs):
    total = refs[0][...].astype(F32)
    for ref in refs[1:-1]:
        total = total + ref[...].astype(F32)
    refs[-1][...] = total.astype(BF)


def update_body(parts, *refs):
    part_refs, (table_ref, state_ref, new_ref, state_new_ref) = refs[:parts], refs[parts:]
    g = part_refs[0][...].astype(F32)
    for ref in part_refs[1:]:
        g = g + ref[...].astype(F32)
    width = g.shape[0]
    state = state_ref[state_ref.shape[0] - 1:, :] + jnp.sum(g * g, axis=0, keepdims=True) * (1.0 / width)
    state_new_ref[...] = state
    new_ref[...] = table_ref[:width, :] - g * (LEARN_RATE * lax.rsqrt(state))


def build(mesh):
    n_left, n_right = mesh.shape["left"], mesh.shape["right"]
    for count in (n_left, n_right):
        assert count & (count - 1) == 0 and count > 3
    outer = n_left // 2
    far_right = n_right // 2

    def swap_left(value, by):
        return lax.ppermute(value, "left", [(i, i ^ by) for i in range(n_left)])

    def swap_right(value, by):
        return lax.ppermute(value, "right", [(i, i ^ by) for i in range(n_right)])

    def next_column(value, by):
        perm = []
        for i in range(n_left):
            for r in range(n_right):
                perm.append((i * n_right + r, (i ^ by) * n_right + (r + 1) % n_right))
        return lax.ppermute(value, ("left", "right"), perm)

    def per_device(
        left_table, left_state, right_table, right_state, relation_table, relation_state,
        source_ids, target_ids, relation_ids, negative_ids,
    ):
        rows = left_table.shape[0]
        width = left_table.shape[1]
        left_t, right_t, relation_t = left_table.T, right_table.T, relation_table.T
        nrel = relation_t.shape[1]
        here_l, here_r = lax.axis_index("left"), lax.axis_index("right")
        me = here_r.astype(jnp.int32).reshape(1)
        edges = source_ids.shape[-1]
        groups = negative_ids.shape[2]
        n_rows = n_left * rows
        half = outer * rows
        one_block = shape(width, rows, dtype=BF)
        table_bf = shape(width, edges, dtype=BF)

        def cast(value, after=()):
            parts = 5 if width % 80 == 0 else 1
            scratch = [pltpu.VMEM(value.shape, F32), pltpu.SemaphoreType.DMA((parts,))]
            return call(cast_body, one_block, scratch, after=after, place=pl.ANY)(value)

        right_bf = right_t.astype(BF)
        near = [right_bf] + [swap_left(right_bf, 2 * k) for k in range(1, outer)]
        some = outer // 2
        cut = some * rows
        chunk = shape(width, cut, dtype=BF)
        joined_low = call(join_body, chunk, flops=COST_JOIN_LOW)(*near[:some])
        other_low = call(join_body, chunk, flops=COST_MIDDLE)(swap_left(joined_low, 1))

        ids = [source_ids, target_ids, relation_ids, negative_ids]
        longest = max(i.shape[-1] for i in ids)
        ids = [i.reshape(-1, i.shape[-1]) for i in ids]
        ids = jnp.concatenate([jnp.pad(i, ((0, 0), (0, longest - i.shape[-1]))) for i in ids], axis=0)
        ids = lax.ppermute(ids, "right", [(i, (i - 1) % n_right) for i in range(n_right)])
        left_bf = cast(left_t)
        half_left = [left_bf] + [swap_right(left_bf, 2 * k) for k in range(1, far_right)]
        place = jnp.stack([here_r, here_l]).astype(jnp.int32)
        weight, relation_bf, ids = call(
            functools.partial(count_body, far_right, outer, rows, negative_ids.shape[-1]),
            (shape(groups, n_rows, LANES), shape(width, nrel, dtype=BF), shape(*ids.shape, dtype=jnp.int32)),
            here=place,
            after=(joined_low,),
        )(ids, relation_t)
        half_joined = call(join_body, shape(width, far_right * rows, dtype=BF), after=(weight,))(*half_left)
        joined = call(join_body, chunk, flops=COST_JOIN_HIGH, after=(half_joined,))(*near[some:])
        other_high = swap_left(joined, 1)
        sibling_left = swap_right(half_joined, 1)
        moved = next_column(call(pack_body, shape(width + 8, rows), after=(joined,))(right_t, right_state[None, :]), 0)

        s, o, q = call(functools.partial(query_body, far_right), (table_bf, table_bf, table_bf), flops=COST_QUERY)(
            *half_left, sibling_left, relation_bf, ids
        )
        right_near, qg = call(
            functools.partial(near_body, outer),
            (shape(width, half), shape(width, edges)),
            [pltpu.VMEM((width, half), BF), pltpu.VMEM((half, edges), BF)],
        )(*near, q, weight, ids)
        right_low, qg = call(
            functools.partial(middle_body, half), (chunk, shape(width, edges)), [pltpu.VMEM((cut, edges), BF)],
        )(other_low, q, weight, ids, qg)
        tall = nrel // LANES * width
        size = -(-tall // (n_right * 16)) * 16
        piece = shape(size, LANES, dtype=BF)
        all_pieces = pltpu.VMEM((size * n_right, LANES), F32)
        m, g, mine, theirs = call(
            functools.partial(far_body, half + cut, n_right),
            (shape(cut, edges, dtype=BF), shape(width, edges), shape(far_right * size, LANES),
             shape(far_right * size, LANES, dtype=BF)),
            [pltpu.VMEM((width, nrel), F32), all_pieces],
            me,
            after=(moved,),
        )(other_high, q, weight, ids, qg, s)
        left_rows = n_right * rows
        left_half = left_rows // 2
        right_high, right_low, left_near, left_far = call(
            rest_body,
            (chunk, chunk, shape(width, left_half), shape(width, left_half, dtype=BF)),
            [pltpu.VMEM((width, left_rows), F32)],
        )(m, q, g, o, ids, right_low)

        mine, *rest = call(
            piece_body, (shape(size, LANES),) + (piece,) * (far_right - 1), flops=COST_SUM
        )(mine, swap_right(theirs, 1))
        got = [swap_right(p, 2 * (k + 1)) for k, p in enumerate(rest)]
        mine = call(sum_body, piece, flops=COST_SUM)(mine, *got)
        bit = n_left // 2
        while bit > 1:
            mine = call(sum_body, piece, flops=COST_SUM)(mine, swap_left(mine, bit))
            bit //= 2
        mine = call(sum_body, piece, flops=COST_SUM)(mine, swap_left(mine, 1))
        pieces = [mine] + [swap_right(mine, 2 * k) for k in range(1, far_right)]
        sibling = swap_right(call(stack_body, shape(far_right * size, LANES, dtype=BF))(*pieces), 1)

        left_own, *blocks = call(left_body, (shape(width, rows),) + (one_block,) * (far_right - 1))(
            left_near, swap_right(left_far, 1)
        )
        left_got = [swap_right(block, 2 * (k + 1)) for k, block in enumerate(blocks)]

        got_low = swap_left(right_low, 1)
        got_high = swap_left(right_high, 1)
        outs = (one_block,) * some
        high = call(functools.partial(chunk_body, cut), outs, flops=COST_HIGH)(right_near, got_high)
        low = call(functools.partial(chunk_body, 0), outs, flops=COST_LOW, after=left_got)(right_near, got_low)
        right_got = [next_column(block, 2 * (some + k)) for k, block in enumerate(high)]
        right_got += [next_column(block, 2 * k) for k, block in enumerate(low)]

        def update(got, table, state, flops=0):
            outs = (shape(width, rows), shape(1, rows))
            return call(functools.partial(update_body, len(got)), outs, flops=flops)(*got, table, state)

        left_new, left_state_new = update([left_own, *left_got], left_t, left_state[None, :])
        right_new, right_state_new = update(right_got, moved, moved, COST_UPDATE)
        relation_new, relation_state_new = call(
            functools.partial(relation_body, n_right), (shape(width, nrel), shape(1, nrel)), [all_pieces], me
        )(*pieces, sibling, relation_t, relation_state[None, :])
        return (
            left_new.T, left_state_new.reshape(-1), right_new.T, right_state_new.reshape(-1),
            relation_new.T, relation_state_new.reshape(-1),
        )

    return per_device


def solution(mesh):
    rows = P(("left", "right"), None)
    vector = P(("left", "right"))
    ids = P("left", "right", None)
    return jax.shard_map(
        build(mesh),
        mesh=mesh,
        in_specs=(rows, vector, rows, vector, P(), P(), ids, ids, ids, P("left", "right", None, None)),
        out_specs=(rows, vector, rows, vector, P(), P()),
        check_vma=False,
    )
```

```python
import functools

import jax
import jax.numpy as jnp
from jax import lax
from jax.experimental import pallas as pl
from jax.experimental.pallas import tpu as pltpu
from jax.sharding import PartitionSpec as P

LEARN_RATE = 0.1
NEG_WEIGHT = 0.03125
BF = jnp.bfloat16
F32 = jnp.float32
VMEM_LIMIT = 32 * 1024 * 1024
LANES = 128
COST_JOIN_LOW = 6e9
COST_JOIN_HIGH = 6e9
COST_UPDATE = 12e9
COST_HIGH = 12e9
COST_LOW = 12e9
COST_SUM = 1e9
COST_MIDDLE = 6e9
COST_QUERY = 6e9


def dot(a, b, a_dim, b_dim):
    return lax.dot_general(a, b, (((a_dim,), (b_dim,)), ((), ())), preferred_element_type=F32)


def hot(ids, count):
    spot = lax.broadcasted_iota(jnp.int32, (count, ids.shape[1]), 0)
    return jnp.where(spot == ids, 1.0, 0.0).astype(BF)


def step_of(size, most=256):
    return most if size % most == 0 else size


def call(body, out_shape, scratch=(), here=None, after=(), flops=0, place=pltpu.VMEM):
    def run(*args):
        specs = [pl.BlockSpec(memory_space=place)] * len(args)
        if here is not None:
            specs.append(pl.BlockSpec(memory_space=pltpu.SMEM))
            args = (*args, here)
        inner = body
        if after:
            used = len(args)

            def inner(*refs):
                body(*refs[:used], *refs[used + len(after):])

            specs += [pl.BlockSpec(memory_space=pl.ANY)] * len(after)
            args = (*args, *after)
        return pl.pallas_call(
            inner,
            out_shape=out_shape,
            in_specs=specs,
            scratch_shapes=list(scratch),
            compiler_params=pltpu.CompilerParams(vmem_limit_bytes=VMEM_LIMIT),
            cost_estimate=pl.CostEstimate(flops=int(flops), bytes_accessed=0, transcendentals=0),
        )(*args)

    return run


def shape(*dims, dtype=F32):
    return jax.ShapeDtypeStruct(dims, dtype)


def cast_body(in_ref, out_ref, held_ref, sems):
    rows = held_ref.shape[0] // sems.shape[0]
    copies = []
    for k in range(sems.shape[0]):
        at = slice(k * rows, (k + 1) * rows)
        copies.append(pltpu.make_async_copy(in_ref.at[at], held_ref.at[at], sems.at[k]))
        copies[-1].start()
    for k, copy in enumerate(copies):
        at = slice(k * rows, (k + 1) * rows)
        copy.wait()
        out_ref[at, :] = held_ref[at, :].astype(BF)


def count_body(far_right, outer, rows, slots, ids_ref, relation_ref, place_ref, out_ref, relation_bf_ref, local_ref):
    def local(ids, here, half):
        block = (ids // rows) ^ here
        return (block % 2 * half + block // 2) * rows + ids % rows

    ids = ids_ref[...]
    local_ref[...] = ids
    local_ref[0:1, :] = local(ids[0:1], place_ref[0], far_right)
    local_ref[1:2, :] = local(ids[1:2], place_ref[1], outer)
    for g in range(out_ref.shape[0]):
        negative = local(ids[3 + g:4 + g, :slots], place_ref[1], outer)
        for at in range(0, out_ref.shape[1], LANES):
            spot = lax.broadcasted_iota(jnp.int32, (LANES, slots), 0) + at
            total = jnp.sum(jnp.where(spot == negative, NEG_WEIGHT, 0.0), axis=1, keepdims=True)
            out_ref[g, at:at + LANES, :] = jnp.broadcast_to(total, (LANES, LANES))
    relation_bf_ref[...] = relation_ref[...].astype(BF)


def pack_body(table_ref, state_ref, pack_ref):
    width = table_ref.shape[0]
    pack_ref[:width, :] = table_ref[...]
    pack_ref[width:, :] = jnp.broadcast_to(state_ref[...], (pack_ref.shape[0] - width, LANES))


def join_body(*refs):
    out_ref = refs[-1]
    at = 0
    for ref in refs[:-1]:
        out_ref[:, at:at + ref.shape[1]] = ref[...]
        at += ref.shape[1]


def query_body(blocks, *refs):
    near_refs, refs = refs[:blocks], refs[blocks:]
    sibling_ref, relation_ref, ids_ref, s_ref, o_ref, q_ref = refs
    relation = relation_ref[...]
    half = s_ref.shape[0] // 2
    edges = s_ref.shape[1]
    step = step_of(edges)
    near = jnp.concatenate([ref[...] for ref in near_refs], axis=1)
    half_rows = near.shape[1]
    for at in range(0, edges, step):
        cols = slice(at, at + step)
        pick = hot(ids_ref[0:1, cols], 2 * half_rows)
        s = dot(near, pick[:half_rows], 1, 0) + dot(sibling_ref[...], pick[half_rows:], 1, 0)
        o = dot(relation, hot(ids_ref[2:3, cols], relation.shape[1]), 1, 0)
        s_ref[:, cols] = s.astype(BF)
        o_ref[:, cols] = o.astype(BF)
        s_re, s_im, o_re, o_im = s[:half], s[half:], o[:half], o[half:]
        q = jnp.concatenate([s_re * o_re - s_im * o_im, s_re * o_im + s_im * o_re], axis=0)
        q_ref[:, cols] = q.astype(BF)


def grad_chunk(rows_t, q_ref, weight_ref, ids_ref, base, at, step):
    count = rows_t.shape[0]
    edges = q_ref.shape[1]
    cols = slice(at, at + step)
    scores = dot(rows_t, q_ref[:, cols], 1, 0)
    spot = lax.broadcasted_iota(jnp.int32, (count, step), 0) + base
    h = jnp.where(spot == ids_ref[1:2, cols], 1.0, 0.0)
    w = weight_ref[at // (edges // weight_ref.shape[0]), base:base + count, :]
    w = jnp.concatenate([w] * (step // LANES), axis=1)
    return ((w + h) * (0.5 * jnp.tanh(0.5 * scores) + 0.5) - h).astype(BF)


def complex_back(g, other):
    half = g.shape[0] // 2
    g_re, g_im, o_re, o_im = g[:half], g[half:], other[:half], other[half:]
    return jnp.concatenate([g_re * o_re + g_im * o_im, g_im * o_re - g_re * o_im], axis=0).astype(BF)


def products(rows_ref, q_ref, weight_ref, ids_ref, m_ref, base):
    rows_t = rows_ref[...].T
    step = step_of(q_ref.shape[1] // weight_ref.shape[0])
    for at in range(0, q_ref.shape[1], step):
        m_ref[:, at:at + step] = grad_chunk(rows_t, q_ref, weight_ref, ids_ref, base, at, step)


def near_body(blocks, *refs):
    block_refs, refs = refs[:blocks], refs[blocks:]
    q_ref, weight_ref, ids_ref, right_ref, qg_ref, rows_ref, m_ref = refs
    join_body(*block_refs, rows_ref)
    products(rows_ref, q_ref, weight_ref, ids_ref, m_ref, 0)
    right_ref[...] = dot(q_ref[...], m_ref[...], 1, 1)
    qg_ref[...] = dot(rows_ref[...], m_ref[...], 1, 0)


def middle_body(base, rows_ref, q_ref, weight_ref, ids_ref, qg_ref, right_ref, qg_out_ref, m_ref):
    products(rows_ref, q_ref, weight_ref, ids_ref, m_ref, base)
    right_ref[...] = dot(q_ref[...], m_ref[...], 1, 1).astype(BF)
    qg_out_ref[...] = qg_ref[...] + dot(rows_ref[...], m_ref[...], 1, 0)


def far_body(
    base, pieces, rows_ref, q_ref, weight_ref, ids_ref, qg_ref, s_ref, here_ref,
    m_ref, g_ref, mine_ref, theirs_ref, kinds_ref, tall_ref,
):
    rows_t = rows_ref[...].T
    width, edges = qg_ref.shape
    step = step_of(edges // weight_ref.shape[0])
    for at in range(0, edges, step):
        cols = slice(at, at + step)
        m = grad_chunk(rows_t, q_ref, weight_ref, ids_ref, base, at, step)
        m_ref[:, cols] = m
        g = qg_ref[:, cols] + dot(rows_ref[...], m, 1, 0)
        g_ref[:, cols] = g
        by_kind = complex_back(g, s_ref[:, cols].astype(F32))
        kinds = dot(by_kind, hot(ids_ref[2:3, cols], kinds_ref.shape[1]), 1, 1)
        if at == 0:
            kinds_ref[...] = kinds
        else:
            kinds_ref[...] += kinds
    parts = kinds_ref.shape[1] // LANES
    for j in range(parts):
        tall_ref[j * width:(j + 1) * width, :] = kinds_ref[:, j * LANES:(j + 1) * LANES]
    rest = tall_ref.shape[0] - parts * width
    if rest:
        tall_ref[parts * width:, :] = jnp.zeros((rest, LANES), F32)
    here = here_ref[0]
    size = tall_ref.shape[0] // pieces
    for k in range(pieces):
        start = pl.multiple_of((here ^ k) * size, 16)
        piece = tall_ref[pl.ds(start, size), :]
        at = slice(k // 2 * size, (k // 2 + 1) * size)
        if k % 2:
            theirs_ref[at, :] = piece.astype(BF)
        else:
            mine_ref[at, :] = piece


def rest_body(m_ref, q_ref, g_ref, o_ref, ids_ref, low_ref, right_ref, low_out_ref, near_ref, far_ref, left_ref):
    low_out_ref[...] = low_ref[...]
    right_ref[...] = dot(q_ref[...], m_ref[...], 1, 1).astype(BF)
    edges = q_ref.shape[1]
    step = step_of(edges)
    for at in range(0, edges, step):
        cols = slice(at, at + step)
        by_source = complex_back(g_ref[:, cols], o_ref[:, cols].astype(F32))
        left = dot(by_source, hot(ids_ref[0:1, cols], left_ref.shape[1]), 1, 1)
        if at == 0:
            left_ref[...] = left
        else:
            left_ref[...] += left
    cut = left_ref.shape[1] // 2
    near_ref[...] = left_ref[:, :cut]
    far_ref[...] = left_ref[:, cut:].astype(BF)


def relation_body(pieces, *refs):
    piece_refs, refs = refs[:pieces // 2], refs[pieces // 2:]
    sibling_ref, table_ref, state_ref, here_ref, new_ref, state_new_ref, tall_ref = refs
    here = here_ref[0]
    size = tall_ref.shape[0] // pieces
    for k in range(pieces):
        start = pl.multiple_of((here ^ k) * size, 16)
        piece = sibling_ref[k // 2 * size:(k // 2 + 1) * size, :] if k % 2 else piece_refs[k // 2][...]
        tall_ref[pl.ds(start, size), :] = piece.astype(F32)
    width, count = table_ref.shape
    for j in range(count // LANES):
        cols = slice(j * LANES, (j + 1) * LANES)
        g = tall_ref[j * width:(j + 1) * width, :]
        state = state_ref[:, cols] + jnp.sum(g * g, axis=0, keepdims=True) * (1.0 / width)
        state_new_ref[:, cols] = state
        new_ref[:, cols] = table_ref[:, cols] - g * (LEARN_RATE * lax.rsqrt(state))


def piece_body(mine_ref, got_ref, own_ref, *other_refs):
    size = own_ref.shape[0]
    for k, ref in enumerate((own_ref, *other_refs)):
        at = slice(k * size, (k + 1) * size)
        ref[...] = (mine_ref[at, :] + got_ref[at, :].astype(F32)).astype(ref.dtype)


def left_body(near_ref, got_ref, own_ref, *other_refs):
    for k, ref in enumerate((own_ref, *other_refs)):
        at = slice(k * LANES, (k + 1) * LANES)
        ref[...] = (near_ref[:, at] + got_ref[:, at].astype(F32)).astype(ref.dtype)


def stack_body(*refs):
    size = refs[0].shape[0]
    for k, ref in enumerate(refs[:-1]):
        refs[-1][k * size:(k + 1) * size, :] = ref[...]


def chunk_body(base, near_ref, got_ref, *block_refs):
    for k, ref in enumerate(block_refs):
        cols = slice(k * LANES, (k + 1) * LANES)
        total = near_ref[:, base + k * LANES:base + (k + 1) * LANES] + got_ref[:, cols].astype(F32)
        ref[...] = total.astype(ref.dtype)


def sum_body(*refs):
    total = refs[0][...].astype(F32)
    for ref in refs[1:-1]:
        total = total + ref[...].astype(F32)
    refs[-1][...] = total.astype(BF)


def update_body(parts, *refs):
    part_refs, (table_ref, state_ref, new_ref, state_new_ref) = refs[:parts], refs[parts:]
    g = part_refs[0][...].astype(F32)
    for ref in part_refs[1:]:
        g = g + ref[...].astype(F32)
    width = g.shape[0]
    state = state_ref[state_ref.shape[0] - 1:, :] + jnp.sum(g * g, axis=0, keepdims=True) * (1.0 / width)
    state_new_ref[...] = state
    new_ref[...] = table_ref[:width, :] - g * (LEARN_RATE * lax.rsqrt(state))


def build(mesh):
    n_left, n_right = mesh.shape["left"], mesh.shape["right"]
    for count in (n_left, n_right):
        assert count & (count - 1) == 0 and count > 3
    outer = n_left // 2
    far_right = n_right // 2

    def swap_left(value, by):
        return lax.ppermute(value, "left", [(i, i ^ by) for i in range(n_left)])

    def swap_right(value, by):
        return lax.ppermute(value, "right", [(i, i ^ by) for i in range(n_right)])

    def next_column(value, by):
        perm = []
        for i in range(n_left):
            for r in range(n_right):
                perm.append((i * n_right + r, (i ^ by) * n_right + (r + 1) % n_right))
        return lax.ppermute(value, ("left", "right"), perm)

    def per_device(
        left_table, left_state, right_table, right_state, relation_table, relation_state,
        source_ids, target_ids, relation_ids, negative_ids,
    ):
        rows = left_table.shape[0]
        width = left_table.shape[1]
        left_t, right_t, relation_t = left_table.T, right_table.T, relation_table.T
        nrel = relation_t.shape[1]
        here_l, here_r = lax.axis_index("left"), lax.axis_index("right")
        me = here_r.astype(jnp.int32).reshape(1)
        edges = source_ids.shape[-1]
        groups = negative_ids.shape[2]
        n_rows = n_left * rows
        half = outer * rows
        one_block = shape(width, rows, dtype=BF)
        table_bf = shape(width, edges, dtype=BF)

        def cast(value, after=()):
            parts = 5 if width % 80 == 0 else 1
            scratch = [pltpu.VMEM(value.shape, F32), pltpu.SemaphoreType.DMA((parts,))]
            return call(cast_body, one_block, scratch, after=after, place=pl.ANY)(value)

        right_bf = right_t.astype(BF)
        near = [next_column(right_bf, 2 * k) for k in range(outer)]
        some = outer // 2
        cut = some * rows
        chunk = shape(width, cut, dtype=BF)
        joined_low = call(join_body, chunk, flops=COST_JOIN_LOW)(*near[:some])
        other_low = call(join_body, chunk, flops=COST_MIDDLE)(swap_left(joined_low, 1))

        ids = [source_ids, target_ids, relation_ids, negative_ids]
        longest = max(i.shape[-1] for i in ids)
        ids = [i.reshape(-1, i.shape[-1]) for i in ids]
        ids = jnp.concatenate([jnp.pad(i, ((0, 0), (0, longest - i.shape[-1]))) for i in ids], axis=0)
        left_bf = cast(left_t)
        half_left = [left_bf] + [swap_right(left_bf, 2 * k) for k in range(1, far_right)]
        place = jnp.stack([here_r, here_l]).astype(jnp.int32)
        weight, relation_bf, ids = call(
            functools.partial(count_body, far_right, outer, rows, negative_ids.shape[-1]),
            (shape(groups, n_rows, LANES), shape(width, nrel, dtype=BF), shape(*ids.shape, dtype=jnp.int32)),
            here=place,
            after=(joined_low,),
        )(ids, relation_t)
        half_joined = call(join_body, shape(width, far_right * rows, dtype=BF), after=(weight,))(*half_left)
        joined = call(join_body, chunk, flops=COST_JOIN_HIGH, after=(half_joined,))(*near[some:])
        other_high = swap_left(joined, 1)
        sibling_left = swap_right(half_joined, 1)
        moved = next_column(call(pack_body, shape(width + 8, rows), after=(joined,))(right_t, right_state[None, :]), 0)

        s, o, q = call(functools.partial(query_body, far_right), (table_bf, table_bf, table_bf), flops=COST_QUERY)(
            *half_left, sibling_left, relation_bf, ids
        )
        right_near, qg = call(
            functools.partial(near_body, outer),
            (shape(width, half), shape(width, edges)),
            [pltpu.VMEM((width, half), BF), pltpu.VMEM((half, edges), BF)],
        )(*near, q, weight, ids)
        right_low, qg = call(
            functools.partial(middle_body, half), (chunk, shape(width, edges)), [pltpu.VMEM((cut, edges), BF)],
        )(other_low, q, weight, ids, qg)
        tall = nrel // LANES * width
        size = -(-tall // (n_right * 16)) * 16
        piece = shape(size, LANES, dtype=BF)
        all_pieces = pltpu.VMEM((size * n_right, LANES), F32)
        m, g, mine, theirs = call(
            functools.partial(far_body, half + cut, n_right),
            (shape(cut, edges, dtype=BF), shape(width, edges), shape(far_right * size, LANES),
             shape(far_right * size, LANES, dtype=BF)),
            [pltpu.VMEM((width, nrel), F32), all_pieces],
            me,
            after=(moved,),
        )(other_high, q, weight, ids, qg, s)
        left_rows = n_right * rows
        left_half = left_rows // 2
        right_high, right_low, left_near, left_far = call(
            rest_body,
            (chunk, chunk, shape(width, left_half), shape(width, left_half, dtype=BF)),
            [pltpu.VMEM((width, left_rows), F32)],
        )(m, q, g, o, ids, right_low)

        mine, *rest = call(
            piece_body, (shape(size, LANES),) + (piece,) * (far_right - 1), flops=COST_SUM
        )(mine, swap_right(theirs, 1))
        got = [swap_right(p, 2 * (k + 1)) for k, p in enumerate(rest)]
        mine = call(sum_body, piece, flops=COST_SUM)(mine, *got)
        bit = n_left // 2
        while bit > 1:
            mine = call(sum_body, piece, flops=COST_SUM)(mine, swap_left(mine, bit))
            bit //= 2
        mine = call(sum_body, piece, flops=COST_SUM)(mine, swap_left(mine, 1))
        pieces = [mine] + [swap_right(mine, 2 * k) for k in range(1, far_right)]
        sibling = swap_right(call(stack_body, shape(far_right * size, LANES, dtype=BF))(*pieces), 1)

        left_own, *blocks = call(left_body, (shape(width, rows),) + (one_block,) * (far_right - 1))(
            left_near, swap_right(left_far, 1)
        )
        left_got = [swap_right(block, 2 * (k + 1)) for k, block in enumerate(blocks)]

        got_low = swap_left(right_low, 1)
        got_high = swap_left(right_high, 1)
        outs = (one_block,) * some
        high = call(functools.partial(chunk_body, cut), outs, flops=COST_HIGH)(right_near, got_high)
        outs = (shape(width, rows),) + outs[1:]
        low = call(functools.partial(chunk_body, 0), outs, flops=COST_LOW, after=left_got)(right_near, got_low)
        right_got = [low[0]] + [swap_left(block, 2 * (some + k)) for k, block in enumerate(high)]
        right_got += [swap_left(low[k], 2 * k) for k in range(1, some)]

        def update(got, table, state, flops=0):
            outs = (shape(width, rows), shape(1, rows))
            return call(functools.partial(update_body, len(got)), outs, flops=flops)(*got, table, state)

        left_new, left_state_new = update([left_own, *left_got], left_t, left_state[None, :])
        right_new, right_state_new = update(right_got, moved, moved, COST_UPDATE)
        relation_new, relation_state_new = call(
            functools.partial(relation_body, n_right), (shape(width, nrel), shape(1, nrel)), [all_pieces], me
        )(*pieces, sibling, relation_t, relation_state[None, :])
        return (
            left_new.T, left_state_new.reshape(-1), right_new.T, right_state_new.reshape(-1),
            relation_new.T, relation_state_new.reshape(-1),
        )

    return per_device


def solution(mesh):
    rows = P(("left", "right"), None)
    vector = P(("left", "right"))
    ids = P("left", "right", None)
    return jax.shard_map(
        build(mesh),
        mesh=mesh,
        in_specs=(rows, vector, rows, vector, P(), P(), ids, ids, ids, P("left", "right", None, None)),
        out_specs=(rows, vector, rows, vector, P(), P()),
        check_vma=False,
    )
```

```python
import functools

import jax
import jax.numpy as jnp
from jax import lax
from jax.experimental import pallas as pl
from jax.experimental.pallas import tpu as pltpu
from jax.sharding import PartitionSpec as P

LEARN_RATE = 0.1
NEG_WEIGHT = 0.03125
BF = jnp.bfloat16
F32 = jnp.float32
VMEM_LIMIT = 32 * 1024 * 1024
LANES = 128
COST_JOIN_LOW = 6e9
COST_JOIN_HIGH = 6e9
COST_UPDATE = 12e9
COST_HIGH = 12e9
COST_LOW = 12e9
COST_SUM = 1e9
COST_MIDDLE = 6e9
COST_QUERY = 6e9


def dot(a, b, a_dim, b_dim):
    return lax.dot_general(a, b, (((a_dim,), (b_dim,)), ((), ())), preferred_element_type=F32)


def hot(ids, count):
    spot = lax.broadcasted_iota(jnp.int32, (count, ids.shape[1]), 0)
    return jnp.where(spot == ids, 1.0, 0.0).astype(BF)


def step_of(size, most=256):
    return most if size % most == 0 else size


def call(body, out_shape, scratch=(), here=None, after=(), flops=0, place=pltpu.VMEM):
    def run(*args):
        specs = [pl.BlockSpec(memory_space=place)] * len(args)
        if here is not None:
            specs.append(pl.BlockSpec(memory_space=pltpu.SMEM))
            args = (*args, here)
        inner = body
        if after:
            used = len(args)

            def inner(*refs):
                body(*refs[:used], *refs[used + len(after):])

            specs += [pl.BlockSpec(memory_space=pl.ANY)] * len(after)
            args = (*args, *after)
        return pl.pallas_call(
            inner,
            out_shape=out_shape,
            in_specs=specs,
            scratch_shapes=list(scratch),
            compiler_params=pltpu.CompilerParams(vmem_limit_bytes=VMEM_LIMIT),
            cost_estimate=pl.CostEstimate(flops=int(flops), bytes_accessed=0, transcendentals=0),
        )(*args)

    return run


def shape(*dims, dtype=F32):
    return jax.ShapeDtypeStruct(dims, dtype)


def cast_body(in_ref, out_ref, held_ref, sems):
    rows = held_ref.shape[0] // sems.shape[0]
    copies = []
    for k in range(sems.shape[0]):
        at = slice(k * rows, (k + 1) * rows)
        copies.append(pltpu.make_async_copy(in_ref.at[at], held_ref.at[at], sems.at[k]))
        copies[-1].start()
    for k, copy in enumerate(copies):
        at = slice(k * rows, (k + 1) * rows)
        copy.wait()
        out_ref[at, :] = held_ref[at, :].astype(BF)


def count_body(far_right, outer, rows, slots, ids_ref, relation_ref, place_ref, out_ref, relation_bf_ref, local_ref):
    def local(ids, here, half):
        block = (ids // rows) ^ here
        return (block % 2 * half + block // 2) * rows + ids % rows

    ids = ids_ref[...]
    local_ref[...] = ids
    local_ref[0:1, :] = local(ids[0:1], place_ref[0], far_right)
    local_ref[1:2, :] = local(ids[1:2], place_ref[1], outer)
    for g in range(out_ref.shape[0]):
        negative = local(ids[3 + g:4 + g, :slots], place_ref[1], outer)
        for at in range(0, out_ref.shape[1], LANES):
            spot = lax.broadcasted_iota(jnp.int32, (LANES, slots), 0) + at
            total = jnp.sum(jnp.where(spot == negative, NEG_WEIGHT, 0.0), axis=1, keepdims=True)
            out_ref[g, at:at + LANES, :] = jnp.broadcast_to(total, (LANES, LANES))
    relation_bf_ref[...] = relation_ref[...].astype(BF)


def pack_body(table_ref, state_ref, pack_ref):
    width = table_ref.shape[0]
    pack_ref[:width, :] = table_ref[...]
    pack_ref[width:, :] = jnp.broadcast_to(state_ref[...], (pack_ref.shape[0] - width, LANES))


def join_body(*refs):
    out_ref = refs[-1]
    at = 0
    for ref in refs[:-1]:
        out_ref[:, at:at + ref.shape[1]] = ref[...]
        at += ref.shape[1]


def query_body(blocks, *refs):
    near_refs, refs = refs[:blocks], refs[blocks:]
    sibling_ref, relation_ref, ids_ref, s_ref, o_ref, q_ref = refs
    relation = relation_ref[...]
    half = s_ref.shape[0] // 2
    edges = s_ref.shape[1]
    step = step_of(edges)
    near = jnp.concatenate([ref[...] for ref in near_refs], axis=1)
    half_rows = near.shape[1]
    for at in range(0, edges, step):
        cols = slice(at, at + step)
        pick = hot(ids_ref[0:1, cols], 2 * half_rows)
        s = dot(near, pick[:half_rows], 1, 0) + dot(sibling_ref[...], pick[half_rows:], 1, 0)
        o = dot(relation, hot(ids_ref[2:3, cols], relation.shape[1]), 1, 0)
        s_ref[:, cols] = s.astype(BF)
        o_ref[:, cols] = o.astype(BF)
        s_re, s_im, o_re, o_im = s[:half], s[half:], o[:half], o[half:]
        q = jnp.concatenate([s_re * o_re - s_im * o_im, s_re * o_im + s_im * o_re], axis=0)
        q_ref[:, cols] = q.astype(BF)


def grad_chunk(rows_t, q_ref, weight_ref, ids_ref, base, at, step):
    count = rows_t.shape[0]
    edges = q_ref.shape[1]
    cols = slice(at, at + step)
    scores = dot(rows_t, q_ref[:, cols], 1, 0)
    spot = lax.broadcasted_iota(jnp.int32, (count, step), 0) + base
    h = jnp.where(spot == ids_ref[1:2, cols], 1.0, 0.0)
    w = weight_ref[at // (edges // weight_ref.shape[0]), base:base + count, :]
    w = jnp.concatenate([w] * (step // LANES), axis=1)
    return ((w + h) * (0.5 * jnp.tanh(0.5 * scores) + 0.5) - h).astype(BF)


def complex_back(g, other):
    half = g.shape[0] // 2
    g_re, g_im, o_re, o_im = g[:half], g[half:], other[:half], other[half:]
    return jnp.concatenate([g_re * o_re + g_im * o_im, g_im * o_re - g_re * o_im], axis=0).astype(BF)


def products(rows_ref, q_ref, weight_ref, ids_ref, m_ref, base):
    rows_t = rows_ref[...].T
    step = step_of(q_ref.shape[1] // weight_ref.shape[0])
    for at in range(0, q_ref.shape[1], step):
        m_ref[:, at:at + step] = grad_chunk(rows_t, q_ref, weight_ref, ids_ref, base, at, step)


def near_body(blocks, *refs):
    block_refs, refs = refs[:blocks], refs[blocks:]
    q_ref, weight_ref, ids_ref, right_ref, qg_ref, rows_ref, m_ref = refs
    join_body(*block_refs, rows_ref)
    products(rows_ref, q_ref, weight_ref, ids_ref, m_ref, 0)
    right_ref[...] = dot(q_ref[...], m_ref[...], 1, 1).astype(BF)
    qg_ref[...] = dot(rows_ref[...], m_ref[...], 1, 0)


def middle_body(base, rows_ref, q_ref, weight_ref, ids_ref, qg_ref, right_ref, qg_out_ref, m_ref):
    products(rows_ref, q_ref, weight_ref, ids_ref, m_ref, base)
    right_ref[...] = dot(q_ref[...], m_ref[...], 1, 1).astype(BF)
    qg_out_ref[...] = qg_ref[...] + dot(rows_ref[...], m_ref[...], 1, 0)


def far_body(
    base, pieces, rows_ref, q_ref, weight_ref, ids_ref, qg_ref, s_ref, here_ref,
    m_ref, g_ref, mine_ref, theirs_ref, kinds_ref, tall_ref,
):
    rows_t = rows_ref[...].T
    width, edges = qg_ref.shape
    step = step_of(edges // weight_ref.shape[0])
    for at in range(0, edges, step):
        cols = slice(at, at + step)
        m = grad_chunk(rows_t, q_ref, weight_ref, ids_ref, base, at, step)
        m_ref[:, cols] = m
        g = qg_ref[:, cols] + dot(rows_ref[...], m, 1, 0)
        g_ref[:, cols] = g
        by_kind = complex_back(g, s_ref[:, cols].astype(F32))
        kinds = dot(by_kind, hot(ids_ref[2:3, cols], kinds_ref.shape[1]), 1, 1)
        if at == 0:
            kinds_ref[...] = kinds
        else:
            kinds_ref[...] += kinds
    parts = kinds_ref.shape[1] // LANES
    for j in range(parts):
        tall_ref[j * width:(j + 1) * width, :] = kinds_ref[:, j * LANES:(j + 1) * LANES]
    rest = tall_ref.shape[0] - parts * width
    if rest:
        tall_ref[parts * width:, :] = jnp.zeros((rest, LANES), F32)
    here = here_ref[0]
    size = tall_ref.shape[0] // pieces
    for k in range(pieces):
        start = pl.multiple_of((here ^ k) * size, 16)
        piece = tall_ref[pl.ds(start, size), :]
        at = slice(k // 2 * size, (k // 2 + 1) * size)
        if k % 2:
            theirs_ref[at, :] = piece.astype(BF)
        else:
            mine_ref[at, :] = piece


def rest_body(m_ref, q_ref, g_ref, o_ref, ids_ref, low_ref, right_ref, low_out_ref, near_ref, far_ref, left_ref):
    low_out_ref[...] = low_ref[...]
    right_ref[...] = dot(q_ref[...], m_ref[...], 1, 1).astype(BF)
    edges = q_ref.shape[1]
    step = step_of(edges)
    for at in range(0, edges, step):
        cols = slice(at, at + step)
        by_source = complex_back(g_ref[:, cols], o_ref[:, cols].astype(F32))
        left = dot(by_source, hot(ids_ref[0:1, cols], left_ref.shape[1]), 1, 1)
        if at == 0:
            left_ref[...] = left
        else:
            left_ref[...] += left
    cut = left_ref.shape[1] // 2
    near_ref[...] = left_ref[:, :cut]
    far_ref[...] = left_ref[:, cut:].astype(BF)


def relation_body(pieces, *refs):
    piece_refs, refs = refs[:pieces // 2], refs[pieces // 2:]
    sibling_ref, table_ref, state_ref, here_ref, new_ref, state_new_ref, tall_ref = refs
    here = here_ref[0]
    size = tall_ref.shape[0] // pieces
    for k in range(pieces):
        start = pl.multiple_of((here ^ k) * size, 16)
        piece = sibling_ref[k // 2 * size:(k // 2 + 1) * size, :] if k % 2 else piece_refs[k // 2][...]
        tall_ref[pl.ds(start, size), :] = piece.astype(F32)
    width, count = table_ref.shape
    for j in range(count // LANES):
        cols = slice(j * LANES, (j + 1) * LANES)
        g = tall_ref[j * width:(j + 1) * width, :]
        state = state_ref[:, cols] + jnp.sum(g * g, axis=0, keepdims=True) * (1.0 / width)
        state_new_ref[:, cols] = state
        new_ref[:, cols] = table_ref[:, cols] - g * (LEARN_RATE * lax.rsqrt(state))


def piece_body(mine_ref, got_ref, own_ref, *other_refs):
    size = own_ref.shape[0]
    for k, ref in enumerate((own_ref, *other_refs)):
        at = slice(k * size, (k + 1) * size)
        ref[...] = (mine_ref[at, :] + got_ref[at, :].astype(F32)).astype(ref.dtype)


def left_body(near_ref, got_ref, own_ref, *other_refs):
    for k, ref in enumerate((own_ref, *other_refs)):
        at = slice(k * LANES, (k + 1) * LANES)
        ref[...] = (near_ref[:, at] + got_ref[:, at].astype(F32)).astype(ref.dtype)


def stack_body(*refs):
    size = refs[0].shape[0]
    for k, ref in enumerate(refs[:-1]):
        refs[-1][k * size:(k + 1) * size, :] = ref[...]


def chunk_body(base, near_ref, got_ref, *block_refs):
    for k, ref in enumerate(block_refs):
        cols = slice(k * LANES, (k + 1) * LANES)
        total = near_ref[:, base + k * LANES:base + (k + 1) * LANES].astype(F32) + got_ref[:, cols].astype(F32)
        ref[...] = total.astype(ref.dtype)


def sum_body(*refs):
    total = refs[0][...].astype(F32)
    for ref in refs[1:-1]:
        total = total + ref[...].astype(F32)
    refs[-1][...] = total.astype(BF)


def update_body(parts, *refs):
    part_refs, (table_ref, state_ref, new_ref, state_new_ref) = refs[:parts], refs[parts:]
    g = part_refs[0][...].astype(F32)
    for ref in part_refs[1:]:
        g = g + ref[...].astype(F32)
    width = g.shape[0]
    state = state_ref[state_ref.shape[0] - 1:, :] + jnp.sum(g * g, axis=0, keepdims=True) * (1.0 / width)
    state_new_ref[...] = state
    new_ref[...] = table_ref[:width, :] - g * (LEARN_RATE * lax.rsqrt(state))


def build(mesh):
    n_left, n_right = mesh.shape["left"], mesh.shape["right"]
    for count in (n_left, n_right):
        assert count & (count - 1) == 0 and count > 3
    outer = n_left // 2
    far_right = n_right // 2

    def swap_left(value, by):
        return lax.ppermute(value, "left", [(i, i ^ by) for i in range(n_left)])

    def swap_right(value, by):
        return lax.ppermute(value, "right", [(i, i ^ by) for i in range(n_right)])

    def next_column(value, by):
        perm = []
        for i in range(n_left):
            for r in range(n_right):
                perm.append((i * n_right + r, (i ^ by) * n_right + (r + 1) % n_right))
        return lax.ppermute(value, ("left", "right"), perm)

    def per_device(
        left_table, left_state, right_table, right_state, relation_table, relation_state,
        source_ids, target_ids, relation_ids, negative_ids,
    ):
        rows = left_table.shape[0]
        width = left_table.shape[1]
        left_t, right_t, relation_t = left_table.T, right_table.T, relation_table.T
        nrel = relation_t.shape[1]
        here_l, here_r = lax.axis_index("left"), lax.axis_index("right")
        me = here_r.astype(jnp.int32).reshape(1)
        edges = source_ids.shape[-1]
        groups = negative_ids.shape[2]
        n_rows = n_left * rows
        half = outer * rows
        one_block = shape(width, rows, dtype=BF)
        table_bf = shape(width, edges, dtype=BF)

        def cast(value, after=()):
            parts = 5 if width % 80 == 0 else 1
            scratch = [pltpu.VMEM(value.shape, F32), pltpu.SemaphoreType.DMA((parts,))]
            return call(cast_body, one_block, scratch, after=after, place=pl.ANY)(value)

        right_bf = right_t.astype(BF)
        near = [right_bf] + [swap_left(right_bf, 2 * k) for k in range(1, outer)]
        some = outer // 2
        cut = some * rows
        chunk = shape(width, cut, dtype=BF)
        joined_low = call(join_body, chunk, flops=COST_JOIN_LOW)(*near[:some])
        other_low = call(join_body, chunk, flops=COST_MIDDLE)(swap_left(joined_low, 1))

        ids = [source_ids, target_ids, relation_ids, negative_ids]
        longest = max(i.shape[-1] for i in ids)
        ids = [i.reshape(-1, i.shape[-1]) for i in ids]
        ids = jnp.concatenate([jnp.pad(i, ((0, 0), (0, longest - i.shape[-1]))) for i in ids], axis=0)
        ids = lax.ppermute(ids, "right", [(i, (i - 1) % n_right) for i in range(n_right)])
        left_bf = cast(left_t)
        half_left = [left_bf] + [swap_right(left_bf, 2 * k) for k in range(1, far_right)]
        place = jnp.stack([here_r, here_l]).astype(jnp.int32)
        weight, relation_bf, ids = call(
            functools.partial(count_body, far_right, outer, rows, negative_ids.shape[-1]),
            (shape(groups, n_rows, LANES), shape(width, nrel, dtype=BF), shape(*ids.shape, dtype=jnp.int32)),
            here=place,
            after=(joined_low,),
        )(ids, relation_t)
        half_joined = call(join_body, shape(width, far_right * rows, dtype=BF), after=(weight,))(*half_left)
        joined = call(join_body, chunk, flops=COST_JOIN_HIGH, after=(half_joined,))(*near[some:])
        other_high = swap_left(joined, 1)
        sibling_left = swap_right(half_joined, 1)
        moved = next_column(call(pack_body, shape(width + 8, rows), after=(joined,))(right_t, right_state[None, :]), 0)

        s, o, q = call(functools.partial(query_body, far_right), (table_bf, table_bf, table_bf), flops=COST_QUERY)(
            *half_left, sibling_left, relation_bf, ids
        )
        right_near, qg = call(
            functools.partial(near_body, outer),
            (shape(width, half, dtype=BF), shape(width, edges)),
            [pltpu.VMEM((width, half), BF), pltpu.VMEM((half, edges), BF)],
        )(*near, q, weight, ids)
        right_low, qg = call(
            functools.partial(middle_body, half), (chunk, shape(width, edges)), [pltpu.VMEM((cut, edges), BF)],
        )(other_low, q, weight, ids, qg)
        tall = nrel // LANES * width
        size = -(-tall // (n_right * 16)) * 16
        piece = shape(size, LANES, dtype=BF)
        all_pieces = pltpu.VMEM((size * n_right, LANES), F32)
        m, g, mine, theirs = call(
            functools.partial(far_body, half + cut, n_right),
            (shape(cut, edges, dtype=BF), shape(width, edges), shape(far_right * size, LANES),
             shape(far_right * size, LANES, dtype=BF)),
            [pltpu.VMEM((width, nrel), F32), all_pieces],
            me,
            after=(moved,),
        )(other_high, q, weight, ids, qg, s)
        left_rows = n_right * rows
        left_half = left_rows // 2
        right_high, right_low, left_near, left_far = call(
            rest_body,
            (chunk, chunk, shape(width, left_half), shape(width, left_half, dtype=BF)),
            [pltpu.VMEM((width, left_rows), F32)],
        )(m, q, g, o, ids, right_low)

        near_got = next_column(right_near, 0)
        got_low = next_column(right_low, 1)
        got_high = next_column(right_high, 1)

        mine, *rest = call(
            piece_body, (shape(size, LANES),) + (piece,) * (far_right - 1), flops=COST_SUM
        )(mine, swap_right(theirs, 1))
        got = [swap_right(p, 2 * (k + 1)) for k, p in enumerate(rest)]
        mine = call(sum_body, piece, flops=COST_SUM, after=(near_got,))(mine, *got)
        bit = n_left // 2
        while bit > 1:
            after = (got_high,) if 2 * bit == n_left else (got_low,)
            mine = call(sum_body, piece, flops=COST_SUM, after=after)(mine, swap_left(mine, bit))
            bit //= 2
        mine = call(sum_body, piece, flops=COST_SUM)(mine, swap_left(mine, 1))
        pieces = [mine] + [swap_right(mine, 2 * k) for k in range(1, far_right)]
        sibling = swap_right(call(stack_body, shape(far_right * size, LANES, dtype=BF))(*pieces), 1)

        left_own, *blocks = call(left_body, (shape(width, rows),) + (one_block,) * (far_right - 1))(
            left_near, swap_right(left_far, 1)
        )
        left_got = [swap_right(block, 2 * (k + 1)) for k, block in enumerate(blocks)]

        outs = (one_block,) * some
        high = call(functools.partial(chunk_body, cut), outs, flops=COST_HIGH)(near_got, got_high)
        outs = (shape(width, rows),) + outs[1:]
        low = call(functools.partial(chunk_body, 0), outs, flops=COST_LOW, after=left_got)(near_got, got_low)
        right_got = [low[0]] + [swap_left(block, 2 * (some + k)) for k, block in enumerate(high)]
        right_got += [swap_left(low[k], 2 * k) for k in range(1, some)]

        def update(got, table, state, flops=0):
            outs = (shape(width, rows), shape(1, rows))
            return call(functools.partial(update_body, len(got)), outs, flops=flops)(*got, table, state)

        left_new, left_state_new = update([left_own, *left_got], left_t, left_state[None, :])
        right_new, right_state_new = update(right_got, moved, moved, COST_UPDATE)
        relation_new, relation_state_new = call(
            functools.partial(relation_body, n_right),
            (shape(width, nrel), shape(1, nrel)),
            [all_pieces],
            me,
            after=(right_state_new,),
        )(*pieces, sibling, relation_t, relation_state[None, :])
        return (
            left_new.T, left_state_new.reshape(-1), right_new.T, right_state_new.reshape(-1),
            relation_new.T, relation_state_new.reshape(-1),
        )

    return per_device


def solution(mesh):
    rows = P(("left", "right"), None)
    vector = P(("left", "right"))
    ids = P("left", "right", None)
    return jax.shard_map(
        build(mesh),
        mesh=mesh,
        in_specs=(rows, vector, rows, vector, P(), P(), ids, ids, ids, P("left", "right", None, None)),
        out_specs=(rows, vector, rows, vector, P(), P()),
        check_vma=False,
    )
```

```python
import functools

import jax
import jax.numpy as jnp
from jax import lax
from jax.experimental import pallas as pl
from jax.experimental.pallas import tpu as pltpu
from jax.sharding import PartitionSpec as P

LEARN_RATE = 0.1
NEG_WEIGHT = 0.03125
BF = jnp.bfloat16
F32 = jnp.float32
VMEM_LIMIT = 32 * 1024 * 1024
LANES = 128
COST_JOIN_LOW = 6e9
COST_JOIN_HIGH = 6e9
COST_UPDATE = 12e9
COST_HIGH = 12e9
COST_LOW = 12e9
COST_SUM = 1e9
COST_MIDDLE = 6e9
COST_QUERY = 6e9


def dot(a, b, a_dim, b_dim):
    return lax.dot_general(a, b, (((a_dim,), (b_dim,)), ((), ())), preferred_element_type=F32)


def hot(ids, count):
    spot = lax.broadcasted_iota(jnp.int32, (count, ids.shape[1]), 0)
    return jnp.where(spot == ids, 1.0, 0.0).astype(BF)


def step_of(size, most=256):
    return most if size % most == 0 else size


def call(body, out_shape, scratch=(), here=None, after=(), flops=0, place=pltpu.VMEM, ahead=()):
    def run(*args):
        specs = [pl.BlockSpec(memory_space=place)] * len(args)
        if here is not None:
            specs.append(pl.BlockSpec(memory_space=pltpu.SMEM))
            args = (*args, here)
        inner = body
        if after or ahead:
            first = len(ahead)
            last = first + len(args)

            def inner(*refs):
                body(*refs[first:last], *refs[last + len(after):])

            unread = pl.BlockSpec(memory_space=pl.ANY)
            specs = [unread] * len(ahead) + specs + [unread] * len(after)
            args = (*ahead, *args, *after)
        return pl.pallas_call(
            inner,
            out_shape=out_shape,
            in_specs=specs,
            scratch_shapes=list(scratch),
            compiler_params=pltpu.CompilerParams(vmem_limit_bytes=VMEM_LIMIT),
            cost_estimate=pl.CostEstimate(flops=int(flops), bytes_accessed=0, transcendentals=0),
        )(*args)

    return run


def shape(*dims, dtype=F32):
    return jax.ShapeDtypeStruct(dims, dtype)


def cast_body(in_ref, out_ref, held_ref, sems):
    rows = held_ref.shape[0] // sems.shape[0]
    copies = []
    for k in range(sems.shape[0]):
        at = slice(k * rows, (k + 1) * rows)
        copies.append(pltpu.make_async_copy(in_ref.at[at], held_ref.at[at], sems.at[k]))
        copies[-1].start()
    for k, copy in enumerate(copies):
        at = slice(k * rows, (k + 1) * rows)
        copy.wait()
        out_ref[at, :] = held_ref[at, :].astype(BF)


def count_body(far_right, outer, rows, slots, ids_ref, relation_ref, place_ref, out_ref, relation_bf_ref, local_ref):
    def local(ids, here, half):
        block = (ids // rows) ^ here
        return (block % 2 * half + block // 2) * rows + ids % rows

    ids = ids_ref[...]
    local_ref[...] = ids
    local_ref[0:1, :] = local(ids[0:1], place_ref[0], far_right)
    local_ref[1:2, :] = local(ids[1:2], place_ref[1], outer)
    for g in range(out_ref.shape[0]):
        negative = local(ids[3 + g:4 + g, :slots], place_ref[1], outer)
        for at in range(0, out_ref.shape[1], LANES):
            spot = lax.broadcasted_iota(jnp.int32, (LANES, slots), 0) + at
            total = jnp.sum(jnp.where(spot == negative, NEG_WEIGHT, 0.0), axis=1, keepdims=True)
            out_ref[g, at:at + LANES, :] = jnp.broadcast_to(total, (LANES, LANES))
    relation_bf_ref[...] = relation_ref[...].astype(BF)


def pack_body(table_ref, state_ref, pack_ref):
    width = table_ref.shape[0]
    pack_ref[:width, :] = table_ref[...]
    pack_ref[width:, :] = jnp.broadcast_to(state_ref[...], (pack_ref.shape[0] - width, LANES))


def join_body(*refs):
    out_ref = refs[-1]
    at = 0
    for ref in refs[:-1]:
        out_ref[:, at:at + ref.shape[1]] = ref[...]
        at += ref.shape[1]


def query_body(blocks, *refs):
    near_refs, refs = refs[:blocks], refs[blocks:]
    sibling_ref, relation_ref, ids_ref, s_ref, o_ref, q_ref = refs
    relation = relation_ref[...]
    half = s_ref.shape[0] // 2
    edges = s_ref.shape[1]
    step = step_of(edges)
    near = jnp.concatenate([ref[...] for ref in near_refs], axis=1)
    half_rows = near.shape[1]
    for at in range(0, edges, step):
        cols = slice(at, at + step)
        pick = hot(ids_ref[0:1, cols], 2 * half_rows)
        s = dot(near, pick[:half_rows], 1, 0) + dot(sibling_ref[...], pick[half_rows:], 1, 0)
        o = dot(relation, hot(ids_ref[2:3, cols], relation.shape[1]), 1, 0)
        s_ref[:, cols] = s.astype(BF)
        o_ref[:, cols] = o.astype(BF)
        s_re, s_im, o_re, o_im = s[:half], s[half:], o[:half], o[half:]
        q = jnp.concatenate([s_re * o_re - s_im * o_im, s_re * o_im + s_im * o_re], axis=0)
        q_ref[:, cols] = q.astype(BF)


def grad_chunk(rows_t, q_ref, weight_ref, ids_ref, base, at, step):
    count = rows_t.shape[0]
    edges = q_ref.shape[1]
    cols = slice(at, at + step)
    scores = dot(rows_t, q_ref[:, cols], 1, 0)
    spot = lax.broadcasted_iota(jnp.int32, (count, step), 0) + base
    h = jnp.where(spot == ids_ref[1:2, cols], 1.0, 0.0)
    w = weight_ref[at // (edges // weight_ref.shape[0]), base:base + count, :]
    w = jnp.concatenate([w] * (step // LANES), axis=1)
    return ((w + h) * (0.5 * jnp.tanh(0.5 * scores) + 0.5) - h).astype(BF)


def complex_back(g, other):
    half = g.shape[0] // 2
    g_re, g_im, o_re, o_im = g[:half], g[half:], other[:half], other[half:]
    return jnp.concatenate([g_re * o_re + g_im * o_im, g_im * o_re - g_re * o_im], axis=0).astype(BF)


def products(rows_ref, q_ref, weight_ref, ids_ref, m_ref, base):
    rows_t = rows_ref[...].T
    step = step_of(q_ref.shape[1] // weight_ref.shape[0])
    for at in range(0, q_ref.shape[1], step):
        m_ref[:, at:at + step] = grad_chunk(rows_t, q_ref, weight_ref, ids_ref, base, at, step)


def near_body(blocks, *refs):
    block_refs, refs = refs[:blocks], refs[blocks:]
    q_ref, weight_ref, ids_ref, right_ref, qg_ref, rows_ref, m_ref = refs
    join_body(*block_refs, rows_ref)
    products(rows_ref, q_ref, weight_ref, ids_ref, m_ref, 0)
    right_ref[...] = dot(q_ref[...], m_ref[...], 1, 1)
    qg_ref[...] = dot(rows_ref[...], m_ref[...], 1, 0)


def middle_body(base, rows_ref, q_ref, weight_ref, ids_ref, qg_ref, right_ref, qg_out_ref, m_ref):
    products(rows_ref, q_ref, weight_ref, ids_ref, m_ref, base)
    right_ref[...] = dot(q_ref[...], m_ref[...], 1, 1).astype(BF)
    qg_out_ref[...] = qg_ref[...] + dot(rows_ref[...], m_ref[...], 1, 0)


def far_body(
    base, pieces, rows_ref, q_ref, weight_ref, ids_ref, qg_ref, s_ref, here_ref,
    m_ref, g_ref, mine_ref, theirs_ref, kinds_ref, tall_ref,
):
    rows_t = rows_ref[...].T
    width, edges = qg_ref.shape
    step = step_of(edges // weight_ref.shape[0])
    for at in range(0, edges, step):
        cols = slice(at, at + step)
        m = grad_chunk(rows_t, q_ref, weight_ref, ids_ref, base, at, step)
        m_ref[:, cols] = m
        g = qg_ref[:, cols] + dot(rows_ref[...], m, 1, 0)
        g_ref[:, cols] = g
        by_kind = complex_back(g, s_ref[:, cols].astype(F32))
        kinds = dot(by_kind, hot(ids_ref[2:3, cols], kinds_ref.shape[1]), 1, 1)
        if at == 0:
            kinds_ref[...] = kinds
        else:
            kinds_ref[...] += kinds
    parts = kinds_ref.shape[1] // LANES
    for j in range(parts):
        tall_ref[j * width:(j + 1) * width, :] = kinds_ref[:, j * LANES:(j + 1) * LANES]
    rest = tall_ref.shape[0] - parts * width
    if rest:
        tall_ref[parts * width:, :] = jnp.zeros((rest, LANES), F32)
    here = here_ref[0]
    size = tall_ref.shape[0] // pieces
    for k in range(pieces):
        start = pl.multiple_of((here ^ k) * size, 16)
        piece = tall_ref[pl.ds(start, size), :]
        at = slice(k // 2 * size, (k // 2 + 1) * size)
        if k % 2:
            theirs_ref[at, :] = piece.astype(BF)
        else:
            mine_ref[at, :] = piece


def rest_body(m_ref, q_ref, g_ref, o_ref, ids_ref, low_ref, right_ref, low_out_ref, near_ref, far_ref, left_ref):
    low_out_ref[...] = low_ref[...]
    right_ref[...] = dot(q_ref[...], m_ref[...], 1, 1).astype(BF)
    edges = q_ref.shape[1]
    step = step_of(edges)
    for at in range(0, edges, step):
        cols = slice(at, at + step)
        by_source = complex_back(g_ref[:, cols], o_ref[:, cols].astype(F32))
        left = dot(by_source, hot(ids_ref[0:1, cols], left_ref.shape[1]), 1, 1)
        if at == 0:
            left_ref[...] = left
        else:
            left_ref[...] += left
    cut = left_ref.shape[1] // 2
    near_ref[...] = left_ref[:, :cut]
    far_ref[...] = left_ref[:, cut:].astype(BF)


def relation_body(pieces, *refs):
    piece_refs, refs = refs[:pieces // 2], refs[pieces // 2:]
    sibling_ref, table_ref, state_ref, here_ref, new_ref, state_new_ref, tall_ref = refs
    here = here_ref[0]
    size = tall_ref.shape[0] // pieces
    for k in range(pieces):
        start = pl.multiple_of((here ^ k) * size, 16)
        piece = sibling_ref[k // 2 * size:(k // 2 + 1) * size, :] if k % 2 else piece_refs[k // 2][...]
        tall_ref[pl.ds(start, size), :] = piece.astype(F32)
    width, count = table_ref.shape
    for j in range(count // LANES):
        cols = slice(j * LANES, (j + 1) * LANES)
        g = tall_ref[j * width:(j + 1) * width, :]
        state = state_ref[:, cols] + jnp.sum(g * g, axis=0, keepdims=True) * (1.0 / width)
        state_new_ref[:, cols] = state
        new_ref[:, cols] = table_ref[:, cols] - g * (LEARN_RATE * lax.rsqrt(state))


def piece_body(mine_ref, got_ref, own_ref, *other_refs):
    size = own_ref.shape[0]
    for k, ref in enumerate((own_ref, *other_refs)):
        at = slice(k * size, (k + 1) * size)
        ref[...] = (mine_ref[at, :] + got_ref[at, :].astype(F32)).astype(ref.dtype)


def left_body(near_ref, got_ref, own_ref, *other_refs):
    for k, ref in enumerate((own_ref, *other_refs)):
        at = slice(k * LANES, (k + 1) * LANES)
        ref[...] = (near_ref[:, at] + got_ref[:, at].astype(F32)).astype(ref.dtype)


def stack_body(*refs):
    size = refs[0].shape[0]
    for k, ref in enumerate(refs[:-1]):
        refs[-1][k * size:(k + 1) * size, :] = ref[...]


def chunk_body(base, first, near_ref, got_ref, *block_refs):
    for k, ref in enumerate(block_refs):
        at = (first + k) * LANES
        total = near_ref[:, at:at + LANES] + got_ref[:, at - base:at - base + LANES].astype(F32)
        ref[...] = total.astype(ref.dtype)


def sum_body(*refs):
    total = refs[0][...].astype(F32)
    for ref in refs[1:-1]:
        total = total + ref[...].astype(F32)
    refs[-1][...] = total.astype(BF)


def update_body(parts, *refs):
    part_refs, (table_ref, state_ref, new_ref, state_new_ref) = refs[:parts], refs[parts:]
    g = part_refs[0][...].astype(F32)
    for ref in part_refs[1:]:
        g = g + ref[...].astype(F32)
    width = g.shape[0]
    state = state_ref[state_ref.shape[0] - 1:, :] + jnp.sum(g * g, axis=0, keepdims=True) * (1.0 / width)
    state_new_ref[...] = state
    new_ref[...] = table_ref[:width, :] - g * (LEARN_RATE * lax.rsqrt(state))


def build(mesh):
    n_left, n_right = mesh.shape["left"], mesh.shape["right"]
    for count in (n_left, n_right):
        assert count & (count - 1) == 0 and count > 3
    outer = n_left // 2
    far_right = n_right // 2

    def swap_left(value, by):
        return lax.ppermute(value, "left", [(i, i ^ by) for i in range(n_left)])

    def swap_right(value, by):
        return lax.ppermute(value, "right", [(i, i ^ by) for i in range(n_right)])

    def next_column(value, by):
        perm = []
        for i in range(n_left):
            for r in range(n_right):
                perm.append((i * n_right + r, (i ^ by) * n_right + (r + 1) % n_right))
        return lax.ppermute(value, ("left", "right"), perm)

    def per_device(
        left_table, left_state, right_table, right_state, relation_table, relation_state,
        source_ids, target_ids, relation_ids, negative_ids,
    ):
        rows = left_table.shape[0]
        width = left_table.shape[1]
        left_t, right_t, relation_t = left_table.T, right_table.T, relation_table.T
        nrel = relation_t.shape[1]
        here_l, here_r = lax.axis_index("left"), lax.axis_index("right")
        me = here_r.astype(jnp.int32).reshape(1)
        edges = source_ids.shape[-1]
        groups = negative_ids.shape[2]
        n_rows = n_left * rows
        half = outer * rows
        one_block = shape(width, rows, dtype=BF)
        table_bf = shape(width, edges, dtype=BF)

        def cast(value, after=()):
            parts = 5 if width % 80 == 0 else 1
            scratch = [pltpu.VMEM(value.shape, F32), pltpu.SemaphoreType.DMA((parts,))]
            return call(cast_body, one_block, scratch, after=after, place=pl.ANY)(value)

        right_bf = right_t.astype(BF)
        near = [next_column(right_bf, 2 * k) for k in range(outer)]
        some = outer // 2
        cut = some * rows
        chunk = shape(width, cut, dtype=BF)
        joined_low = call(join_body, chunk, flops=COST_JOIN_LOW)(*near[:some])
        other_low = call(join_body, chunk, flops=COST_MIDDLE)(swap_left(joined_low, 1))

        ids = [source_ids, target_ids, relation_ids, negative_ids]
        longest = max(i.shape[-1] for i in ids)
        ids = [i.reshape(-1, i.shape[-1]) for i in ids]
        ids = jnp.concatenate([jnp.pad(i, ((0, 0), (0, longest - i.shape[-1]))) for i in ids], axis=0)
        left_bf = cast(left_t)
        half_left = [left_bf] + [swap_right(left_bf, 2 * k) for k in range(1, far_right)]
        place = jnp.stack([here_r, here_l]).astype(jnp.int32)
        weight, relation_bf, ids = call(
            functools.partial(count_body, far_right, outer, rows, negative_ids.shape[-1]),
            (shape(groups, n_rows, LANES), shape(width, nrel, dtype=BF), shape(*ids.shape, dtype=jnp.int32)),
            here=place,
            after=(joined_low,),
        )(ids, relation_t)
        half_joined = call(join_body, shape(width, far_right * rows, dtype=BF), after=(weight,))(*half_left)
        joined = call(join_body, chunk, flops=COST_JOIN_HIGH, after=(half_joined,), ahead=(near[0],))(*near[some:])
        other_high = swap_left(joined, 1)
        sibling_left = swap_right(half_joined, 1)
        moved = next_column(call(pack_body, shape(width + 8, rows), after=(joined,))(right_t, right_state[None, :]), 0)

        s, o, q = call(functools.partial(query_body, far_right), (table_bf, table_bf, table_bf), flops=COST_QUERY)(
            *half_left, sibling_left, relation_bf, ids
        )
        right_near, qg = call(
            functools.partial(near_body, outer),
            (shape(width, half), shape(width, edges)),
            [pltpu.VMEM((width, half), BF), pltpu.VMEM((half, edges), BF)],
        )(*near, q, weight, ids)
        right_low, qg = call(
            functools.partial(middle_body, half), (chunk, shape(width, edges)), [pltpu.VMEM((cut, edges), BF)],
        )(other_low, q, weight, ids, qg)
        tall = nrel // LANES * width
        size = -(-tall // (n_right * 16)) * 16
        piece = shape(size, LANES, dtype=BF)
        all_pieces = pltpu.VMEM((size * n_right, LANES), F32)
        m, g, mine, theirs = call(
            functools.partial(far_body, half + cut, n_right),
            (shape(cut, edges, dtype=BF), shape(width, edges), shape(far_right * size, LANES),
             shape(far_right * size, LANES, dtype=BF)),
            [pltpu.VMEM((width, nrel), F32), all_pieces],
            me,
            after=(moved,),
        )(other_high, q, weight, ids, qg, s)
        left_rows = n_right * rows
        left_half = left_rows // 2
        right_high, right_low, left_near, left_far = call(
            rest_body,
            (chunk, chunk, shape(width, left_half), shape(width, left_half, dtype=BF)),
            [pltpu.VMEM((width, left_rows), F32)],
        )(m, q, g, o, ids, right_low)

        mine, *rest = call(
            piece_body, (shape(size, LANES),) + (piece,) * (far_right - 1), flops=COST_SUM
        )(mine, swap_right(theirs, 1))
        got = [swap_right(p, 2 * (k + 1)) for k, p in enumerate(rest)]
        mine = call(sum_body, piece, flops=COST_SUM)(mine, *got)
        bit = n_left // 2
        while bit > 1:
            mine = call(sum_body, piece, flops=COST_SUM)(mine, swap_left(mine, bit))
            bit //= 2
        over_z = mine
        mine = call(sum_body, piece, flops=COST_SUM)(mine, swap_left(mine, 1))
        pieces = [mine] + [swap_right(mine, 2 * k) for k in range(1, far_right)]
        sibling = swap_right(call(stack_body, shape(far_right * size, LANES, dtype=BF))(*pieces), 1)

        left_own, *blocks = call(left_body, (shape(width, rows),) + (one_block,) * (far_right - 1))(
            left_near, swap_right(left_far, 1)
        )
        left_got = [swap_right(block, 2 * (k + 1)) for k, block in enumerate(blocks)]

        got_low = swap_left(right_low, 1)
        got_high = swap_left(right_high, 1)
        def chunk_of(first, outs, got, flops, after=()):
            base = cut if first >= some else 0
            body = functools.partial(chunk_body, base, first)
            return call(body, outs, flops=flops, after=after)(right_near, got)

        high = chunk_of(some, (one_block,) * (some - 1), got_high, COST_HIGH)
        last = chunk_of(outer - 1, (one_block,), got_high, COST_HIGH, (over_z,))
        high = [swap_left(block, 2 * (some + k)) for k, block in enumerate([*high, *last])]
        outs = (shape(width, rows),) + (one_block,) * (some - 1)
        low = chunk_of(0, outs, got_low, COST_LOW, left_got)
        right_got = [low[0], *high] + [swap_left(low[k], 2 * k) for k in range(1, some)]

        def update(got, table, state, flops=0):
            outs = (shape(width, rows), shape(1, rows))
            return call(functools.partial(update_body, len(got)), outs, flops=flops)(*got, table, state)

        left_new, left_state_new = update([left_own, *left_got], left_t, left_state[None, :])
        right_new, right_state_new = update(right_got, moved, moved, COST_UPDATE)
        relation_new, relation_state_new = call(
            functools.partial(relation_body, n_right), (shape(width, nrel), shape(1, nrel)), [all_pieces], me
        )(*pieces, sibling, relation_t, relation_state[None, :])
        return (
            left_new.T, left_state_new.reshape(-1), right_new.T, right_state_new.reshape(-1),
            relation_new.T, relation_state_new.reshape(-1),
        )

    return per_device


def solution(mesh):
    rows = P(("left", "right"), None)
    vector = P(("left", "right"))
    ids = P("left", "right", None)
    return jax.shard_map(
        build(mesh),
        mesh=mesh,
        in_specs=(rows, vector, rows, vector, P(), P(), ids, ids, ids, P("left", "right", None, None)),
        out_specs=(rows, vector, rows, vector, P(), P()),
        check_vma=False,
    )
```

```python
import functools

import jax
import jax.numpy as jnp
from jax import lax
from jax.experimental import pallas as pl
from jax.experimental.pallas import tpu as pltpu
from jax.sharding import PartitionSpec as P

LEARN_RATE = 0.1
NEG_WEIGHT = 0.03125
BF = jnp.bfloat16
F32 = jnp.float32
VMEM_LIMIT = 32 * 1024 * 1024
LANES = 128
COST_JOIN_LOW = 6e9
COST_JOIN_HIGH = 6e9
COST_UPDATE = 12e9
COST_HIGH = 12e9
COST_LOW = 12e9
COST_SUM = 1e9
COST_MIDDLE = 6e9
COST_QUERY = 6e9


def dot(a, b, a_dim, b_dim):
    return lax.dot_general(a, b, (((a_dim,), (b_dim,)), ((), ())), preferred_element_type=F32)


def hot(ids, count):
    spot = lax.broadcasted_iota(jnp.int32, (count, ids.shape[1]), 0)
    return jnp.where(spot == ids, 1.0, 0.0).astype(BF)


def step_of(size, most=512):
    return most if size % most == 0 else size


def call(body, out_shape, scratch=(), here=None, after=(), flops=0, place=pltpu.VMEM, ahead=()):
    def run(*args):
        specs = [pl.BlockSpec(memory_space=place)] * len(args)
        if here is not None:
            specs.append(pl.BlockSpec(memory_space=pltpu.SMEM))
            args = (*args, here)
        inner = body
        if after or ahead:
            first = len(ahead)
            last = first + len(args)

            def inner(*refs):
                body(*refs[first:last], *refs[last + len(after):])

            unread = pl.BlockSpec(memory_space=pl.ANY)
            specs = [unread] * len(ahead) + specs + [unread] * len(after)
            args = (*ahead, *args, *after)
        return pl.pallas_call(
            inner,
            out_shape=out_shape,
            in_specs=specs,
            scratch_shapes=list(scratch),
            compiler_params=pltpu.CompilerParams(vmem_limit_bytes=VMEM_LIMIT),
            cost_estimate=pl.CostEstimate(flops=int(flops), bytes_accessed=0, transcendentals=0),
        )(*args)

    return run


def shape(*dims, dtype=F32):
    return jax.ShapeDtypeStruct(dims, dtype)


def cast_body(in_ref, out_ref, held_ref, sems):
    rows = held_ref.shape[0] // sems.shape[0]
    copies = []
    for k in range(sems.shape[0]):
        at = slice(k * rows, (k + 1) * rows)
        copies.append(pltpu.make_async_copy(in_ref.at[at], held_ref.at[at], sems.at[k]))
        copies[-1].start()
    for k, copy in enumerate(copies):
        at = slice(k * rows, (k + 1) * rows)
        copy.wait()
        out_ref[at, :] = held_ref[at, :].astype(BF)


def count_body(far_right, outer, rows, slots, ids_ref, relation_ref, place_ref, out_ref, relation_bf_ref, local_ref):
    def local(ids, here, half):
        block = (ids // rows) ^ here
        return (block % 2 * half + block // 2) * rows + ids % rows

    ids = ids_ref[...]
    local_ref[...] = ids
    local_ref[0:1, :] = local(ids[0:1], place_ref[0], far_right)
    local_ref[1:2, :] = local(ids[1:2], place_ref[1], outer)
    for g in range(out_ref.shape[0]):
        negative = local(ids[3 + g:4 + g, :slots], place_ref[1], outer)
        for at in range(0, out_ref.shape[1], LANES):
            spot = lax.broadcasted_iota(jnp.int32, (LANES, slots), 0) + at
            total = jnp.sum(jnp.where(spot == negative, NEG_WEIGHT, 0.0), axis=1, keepdims=True)
            out_ref[g, at:at + LANES, :] = jnp.broadcast_to(total, (LANES, LANES))
    relation_bf_ref[...] = relation_ref[...].astype(BF)


def pack_body(table_ref, state_ref, pack_ref):
    width = table_ref.shape[0]
    pack_ref[:width, :] = table_ref[...]
    pack_ref[width:, :] = jnp.broadcast_to(state_ref[...], (pack_ref.shape[0] - width, LANES))


def join_body(*refs):
    out_ref = refs[-1]
    at = 0
    for ref in refs[:-1]:
        out_ref[:, at:at + ref.shape[1]] = ref[...]
        at += ref.shape[1]


def query_body(blocks, *refs):
    near_refs, refs = refs[:blocks], refs[blocks:]
    sibling_ref, relation_ref, ids_ref, s_ref, o_ref, q_ref = refs
    relation = relation_ref[...]
    half = s_ref.shape[0] // 2
    edges = s_ref.shape[1]
    step = step_of(edges)
    near = jnp.concatenate([ref[...] for ref in near_refs], axis=1)
    half_rows = near.shape[1]
    for at in range(0, edges, step):
        cols = slice(at, at + step)
        pick = hot(ids_ref[0:1, cols], 2 * half_rows)
        s = dot(near, pick[:half_rows], 1, 0) + dot(sibling_ref[...], pick[half_rows:], 1, 0)
        o = dot(relation, hot(ids_ref[2:3, cols], relation.shape[1]), 1, 0)
        s_ref[:, cols] = s.astype(BF)
        o_ref[:, cols] = o.astype(BF)
        s_re, s_im, o_re, o_im = s[:half], s[half:], o[:half], o[half:]
        q = jnp.concatenate([s_re * o_re - s_im * o_im, s_re * o_im + s_im * o_re], axis=0)
        q_ref[:, cols] = q.astype(BF)


def grad_chunk(rows_t, q_ref, weight_ref, ids_ref, base, at, step):
    count = rows_t.shape[0]
    edges = q_ref.shape[1]
    cols = slice(at, at + step)
    scores = dot(rows_t, q_ref[:, cols], 1, 0)
    spot = lax.broadcasted_iota(jnp.int32, (count, step), 0) + base
    h = jnp.where(spot == ids_ref[1:2, cols], 1.0, 0.0)
    w = weight_ref[at // (edges // weight_ref.shape[0]), base:base + count, :]
    w = jnp.concatenate([w] * (step // LANES), axis=1)
    return ((w + h) * (0.5 * jnp.tanh(0.5 * scores) + 0.5) - h).astype(BF)


def complex_back(g, other):
    half = g.shape[0] // 2
    g_re, g_im, o_re, o_im = g[:half], g[half:], other[:half], other[half:]
    return jnp.concatenate([g_re * o_re + g_im * o_im, g_im * o_re - g_re * o_im], axis=0).astype(BF)


def products(rows_ref, q_ref, weight_ref, ids_ref, m_ref, base):
    rows_t = rows_ref[...].T
    step = step_of(q_ref.shape[1] // weight_ref.shape[0])
    for at in range(0, q_ref.shape[1], step):
        m_ref[:, at:at + step] = grad_chunk(rows_t, q_ref, weight_ref, ids_ref, base, at, step)


def near_body(blocks, *refs):
    block_refs, refs = refs[:blocks], refs[blocks:]
    q_ref, weight_ref, ids_ref, right_ref, qg_ref, rows_ref, m_ref = refs
    join_body(*block_refs, rows_ref)
    products(rows_ref, q_ref, weight_ref, ids_ref, m_ref, 0)
    right_ref[...] = dot(q_ref[...], m_ref[...], 1, 1)
    qg_ref[...] = dot(rows_ref[...], m_ref[...], 1, 0)


def middle_body(base, rows_ref, q_ref, weight_ref, ids_ref, qg_ref, right_ref, qg_out_ref, m_ref):
    products(rows_ref, q_ref, weight_ref, ids_ref, m_ref, base)
    right_ref[...] = dot(q_ref[...], m_ref[...], 1, 1).astype(BF)
    qg_out_ref[...] = qg_ref[...] + dot(rows_ref[...], m_ref[...], 1, 0)


def far_body(
    base, pieces, rows_ref, q_ref, weight_ref, ids_ref, qg_ref, s_ref, here_ref,
    m_ref, g_ref, mine_ref, theirs_ref, kinds_ref, tall_ref,
):
    rows_t = rows_ref[...].T
    width, edges = qg_ref.shape
    step = step_of(edges // weight_ref.shape[0])
    for at in range(0, edges, step):
        cols = slice(at, at + step)
        m = grad_chunk(rows_t, q_ref, weight_ref, ids_ref, base, at, step)
        m_ref[:, cols] = m
        g = qg_ref[:, cols] + dot(rows_ref[...], m, 1, 0)
        g_ref[:, cols] = g
        by_kind = complex_back(g, s_ref[:, cols].astype(F32))
        kinds = dot(by_kind, hot(ids_ref[2:3, cols], kinds_ref.shape[1]), 1, 1)
        if at == 0:
            kinds_ref[...] = kinds
        else:
            kinds_ref[...] += kinds
    parts = kinds_ref.shape[1] // LANES
    for j in range(parts):
        tall_ref[j * width:(j + 1) * width, :] = kinds_ref[:, j * LANES:(j + 1) * LANES]
    rest = tall_ref.shape[0] - parts * width
    if rest:
        tall_ref[parts * width:, :] = jnp.zeros((rest, LANES), F32)
    here = here_ref[0]
    size = tall_ref.shape[0] // pieces
    for k in range(pieces):
        start = pl.multiple_of((here ^ k) * size, 16)
        piece = tall_ref[pl.ds(start, size), :]
        at = slice(k // 2 * size, (k // 2 + 1) * size)
        if k % 2:
            theirs_ref[at, :] = piece.astype(BF)
        else:
            mine_ref[at, :] = piece


def rest_body(m_ref, q_ref, g_ref, o_ref, ids_ref, low_ref, right_ref, low_out_ref, near_ref, far_ref, left_ref):
    low_out_ref[...] = low_ref[...]
    right_ref[...] = dot(q_ref[...], m_ref[...], 1, 1).astype(BF)
    edges = q_ref.shape[1]
    step = step_of(edges)
    for at in range(0, edges, step):
        cols = slice(at, at + step)
        by_source = complex_back(g_ref[:, cols], o_ref[:, cols].astype(F32))
        left = dot(by_source, hot(ids_ref[0:1, cols], left_ref.shape[1]), 1, 1)
        if at == 0:
            left_ref[...] = left
        else:
            left_ref[...] += left
    cut = left_ref.shape[1] // 2
    near_ref[...] = left_ref[:, :cut]
    far_ref[...] = left_ref[:, cut:].astype(BF)


def relation_body(pieces, *refs):
    piece_refs, refs = refs[:pieces // 2], refs[pieces // 2:]
    sibling_ref, table_ref, state_ref, here_ref, new_ref, state_new_ref, tall_ref = refs
    here = here_ref[0]
    size = tall_ref.shape[0] // pieces
    for k in range(pieces):
        start = pl.multiple_of((here ^ k) * size, 16)
        piece = sibling_ref[k // 2 * size:(k // 2 + 1) * size, :] if k % 2 else piece_refs[k // 2][...]
        tall_ref[pl.ds(start, size), :] = piece.astype(F32)
    width, count = table_ref.shape
    for j in range(count // LANES):
        cols = slice(j * LANES, (j + 1) * LANES)
        g = tall_ref[j * width:(j + 1) * width, :]
        state = state_ref[:, cols] + jnp.sum(g * g, axis=0, keepdims=True) * (1.0 / width)
        state_new_ref[:, cols] = state
        new_ref[:, cols] = table_ref[:, cols] - g * (LEARN_RATE * lax.rsqrt(state))


def piece_body(mine_ref, got_ref, own_ref, *other_refs):
    size = own_ref.shape[0]
    for k, ref in enumerate((own_ref, *other_refs)):
        at = slice(k * size, (k + 1) * size)
        ref[...] = (mine_ref[at, :] + got_ref[at, :].astype(F32)).astype(ref.dtype)


def left_body(near_ref, got_ref, own_ref, *other_refs):
    for k, ref in enumerate((own_ref, *other_refs)):
        at = slice(k * LANES, (k + 1) * LANES)
        ref[...] = (near_ref[:, at] + got_ref[:, at].astype(F32)).astype(ref.dtype)


def stack_body(*refs):
    size = refs[0].shape[0]
    for k, ref in enumerate(refs[:-1]):
        refs[-1][k * size:(k + 1) * size, :] = ref[...]


def chunk_body(base, first, near_ref, got_ref, *block_refs):
    for k, ref in enumerate(block_refs):
        at = (first + k) * LANES
        total = near_ref[:, at:at + LANES] + got_ref[:, at - base:at - base + LANES].astype(F32)
        ref[...] = total.astype(ref.dtype)


def sum_body(*refs):
    total = refs[0][...].astype(F32)
    for ref in refs[1:-1]:
        total = total + ref[...].astype(F32)
    refs[-1][...] = total.astype(BF)


def update_body(parts, *refs):
    part_refs, (table_ref, state_ref, new_ref, state_new_ref) = refs[:parts], refs[parts:]
    g = part_refs[0][...].astype(F32)
    for ref in part_refs[1:]:
        g = g + ref[...].astype(F32)
    width = g.shape[0]
    state = state_ref[state_ref.shape[0] - 1:, :] + jnp.sum(g * g, axis=0, keepdims=True) * (1.0 / width)
    state_new_ref[...] = state
    new_ref[...] = table_ref[:width, :] - g * (LEARN_RATE * lax.rsqrt(state))


def build(mesh):
    n_left, n_right = mesh.shape["left"], mesh.shape["right"]
    for count in (n_left, n_right):
        assert count & (count - 1) == 0 and count > 3
    outer = n_left // 2
    far_right = n_right // 2

    def swap_left(value, by):
        return lax.ppermute(value, "left", [(i, i ^ by) for i in range(n_left)])

    def swap_right(value, by):
        return lax.ppermute(value, "right", [(i, i ^ by) for i in range(n_right)])

    def next_column(value, by):
        perm = []
        for i in range(n_left):
            for r in range(n_right):
                perm.append((i * n_right + r, (i ^ by) * n_right + (r + 1) % n_right))
        return lax.ppermute(value, ("left", "right"), perm)

    def per_device(
        left_table, left_state, right_table, right_state, relation_table, relation_state,
        source_ids, target_ids, relation_ids, negative_ids,
    ):
        rows = left_table.shape[0]
        width = left_table.shape[1]
        left_t, right_t, relation_t = left_table.T, right_table.T, relation_table.T
        nrel = relation_t.shape[1]
        here_l, here_r = lax.axis_index("left"), lax.axis_index("right")
        me = here_r.astype(jnp.int32).reshape(1)
        edges = source_ids.shape[-1]
        groups = negative_ids.shape[2]
        n_rows = n_left * rows
        half = outer * rows
        one_block = shape(width, rows, dtype=BF)
        table_bf = shape(width, edges, dtype=BF)

        def cast(value, after=()):
            parts = 5 if width % 80 == 0 else 1
            scratch = [pltpu.VMEM(value.shape, F32), pltpu.SemaphoreType.DMA((parts,))]
            return call(cast_body, one_block, scratch, after=after, place=pl.ANY)(value)

        right_bf = right_t.astype(BF)
        near = [next_column(right_bf, 2 * k) for k in range(outer)]
        some = outer // 2
        cut = some * rows
        chunk = shape(width, cut, dtype=BF)
        joined_low = call(join_body, chunk, flops=COST_JOIN_LOW)(*near[:some])
        other_low = call(join_body, chunk, flops=COST_MIDDLE)(swap_left(joined_low, 1))

        ids = [source_ids, target_ids, relation_ids, negative_ids]
        longest = max(i.shape[-1] for i in ids)
        ids = [i.reshape(-1, i.shape[-1]) for i in ids]
        ids = jnp.concatenate([jnp.pad(i, ((0, 0), (0, longest - i.shape[-1]))) for i in ids], axis=0)
        left_bf = cast(left_t)
        half_left = [left_bf] + [swap_right(left_bf, 2 * k) for k in range(1, far_right)]
        place = jnp.stack([here_r, here_l]).astype(jnp.int32)
        weight, relation_bf, ids = call(
            functools.partial(count_body, far_right, outer, rows, negative_ids.shape[-1]),
            (shape(groups, n_rows, LANES), shape(width, nrel, dtype=BF), shape(*ids.shape, dtype=jnp.int32)),
            here=place,
            after=(joined_low,),
        )(ids, relation_t)
        half_joined = call(join_body, shape(width, far_right * rows, dtype=BF), after=(weight,))(*half_left)
        joined = call(join_body, chunk, flops=COST_JOIN_HIGH, after=(half_joined,), ahead=(near[0],))(*near[some:])
        other_high = swap_left(joined, 1)
        sibling_left = swap_right(half_joined, 1)
        moved = next_column(call(pack_body, shape(width + 8, rows), after=(joined,))(right_t, right_state[None, :]), 0)

        s, o, q = call(functools.partial(query_body, far_right), (table_bf, table_bf, table_bf), flops=COST_QUERY)(
            *half_left, sibling_left, relation_bf, ids
        )
        right_near, qg = call(
            functools.partial(near_body, outer),
            (shape(width, half), shape(width, edges)),
            [pltpu.VMEM((width, half), BF), pltpu.VMEM((half, edges), BF)],
        )(*near, q, weight, ids)
        right_low, qg = call(
            functools.partial(middle_body, half), (chunk, shape(width, edges)), [pltpu.VMEM((cut, edges), BF)],
        )(other_low, q, weight, ids, qg)
        tall = nrel // LANES * width
        size = -(-tall // (n_right * 16)) * 16
        piece = shape(size, LANES, dtype=BF)
        all_pieces = pltpu.VMEM((size * n_right, LANES), F32)
        m, g, mine, theirs = call(
            functools.partial(far_body, half + cut, n_right),
            (shape(cut, edges, dtype=BF), shape(width, edges), shape(far_right * size, LANES),
             shape(far_right * size, LANES, dtype=BF)),
            [pltpu.VMEM((width, nrel), F32), all_pieces],
            me,
        )(other_high, q, weight, ids, qg, s)
        left_rows = n_right * rows
        left_half = left_rows // 2
        right_high, right_low, left_near, left_far = call(
            rest_body,
            (chunk, chunk, shape(width, left_half), shape(width, left_half, dtype=BF)),
            [pltpu.VMEM((width, left_rows), F32)],
            after=(moved,),
        )(m, q, g, o, ids, right_low)

        mine, *rest = call(
            piece_body, (shape(size, LANES),) + (piece,) * (far_right - 1), flops=COST_SUM
        )(mine, swap_right(theirs, 1))
        got = [swap_right(p, 2 * (k + 1)) for k, p in enumerate(rest)]
        mine = call(sum_body, piece, flops=COST_SUM)(mine, *got)
        bit = n_left // 2
        while bit > 1:
            mine = call(sum_body, piece, flops=COST_SUM)(mine, swap_left(mine, bit))
            bit //= 2
        over_z = mine
        mine = call(sum_body, piece, flops=COST_SUM)(mine, swap_left(mine, 1))
        pieces = [mine] + [swap_right(mine, 2 * k) for k in range(1, far_right)]
        sibling = swap_right(call(stack_body, shape(far_right * size, LANES, dtype=BF))(*pieces), 1)

        left_own, *blocks = call(left_body, (shape(width, rows),) + (one_block,) * (far_right - 1))(
            left_near, swap_right(left_far, 1)
        )
        left_got = [swap_right(block, 2 * (k + 1)) for k, block in enumerate(blocks)]

        got_low = swap_left(right_low, 1)
        got_high = swap_left(right_high, 1)
        def chunk_of(first, outs, got, flops, after=()):
            base = cut if first >= some else 0
            body = functools.partial(chunk_body, base, first)
            return call(body, outs, flops=flops, after=after)(right_near, got)

        high = chunk_of(some, (one_block,) * (some - 1), got_high, COST_HIGH)
        last = chunk_of(outer - 1, (one_block,), got_high, COST_HIGH, (over_z,))
        high = [swap_left(block, 2 * (some + k)) for k, block in enumerate([*high, *last])]
        outs = (shape(width, rows),) + (one_block,) * (some - 1)
        low = chunk_of(0, outs, got_low, COST_LOW, left_got)
        right_got = [low[0], *high] + [swap_left(low[k], 2 * k) for k in range(1, some)]

        def update(got, table, state, flops=0):
            outs = (shape(width, rows), shape(1, rows))
            return call(functools.partial(update_body, len(got)), outs, flops=flops)(*got, table, state)

        left_new, left_state_new = update([left_own, *left_got], left_t, left_state[None, :])
        right_new, right_state_new = update(right_got, moved, moved, COST_UPDATE)
        relation_new, relation_state_new = call(
            functools.partial(relation_body, n_right), (shape(width, nrel), shape(1, nrel)), [all_pieces], me
        )(*pieces, sibling, relation_t, relation_state[None, :])
        return (
            left_new.T, left_state_new.reshape(-1), right_new.T, right_state_new.reshape(-1),
            relation_new.T, relation_state_new.reshape(-1),
        )

    return per_device


def solution(mesh):
    rows = P(("left", "right"), None)
    vector = P(("left", "right"))
    ids = P("left", "right", None)
    return jax.shard_map(
        build(mesh),
        mesh=mesh,
        in_specs=(rows, vector, rows, vector, P(), P(), ids, ids, ids, P("left", "right", None, None)),
        out_specs=(rows, vector, rows, vector, P(), P()),
        check_vma=False,
    )
```

```python
import functools

import jax
import jax.numpy as jnp
from jax import lax
from jax.experimental import pallas as pl
from jax.experimental.pallas import tpu as pltpu
from jax.sharding import PartitionSpec as P

LEARN_RATE = 0.1
NEG_WEIGHT = 0.03125
BF = jnp.bfloat16
F32 = jnp.float32
VMEM_LIMIT = 32 * 1024 * 1024
LANES = 128
COST_JOIN_LOW = 6e9
COST_JOIN_HIGH = 6e9
COST_UPDATE = 12e9
COST_HIGH = 12e9
COST_LOW = 12e9
COST_SUM = 1e9
COST_MIDDLE = 6e9
COST_QUERY = 6e9


def dot(a, b, a_dim, b_dim):
    return lax.dot_general(a, b, (((a_dim,), (b_dim,)), ((), ())), preferred_element_type=F32)


def hot(ids, count):
    spot = lax.broadcasted_iota(jnp.int32, (count, ids.shape[1]), 0)
    return jnp.where(spot == ids, 1.0, 0.0).astype(BF)


def step_of(size, most=512):
    return most if size % most == 0 else size


def call(body, out_shape, scratch=(), here=None, after=(), flops=0, place=pltpu.VMEM, ahead=()):
    def run(*args):
        specs = [pl.BlockSpec(memory_space=place)] * len(args)
        if here is not None:
            specs.append(pl.BlockSpec(memory_space=pltpu.SMEM))
            args = (*args, here)
        inner = body
        if after or ahead:
            first = len(ahead)
            last = first + len(args)

            def inner(*refs):
                body(*refs[first:last], *refs[last + len(after):])

            unread = pl.BlockSpec(memory_space=pl.ANY)
            specs = [unread] * len(ahead) + specs + [unread] * len(after)
            args = (*ahead, *args, *after)
        return pl.pallas_call(
            inner,
            out_shape=out_shape,
            in_specs=specs,
            scratch_shapes=list(scratch),
            compiler_params=pltpu.CompilerParams(vmem_limit_bytes=VMEM_LIMIT),
            cost_estimate=pl.CostEstimate(flops=int(flops), bytes_accessed=0, transcendentals=0),
        )(*args)

    return run


def shape(*dims, dtype=F32):
    return jax.ShapeDtypeStruct(dims, dtype)


def cast_body(in_ref, out_ref, held_ref, sems):
    rows = held_ref.shape[0] // sems.shape[0]
    copies = []
    for k in range(sems.shape[0]):
        at = slice(k * rows, (k + 1) * rows)
        copies.append(pltpu.make_async_copy(in_ref.at[at], held_ref.at[at], sems.at[k]))
        copies[-1].start()
    for k, copy in enumerate(copies):
        at = slice(k * rows, (k + 1) * rows)
        copy.wait()
        out_ref[at, :] = held_ref[at, :].astype(BF)


def count_body(far_right, outer, rows, slots, ids_ref, relation_ref, place_ref, out_ref, relation_bf_ref, local_ref):
    def local(ids, here, half):
        block = (ids // rows) ^ here
        return (block % 2 * half + block // 2) * rows + ids % rows

    ids = ids_ref[...]
    local_ref[...] = ids
    local_ref[0:1, :] = local(ids[0:1], place_ref[0], far_right)
    local_ref[1:2, :] = local(ids[1:2], place_ref[1], outer)
    for g in range(out_ref.shape[0]):
        negative = local(ids[3 + g:4 + g, :slots], place_ref[1], outer)
        for at in range(0, out_ref.shape[1], LANES):
            spot = lax.broadcasted_iota(jnp.int32, (LANES, slots), 0) + at
            total = jnp.sum(jnp.where(spot == negative, NEG_WEIGHT, 0.0), axis=1, keepdims=True)
            out_ref[g, at:at + LANES, :] = jnp.broadcast_to(total, (LANES, LANES))
    relation_bf_ref[...] = relation_ref[...].astype(BF)


def pack_body(table_ref, state_ref, pack_ref):
    width = table_ref.shape[0]
    pack_ref[:width, :] = table_ref[...]
    pack_ref[width:, :] = jnp.broadcast_to(state_ref[...], (pack_ref.shape[0] - width, LANES))


def join_body(*refs):
    out_ref = refs[-1]
    at = 0
    for ref in refs[:-1]:
        out_ref[:, at:at + ref.shape[1]] = ref[...]
        at += ref.shape[1]


def query_body(blocks, *refs):
    near_refs, refs = refs[:blocks], refs[blocks:]
    sibling_ref, relation_ref, ids_ref, s_ref, o_ref, q_ref = refs
    relation = relation_ref[...]
    half = s_ref.shape[0] // 2
    edges = s_ref.shape[1]
    step = step_of(edges)
    near = jnp.concatenate([ref[...] for ref in near_refs], axis=1)
    half_rows = near.shape[1]
    for at in range(0, edges, step):
        cols = slice(at, at + step)
        pick = hot(ids_ref[0:1, cols], 2 * half_rows)
        s = dot(near, pick[:half_rows], 1, 0) + dot(sibling_ref[...], pick[half_rows:], 1, 0)
        o = dot(relation, hot(ids_ref[2:3, cols], relation.shape[1]), 1, 0)
        s_ref[:, cols] = s.astype(BF)
        o_ref[:, cols] = o.astype(BF)
        s_re, s_im, o_re, o_im = s[:half], s[half:], o[:half], o[half:]
        q = jnp.concatenate([s_re * o_re - s_im * o_im, s_re * o_im + s_im * o_re], axis=0)
        q_ref[:, cols] = q.astype(BF)


def grad_chunk(rows_t, q_ref, weight_ref, ids_ref, base, at, step):
    count = rows_t.shape[0]
    edges = q_ref.shape[1]
    cols = slice(at, at + step)
    scores = dot(rows_t, q_ref[:, cols], 1, 0)
    spot = lax.broadcasted_iota(jnp.int32, (count, step), 0) + base
    h = jnp.where(spot == ids_ref[1:2, cols], 1.0, 0.0)
    w = weight_ref[at // (edges // weight_ref.shape[0]), base:base + count, :]
    w = jnp.concatenate([w] * (step // LANES), axis=1)
    return ((w + h) * (0.5 * jnp.tanh(0.5 * scores) + 0.5) - h).astype(BF)


def complex_back(g, other):
    half = g.shape[0] // 2
    g_re, g_im, o_re, o_im = g[:half], g[half:], other[:half], other[half:]
    return jnp.concatenate([g_re * o_re + g_im * o_im, g_im * o_re - g_re * o_im], axis=0).astype(BF)


def products(rows_ref, q_ref, weight_ref, ids_ref, m_ref, base):
    rows_t = rows_ref[...].T
    step = step_of(q_ref.shape[1] // weight_ref.shape[0])
    for at in range(0, q_ref.shape[1], step):
        m_ref[:, at:at + step] = grad_chunk(rows_t, q_ref, weight_ref, ids_ref, base, at, step)


def near_body(blocks, *refs):
    block_refs, refs = refs[:blocks], refs[blocks:]
    q_ref, weight_ref, ids_ref, right_ref, qg_ref, rows_ref, m_ref = refs
    join_body(*block_refs, rows_ref)
    products(rows_ref, q_ref, weight_ref, ids_ref, m_ref, 0)
    right_ref[...] = dot(q_ref[...], m_ref[...], 1, 1)
    qg_ref[...] = dot(rows_ref[...], m_ref[...], 1, 0)


def middle_body(base, rows_ref, q_ref, weight_ref, ids_ref, qg_ref, right_ref, qg_out_ref, m_ref):
    products(rows_ref, q_ref, weight_ref, ids_ref, m_ref, base)
    right_ref[...] = dot(q_ref[...], m_ref[...], 1, 1).astype(BF)
    qg_out_ref[...] = qg_ref[...] + dot(rows_ref[...], m_ref[...], 1, 0)


def far_body(
    base, pieces, rows_ref, q_ref, weight_ref, ids_ref, qg_ref, s_ref, here_ref,
    m_ref, g_ref, mine_ref, theirs_ref, kinds_ref, tall_ref,
):
    rows_t = rows_ref[...].T
    width, edges = qg_ref.shape
    step = step_of(edges // weight_ref.shape[0])
    for at in range(0, edges, step):
        cols = slice(at, at + step)
        m = grad_chunk(rows_t, q_ref, weight_ref, ids_ref, base, at, step)
        m_ref[:, cols] = m
        g = qg_ref[:, cols] + dot(rows_ref[...], m, 1, 0)
        g_ref[:, cols] = g
        by_kind = complex_back(g, s_ref[:, cols].astype(F32))
        kinds = dot(by_kind, hot(ids_ref[2:3, cols], kinds_ref.shape[1]), 1, 1)
        if at == 0:
            kinds_ref[...] = kinds
        else:
            kinds_ref[...] += kinds
    parts = kinds_ref.shape[1] // LANES
    for j in range(parts):
        tall_ref[j * width:(j + 1) * width, :] = kinds_ref[:, j * LANES:(j + 1) * LANES]
    rest = tall_ref.shape[0] - parts * width
    if rest:
        tall_ref[parts * width:, :] = jnp.zeros((rest, LANES), F32)
    here = here_ref[0]
    size = tall_ref.shape[0] // pieces
    for k in range(pieces):
        start = pl.multiple_of((here ^ k) * size, 16)
        piece = tall_ref[pl.ds(start, size), :]
        at = slice(k // 2 * size, (k // 2 + 1) * size)
        if k % 2:
            theirs_ref[at, :] = piece.astype(BF)
        else:
            mine_ref[at, :] = piece


def rest_body(m_ref, q_ref, g_ref, o_ref, ids_ref, low_ref, right_ref, low_out_ref, near_ref, far_ref, left_ref):
    low_out_ref[...] = low_ref[...]
    right_ref[...] = dot(q_ref[...], m_ref[...], 1, 1).astype(BF)
    edges = q_ref.shape[1]
    step = step_of(edges)
    for at in range(0, edges, step):
        cols = slice(at, at + step)
        by_source = complex_back(g_ref[:, cols], o_ref[:, cols].astype(F32))
        left = dot(by_source, hot(ids_ref[0:1, cols], left_ref.shape[1]), 1, 1)
        if at == 0:
            left_ref[...] = left
        else:
            left_ref[...] += left
    cut = left_ref.shape[1] // 2
    near_ref[...] = left_ref[:, :cut]
    far_ref[...] = left_ref[:, cut:].astype(BF)


def relation_body(pieces, *refs):
    piece_refs, refs = refs[:pieces // 2], refs[pieces // 2:]
    sibling_ref, table_ref, state_ref, here_ref, new_ref, state_new_ref, tall_ref = refs
    here = here_ref[0]
    size = tall_ref.shape[0] // pieces
    for k in range(pieces):
        start = pl.multiple_of((here ^ k) * size, 16)
        piece = sibling_ref[k // 2 * size:(k // 2 + 1) * size, :] if k % 2 else piece_refs[k // 2][...]
        tall_ref[pl.ds(start, size), :] = piece.astype(F32)
    width, count = table_ref.shape
    for j in range(count // LANES):
        cols = slice(j * LANES, (j + 1) * LANES)
        g = tall_ref[j * width:(j + 1) * width, :]
        state = state_ref[:, cols] + jnp.sum(g * g, axis=0, keepdims=True) * (1.0 / width)
        state_new_ref[:, cols] = state
        new_ref[:, cols] = table_ref[:, cols] - g * (LEARN_RATE * lax.rsqrt(state))


def piece_body(mine_ref, got_ref, own_ref, *other_refs):
    size = own_ref.shape[0]
    for k, ref in enumerate((own_ref, *other_refs)):
        at = slice(k * size, (k + 1) * size)
        ref[...] = (mine_ref[at, :] + got_ref[at, :].astype(F32)).astype(ref.dtype)


def left_body(near_ref, got_ref, own_ref, *other_refs):
    for k, ref in enumerate((own_ref, *other_refs)):
        at = slice(k * LANES, (k + 1) * LANES)
        ref[...] = (near_ref[:, at] + got_ref[:, at].astype(F32)).astype(ref.dtype)


def stack_body(*refs):
    size = refs[0].shape[0]
    for k, ref in enumerate(refs[:-1]):
        refs[-1][k * size:(k + 1) * size, :] = ref[...]


def chunk_body(base, first, near_ref, got_ref, *block_refs):
    for k, ref in enumerate(block_refs):
        at = (first + k) * LANES
        total = near_ref[:, at:at + LANES] + got_ref[:, at - base:at - base + LANES].astype(F32)
        ref[...] = total.astype(ref.dtype)


def sum_body(*refs):
    total = refs[0][...].astype(F32)
    for ref in refs[1:-1]:
        total = total + ref[...].astype(F32)
    refs[-1][...] = total.astype(BF)


def update_body(parts, *refs):
    part_refs, (table_ref, state_ref, new_ref, state_new_ref) = refs[:parts], refs[parts:]
    g = part_refs[0][...].astype(F32)
    for ref in part_refs[1:]:
        g = g + ref[...].astype(F32)
    width = g.shape[0]
    state = state_ref[state_ref.shape[0] - 1:, :] + jnp.sum(g * g, axis=0, keepdims=True) * (1.0 / width)
    state_new_ref[...] = state
    new_ref[...] = table_ref[:width, :] - g * (LEARN_RATE * lax.rsqrt(state))


def build(mesh):
    n_left, n_right = mesh.shape["left"], mesh.shape["right"]
    for count in (n_left, n_right):
        assert count & (count - 1) == 0 and count > 3
    outer = n_left // 2
    far_right = n_right // 2

    def swap_left(value, by):
        return lax.ppermute(value, "left", [(i, i ^ by) for i in range(n_left)])

    def swap_right(value, by):
        return lax.ppermute(value, "right", [(i, i ^ by) for i in range(n_right)])

    def next_column(value, by):
        perm = []
        for i in range(n_left):
            for r in range(n_right):
                perm.append((i * n_right + r, (i ^ by) * n_right + (r + 1) % n_right))
        return lax.ppermute(value, ("left", "right"), perm)

    def per_device(
        left_table, left_state, right_table, right_state, relation_table, relation_state,
        source_ids, target_ids, relation_ids, negative_ids,
    ):
        rows = left_table.shape[0]
        width = left_table.shape[1]
        left_t, right_t, relation_t = left_table.T, right_table.T, relation_table.T
        nrel = relation_t.shape[1]
        here_l, here_r = lax.axis_index("left"), lax.axis_index("right")
        me = here_r.astype(jnp.int32).reshape(1)
        edges = source_ids.shape[-1]
        groups = negative_ids.shape[2]
        n_rows = n_left * rows
        half = outer * rows
        one_block = shape(width, rows, dtype=BF)
        table_bf = shape(width, edges, dtype=BF)

        def cast(value, after=()):
            parts = 5 if width % 80 == 0 else 1
            scratch = [pltpu.VMEM(value.shape, F32), pltpu.SemaphoreType.DMA((parts,))]
            return call(cast_body, one_block, scratch, after=after, place=pl.ANY)(value)

        right_bf = right_t.astype(BF)
        near = [next_column(right_bf, 2 * k) for k in range(outer)]
        some = outer // 2
        cut = some * rows
        chunk = shape(width, cut, dtype=BF)
        joined_low = call(join_body, chunk, flops=COST_JOIN_LOW)(*near[:some])
        other_low = call(join_body, chunk, flops=COST_MIDDLE)(swap_left(joined_low, 1))

        ids = [source_ids, target_ids, relation_ids, negative_ids]
        longest = max(i.shape[-1] for i in ids)
        ids = [i.reshape(-1, i.shape[-1]) for i in ids]
        ids = jnp.concatenate([jnp.pad(i, ((0, 0), (0, longest - i.shape[-1]))) for i in ids], axis=0)
        left_bf = cast(left_t)
        half_left = [left_bf] + [swap_right(left_bf, 2 * k) for k in range(1, far_right)]
        place = jnp.stack([here_r, here_l]).astype(jnp.int32)
        weight, relation_bf, ids = call(
            functools.partial(count_body, far_right, outer, rows, negative_ids.shape[-1]),
            (shape(groups, n_rows, LANES), shape(width, nrel, dtype=BF), shape(*ids.shape, dtype=jnp.int32)),
            here=place,
            after=(joined_low,),
        )(ids, relation_t)
        half_joined = call(join_body, shape(width, far_right * rows, dtype=BF), after=(weight,))(*half_left)
        joined = call(join_body, chunk, flops=COST_JOIN_HIGH, after=(half_joined,), ahead=(near[0],))(*near[some:])
        other_high = swap_left(joined, 1)
        sibling_left = swap_right(half_joined, 1)
        moved = next_column(call(pack_body, shape(width + 8, rows), after=(joined,))(right_t, right_state[None, :]), 0)

        s, o, q = call(functools.partial(query_body, far_right), (table_bf, table_bf, table_bf), flops=COST_QUERY)(
            *half_left, sibling_left, relation_bf, ids
        )
        right_near, qg = call(
            functools.partial(near_body, outer),
            (shape(width, half), shape(width, edges)),
            [pltpu.VMEM((width, half), BF), pltpu.VMEM((half, edges), BF)],
        )(*near, q, weight, ids)
        right_low, qg = call(
            functools.partial(middle_body, half), (chunk, shape(width, edges)), [pltpu.VMEM((cut, edges), BF)],
        )(other_low, q, weight, ids, qg)
        tall = nrel // LANES * width
        size = -(-tall // (n_right * 16)) * 16
        piece = shape(size, LANES, dtype=BF)
        all_pieces = pltpu.VMEM((size * n_right, LANES), F32)
        m, g, mine, theirs = call(
            functools.partial(far_body, half + cut, n_right),
            (shape(cut, edges, dtype=BF), shape(width, edges), shape(far_right * size, LANES),
             shape(far_right * size, LANES, dtype=BF)),
            [pltpu.VMEM((width, nrel), F32), all_pieces],
            me,
            after=(moved,),
        )(other_high, q, weight, ids, qg, s)
        left_rows = n_right * rows
        left_half = left_rows // 2
        right_high, right_low, left_near, left_far = call(
            rest_body,
            (chunk, chunk, shape(width, left_half), shape(width, left_half, dtype=BF)),
            [pltpu.VMEM((width, left_rows), F32)],
        )(m, q, g, o, ids, right_low)

        mine, *rest = call(
            piece_body, (shape(size, LANES),) + (piece,) * (far_right - 1), flops=COST_SUM
        )(mine, swap_right(theirs, 1))
        got = [swap_right(p, 2 * (k + 1)) for k, p in enumerate(rest)]
        mine = call(sum_body, piece, flops=COST_SUM)(mine, *got)
        bit = n_left // 2
        while bit > 1:
            mine = call(sum_body, piece, flops=COST_SUM)(mine, swap_left(mine, bit))
            bit //= 2
        over_z = mine
        mine = call(sum_body, piece, flops=COST_SUM)(mine, swap_left(mine, 1))
        pieces = [mine] + [swap_right(mine, 2 * k) for k in range(1, far_right)]
        sibling = swap_right(call(stack_body, shape(far_right * size, LANES, dtype=BF))(*pieces), 1)

        left_own, *blocks = call(left_body, (shape(width, rows),) + (one_block,) * (far_right - 1))(
            left_near, swap_right(left_far, 1)
        )
        left_got = [swap_right(block, 2 * (k + 1)) for k, block in enumerate(blocks)]

        got_low = swap_left(right_low, 1)
        got_high = swap_left(right_high, 1)
        def chunk_of(first, outs, got, flops, after=()):
            base = cut if first >= some else 0
            body = functools.partial(chunk_body, base, first)
            return call(body, outs, flops=flops, after=after)(right_near, got)

        high = chunk_of(some, (one_block,) * (some - 1), got_high, COST_HIGH)
        last = chunk_of(outer - 1, (one_block,), got_high, COST_HIGH, (over_z,))
        high = [swap_left(block, 2 * (some + k)) for k, block in enumerate([*high, *last])]
        outs = (shape(width, rows),) + (one_block,) * (some - 1)
        low = chunk_of(0, outs, got_low, COST_LOW, left_got)
        right_got = [low[0], *high] + [swap_left(low[k], 2 * k) for k in range(1, some)]

        def update(got, table, state, flops=0):
            outs = (shape(width, rows), shape(1, rows))
            return call(functools.partial(update_body, len(got)), outs, flops=flops)(*got, table, state)

        left_new, left_state_new = update([left_own, *left_got], left_t, left_state[None, :])
        right_new, right_state_new = update(right_got, moved, moved, COST_UPDATE)
        relation_new, relation_state_new = call(
            functools.partial(relation_body, n_right), (shape(width, nrel), shape(1, nrel)), [all_pieces], me
        )(*pieces, sibling, relation_t, relation_state[None, :])
        return (
            left_new.T, left_state_new.reshape(-1), right_new.T, right_state_new.reshape(-1),
            relation_new.T, relation_state_new.reshape(-1),
        )

    return per_device


def solution(mesh):
    rows = P(("left", "right"), None)
    vector = P(("left", "right"))
    ids = P("left", "right", None)
    return jax.shard_map(
        build(mesh),
        mesh=mesh,
        in_specs=(rows, vector, rows, vector, P(), P(), ids, ids, ids, P("left", "right", None, None)),
        out_specs=(rows, vector, rows, vector, P(), P()),
        check_vma=False,
    )
```

```python
import functools

import jax
import jax.numpy as jnp
from jax import lax
from jax.experimental import pallas as pl
from jax.experimental.pallas import tpu as pltpu
from jax.sharding import PartitionSpec as P

LEARN_RATE = 0.1
NEG_WEIGHT = 0.03125
BF = jnp.bfloat16
F32 = jnp.float32
VMEM_LIMIT = 32 * 1024 * 1024
LANES = 128
COST_JOIN_LOW = 6e9
COST_JOIN_HIGH = 6e9
COST_UPDATE = 12e9
COST_HIGH = 12e9
COST_LOW = 12e9
COST_SUM = 1e9
COST_MIDDLE = 6e9
COST_QUERY = 6e9


def dot(a, b, a_dim, b_dim):
    return lax.dot_general(a, b, (((a_dim,), (b_dim,)), ((), ())), preferred_element_type=F32)


def hot(ids, count):
    spot = lax.broadcasted_iota(jnp.int32, (count, ids.shape[1]), 0)
    return jnp.where(spot == ids, 1.0, 0.0).astype(BF)


def step_of(size, most=512):
    return most if size % most == 0 else size


def call(body, out_shape, scratch=(), here=None, after=(), flops=0, place=pltpu.VMEM, ahead=()):
    def run(*args):
        specs = [pl.BlockSpec(memory_space=place)] * len(args)
        if here is not None:
            specs.append(pl.BlockSpec(memory_space=pltpu.SMEM))
            args = (*args, here)
        inner = body
        if after or ahead:
            first = len(ahead)
            last = first + len(args)

            def inner(*refs):
                body(*refs[first:last], *refs[last + len(after):])

            unread = pl.BlockSpec(memory_space=pl.ANY)
            specs = [unread] * len(ahead) + specs + [unread] * len(after)
            args = (*ahead, *args, *after)
        return pl.pallas_call(
            inner,
            out_shape=out_shape,
            in_specs=specs,
            scratch_shapes=list(scratch),
            compiler_params=pltpu.CompilerParams(vmem_limit_bytes=VMEM_LIMIT),
            cost_estimate=pl.CostEstimate(flops=int(flops), bytes_accessed=0, transcendentals=0),
        )(*args)

    return run


def shape(*dims, dtype=F32):
    return jax.ShapeDtypeStruct(dims, dtype)


def cast_body(in_ref, out_ref, held_ref, sems):
    rows = held_ref.shape[0] // sems.shape[0]
    copies = []
    for k in range(sems.shape[0]):
        at = slice(k * rows, (k + 1) * rows)
        copies.append(pltpu.make_async_copy(in_ref.at[at], held_ref.at[at], sems.at[k]))
        copies[-1].start()
    for k, copy in enumerate(copies):
        at = slice(k * rows, (k + 1) * rows)
        copy.wait()
        out_ref[at, :] = held_ref[at, :].astype(BF)


def count_body(far_right, outer, rows, slots, ids_ref, relation_ref, place_ref, out_ref, relation_bf_ref, local_ref):
    def local(ids, here, half):
        block = (ids // rows) ^ here
        return (block % 2 * half + block // 2) * rows + ids % rows

    ids = ids_ref[...]
    local_ref[...] = ids
    local_ref[0:1, :] = local(ids[0:1], place_ref[0], far_right)
    local_ref[1:2, :] = local(ids[1:2], place_ref[1], outer)
    for g in range(out_ref.shape[0]):
        negative = local(ids[3 + g:4 + g, :slots], place_ref[1], outer)
        for at in range(0, out_ref.shape[1], LANES):
            spot = lax.broadcasted_iota(jnp.int32, (LANES, slots), 0) + at
            total = jnp.sum(jnp.where(spot == negative, NEG_WEIGHT, 0.0), axis=1, keepdims=True)
            out_ref[g, at:at + LANES, :] = jnp.broadcast_to(total, (LANES, LANES))
    relation_bf_ref[...] = relation_ref[...].astype(BF)


def pack_body(table_ref, state_ref, pack_ref):
    width = table_ref.shape[0]
    pack_ref[:width, :] = table_ref[...]
    pack_ref[width:, :] = jnp.broadcast_to(state_ref[...], (pack_ref.shape[0] - width, LANES))


def join_body(*refs):
    out_ref = refs[-1]
    at = 0
    for ref in refs[:-1]:
        out_ref[:, at:at + ref.shape[1]] = ref[...]
        at += ref.shape[1]


def query_body(blocks, *refs):
    near_refs, refs = refs[:blocks], refs[blocks:]
    sibling_ref, relation_ref, ids_ref, s_ref, o_ref, q_ref = refs
    relation = relation_ref[...]
    half = s_ref.shape[0] // 2
    edges = s_ref.shape[1]
    step = step_of(edges)
    near = jnp.concatenate([ref[...] for ref in near_refs], axis=1)
    half_rows = near.shape[1]
    for at in range(0, edges, step):
        cols = slice(at, at + step)
        pick = hot(ids_ref[0:1, cols], 2 * half_rows)
        s = dot(near, pick[:half_rows], 1, 0) + dot(sibling_ref[...], pick[half_rows:], 1, 0)
        o = dot(relation, hot(ids_ref[2:3, cols], relation.shape[1]), 1, 0)
        s_ref[:, cols] = s.astype(BF)
        o_ref[:, cols] = o.astype(BF)
        s_re, s_im, o_re, o_im = s[:half], s[half:], o[:half], o[half:]
        q = jnp.concatenate([s_re * o_re - s_im * o_im, s_re * o_im + s_im * o_re], axis=0)
        q_ref[:, cols] = q.astype(BF)


def grad_chunk(rows_t, q_ref, weight_ref, ids_ref, base, at, step):
    count = rows_t.shape[0]
    edges = q_ref.shape[1]
    cols = slice(at, at + step)
    scores = dot(rows_t, q_ref[:, cols], 1, 0)
    spot = lax.broadcasted_iota(jnp.int32, (count, step), 0) + base
    h = jnp.where(spot == ids_ref[1:2, cols], 1.0, 0.0)
    w = weight_ref[at // (edges // weight_ref.shape[0]), base:base + count, :]
    w = jnp.concatenate([w] * (step // LANES), axis=1)
    return ((w + h) * (0.5 * jnp.tanh(0.5 * scores) + 0.5) - h).astype(BF)


def complex_back(g, other):
    half = g.shape[0] // 2
    g_re, g_im, o_re, o_im = g[:half], g[half:], other[:half], other[half:]
    return jnp.concatenate([g_re * o_re + g_im * o_im, g_im * o_re - g_re * o_im], axis=0).astype(BF)


def products(rows_ref, q_ref, weight_ref, ids_ref, m_ref, base):
    rows_t = rows_ref[...].T
    step = step_of(q_ref.shape[1] // weight_ref.shape[0])
    for at in range(0, q_ref.shape[1], step):
        m_ref[:, at:at + step] = grad_chunk(rows_t, q_ref, weight_ref, ids_ref, base, at, step)


def near_body(blocks, *refs):
    block_refs, refs = refs[:blocks], refs[blocks:]
    q_ref, weight_ref, ids_ref, right_ref, qg_ref, rows_ref, m_ref = refs
    join_body(*block_refs, rows_ref)
    products(rows_ref, q_ref, weight_ref, ids_ref, m_ref, 0)
    right_ref[...] = dot(q_ref[...], m_ref[...], 1, 1)
    qg_ref[...] = dot(rows_ref[...], m_ref[...], 1, 0)


def middle_body(base, rows_ref, q_ref, weight_ref, ids_ref, qg_ref, right_ref, qg_out_ref, m_ref):
    products(rows_ref, q_ref, weight_ref, ids_ref, m_ref, base)
    right_ref[...] = dot(q_ref[...], m_ref[...], 1, 1).astype(BF)
    qg_out_ref[...] = qg_ref[...] + dot(rows_ref[...], m_ref[...], 1, 0)


def far_body(
    base, pieces, rows_ref, q_ref, weight_ref, ids_ref, qg_ref, s_ref, here_ref,
    m_ref, g_ref, mine_ref, theirs_ref, kinds_ref, tall_ref,
):
    rows_t = rows_ref[...].T
    width, edges = qg_ref.shape
    step = step_of(edges // weight_ref.shape[0])
    for at in range(0, edges, step):
        cols = slice(at, at + step)
        m = grad_chunk(rows_t, q_ref, weight_ref, ids_ref, base, at, step)
        m_ref[:, cols] = m
        g = qg_ref[:, cols] + dot(rows_ref[...], m, 1, 0)
        g_ref[:, cols] = g
        by_kind = complex_back(g, s_ref[:, cols].astype(F32))
        kinds = dot(by_kind, hot(ids_ref[2:3, cols], kinds_ref.shape[1]), 1, 1)
        if at == 0:
            kinds_ref[...] = kinds
        else:
            kinds_ref[...] += kinds
    parts = kinds_ref.shape[1] // LANES
    for j in range(parts):
        tall_ref[j * width:(j + 1) * width, :] = kinds_ref[:, j * LANES:(j + 1) * LANES]
    rest = tall_ref.shape[0] - parts * width
    if rest:
        tall_ref[parts * width:, :] = jnp.zeros((rest, LANES), F32)
    here = here_ref[0]
    size = tall_ref.shape[0] // pieces
    for k in range(pieces):
        start = pl.multiple_of((here ^ k) * size, 16)
        piece = tall_ref[pl.ds(start, size), :]
        at = slice(k // 2 * size, (k // 2 + 1) * size)
        if k % 2:
            theirs_ref[at, :] = piece.astype(BF)
        else:
            mine_ref[at, :] = piece


def rest_body(m_ref, q_ref, g_ref, o_ref, ids_ref, low_ref, right_ref, low_out_ref, near_ref, far_ref, left_ref):
    low_out_ref[...] = low_ref[...]
    right_ref[...] = dot(q_ref[...], m_ref[...], 1, 1).astype(BF)
    edges = q_ref.shape[1]
    step = step_of(edges)
    for at in range(0, edges, step):
        cols = slice(at, at + step)
        by_source = complex_back(g_ref[:, cols], o_ref[:, cols].astype(F32))
        left = dot(by_source, hot(ids_ref[0:1, cols], left_ref.shape[1]), 1, 1)
        if at == 0:
            left_ref[...] = left
        else:
            left_ref[...] += left
    cut = left_ref.shape[1] // 2
    near_ref[...] = left_ref[:, :cut]
    far_ref[...] = left_ref[:, cut:].astype(BF)


def relation_body(pieces, *refs):
    piece_refs, refs = refs[:pieces // 2], refs[pieces // 2:]
    sibling_ref, table_ref, state_ref, here_ref, new_ref, state_new_ref, tall_ref = refs
    here = here_ref[0]
    size = tall_ref.shape[0] // pieces
    for k in range(pieces):
        start = pl.multiple_of((here ^ k) * size, 16)
        piece = sibling_ref[k // 2 * size:(k // 2 + 1) * size, :] if k % 2 else piece_refs[k // 2][...]
        tall_ref[pl.ds(start, size), :] = piece.astype(F32)
    width, count = table_ref.shape
    for j in range(count // LANES):
        cols = slice(j * LANES, (j + 1) * LANES)
        g = tall_ref[j * width:(j + 1) * width, :]
        state = state_ref[:, cols] + jnp.sum(g * g, axis=0, keepdims=True) * (1.0 / width)
        state_new_ref[:, cols] = state
        new_ref[:, cols] = table_ref[:, cols] - g * (LEARN_RATE * lax.rsqrt(state))


def piece_body(mine_ref, got_ref, own_ref, *other_refs):
    size = own_ref.shape[0]
    for k, ref in enumerate((own_ref, *other_refs)):
        at = slice(k * size, (k + 1) * size)
        ref[...] = (mine_ref[at, :] + got_ref[at, :].astype(F32)).astype(ref.dtype)


def left_body(near_ref, got_ref, own_ref, *other_refs):
    for k, ref in enumerate((own_ref, *other_refs)):
        at = slice(k * LANES, (k + 1) * LANES)
        ref[...] = (near_ref[:, at] + got_ref[:, at].astype(F32)).astype(ref.dtype)


def stack_body(*refs):
    size = refs[0].shape[0]
    for k, ref in enumerate(refs[:-1]):
        refs[-1][k * size:(k + 1) * size, :] = ref[...]


def chunk_body(base, first, near_ref, got_ref, *block_refs):
    for k, ref in enumerate(block_refs):
        at = (first + k) * LANES
        total = near_ref[:, at:at + LANES] + got_ref[:, at - base:at - base + LANES].astype(F32)
        ref[...] = total.astype(ref.dtype)


def sum_body(*refs):
    total = refs[0][...].astype(F32)
    for ref in refs[1:-1]:
        total = total + ref[...].astype(F32)
    refs[-1][...] = total.astype(BF)


def update_body(parts, *refs):
    part_refs, (table_ref, state_ref, new_ref, state_new_ref) = refs[:parts], refs[parts:]
    g = part_refs[0][...].astype(F32)
    for ref in part_refs[1:]:
        g = g + ref[...].astype(F32)
    width = g.shape[0]
    state = state_ref[state_ref.shape[0] - 1:, :] + jnp.sum(g * g, axis=0, keepdims=True) * (1.0 / width)
    state_new_ref[...] = state
    new_ref[...] = table_ref[:width, :] - g * (LEARN_RATE * lax.rsqrt(state))


def build(mesh):
    n_left, n_right = mesh.shape["left"], mesh.shape["right"]
    for count in (n_left, n_right):
        assert count & (count - 1) == 0 and count > 3
    outer = n_left // 2
    far_right = n_right // 2

    def swap_left(value, by):
        return lax.ppermute(value, "left", [(i, i ^ by) for i in range(n_left)])

    def swap_right(value, by):
        return lax.ppermute(value, "right", [(i, i ^ by) for i in range(n_right)])

    def next_column(value, by):
        perm = []
        for i in range(n_left):
            for r in range(n_right):
                perm.append((i * n_right + r, (i ^ by) * n_right + (r + 1) % n_right))
        return lax.ppermute(value, ("left", "right"), perm)

    def per_device(
        left_table, left_state, right_table, right_state, relation_table, relation_state,
        source_ids, target_ids, relation_ids, negative_ids,
    ):
        rows = left_table.shape[0]
        width = left_table.shape[1]
        left_t, right_t, relation_t = left_table.T, right_table.T, relation_table.T
        nrel = relation_t.shape[1]
        here_l, here_r = lax.axis_index("left"), lax.axis_index("right")
        me = here_r.astype(jnp.int32).reshape(1)
        edges = source_ids.shape[-1]
        groups = negative_ids.shape[2]
        n_rows = n_left * rows
        half = outer * rows
        one_block = shape(width, rows, dtype=BF)
        table_bf = shape(width, edges, dtype=BF)

        def cast(value, after=()):
            parts = 5 if width % 80 == 0 else 1
            scratch = [pltpu.VMEM(value.shape, F32), pltpu.SemaphoreType.DMA((parts,))]
            return call(cast_body, one_block, scratch, after=after, place=pl.ANY)(value)

        right_bf = right_t.astype(BF)
        near = [next_column(right_bf, 2 * k) for k in range(outer)]
        some = outer // 2
        cut = some * rows
        chunk = shape(width, cut, dtype=BF)
        joined_low = call(join_body, chunk, flops=COST_JOIN_LOW)(*near[:some])
        other_low = call(join_body, chunk, flops=COST_MIDDLE)(swap_left(joined_low, 1))

        ids = [source_ids, target_ids, relation_ids, negative_ids]
        longest = max(i.shape[-1] for i in ids)
        ids = [i.reshape(-1, i.shape[-1]) for i in ids]
        ids = jnp.concatenate([jnp.pad(i, ((0, 0), (0, longest - i.shape[-1]))) for i in ids], axis=0)
        left_bf = call(join_body, one_block, after=(joined_low,))(cast(left_t))
        half_left = [left_bf] + [swap_right(left_bf, 2 * k) for k in range(1, far_right)]
        place = jnp.stack([here_r, here_l]).astype(jnp.int32)
        weight, relation_bf, ids = call(
            functools.partial(count_body, far_right, outer, rows, negative_ids.shape[-1]),
            (shape(groups, n_rows, LANES), shape(width, nrel, dtype=BF), shape(*ids.shape, dtype=jnp.int32)),
            here=place,
            after=(joined_low,),
        )(ids, relation_t)
        joined = call(join_body, chunk, flops=COST_JOIN_HIGH, after=(weight,), ahead=(near[0],))(*near[some:])
        other_high = swap_left(joined, 1)
        half_joined = call(join_body, shape(width, far_right * rows, dtype=BF), after=(joined,))(*half_left)
        sibling_left = swap_right(half_joined, 1)
        moved = next_column(call(pack_body, shape(width + 8, rows), after=(half_joined,))(right_t, right_state[None, :]), 0)

        s, o, q = call(functools.partial(query_body, far_right), (table_bf, table_bf, table_bf), flops=COST_QUERY)(
            *half_left, sibling_left, relation_bf, ids
        )
        right_near, qg = call(
            functools.partial(near_body, outer),
            (shape(width, half), shape(width, edges)),
            [pltpu.VMEM((width, half), BF), pltpu.VMEM((half, edges), BF)],
        )(*near, q, weight, ids)
        right_low, qg = call(
            functools.partial(middle_body, half), (chunk, shape(width, edges)), [pltpu.VMEM((cut, edges), BF)],
        )(other_low, q, weight, ids, qg)
        tall = nrel // LANES * width
        size = -(-tall // (n_right * 16)) * 16
        piece = shape(size, LANES, dtype=BF)
        all_pieces = pltpu.VMEM((size * n_right, LANES), F32)
        m, g, mine, theirs = call(
            functools.partial(far_body, half + cut, n_right),
            (shape(cut, edges, dtype=BF), shape(width, edges), shape(far_right * size, LANES),
             shape(far_right * size, LANES, dtype=BF)),
            [pltpu.VMEM((width, nrel), F32), all_pieces],
            me,
            after=(moved,),
        )(other_high, q, weight, ids, qg, s)
        left_rows = n_right * rows
        left_half = left_rows // 2
        right_high, right_low, left_near, left_far = call(
            rest_body,
            (chunk, chunk, shape(width, left_half), shape(width, left_half, dtype=BF)),
            [pltpu.VMEM((width, left_rows), F32)],
        )(m, q, g, o, ids, right_low)

        mine, *rest = call(
            piece_body, (shape(size, LANES),) + (piece,) * (far_right - 1), flops=COST_SUM
        )(mine, swap_right(theirs, 1))
        got = [swap_right(p, 2 * (k + 1)) for k, p in enumerate(rest)]
        mine = call(sum_body, piece, flops=COST_SUM)(mine, *got)
        bit = n_left // 2
        while bit > 1:
            mine = call(sum_body, piece, flops=COST_SUM)(mine, swap_left(mine, bit))
            bit //= 2
        over_z = mine
        mine = call(sum_body, piece, flops=COST_SUM)(mine, swap_left(mine, 1))
        pieces = [mine] + [swap_right(mine, 2 * k) for k in range(1, far_right)]
        sibling = swap_right(call(stack_body, shape(far_right * size, LANES, dtype=BF))(*pieces), 1)

        left_own, *blocks = call(left_body, (shape(width, rows),) + (one_block,) * (far_right - 1))(
            left_near, swap_right(left_far, 1)
        )
        left_got = [swap_right(block, 2 * (k + 1)) for k, block in enumerate(blocks)]

        got_low = swap_left(right_low, 1)
        got_high = swap_left(right_high, 1)
        def chunk_of(first, outs, got, flops, after=()):
            base = cut if first >= some else 0
            body = functools.partial(chunk_body, base, first)
            return call(body, outs, flops=flops, after=after)(right_near, got)

        high = chunk_of(some, (one_block,) * (some - 1), got_high, COST_HIGH)
        last = chunk_of(outer - 1, (one_block,), got_high, COST_HIGH, (over_z,))
        high = [swap_left(block, 2 * (some + k)) for k, block in enumerate([*high, *last])]
        outs = (shape(width, rows),) + (one_block,) * (some - 1)
        low = chunk_of(0, outs, got_low, COST_LOW, left_got)
        right_got = [low[0], *high] + [swap_left(low[k], 2 * k) for k in range(1, some)]

        def update(got, table, state, flops=0):
            outs = (shape(width, rows), shape(1, rows))
            return call(functools.partial(update_body, len(got)), outs, flops=flops)(*got, table, state)

        left_new, left_state_new = update([left_own, *left_got], left_t, left_state[None, :])
        right_new, right_state_new = update(right_got, moved, moved, COST_UPDATE)
        relation_new, relation_state_new = call(
            functools.partial(relation_body, n_right), (shape(width, nrel), shape(1, nrel)), [all_pieces], me
        )(*pieces, sibling, relation_t, relation_state[None, :])
        return (
            left_new.T, left_state_new.reshape(-1), right_new.T, right_state_new.reshape(-1),
            relation_new.T, relation_state_new.reshape(-1),
        )

    return per_device


def solution(mesh):
    rows = P(("left", "right"), None)
    vector = P(("left", "right"))
    ids = P("left", "right", None)
    return jax.shard_map(
        build(mesh),
        mesh=mesh,
        in_specs=(rows, vector, rows, vector, P(), P(), ids, ids, ids, P("left", "right", None, None)),
        out_specs=(rows, vector, rows, vector, P(), P()),
        check_vma=False,
    )
```

```python
import functools

import jax
import jax.numpy as jnp
from jax import lax
from jax.experimental import pallas as pl
from jax.experimental.pallas import tpu as pltpu
from jax.sharding import PartitionSpec as P

LEARN_RATE = 0.1
NEG_WEIGHT = 0.03125
BF = jnp.bfloat16
F32 = jnp.float32
VMEM_LIMIT = 32 * 1024 * 1024
LANES = 128
COST_JOIN_LOW = 6e9
COST_JOIN_HIGH = 6e9
COST_UPDATE = 12e9
COST_HIGH = 12e9
COST_LOW = 12e9
COST_SUM = 1e9
COST_MIDDLE = 6e9
COST_QUERY = 6e9


def dot(a, b, a_dim, b_dim):
    return lax.dot_general(a, b, (((a_dim,), (b_dim,)), ((), ())), preferred_element_type=F32)


def hot(ids, count):
    spot = lax.broadcasted_iota(jnp.int32, (count, ids.shape[1]), 0)
    return jnp.where(spot == ids, 1.0, 0.0).astype(BF)


def step_of(size, most=512):
    return most if size % most == 0 else size


def call(body, out_shape, scratch=(), here=None, after=(), flops=0, place=pltpu.VMEM, ahead=()):
    def run(*args):
        specs = [pl.BlockSpec(memory_space=place)] * len(args)
        if here is not None:
            specs.append(pl.BlockSpec(memory_space=pltpu.SMEM))
            args = (*args, here)
        inner = body
        if after or ahead:
            first = len(ahead)
            last = first + len(args)

            def inner(*refs):
                body(*refs[first:last], *refs[last + len(after):])

            unread = pl.BlockSpec(memory_space=pl.ANY)
            specs = [unread] * len(ahead) + specs + [unread] * len(after)
            args = (*ahead, *args, *after)
        return pl.pallas_call(
            inner,
            out_shape=out_shape,
            in_specs=specs,
            scratch_shapes=list(scratch),
            compiler_params=pltpu.CompilerParams(vmem_limit_bytes=VMEM_LIMIT),
            cost_estimate=pl.CostEstimate(flops=int(flops), bytes_accessed=0, transcendentals=0),
        )(*args)

    return run


def shape(*dims, dtype=F32):
    return jax.ShapeDtypeStruct(dims, dtype)


def cast_body(in_ref, out_ref, held_ref, sems):
    rows = held_ref.shape[0] // sems.shape[0]
    copies = []
    for k in range(sems.shape[0]):
        at = slice(k * rows, (k + 1) * rows)
        copies.append(pltpu.make_async_copy(in_ref.at[at], held_ref.at[at], sems.at[k]))
        copies[-1].start()
    for k, copy in enumerate(copies):
        at = slice(k * rows, (k + 1) * rows)
        copy.wait()
        out_ref[at, :] = held_ref[at, :].astype(BF)


def count_body(far_right, outer, rows, slots, ids_ref, relation_ref, place_ref, out_ref, relation_bf_ref, local_ref):
    def local(ids, here, half):
        block = (ids // rows) ^ here
        return (block % 2 * half + block // 2) * rows + ids % rows

    ids = ids_ref[...]
    local_ref[...] = ids
    local_ref[0:1, :] = local(ids[0:1], place_ref[0], far_right)
    local_ref[1:2, :] = local(ids[1:2], place_ref[1], outer)
    for g in range(out_ref.shape[0]):
        negative = local(ids[3 + g:4 + g, :slots], place_ref[1], outer)
        for at in range(0, out_ref.shape[1], LANES):
            spot = lax.broadcasted_iota(jnp.int32, (LANES, slots), 0) + at
            total = jnp.sum(jnp.where(spot == negative, NEG_WEIGHT, 0.0), axis=1, keepdims=True)
            out_ref[g, at:at + LANES, :] = jnp.broadcast_to(total, (LANES, LANES))
    relation_bf_ref[...] = relation_ref[...].astype(BF)


def pack_body(table_ref, state_ref, pack_ref):
    width = table_ref.shape[0]
    pack_ref[:width, :] = table_ref[...]
    pack_ref[width:, :] = jnp.broadcast_to(state_ref[...], (pack_ref.shape[0] - width, LANES))


def join_body(*refs):
    out_ref = refs[-1]
    at = 0
    for ref in refs[:-1]:
        out_ref[:, at:at + ref.shape[1]] = ref[...]
        at += ref.shape[1]


def query_body(blocks, *refs):
    near_refs, refs = refs[:blocks], refs[blocks:]
    sibling_ref, relation_ref, ids_ref, s_ref, o_ref, q_ref = refs
    relation = relation_ref[...]
    half = s_ref.shape[0] // 2
    edges = s_ref.shape[1]
    step = step_of(edges)
    near = jnp.concatenate([ref[...] for ref in near_refs], axis=1)
    half_rows = near.shape[1]
    for at in range(0, edges, step):
        cols = slice(at, at + step)
        pick = hot(ids_ref[0:1, cols], 2 * half_rows)
        s = dot(near, pick[:half_rows], 1, 0) + dot(sibling_ref[...], pick[half_rows:], 1, 0)
        o = dot(relation, hot(ids_ref[2:3, cols], relation.shape[1]), 1, 0)
        s_ref[:, cols] = s.astype(BF)
        o_ref[:, cols] = o.astype(BF)
        s_re, s_im, o_re, o_im = s[:half], s[half:], o[:half], o[half:]
        q = jnp.concatenate([s_re * o_re - s_im * o_im, s_re * o_im + s_im * o_re], axis=0)
        q_ref[:, cols] = q.astype(BF)


def grad_chunk(rows_t, q_ref, weight_ref, ids_ref, base, at, step):
    count = rows_t.shape[0]
    edges = q_ref.shape[1]
    cols = slice(at, at + step)
    scores = dot(rows_t, q_ref[:, cols], 1, 0)
    spot = lax.broadcasted_iota(jnp.int32, (count, step), 0) + base
    h = jnp.where(spot == ids_ref[1:2, cols], 1.0, 0.0)
    w = weight_ref[at // (edges // weight_ref.shape[0]), base:base + count, :]
    w = jnp.concatenate([w] * (step // LANES), axis=1)
    return ((w + h) * (0.5 * jnp.tanh(0.5 * scores) + 0.5) - h).astype(BF)


def complex_back(g, other):
    half = g.shape[0] // 2
    g_re, g_im, o_re, o_im = g[:half], g[half:], other[:half], other[half:]
    return jnp.concatenate([g_re * o_re + g_im * o_im, g_im * o_re - g_re * o_im], axis=0).astype(BF)


def products(rows_ref, q_ref, weight_ref, ids_ref, m_ref, base):
    rows_t = rows_ref[...].T
    step = step_of(q_ref.shape[1] // weight_ref.shape[0])
    for at in range(0, q_ref.shape[1], step):
        m_ref[:, at:at + step] = grad_chunk(rows_t, q_ref, weight_ref, ids_ref, base, at, step)


def near_body(blocks, *refs):
    block_refs, refs = refs[:blocks], refs[blocks:]
    q_ref, weight_ref, ids_ref, right_ref, qg_ref, rows_ref, m_ref = refs
    join_body(*block_refs, rows_ref)
    products(rows_ref, q_ref, weight_ref, ids_ref, m_ref, 0)
    right_ref[...] = dot(q_ref[...], m_ref[...], 1, 1)
    qg_ref[...] = dot(rows_ref[...], m_ref[...], 1, 0)


def middle_body(base, rows_ref, q_ref, weight_ref, ids_ref, qg_ref, right_ref, qg_out_ref, m_ref):
    products(rows_ref, q_ref, weight_ref, ids_ref, m_ref, base)
    right_ref[...] = dot(q_ref[...], m_ref[...], 1, 1).astype(BF)
    qg_out_ref[...] = qg_ref[...] + dot(rows_ref[...], m_ref[...], 1, 0)


def far_body(
    base, pieces, rows_ref, q_ref, weight_ref, ids_ref, qg_ref, s_ref, here_ref,
    m_ref, g_ref, mine_ref, theirs_ref, kinds_ref, tall_ref,
):
    rows_t = rows_ref[...].T
    width, edges = qg_ref.shape
    step = step_of(edges // weight_ref.shape[0])
    for at in range(0, edges, step):
        cols = slice(at, at + step)
        m = grad_chunk(rows_t, q_ref, weight_ref, ids_ref, base, at, step)
        m_ref[:, cols] = m
        g = qg_ref[:, cols] + dot(rows_ref[...], m, 1, 0)
        g_ref[:, cols] = g
        by_kind = complex_back(g, s_ref[:, cols].astype(F32))
        kinds = dot(by_kind, hot(ids_ref[2:3, cols], kinds_ref.shape[1]), 1, 1)
        if at == 0:
            kinds_ref[...] = kinds
        else:
            kinds_ref[...] += kinds
    parts = kinds_ref.shape[1] // LANES
    for j in range(parts):
        tall_ref[j * width:(j + 1) * width, :] = kinds_ref[:, j * LANES:(j + 1) * LANES]
    rest = tall_ref.shape[0] - parts * width
    if rest:
        tall_ref[parts * width:, :] = jnp.zeros((rest, LANES), F32)
    here = here_ref[0]
    size = tall_ref.shape[0] // pieces
    for k in range(pieces):
        start = pl.multiple_of((here ^ k) * size, 16)
        piece = tall_ref[pl.ds(start, size), :]
        at = slice(k * size, (k + 1) * size)
        mine_ref[at, :] = piece
        theirs_ref[at, :] = piece.astype(BF)


def rest_body(m_ref, q_ref, g_ref, o_ref, ids_ref, low_ref, right_ref, low_out_ref, near_ref, far_ref, left_ref):
    low_out_ref[...] = low_ref[...]
    right_ref[...] = dot(q_ref[...], m_ref[...], 1, 1).astype(BF)
    edges = q_ref.shape[1]
    step = step_of(edges)
    for at in range(0, edges, step):
        cols = slice(at, at + step)
        by_source = complex_back(g_ref[:, cols], o_ref[:, cols].astype(F32))
        left = dot(by_source, hot(ids_ref[0:1, cols], left_ref.shape[1]), 1, 1)
        if at == 0:
            left_ref[...] = left
        else:
            left_ref[...] += left
    cut = left_ref.shape[1] // 2
    near_ref[...] = left_ref[:, :cut]
    far_ref[...] = left_ref[:, cut:].astype(BF)


def relation_body(pieces, own_ref, got_ref, table_ref, state_ref, here_ref, new_ref, state_new_ref, tall_ref):
    here = here_ref[0]
    second = here_ref[1] == 1
    size = tall_ref.shape[0] // pieces
    for k in range(pieces):
        start = pl.multiple_of((here ^ k) * size, 16)
        at = slice(k * size, (k + 1) * size)
        tall_ref[pl.ds(start, size), :] = jnp.where(second, own_ref[at, :].astype(F32), got_ref[at, :].astype(F32))
    width, count = table_ref.shape
    for j in range(count // LANES):
        cols = slice(j * LANES, (j + 1) * LANES)
        g = tall_ref[j * width:(j + 1) * width, :]
        state = state_ref[:, cols] + jnp.sum(g * g, axis=0, keepdims=True) * (1.0 / width)
        state_new_ref[:, cols] = state
        new_ref[:, cols] = table_ref[:, cols] - g * (LEARN_RATE * lax.rsqrt(state))


def piece_body(mine_ref, got_ref, own_ref, *other_refs):
    size = own_ref.shape[0]
    for k, ref in enumerate((own_ref, *other_refs)):
        at = slice(k * size, (k + 1) * size)
        ref[...] = (mine_ref[at, :] + got_ref[at, :].astype(F32)).astype(ref.dtype)


def left_body(near_ref, got_ref, own_ref, *other_refs):
    for k, ref in enumerate((own_ref, *other_refs)):
        at = slice(k * LANES, (k + 1) * LANES)
        ref[...] = (near_ref[:, at] + got_ref[:, at].astype(F32)).astype(ref.dtype)


def stack_body(*refs):
    size = refs[0].shape[0]
    for k, ref in enumerate(refs[:-1]):
        refs[-1][k * size:(k + 1) * size, :] = ref[...]


def chunk_body(base, first, near_ref, got_ref, *block_refs):
    for k, ref in enumerate(block_refs):
        at = (first + k) * LANES
        total = near_ref[:, at:at + LANES] + got_ref[:, at - base:at - base + LANES].astype(F32)
        ref[...] = total.astype(ref.dtype)


def sum_body(*refs):
    total = refs[0][...].astype(F32)
    for ref in refs[1:-1]:
        total = total + ref[...].astype(F32)
    refs[-1][...] = total.astype(BF)


def update_body(parts, *refs):
    part_refs, (table_ref, state_ref, new_ref, state_new_ref) = refs[:parts], refs[parts:]
    g = part_refs[0][...].astype(F32)
    for ref in part_refs[1:]:
        g = g + ref[...].astype(F32)
    width = g.shape[0]
    state = state_ref[state_ref.shape[0] - 1:, :] + jnp.sum(g * g, axis=0, keepdims=True) * (1.0 / width)
    state_new_ref[...] = state
    new_ref[...] = table_ref[:width, :] - g * (LEARN_RATE * lax.rsqrt(state))


def build(mesh):
    n_left, n_right = mesh.shape["left"], mesh.shape["right"]
    for count in (n_left, n_right):
        assert count & (count - 1) == 0 and count > 3
    outer = n_left // 2
    far_right = n_right // 2

    def swap_left(value, by):
        return lax.ppermute(value, "left", [(i, i ^ by) for i in range(n_left)])

    def swap_right(value, by):
        return lax.ppermute(value, "right", [(i, i ^ by) for i in range(n_right)])

    def between(value, core, to):
        perm = []
        for i in range(n_left):
            for r in range(core, n_right, 2):
                left, right = to(i, r)
                perm.append((i * n_right + r, left * n_right + right))
        return lax.ppermute(value, ("left", "right"), perm)

    def next_column(value, by):
        perm = []
        for i in range(n_left):
            for r in range(n_right):
                perm.append((i * n_right + r, (i ^ by) * n_right + (r + 1) % n_right))
        return lax.ppermute(value, ("left", "right"), perm)

    def per_device(
        left_table, left_state, right_table, right_state, relation_table, relation_state,
        source_ids, target_ids, relation_ids, negative_ids,
    ):
        rows = left_table.shape[0]
        width = left_table.shape[1]
        left_t, right_t, relation_t = left_table.T, right_table.T, relation_table.T
        nrel = relation_t.shape[1]
        here_l, here_r = lax.axis_index("left"), lax.axis_index("right")
        me = jnp.stack([here_r // 2, here_r % 2]).astype(jnp.int32)
        edges = source_ids.shape[-1]
        groups = negative_ids.shape[2]
        n_rows = n_left * rows
        half = outer * rows
        one_block = shape(width, rows, dtype=BF)
        table_bf = shape(width, edges, dtype=BF)

        def cast(value, after=()):
            parts = 5 if width % 80 == 0 else 1
            scratch = [pltpu.VMEM(value.shape, F32), pltpu.SemaphoreType.DMA((parts,))]
            return call(cast_body, one_block, scratch, after=after, place=pl.ANY)(value)

        right_bf = right_t.astype(BF)
        near = [next_column(right_bf, 2 * k) for k in range(outer)]
        some = outer // 2
        cut = some * rows
        chunk = shape(width, cut, dtype=BF)
        joined_low = call(join_body, chunk, flops=COST_JOIN_LOW)(*near[:some])
        other_low = call(join_body, chunk, flops=COST_MIDDLE)(swap_left(joined_low, 1))

        ids = [source_ids, target_ids, relation_ids, negative_ids]
        longest = max(i.shape[-1] for i in ids)
        ids = [i.reshape(-1, i.shape[-1]) for i in ids]
        ids = jnp.concatenate([jnp.pad(i, ((0, 0), (0, longest - i.shape[-1]))) for i in ids], axis=0)
        left_bf = cast(left_t)
        half_left = [left_bf] + [swap_right(left_bf, 2 * k) for k in range(1, far_right)]
        place = jnp.stack([here_r, here_l]).astype(jnp.int32)
        weight, relation_bf, ids = call(
            functools.partial(count_body, far_right, outer, rows, negative_ids.shape[-1]),
            (shape(groups, n_rows, LANES), shape(width, nrel, dtype=BF), shape(*ids.shape, dtype=jnp.int32)),
            here=place,
            after=(joined_low,),
        )(ids, relation_t)
        half_joined = call(join_body, shape(width, far_right * rows, dtype=BF), after=(weight,))(*half_left)
        joined = call(join_body, chunk, flops=COST_JOIN_HIGH, after=(half_joined,), ahead=(near[0],))(*near[some:])
        other_high = swap_left(joined, 1)
        sibling_left = swap_right(half_joined, 1)
        moved = next_column(call(pack_body, shape(width + 8, rows), after=(joined,))(right_t, right_state[None, :]), 0)

        s, o, q = call(functools.partial(query_body, far_right), (table_bf, table_bf, table_bf), flops=COST_QUERY)(
            *half_left, sibling_left, relation_bf, ids
        )
        right_near, qg = call(
            functools.partial(near_body, outer),
            (shape(width, half), shape(width, edges)),
            [pltpu.VMEM((width, half), BF), pltpu.VMEM((half, edges), BF)],
        )(*near, q, weight, ids)
        right_low, qg = call(
            functools.partial(middle_body, half), (chunk, shape(width, edges)), [pltpu.VMEM((cut, edges), BF)],
        )(other_low, q, weight, ids, qg)
        tall = nrel // LANES * width
        size = -(-tall // (far_right * 16)) * 16
        piece = shape(size, LANES, dtype=BF)
        all_pieces = pltpu.VMEM((size * far_right, LANES), F32)
        m, g, mine, theirs = call(
            functools.partial(far_body, half + cut, far_right),
            (shape(cut, edges, dtype=BF), shape(width, edges), shape(far_right * size, LANES),
             shape(far_right * size, LANES, dtype=BF)),
            [pltpu.VMEM((width, nrel), F32), all_pieces],
            me,
            after=(moved,),
        )(other_high, q, weight, ids, qg, s)
        left_rows = n_right * rows
        left_half = left_rows // 2
        right_high, right_low, left_near, left_far = call(
            rest_body,
            (chunk, chunk, shape(width, left_half), shape(width, left_half, dtype=BF)),
            [pltpu.VMEM((width, left_rows), F32)],
        )(m, q, g, o, ids, right_low)

        mine, *rest = call(
            piece_body, (shape(size, LANES),) + (piece,) * (far_right - 1), flops=COST_SUM
        )(mine, between(theirs, 0, lambda l, r: (l, r + 1)))
        got = [between(p, 1, lambda l, r, k=k: (l, r ^ 2 * (k + 1))) for k, p in enumerate(rest)]
        mine = call(sum_body, piece, flops=COST_SUM)(mine, *got)
        bit = n_left // 2
        while bit > 0:
            over_z = mine
            got = between(mine, 1, lambda l, r: (l ^ bit, r))
            mine = call(sum_body, piece, flops=COST_SUM)(mine, got)
            bit //= 2
        pieces = [mine] + [between(mine, 1, lambda l, r, k=k: (l, r ^ 2 * k)) for k in range(1, far_right)]
        stacked = call(stack_body, shape(far_right * size, LANES, dtype=BF))(*pieces)
        sibling = between(stacked, 1, lambda l, r: (l, r - 1))

        left_own, *blocks = call(left_body, (shape(width, rows),) + (one_block,) * (far_right - 1))(
            left_near, swap_right(left_far, 1)
        )
        left_got = [swap_right(block, 2 * (k + 1)) for k, block in enumerate(blocks)]

        got_low = swap_left(right_low, 1)
        got_high = swap_left(right_high, 1)
        def chunk_of(first, outs, got, flops, after=()):
            base = cut if first >= some else 0
            body = functools.partial(chunk_body, base, first)
            return call(body, outs, flops=flops, after=after)(right_near, got)

        high = chunk_of(some, (one_block,) * (some - 1), got_high, COST_HIGH)
        last = chunk_of(outer - 1, (one_block,), got_high, COST_HIGH, (over_z,))
        high = [swap_left(block, 2 * (some + k)) for k, block in enumerate([*high, *last])]
        outs = (shape(width, rows),) + (one_block,) * (some - 1)
        low = chunk_of(0, outs, got_low, COST_LOW, left_got)
        right_got = [low[0], *high] + [swap_left(low[k], 2 * k) for k in range(1, some)]

        def update(got, table, state, flops=0):
            outs = (shape(width, rows), shape(1, rows))
            return call(functools.partial(update_body, len(got)), outs, flops=flops)(*got, table, state)

        left_new, left_state_new = update([left_own, *left_got], left_t, left_state[None, :])
        right_new, right_state_new = update(right_got, moved, moved, COST_UPDATE)
        relation_new, relation_state_new = call(
            functools.partial(relation_body, far_right), (shape(width, nrel), shape(1, nrel)), [all_pieces], me
        )(stacked, sibling, relation_t, relation_state[None, :])
        return (
            left_new.T, left_state_new.reshape(-1), right_new.T, right_state_new.reshape(-1),
            relation_new.T, relation_state_new.reshape(-1),
        )

    return per_device


def solution(mesh):
    rows = P(("left", "right"), None)
    vector = P(("left", "right"))
    ids = P("left", "right", None)
    return jax.shard_map(
        build(mesh),
        mesh=mesh,
        in_specs=(rows, vector, rows, vector, P(), P(), ids, ids, ids, P("left", "right", None, None)),
        out_specs=(rows, vector, rows, vector, P(), P()),
        check_vma=False,
    )
```

```python
import functools

import jax
import jax.numpy as jnp
from jax import lax
from jax.experimental import pallas as pl
from jax.experimental.pallas import tpu as pltpu
from jax.sharding import PartitionSpec as P

LEARN_RATE = 0.1
NEG_WEIGHT = 0.03125
BF = jnp.bfloat16
F32 = jnp.float32
VMEM_LIMIT = 32 * 1024 * 1024
LANES = 128
COST_JOIN_LOW = 6e9
COST_JOIN_HIGH = 6e9
COST_UPDATE = 12e9
COST_HIGH = 12e9
COST_LOW = 12e9
COST_SUM = 1e9
COST_MIDDLE = 6e9
COST_QUERY = 6e9
COST_MOVED = 12e9


def dot(a, b, a_dim, b_dim):
    return lax.dot_general(a, b, (((a_dim,), (b_dim,)), ((), ())), preferred_element_type=F32)


def hot(ids, count):
    spot = lax.broadcasted_iota(jnp.int32, (count, ids.shape[1]), 0)
    return jnp.where(spot == ids, 1.0, 0.0).astype(BF)


def step_of(size, most=512):
    return most if size % most == 0 else size


def call(body, out_shape, scratch=(), here=None, after=(), flops=0, place=pltpu.VMEM, ahead=()):
    def run(*args):
        specs = [pl.BlockSpec(memory_space=place)] * len(args)
        if here is not None:
            specs.append(pl.BlockSpec(memory_space=pltpu.SMEM))
            args = (*args, here)
        inner = body
        if after or ahead:
            first = len(ahead)
            last = first + len(args)

            def inner(*refs):
                body(*refs[first:last], *refs[last + len(after):])

            unread = pl.BlockSpec(memory_space=pl.ANY)
            specs = [unread] * len(ahead) + specs + [unread] * len(after)
            args = (*ahead, *args, *after)
        return pl.pallas_call(
            inner,
            out_shape=out_shape,
            in_specs=specs,
            scratch_shapes=list(scratch),
            compiler_params=pltpu.CompilerParams(vmem_limit_bytes=VMEM_LIMIT),
            cost_estimate=pl.CostEstimate(flops=int(flops), bytes_accessed=0, transcendentals=0),
        )(*args)

    return run


def shape(*dims, dtype=F32):
    return jax.ShapeDtypeStruct(dims, dtype)


def cast_body(in_ref, out_ref, held_ref, sems):
    rows = held_ref.shape[0] // sems.shape[0]
    copies = []
    for k in range(sems.shape[0]):
        at = slice(k * rows, (k + 1) * rows)
        copies.append(pltpu.make_async_copy(in_ref.at[at], held_ref.at[at], sems.at[k]))
        copies[-1].start()
    for k, copy in enumerate(copies):
        at = slice(k * rows, (k + 1) * rows)
        copy.wait()
        out_ref[at, :] = held_ref[at, :].astype(BF)


def count_body(far_right, outer, rows, slots, ids_ref, relation_ref, place_ref, out_ref, relation_bf_ref, local_ref):
    def local(ids, here, half):
        block = (ids // rows) ^ here
        return (block % 2 * half + block // 2) * rows + ids % rows

    ids = ids_ref[...]
    local_ref[...] = ids
    local_ref[0:1, :] = local(ids[0:1], place_ref[0], far_right)
    local_ref[1:2, :] = local(ids[1:2], place_ref[1], outer)
    for g in range(out_ref.shape[0]):
        negative = local(ids[3 + g:4 + g, :slots], place_ref[1], outer)
        for at in range(0, out_ref.shape[1], LANES):
            spot = lax.broadcasted_iota(jnp.int32, (LANES, slots), 0) + at
            total = jnp.sum(jnp.where(spot == negative, NEG_WEIGHT, 0.0), axis=1, keepdims=True)
            out_ref[g, at:at + LANES, :] = jnp.broadcast_to(total, (LANES, LANES))
    relation_bf_ref[...] = relation_ref[...].astype(BF)


def pack_body(table_ref, state_ref, pack_ref):
    width = table_ref.shape[0]
    pack_ref[:width, :] = table_ref[...]
    pack_ref[width:, :] = jnp.broadcast_to(state_ref[...], (pack_ref.shape[0] - width, LANES))


def join_body(*refs):
    out_ref = refs[-1]
    at = 0
    for ref in refs[:-1]:
        out_ref[:, at:at + ref.shape[1]] = ref[...]
        at += ref.shape[1]


def query_body(blocks, *refs):
    near_refs, refs = refs[:blocks], refs[blocks:]
    sibling_ref, relation_ref, ids_ref, s_ref, o_ref, q_ref = refs
    relation = relation_ref[...]
    half = s_ref.shape[0] // 2
    edges = s_ref.shape[1]
    step = step_of(edges)
    near = jnp.concatenate([ref[...] for ref in near_refs], axis=1)
    half_rows = near.shape[1]
    for at in range(0, edges, step):
        cols = slice(at, at + step)
        pick = hot(ids_ref[0:1, cols], 2 * half_rows)
        s = dot(near, pick[:half_rows], 1, 0) + dot(sibling_ref[...], pick[half_rows:], 1, 0)
        o = dot(relation, hot(ids_ref[2:3, cols], relation.shape[1]), 1, 0)
        s_ref[:, cols] = s.astype(BF)
        o_ref[:, cols] = o.astype(BF)
        s_re, s_im, o_re, o_im = s[:half], s[half:], o[:half], o[half:]
        q = jnp.concatenate([s_re * o_re - s_im * o_im, s_re * o_im + s_im * o_re], axis=0)
        q_ref[:, cols] = q.astype(BF)


def grad_chunk(rows_t, q_ref, weight_ref, ids_ref, base, at, step):
    count = rows_t.shape[0]
    edges = q_ref.shape[1]
    cols = slice(at, at + step)
    scores = dot(rows_t, q_ref[:, cols], 1, 0)
    spot = lax.broadcasted_iota(jnp.int32, (count, step), 0) + base
    h = jnp.where(spot == ids_ref[1:2, cols], 1.0, 0.0)
    w = weight_ref[at // (edges // weight_ref.shape[0]), base:base + count, :]
    w = jnp.concatenate([w] * (step // LANES), axis=1)
    return ((w + h) * (0.5 * jnp.tanh(0.5 * scores) + 0.5) - h).astype(BF)


def complex_back(g, other):
    half = g.shape[0] // 2
    g_re, g_im, o_re, o_im = g[:half], g[half:], other[:half], other[half:]
    return jnp.concatenate([g_re * o_re + g_im * o_im, g_im * o_re - g_re * o_im], axis=0).astype(BF)


def products(rows_ref, q_ref, weight_ref, ids_ref, m_ref, base):
    rows_t = rows_ref[...].T
    step = step_of(q_ref.shape[1] // weight_ref.shape[0])
    for at in range(0, q_ref.shape[1], step):
        m_ref[:, at:at + step] = grad_chunk(rows_t, q_ref, weight_ref, ids_ref, base, at, step)


def near_body(blocks, *refs):
    block_refs, refs = refs[:blocks], refs[blocks:]
    q_ref, weight_ref, ids_ref, right_ref, qg_ref, rows_ref, m_ref = refs
    join_body(*block_refs, rows_ref)
    products(rows_ref, q_ref, weight_ref, ids_ref, m_ref, 0)
    right_ref[...] = dot(q_ref[...], m_ref[...], 1, 1)
    qg_ref[...] = dot(rows_ref[...], m_ref[...], 1, 0)


def middle_body(base, rows_ref, q_ref, weight_ref, ids_ref, qg_ref, right_ref, qg_out_ref, m_ref):
    products(rows_ref, q_ref, weight_ref, ids_ref, m_ref, base)
    right_ref[...] = dot(q_ref[...], m_ref[...], 1, 1).astype(BF)
    qg_out_ref[...] = qg_ref[...] + dot(rows_ref[...], m_ref[...], 1, 0)


def far_body(
    base, pieces, rows_ref, q_ref, weight_ref, ids_ref, qg_ref, s_ref, here_ref,
    m_ref, g_ref, mine_ref, theirs_ref, kinds_ref, tall_ref,
):
    rows_t = rows_ref[...].T
    width, edges = qg_ref.shape
    step = step_of(edges // weight_ref.shape[0])
    for at in range(0, edges, step):
        cols = slice(at, at + step)
        m = grad_chunk(rows_t, q_ref, weight_ref, ids_ref, base, at, step)
        m_ref[:, cols] = m
        g = qg_ref[:, cols] + dot(rows_ref[...], m, 1, 0)
        g_ref[:, cols] = g
        by_kind = complex_back(g, s_ref[:, cols].astype(F32))
        kinds = dot(by_kind, hot(ids_ref[2:3, cols], kinds_ref.shape[1]), 1, 1)
        if at == 0:
            kinds_ref[...] = kinds
        else:
            kinds_ref[...] += kinds
    parts = kinds_ref.shape[1] // LANES
    for j in range(parts):
        tall_ref[j * width:(j + 1) * width, :] = kinds_ref[:, j * LANES:(j + 1) * LANES]
    rest = tall_ref.shape[0] - parts * width
    if rest:
        tall_ref[parts * width:, :] = jnp.zeros((rest, LANES), F32)
    here = here_ref[0]
    size = tall_ref.shape[0] // pieces
    for k in range(pieces):
        start = pl.multiple_of((here ^ k) * size, 16)
        piece = tall_ref[pl.ds(start, size), :]
        at = slice(k // 2 * size, (k // 2 + 1) * size)
        if k % 2:
            theirs_ref[at, :] = piece.astype(BF)
        else:
            mine_ref[at, :] = piece


def rest_body(m_ref, q_ref, g_ref, o_ref, ids_ref, low_ref, right_ref, low_out_ref, near_ref, far_ref, left_ref):
    low_out_ref[...] = low_ref[...]
    right_ref[...] = dot(q_ref[...], m_ref[...], 1, 1).astype(BF)
    edges = q_ref.shape[1]
    step = step_of(edges)
    for at in range(0, edges, step):
        cols = slice(at, at + step)
        by_source = complex_back(g_ref[:, cols], o_ref[:, cols].astype(F32))
        left = dot(by_source, hot(ids_ref[0:1, cols], left_ref.shape[1]), 1, 1)
        if at == 0:
            left_ref[...] = left
        else:
            left_ref[...] += left
    cut = left_ref.shape[1] // 2
    near_ref[...] = left_ref[:, :cut]
    far_ref[...] = left_ref[:, cut:].astype(BF)


def relation_body(pieces, *refs):
    piece_refs, refs = refs[:pieces // 2], refs[pieces // 2:]
    sibling_ref, table_ref, state_ref, here_ref, new_ref, state_new_ref, tall_ref = refs
    here = here_ref[0]
    size = tall_ref.shape[0] // pieces
    for k in range(pieces):
        start = pl.multiple_of((here ^ k) * size, 16)
        piece = sibling_ref[k // 2 * size:(k // 2 + 1) * size, :] if k % 2 else piece_refs[k // 2][...]
        tall_ref[pl.ds(start, size), :] = piece.astype(F32)
    width, count = table_ref.shape
    for j in range(count // LANES):
        cols = slice(j * LANES, (j + 1) * LANES)
        g = tall_ref[j * width:(j + 1) * width, :]
        state = state_ref[:, cols] + jnp.sum(g * g, axis=0, keepdims=True) * (1.0 / width)
        state_new_ref[:, cols] = state
        new_ref[:, cols] = table_ref[:, cols] - g * (LEARN_RATE * lax.rsqrt(state))


def piece_body(mine_ref, got_ref, own_ref, *other_refs):
    size = own_ref.shape[0]
    for k, ref in enumerate((own_ref, *other_refs)):
        at = slice(k * size, (k + 1) * size)
        ref[...] = (mine_ref[at, :] + got_ref[at, :].astype(F32)).astype(ref.dtype)


def left_body(near_ref, got_ref, own_ref, *other_refs):
    for k, ref in enumerate((own_ref, *other_refs)):
        at = slice(k * LANES, (k + 1) * LANES)
        ref[...] = (near_ref[:, at] + got_ref[:, at].astype(F32)).astype(ref.dtype)


def stack_body(*refs):
    size = refs[0].shape[0]
    for k, ref in enumerate(refs[:-1]):
        refs[-1][k * size:(k + 1) * size, :] = ref[...]


def chunk_body(base, first, near_ref, got_ref, *block_refs):
    for k, ref in enumerate(block_refs):
        at = (first + k) * LANES
        total = near_ref[:, at:at + LANES] + got_ref[:, at - base:at - base + LANES].astype(F32)
        ref[...] = total.astype(ref.dtype)


def sum_body(*refs):
    total = refs[0][...].astype(F32)
    for ref in refs[1:-1]:
        total = total + ref[...].astype(F32)
    refs[-1][...] = total.astype(BF)


def update_body(parts, *refs):
    part_refs, (table_ref, state_ref, new_ref, state_new_ref) = refs[:parts], refs[parts:]
    g = part_refs[0][...].astype(F32)
    for ref in part_refs[1:]:
        g = g + ref[...].astype(F32)
    width = g.shape[0]
    state = state_ref[state_ref.shape[0] - 1:, :] + jnp.sum(g * g, axis=0, keepdims=True) * (1.0 / width)
    state_new_ref[...] = state
    new_ref[...] = table_ref[:width, :] - g * (LEARN_RATE * lax.rsqrt(state))


def build(mesh):
    n_left, n_right = mesh.shape["left"], mesh.shape["right"]
    for count in (n_left, n_right):
        assert count & (count - 1) == 0 and count > 3
    outer = n_left // 2
    far_right = n_right // 2

    def swap_left(value, by):
        return lax.ppermute(value, "left", [(i, i ^ by) for i in range(n_left)])

    def swap_right(value, by):
        return lax.ppermute(value, "right", [(i, i ^ by) for i in range(n_right)])

    def next_column(value, by):
        perm = []
        for i in range(n_left):
            for r in range(n_right):
                perm.append((i * n_right + r, (i ^ by) * n_right + (r + 1) % n_right))
        return lax.ppermute(value, ("left", "right"), perm)

    def per_device(
        left_table, left_state, right_table, right_state, relation_table, relation_state,
        source_ids, target_ids, relation_ids, negative_ids,
    ):
        rows = left_table.shape[0]
        width = left_table.shape[1]
        left_t, right_t, relation_t = left_table.T, right_table.T, relation_table.T
        nrel = relation_t.shape[1]
        here_l, here_r = lax.axis_index("left"), lax.axis_index("right")
        me = here_r.astype(jnp.int32).reshape(1)
        edges = source_ids.shape[-1]
        groups = negative_ids.shape[2]
        n_rows = n_left * rows
        half = outer * rows
        one_block = shape(width, rows, dtype=BF)
        table_bf = shape(width, edges, dtype=BF)

        def cast(value, after=()):
            parts = 5 if width % 80 == 0 else 1
            scratch = [pltpu.VMEM(value.shape, F32), pltpu.SemaphoreType.DMA((parts,))]
            return call(cast_body, one_block, scratch, after=after, place=pl.ANY)(value)

        right_bf = right_t.astype(BF)
        near = [next_column(right_bf, 2 * k) for k in range(outer)]
        some = outer // 2
        cut = some * rows
        chunk = shape(width, cut, dtype=BF)
        joined_low = call(join_body, chunk, flops=COST_JOIN_LOW)(*near[:some])
        other_low = call(join_body, chunk, flops=COST_MIDDLE)(swap_left(joined_low, 1))

        ids = [source_ids, target_ids, relation_ids, negative_ids]
        longest = max(i.shape[-1] for i in ids)
        ids = [i.reshape(-1, i.shape[-1]) for i in ids]
        ids = jnp.concatenate([jnp.pad(i, ((0, 0), (0, longest - i.shape[-1]))) for i in ids], axis=0)
        left_bf = cast(left_t)
        half_left = [left_bf] + [swap_right(left_bf, 2 * k) for k in range(1, far_right)]
        place = jnp.stack([here_r, here_l]).astype(jnp.int32)
        weight, relation_bf, ids = call(
            functools.partial(count_body, far_right, outer, rows, negative_ids.shape[-1]),
            (shape(groups, n_rows, LANES), shape(width, nrel, dtype=BF), shape(*ids.shape, dtype=jnp.int32)),
            here=place,
            after=(joined_low,),
        )(ids, relation_t)
        half_joined = call(join_body, shape(width, far_right * rows, dtype=BF), after=(weight,))(*half_left)
        joined = call(join_body, chunk, flops=COST_JOIN_HIGH, after=(half_joined,), ahead=(near[0],))(*near[some:])
        other_high = swap_left(joined, 1)
        sibling_left = swap_right(half_joined, 1)
        pack = call(pack_body, shape(width + 8, rows), after=(joined,))(right_t, right_state[None, :])
        moved = call(join_body, shape(width + 8, rows), flops=COST_MOVED)(next_column(pack, 0))

        s, o, q = call(functools.partial(query_body, far_right), (table_bf, table_bf, table_bf), flops=COST_QUERY)(
            *half_left, sibling_left, relation_bf, ids
        )
        right_near, qg = call(
            functools.partial(near_body, outer),
            (shape(width, half), shape(width, edges)),
            [pltpu.VMEM((width, half), BF), pltpu.VMEM((half, edges), BF)],
        )(*near, q, weight, ids)
        right_low, qg = call(
            functools.partial(middle_body, half), (chunk, shape(width, edges)), [pltpu.VMEM((cut, edges), BF)],
        )(other_low, q, weight, ids, qg)
        tall = nrel // LANES * width
        size = -(-tall // (n_right * 16)) * 16
        piece = shape(size, LANES, dtype=BF)
        all_pieces = pltpu.VMEM((size * n_right, LANES), F32)
        m, g, mine, theirs = call(
            functools.partial(far_body, half + cut, n_right),
            (shape(cut, edges, dtype=BF), shape(width, edges), shape(far_right * size, LANES),
             shape(far_right * size, LANES, dtype=BF)),
            [pltpu.VMEM((width, nrel), F32), all_pieces],
            me,
        )(other_high, q, weight, ids, qg, s)
        left_rows = n_right * rows
        left_half = left_rows // 2
        right_high, right_low, left_near, left_far = call(
            rest_body,
            (chunk, chunk, shape(width, left_half), shape(width, left_half, dtype=BF)),
            [pltpu.VMEM((width, left_rows), F32)],
            after=(moved,),
        )(m, q, g, o, ids, right_low)

        mine, *rest = call(
            piece_body, (shape(size, LANES),) + (piece,) * (far_right - 1), flops=COST_SUM
        )(mine, swap_right(theirs, 1))
        got = [swap_right(p, 2 * (k + 1)) for k, p in enumerate(rest)]
        mine = call(sum_body, piece, flops=COST_SUM)(mine, *got)
        bit = n_left // 2
        while bit > 1:
            mine = call(sum_body, piece, flops=COST_SUM)(mine, swap_left(mine, bit))
            bit //= 2
        over_z = mine
        mine = call(sum_body, piece, flops=COST_SUM)(mine, swap_left(mine, 1))
        pieces = [mine] + [swap_right(mine, 2 * k) for k in range(1, far_right)]
        sibling = swap_right(call(stack_body, shape(far_right * size, LANES, dtype=BF))(*pieces), 1)

        left_own, *blocks = call(left_body, (shape(width, rows),) + (one_block,) * (far_right - 1))(
            left_near, swap_right(left_far, 1)
        )
        left_got = [swap_right(block, 2 * (k + 1)) for k, block in enumerate(blocks)]

        got_low = swap_left(right_low, 1)
        got_high = swap_left(right_high, 1)
        def chunk_of(first, outs, got, flops, after=()):
            base = cut if first >= some else 0
            body = functools.partial(chunk_body, base, first)
            return call(body, outs, flops=flops, after=after)(right_near, got)

        high = chunk_of(some, (one_block,) * (some - 1), got_high, COST_HIGH)
        last = chunk_of(outer - 1, (one_block,), got_high, COST_HIGH, (over_z,))
        high = [swap_left(block, 2 * (some + k)) for k, block in enumerate([*high, *last])]
        outs = (shape(width, rows),) + (one_block,) * (some - 1)
        low = chunk_of(0, outs, got_low, COST_LOW, left_got)
        right_got = [low[0], *high] + [swap_left(low[k], 2 * k) for k in range(1, some)]

        def update(got, table, state, flops=0):
            outs = (shape(width, rows), shape(1, rows))
            return call(functools.partial(update_body, len(got)), outs, flops=flops)(*got, table, state)

        left_new, left_state_new = update([left_own, *left_got], left_t, left_state[None, :])
        right_new, right_state_new = update(right_got, moved, moved, COST_UPDATE)
        relation_new, relation_state_new = call(
            functools.partial(relation_body, n_right), (shape(width, nrel), shape(1, nrel)), [all_pieces], me
        )(*pieces, sibling, relation_t, relation_state[None, :])
        return (
            left_new.T, left_state_new.reshape(-1), right_new.T, right_state_new.reshape(-1),
            relation_new.T, relation_state_new.reshape(-1),
        )

    return per_device


def solution(mesh):
    rows = P(("left", "right"), None)
    vector = P(("left", "right"))
    ids = P("left", "right", None)
    return jax.shard_map(
        build(mesh),
        mesh=mesh,
        in_specs=(rows, vector, rows, vector, P(), P(), ids, ids, ids, P("left", "right", None, None)),
        out_specs=(rows, vector, rows, vector, P(), P()),
        check_vma=False,
    )
```
